32 devices in a mesh: dp: 4 (over y, x), ctx: 8 (over z, core).
Axes of the slice: x: 2, y: 2, z: 4, core: 2. Of those that a mesh axis runs over, the one named last changes fastest.
Arguments:
- hidden_in: bfloat16 [4, 1024, 1600], P('dp', 'ctx'), may hold values from -6 to 6
- qkv_weight: bfloat16 [7680000], P(('dp', 'ctx')), may hold values from -0.15625 to 0.15625
- proj_weight: bfloat16 [2560000], P(('dp', 'ctx')), may hold values from -0.625 to 0.625
- fc_weight: bfloat16 [10240000], P(('dp', 'ctx')), may hold values from -0.15625 to 0.15625
- out_weight: bfloat16 [10240000], P(('dp', 'ctx')), may hold values from -0.078125 to 0.078125
- small_params: bfloat16 [19200], P(('dp', 'ctx')), may hold values from -0.9 to 1.5
- segments: int32 [4, 1024], P('dp'), may hold values from 0 to 5, as said below
- cotangent: bfloat16 [4, 1024, 1600], P('dp', 'ctx'), may hold values from -6 to 6
Outputs:
- output: float32 [4, 1024, 1600], P('dp', 'ctx')
- grad_input: float32 [4, 1024, 1600], P('dp', 'ctx')
- grad_qkv: float32 [7680000], P(('dp', 'ctx'))
- grad_proj: float32 [2560000], P(('dp', 'ctx'))
- grad_fc: float32 [10240000], P(('dp', 'ctx'))
- grad_out: float32 [10240000], P(('dp', 'ctx'))
- grad_small: float32 [19200], P(('dp', 'ctx'))
The draws below stay inside these ranges and needn't reach their ends.
Inputs may be any that keep to these rules, and one draw needn't show every extreme that they name: `segments`: each sequence is packed with documents end to end, numbered 0, 1, 2, ... from its start; every document has at least 200 positions except that the last one of a sequence may be cut short by the sequence's end. In one sequence the first document reaches into the positions of every device of ctx; another sequence is made of documents of exactly 200 positions.
All inputs are finite; a program needn't handle non-finite values.
Results may differ from the reference program's by a relative error of at most 0.0095.
Values may be sent and summed in bfloat16 or wider, within the bound.
A program may use at most 512 MiB of HBM per device.

```python
from functools import partial
import jax
import jax.numpy as jnp
from jax import lax

D = 1600
HEADS = 25
HEAD_DIM = 64
FF = 6400
TOK_SEQ = 128
MIN_DOC = 200
SEQUENCES = 4
LENGTH = 1024
VECTOR_LEN = 19200


def draw_small_params(key, part):
    key = jax.random.fold_in(key, 11)
    first_key, second_key = jax.random.split(key)
    base = jnp.clip(jax.random.normal(first_key, (VECTOR_LEN,), jnp.float32), -3.0, 3.0)
    gains = jax.random.uniform(second_key, (VECTOR_LEN,), jnp.float32, 0.7, 1.3)
    index = jnp.arange(VECTOR_LEN)
    is_gain = (index < D) | (index >= 5 * D) & (index < 6 * D)
    is_value_bias = (index >= 3 * D) & (index < 4 * D)
    scale = jnp.where(is_value_bias, 0.08, 0.3)
    return jnp.where(is_gain, gains, base * scale).astype(jnp.bfloat16)


def draw_segments(key, part):
    key = jax.random.fold_in(key, 5)
    length_key, chosen_key, long_key = jax.random.split(key, 3)
    doc_count = LENGTH // MIN_DOC + 1
    doc_lengths = jax.random.randint(length_key, (SEQUENCES, doc_count), MIN_DOC, LENGTH + 1)
    chosen = jax.random.randint(chosen_key, (), 0, SEQUENCES)
    short_seq = (chosen + 1) % SEQUENCES
    seq_index = jnp.arange(SEQUENCES)
    doc_lengths = jnp.where((seq_index == short_seq)[:, None], MIN_DOC, doc_lengths)
    long_first = jax.random.randint(long_key, (SEQUENCES,), LENGTH - TOK_SEQ + 1, LENGTH + 1)
    first_col = jnp.where(seq_index == chosen, long_first, doc_lengths[:, 0])
    doc_lengths = jnp.concatenate([first_col[:, None], doc_lengths[:, 1:]], 1)
    doc_ends = jnp.cumsum(doc_lengths, 1)
    positions = jnp.arange(LENGTH)
    passed = (positions[None, :, None] >= doc_ends[:, None, :]).astype(jnp.int32)
    return jnp.sum(passed, -1).astype(jnp.int32)


def levels(key, extent, cuts, smallest, high):
    def one(dim, blocks):
        steps = jax.random.uniform(jax.random.fold_in(jax.random.fold_in(key, 6), dim), (blocks,), jnp.float32, smallest / len(cuts), high / len(cuts))
        return jnp.repeat(jnp.exp(steps), extent[dim] // blocks).reshape((-1,) + (1,) * (len(extent) - dim - 1))

    factor_of = one(*cuts[0])
    for cut in cuts[1:]:
        factor_of = factor_of * one(*cut)
    return factor_of


def gaussian(stream_key, shape, scale, bound, cuts=(), kind=jnp.bfloat16):
    drawn = scale * jax.random.normal(stream_key, shape, jnp.float32)
    if cuts:
        drawn = drawn * levels(stream_key, shape, cuts, -0.22, 0.18)
    return jnp.clip(drawn, -bound, bound).astype(kind)


def setup_inputs(seed: int = 0) -> dict:
    key_list = jax.random.split(jax.random.key(seed), 9)
    return {
        "hidden_in": gaussian(key_list[0], (SEQUENCES, LENGTH, D), 1.0, 6.0, ((0, 4), (1, 8))),
        "qkv_weight": gaussian(key_list[1], (3 * D * D,), D ** -0.5, 0.15625, ((0, 32),)),
        "proj_weight": gaussian(key_list[2], (D * D,), (max(D // 16, 1)) ** -0.5, 0.625, ((0, 32),)),
        "fc_weight": gaussian(key_list[3], (D * FF,), D ** -0.5, 0.15625, ((0, 32),)),
        "out_weight": gaussian(key_list[4], (FF * D,), FF ** -0.5, 0.078125, ((0, 32),)),
        "small_params": draw_small_params(jax.random.fold_in(key_list[8], 71), 0),
        "segments": draw_segments(jax.random.fold_in(key_list[8], 71), 0),
        "cotangent": gaussian(key_list[7], (SEQUENCES, LENGTH, D), 1.0, 6.0, ((0, 4), (1, 8))),
    }


EPSILON = 1e-05
PRECISION = lax.Precision.HIGHEST

@jax.custom_vjp
def low(v):
    return lax.optimization_barrier(v.astype(jnp.bfloat16)).astype(jnp.float32)

@jax.custom_vjp
def low_back(v):
    return v

def low_keep(v):
    return (low(v), None)

def low_pass(kept, grad):
    return (grad,)

def back_keep(v):
    return (v, None)

def back_low(kept, grad):
    return (low(grad),)
low.defvjp(low_keep, low_pass)
low_back.defvjp(back_keep, back_low)

def norm_affine(hidden_rows, gain, shift):
    centre = hidden_rows - lax.optimization_barrier(jnp.mean(hidden_rows, -1, keepdims=True))
    spread = lax.optimization_barrier(jnp.mean(centre * centre, -1, keepdims=True))
    return centre * lax.rsqrt(spread + EPSILON) * gain + shift

def gelu_tanh(inner):
    return 0.5 * inner * (1.0 + jnp.tanh(0.7978845608028654 * (inner + 0.044715 * inner * inner * inner)))

def unpack(vector):
    return (vector[0:D], vector[D:2 * D], vector[2 * D:3 * D], vector[3 * D:4 * D], vector[4 * D:5 * D], vector[5 * D:6 * D], vector[6 * D:7 * D], vector[7 * D:7 * D + FF], vector[7 * D + FF:8 * D + FF])

def matmul(left, right):
    return jnp.dot(left, right, precision=PRECISION, preferred_element_type=jnp.float32)

def head_attention(allowed, query_head, key_head, value_head):
    scores = low_back(matmul(query_head, key_head.T) * HEAD_DIM ** (-0.5))
    scores = jnp.where(allowed, scores, -1e+30)
    row_max = lax.optimization_barrier(jnp.max(scores, -1, keepdims=True))
    expo = jnp.exp(scores - row_max)
    probs = expo / lax.optimization_barrier(jnp.sum(expo, -1, keepdims=True))
    return matmul(low(probs), value_head)

def layer(seq_rows, seq_segments, mat_qkv, mat_proj, mat_fc, mat_out, vector):
    gain_one, shift_one, bias_query, bias_value, bias_proj, gain_two, shift_two, bias_fc, bias_out = unpack(vector)
    seq_len = seq_rows.shape[0]
    attn_in = low(norm_affine(seq_rows, gain_one, shift_one))
    qkv_rows = matmul(attn_in, mat_qkv.reshape(D, 3 * D))
    queries = low_back(low(qkv_rows[:, :D] + bias_query))
    key_rows = low_back(low(qkv_rows[:, D:2 * D]))
    value_rows = low_back(low(qkv_rows[:, 2 * D:] + bias_value))
    positions = jnp.arange(seq_len)
    allowed = (seq_segments[:, None] == seq_segments[None, :]) & (positions[:, None] >= positions[None, :])

    def to_heads(matrix):
        return matrix.reshape(seq_len, HEADS, HEAD_DIM).transpose(1, 0, 2)
    checked = jax.checkpoint(partial(head_attention, allowed))

    def per_head(triple):
        return checked(triple[0], triple[1], triple[2])
    attention = lax.map(per_head, (to_heads(queries), to_heads(key_rows), to_heads(value_rows)))
    attention = attention.transpose(1, 0, 2).reshape(seq_len, D)
    mixed = low_back(low(attention))
    resid = seq_rows + low_back(matmul(mixed, mat_proj.reshape(D, D))) + bias_proj
    ffn_in = low(norm_affine(resid, gain_two, shift_two))
    pre_act = low_back(matmul(ffn_in, mat_fc.reshape(D, FF)) + bias_fc)
    act_rows = low(gelu_tanh(pre_act))
    return resid + matmul(act_rows, mat_out.reshape(FF, D)) + bias_out

def reference(hidden_in, qkv_weight, proj_weight, fc_weight, out_weight, small_params, segments, cotangent):
    params = (qkv_weight.astype(jnp.float32), proj_weight.astype(jnp.float32), fc_weight.astype(jnp.float32), out_weight.astype(jnp.float32), small_params.astype(jnp.float32))

    def one_sequence(totals, item):
        seq_rows, seq_segments, seq_cot = item

        def layer_of(rows_in, mat_qkv, mat_proj, mat_fc, mat_out, vector):
            return layer(rows_in, seq_segments, mat_qkv, mat_proj, mat_fc, mat_out, vector)
        layer_out, pull_back = jax.vjp(layer_of, seq_rows.astype(jnp.float32), *params)
        grads = pull_back(seq_cot.astype(jnp.float32))
        totals = tuple((total + grad for total, grad in zip(totals, grads[1:])))
        return (totals, (layer_out, grads[0]))
    start = tuple((jnp.zeros(param.shape, jnp.float32) for param in params))
    totals, (outputs, grad_rows) = lax.scan(one_sequence, start, (hidden_in, segments, cotangent))
    return (outputs, grad_rows, totals[0], totals[1], totals[2], totals[3], totals[4])
```

```python
import functools

import jax
import jax.numpy as jnp
from jax import lax
from jax.experimental import pallas as pl
from jax.experimental.pallas import tpu as pltpu
from jax.sharding import PartitionSpec as P

D = 1600
HEADS = 25
HEAD_DIM = 64
FF = 6400
EPSILON = 1e-05
LOW = jnp.bfloat16
WIDE = jnp.float32
MIB = 1024 * 1024


def dot(left, right, left_dim=1, right_dim=0):
    return lax.dot_general(
        left, right, (((left_dim,), (right_dim,)), ((), ())), preferred_element_type=WIDE
    )


def normalize(rows):
    centre = rows - jnp.mean(rows, -1, keepdims=True)
    spread = jnp.mean(centre * centre, -1, keepdims=True)
    scale = lax.rsqrt(spread + EPSILON)
    return centre * scale, scale


def norm_back(normed, scale, gain, incoming):
    scaled = gain * incoming
    return scale * (
        scaled
        - jnp.mean(scaled, -1, keepdims=True)
        - normed * jnp.mean(scaled * normed, -1, keepdims=True)
    )


def head_lanes(head, width):
    lane = lax.broadcasted_iota(jnp.int32, (1, width), 1)
    return (lane // HEAD_DIM) == head


def allowed_scores(scores, doc_start, first_query, keys, block):
    key_pos = lax.broadcasted_iota(jnp.int32, (keys, block), 0)
    query_pos = first_query + lax.broadcasted_iota(jnp.int32, (keys, block), 1)
    seen = (key_pos >= doc_start) & (key_pos <= query_pos)
    return jnp.where(seen, scores, -1e30)


def attend_kernel(block, qkv_ref, start_ref, mixed_ref, stat_ref, value_t):
    length = qkv_ref.shape[0]
    width = mixed_ref.shape[1]
    slots = width // HEAD_DIM
    value_t[...] = qkv_ref[:, 2 * width : 3 * width].astype(WIDE).T.astype(LOW)
    for index in range(length // block):
        keys = (index + 1) * block
        rows = pl.ds(index * block, block)
        key_rows = qkv_ref[0:keys, width : 2 * width]
        doc_start = start_ref[0:1, rows]
        outs = []
        for head in range(slots):
            query = jnp.where(
                head_lanes(head, width), qkv_ref[rows, 0:width] * LOW(HEAD_DIM**-0.5), LOW(0)
            )
            scores = dot(key_rows, query, 1, 1)
            scores = allowed_scores(scores, doc_start, index * block, keys, block)
            top = jnp.max(scores, 0, keepdims=True)
            expo = jnp.exp(scores - top)
            total = jnp.sum(expo, 0, keepdims=True)
            head_rows = slice(head * HEAD_DIM, (head + 1) * HEAD_DIM)
            out = dot(value_t[head_rows, 0:keys], expo.astype(LOW))
            outs.append(out / total)
            stat_ref[head : head + 1, rows] = top + jnp.log(total)
        mixed_ref[rows, :] = jnp.concatenate(outs, 0).T.astype(LOW)


def attend(qkv, doc_start, block):
    length, width = qkv.shape[0], qkv.shape[1] // 3
    return pl.pallas_call(
        functools.partial(attend_kernel, block),
        out_shape=(
            jax.ShapeDtypeStruct((length, width), LOW),
            jax.ShapeDtypeStruct((8, length), WIDE),
        ),
        scratch_shapes=[pltpu.VMEM((width, length), LOW)],
        compiler_params=pltpu.CompilerParams(vmem_limit_bytes=48 * MIB),
        name="attend",
    )(qkv, doc_start)


def attend_back_kernel(
    block, qkv_ref, start_ref, stat_ref, mixed_ref, grad_ref, out_ref, key_t, key_grad, value_grad
):
    length = qkv_ref.shape[0]
    width = mixed_ref.shape[1]
    slots = width // HEAD_DIM
    scale = HEAD_DIM**-0.5
    key_t[...] = qkv_ref[:, width : 2 * width].astype(WIDE).T.astype(LOW)
    key_grad[...] = jnp.zeros_like(key_grad)
    value_grad[...] = jnp.zeros_like(value_grad)
    for index in range(length // block):
        keys = (index + 1) * block
        rows = pl.ds(index * block, block)
        key_rows = qkv_ref[0:keys, width : 2 * width]
        value_rows = qkv_ref[0:keys, 2 * width : 3 * width]
        doc_start = start_ref[0:1, rows]
        outs = []
        for head in range(slots):
            lanes = head_lanes(head, width)
            head_rows = slice(head * HEAD_DIM, (head + 1) * HEAD_DIM)
            query = jnp.where(lanes, qkv_ref[rows, 0:width] * LOW(scale), LOW(0))
            grad = jnp.where(lanes, grad_ref[rows, :], LOW(0))
            scores = dot(key_rows, query, 1, 1)
            scores = allowed_scores(scores, doc_start, index * block, keys, block)
            probs = jnp.exp(scores - stat_ref[head : head + 1, rows])
            grad_probs = dot(value_rows, grad, 1, 1)
            delta = jnp.sum(probs * grad_probs, 0, keepdims=True)
            grad_scores = (probs * (grad_probs - delta)).astype(LOW)
            value_grad[0:keys, :] += dot(probs.astype(LOW), grad)
            key_grad[0:keys, :] += dot(grad_scores, query)
            outs.append(dot(key_t[head_rows, 0:keys], grad_scores))
        out_ref[rows, 0:width] = (jnp.concatenate(outs, 0).T * scale).astype(LOW)
    out_ref[:, width : 2 * width] = key_grad[...].astype(LOW)
    out_ref[:, 2 * width : 3 * width] = value_grad[...].astype(LOW)


def attend_back(qkv, doc_start, stats, mixed, grad, block):
    length, width = mixed.shape
    return pl.pallas_call(
        functools.partial(attend_back_kernel, block),
        out_shape=jax.ShapeDtypeStruct((length, 3 * width), LOW),
        scratch_shapes=[
            pltpu.VMEM((width, length), LOW),
            pltpu.VMEM((length, width), WIDE),
            pltpu.VMEM((length, width), WIDE),
        ],
        compiler_params=pltpu.CompilerParams(vmem_limit_bytes=56 * MIB),
        name="attend_back",
    )(qkv, doc_start, stats, mixed, grad)


def gather_rows(block):
    return lax.all_gather(block, ("dp", "ctx"), axis=0, tiled=True)


def swap_rows(blocks):
    swapped = lax.all_to_all(blocks, "ctx", 0, 0, tiled=True)
    swapped = swapped.reshape(-1, blocks.shape[-1])
    return lax.all_gather(swapped, "dp", axis=0, tiled=True)


def swap_back(rows, ctx):
    mine = lax.psum_scatter(rows.astype(LOW), "dp", scatter_dimension=0, tiled=True)
    blocks = mine.reshape(ctx, -1, rows.shape[-1])
    return lax.all_to_all(blocks, "ctx", 0, 0, tiled=True)


def by_rank_heads(rows, ctx, slots):
    count = rows.shape[0]
    split = rows.reshape(count, 3, D)
    split = jnp.pad(split, ((0, 0), (0, 0), (0, (ctx * slots - HEADS) * HEAD_DIM)))
    split = split.reshape(count, 3, ctx, slots * HEAD_DIM)
    return split.transpose(2, 0, 1, 3).reshape(ctx, count, 3 * slots * HEAD_DIM)


def from_rank_heads(blocks, slots):
    ctx, count = blocks.shape[:2]
    split = blocks.reshape(ctx, count, 3, slots * HEAD_DIM).transpose(1, 2, 0, 3)
    return split.reshape(count, 3, ctx * slots * HEAD_DIM)[:, :, :D].reshape(count, 3 * D)


def by_rank_units(rows, ctx, dp):
    count = rows.shape[0]
    split = rows.reshape(count, dp, ctx, FF // (dp * ctx)).transpose(2, 0, 1, 3)
    return split.reshape(ctx, count, FF // ctx)


def from_rank_units(blocks, dp):
    ctx, count = blocks.shape[:2]
    split = blocks.reshape(ctx, count, dp, FF // (dp * ctx)).transpose(1, 2, 0, 3)
    return split.reshape(count, FF)


def rank_vector(vector, ctx, slots, rank):
    padded = jnp.pad(vector, (0, (ctx * slots - HEADS) * HEAD_DIM))
    width = slots * HEAD_DIM
    return lax.dynamic_slice_in_dim(padded, rank * width, width, 0)


def shards(
    hidden_in, qkv_weight, proj_weight, fc_weight, out_weight, small_params, segments, cotangent
):
    tokens = hidden_in.shape[1]
    length = segments.shape[1]
    ctx = lax.axis_size("ctx")
    dp = lax.axis_size("dp")
    owners = dp * ctx
    rank = lax.axis_index("ctx")
    slots = -(-HEADS // ctx)
    width = slots * HEAD_DIM
    units = FF // owners
    whole_rows = D % owners == 0
    block = min(256, length)

    vec_count = small_params.shape[0]
    vec_pad = -(-vec_count // 1024) * 1024
    small = lax.all_gather(
        jnp.pad(small_params, (0, vec_pad - vec_count)).reshape(1, -1, 128),
        ("dp", "ctx"),
        axis=0,
        tiled=True,
    )
    small = small.reshape(owners, vec_pad)[:, :vec_count].reshape(-1).astype(WIDE)
    gain_one, shift_one, bias_query, bias_value, bias_proj, gain_two, shift_two = [
        small[i * D : (i + 1) * D] for i in range(7)
    ]
    bias_fc = small[7 * D : 7 * D + FF]
    bias_out = small[7 * D + FF :]
    bias_units = lax.dynamic_index_in_dim(
        bias_fc.reshape(dp, ctx, units), rank, 1, keepdims=False
    ).reshape(-1)
    if whole_rows:
        mat_qkv = swap_rows(by_rank_heads(qkv_weight.reshape(-1, 3 * D), ctx, slots))
        mat_fc = swap_rows(by_rank_units(fc_weight.reshape(-1, FF), ctx, dp))
        mat_proj = gather_rows(proj_weight.reshape(1, -1, D)).reshape(D, D)
    else:
        mat_qkv = by_rank_heads(gather_rows(qkv_weight).reshape(D, 3 * D), ctx, slots)
        mat_qkv = lax.dynamic_index_in_dim(mat_qkv, rank, 0, keepdims=False)
        mat_fc = by_rank_units(gather_rows(fc_weight).reshape(D, FF), ctx, dp)
        mat_fc = lax.dynamic_index_in_dim(mat_fc, rank, 0, keepdims=False)
        mat_proj = gather_rows(proj_weight).reshape(D, D)
    mat_out = lax.all_gather(
        out_weight.reshape(1, units, D), "dp", axis=0, tiled=True
    ).reshape(dp * units, D)

    own_in = hidden_in[0].astype(WIDE)
    normed_one, scale_one = normalize(own_in)
    attn_in = lax.all_gather(
        (normed_one * gain_one + shift_one).astype(LOW), "ctx", axis=0, tiled=True
    )
    cot = lax.all_gather(cotangent[0], "ctx", axis=0, tiled=True)
    zeros = jnp.zeros((width,), WIDE)
    bias_qkv = jnp.concatenate(
        [
            rank_vector(bias_query, ctx, slots, rank),
            zeros,
            rank_vector(bias_value, ctx, slots, rank),
        ]
    )
    qkv = (dot(attn_in, mat_qkv) + bias_qkv).astype(LOW)
    docs = segments[0]
    doc_start = jnp.sum((docs[:, None] < docs[None, :]).astype(jnp.int32), 0)[None]
    mixed, stats = attend(qkv, doc_start, block)
    own_mixed = lax.all_to_all(mixed.reshape(ctx, tokens, width), "ctx", 0, 0, tiled=True)
    own_mixed = own_mixed.transpose(1, 0, 2).reshape(tokens, ctx * width)[:, :D]

    resid = own_in + dot(own_mixed, mat_proj) + bias_proj
    normed_two, scale_two = normalize(resid)
    ffn_in = lax.all_gather(
        (normed_two * gain_two + shift_two).astype(LOW), "ctx", axis=0, tiled=True
    )
    pre_act = dot(ffn_in, mat_fc) + bias_units
    bend = jnp.tanh(0.7978845608028654 * (pre_act + 0.044715 * pre_act * pre_act * pre_act))
    act = (0.5 * pre_act * (1.0 + bend)).astype(LOW)
    slope = 0.5 * (1.0 + bend) + 0.5 * pre_act * (1.0 - bend * bend) * 0.7978845608028654 * (
        1.0 + 3 * 0.044715 * pre_act * pre_act
    )
    output = (
        resid
        + lax.psum_scatter(
            dot(act, mat_out).astype(LOW), "ctx", scatter_dimension=0, tiled=True
        ).astype(WIDE)
        + bias_out
    )
    grad_pre = (slope * dot(cot, mat_out, 1, 1)).astype(LOW)
    grad_normed_two = lax.psum_scatter(
        dot(grad_pre, mat_fc, 1, 1).astype(LOW), "ctx", scatter_dimension=0, tiled=True
    ).astype(WIDE)
    grad_out = lax.psum_scatter(
        dot(act, cot, 0, 0).astype(LOW).reshape(dp, units, D), "dp", scatter_dimension=0, tiled=True
    )
    grad_fc = dot(ffn_in, grad_pre, 0, 0)

    own_cot = cotangent[0].astype(WIDE)
    grad_resid = own_cot + norm_back(normed_two, scale_two, gain_two, grad_normed_two)
    resid_low = grad_resid.astype(LOW)
    grad_mixed = dot(resid_low, mat_proj, 1, 1).astype(LOW)
    grad_mixed = jnp.pad(grad_mixed, ((0, 0), (0, ctx * width - D)))
    grad_mixed = grad_mixed.reshape(tokens, ctx, width).transpose(1, 0, 2)
    grad_mixed = lax.all_to_all(grad_mixed, "ctx", 0, 0, tiled=True).reshape(length, width)
    grad_rows = attend_back(qkv, doc_start, stats, mixed, grad_mixed, block)
    grad_normed_one = lax.psum_scatter(
        dot(grad_rows, mat_qkv, 1, 1).astype(LOW), "ctx", scatter_dimension=0, tiled=True
    ).astype(WIDE)
    grad_input = grad_resid + norm_back(normed_one, scale_one, gain_one, grad_normed_one)
    grad_qkv = dot(attn_in, grad_rows, 0, 0)
    grad_proj = dot(own_mixed, resid_low, 0, 0)

    if whole_rows:
        share_fc = from_rank_units(swap_back(grad_fc, ctx), dp)
        share_qkv = from_rank_heads(swap_back(grad_qkv, ctx), slots)
        part = lax.psum_scatter(grad_proj.astype(LOW), "dp", scatter_dimension=0, tiled=True)
        part = part.reshape(ctx, D // owners, D)
        share_proj = lax.psum_scatter(part, "ctx", scatter_dimension=0, tiled=True)
    else:
        here = (jnp.arange(ctx) == rank)[:, None, None]
        full_fc = from_rank_units(jnp.where(here, grad_fc[None], 0.0), dp).reshape(-1)
        full_qkv = from_rank_heads(jnp.where(here, grad_qkv[None], 0.0), slots).reshape(-1)
        both = ("dp", "ctx")
        share_fc = lax.psum_scatter(full_fc, both, scatter_dimension=0, tiled=True)
        share_qkv = lax.psum_scatter(full_qkv, both, scatter_dimension=0, tiled=True)
        share_proj = lax.psum_scatter(
            grad_proj.reshape(-1), both, scatter_dimension=0, tiled=True
        )

    def column_sum(values):
        return jnp.sum(values.astype(WIDE), 0)

    def spread_heads(part):
        padded = jnp.zeros((ctx * width,), WIDE)
        return lax.dynamic_update_slice_in_dim(padded, part, rank * width, 0)[:D]

    grads = column_sum(grad_rows)
    pre_sum = column_sum(grad_pre).reshape(dp, 1, units)
    pre_sum = lax.dynamic_update_slice_in_dim(
        jnp.zeros((dp, ctx, units), WIDE), pre_sum, rank, 1
    ).reshape(FF)
    vector = jnp.concatenate(
        [
            column_sum(grad_normed_one * normed_one),
            column_sum(grad_normed_one),
            spread_heads(grads[:width]),
            spread_heads(grads[2 * width :]),
            column_sum(grad_resid),
            column_sum(grad_normed_two * normed_two),
            column_sum(grad_normed_two),
            pre_sum,
            column_sum(own_cot),
        ]
    ).reshape(owners, vec_count)
    vector = jnp.pad(vector, ((0, 0), (0, vec_pad - vec_count))).reshape(owners, -1, 128)
    share_vector = lax.psum_scatter(vector, ("dp", "ctx"), scatter_dimension=0, tiled=True)
    return (
        output[None],
        grad_input[None],
        share_qkv.astype(WIDE).reshape(-1),
        share_proj.astype(WIDE).reshape(-1),
        share_fc.astype(WIDE).reshape(-1),
        grad_out.astype(WIDE).reshape(-1),
        share_vector.reshape(-1)[:vec_count],
    )


def solution(mesh):
    flat = P(("dp", "ctx"))
    rows = P("dp", "ctx", None)
    return jax.shard_map(
        shards,
        mesh=mesh,
        in_specs=(rows, flat, flat, flat, flat, flat, P("dp", None), rows),
        out_specs=(rows, rows, flat, flat, flat, flat, flat),
        check_vma=False,
    )
```

```python
import functools

import jax
import jax.numpy as jnp
from jax import lax
from jax.experimental import pallas as pl
from jax.experimental.pallas import tpu as pltpu
from jax.sharding import PartitionSpec as P

D = 1600
HEADS = 25
HEAD_DIM = 64
FF = 6400
EPSILON = 1e-05
LOW = jnp.bfloat16
WIDE = jnp.float32
MIB = 1024 * 1024


def dot(left, right, left_dim=1, right_dim=0):
    return lax.dot_general(
        left, right, (((left_dim,), (right_dim,)), ((), ())), preferred_element_type=WIDE
    )


def normalize(rows):
    centre = rows - jnp.mean(rows, -1, keepdims=True)
    spread = jnp.mean(centre * centre, -1, keepdims=True)
    scale = lax.rsqrt(spread + EPSILON)
    return centre * scale, scale


def norm_back(normed, scale, gain, incoming):
    scaled = gain * incoming
    return scale * (
        scaled
        - jnp.mean(scaled, -1, keepdims=True)
        - normed * jnp.mean(scaled * normed, -1, keepdims=True)
    )


def head_lanes(head, width):
    lane = lax.broadcasted_iota(jnp.int32, (1, width), 1)
    return (lane // HEAD_DIM) == head


def allowed_scores(scores, doc_start, first_query, keys, block):
    key_pos = lax.broadcasted_iota(jnp.int32, (keys, block), 0)
    query_pos = first_query + lax.broadcasted_iota(jnp.int32, (keys, block), 1)
    seen = (key_pos >= doc_start) & (key_pos <= query_pos)
    return jnp.where(seen, scores, -1e30)


def attend_kernel(block, qkv_ref, start_ref, mixed_ref, stat_ref, value_t):
    length = qkv_ref.shape[0]
    width = mixed_ref.shape[1]
    slots = width // HEAD_DIM
    value_t[...] = qkv_ref[:, 2 * width : 3 * width].astype(WIDE).T.astype(LOW)
    for index in range(length // block):
        keys = (index + 1) * block
        rows = pl.ds(index * block, block)
        key_rows = qkv_ref[0:keys, width : 2 * width]
        doc_start = start_ref[0:1, rows]
        outs = []
        for head in range(slots):
            query = jnp.where(
                head_lanes(head, width), qkv_ref[rows, 0:width] * LOW(HEAD_DIM**-0.5), LOW(0)
            )
            scores = dot(key_rows, query, 1, 1)
            scores = allowed_scores(scores, doc_start, index * block, keys, block)
            top = jnp.max(scores, 0, keepdims=True)
            expo = jnp.exp(scores - top)
            total = jnp.sum(expo, 0, keepdims=True)
            head_rows = slice(head * HEAD_DIM, (head + 1) * HEAD_DIM)
            out = dot(value_t[head_rows, 0:keys], expo.astype(LOW))
            outs.append(out / total)
            stat_ref[head : head + 1, rows] = top + jnp.log(total)
        mixed_ref[rows, :] = jnp.concatenate(outs, 0).T.astype(LOW)


def attend(qkv, doc_start, block):
    length, width = qkv.shape[0], qkv.shape[1] // 3
    return pl.pallas_call(
        functools.partial(attend_kernel, block),
        out_shape=(
            jax.ShapeDtypeStruct((length, width), LOW),
            jax.ShapeDtypeStruct((8, length), WIDE),
        ),
        scratch_shapes=[pltpu.VMEM((width, length), LOW)],
        compiler_params=pltpu.CompilerParams(vmem_limit_bytes=48 * MIB),
        name="attend",
    )(qkv, doc_start)


def attend_back_kernel(
    block, qkv_ref, start_ref, stat_ref, mixed_ref, grad_ref, out_ref, key_t, key_grad, value_grad
):
    length = qkv_ref.shape[0]
    width = mixed_ref.shape[1]
    slots = width // HEAD_DIM
    scale = HEAD_DIM**-0.5
    key_t[...] = qkv_ref[:, width : 2 * width].astype(WIDE).T.astype(LOW)
    key_grad[...] = jnp.zeros_like(key_grad)
    value_grad[...] = jnp.zeros_like(value_grad)
    for index in range(length // block):
        keys = (index + 1) * block
        rows = pl.ds(index * block, block)
        key_rows = qkv_ref[0:keys, width : 2 * width]
        value_rows = qkv_ref[0:keys, 2 * width : 3 * width]
        doc_start = start_ref[0:1, rows]
        outs = []
        for head in range(slots):
            lanes = head_lanes(head, width)
            head_rows = slice(head * HEAD_DIM, (head + 1) * HEAD_DIM)
            query = jnp.where(lanes, qkv_ref[rows, 0:width] * LOW(scale), LOW(0))
            grad = jnp.where(lanes, grad_ref[rows, :], LOW(0))
            scores = dot(key_rows, query, 1, 1)
            scores = allowed_scores(scores, doc_start, index * block, keys, block)
            probs = jnp.exp(scores - stat_ref[head : head + 1, rows])
            grad_probs = dot(value_rows, grad, 1, 1)
            delta = jnp.sum(probs * grad_probs, 0, keepdims=True)
            grad_scores = (probs * (grad_probs - delta)).astype(LOW)
            value_grad[0:keys, :] += dot(probs.astype(LOW), grad)
            key_grad[0:keys, :] += dot(grad_scores, query)
            outs.append(dot(key_t[head_rows, 0:keys], grad_scores))
        out_ref[rows, 0:width] = (jnp.concatenate(outs, 0).T * scale).astype(LOW)
    out_ref[:, width : 2 * width] = key_grad[...].astype(LOW)
    out_ref[:, 2 * width : 3 * width] = value_grad[...].astype(LOW)


def attend_back(qkv, doc_start, stats, mixed, grad, block):
    length, width = mixed.shape
    return pl.pallas_call(
        functools.partial(attend_back_kernel, block),
        out_shape=jax.ShapeDtypeStruct((length, 3 * width), LOW),
        scratch_shapes=[
            pltpu.VMEM((width, length), LOW),
            pltpu.VMEM((length, width), WIDE),
            pltpu.VMEM((length, width), WIDE),
        ],
        compiler_params=pltpu.CompilerParams(vmem_limit_bytes=56 * MIB),
        name="attend_back",
    )(qkv, doc_start, stats, mixed, grad)


MESH = pl.DeviceIdType.MESH


def send(src, dst, send_sem, recv_sem, **target):
    return pltpu.make_async_remote_copy(
        src_ref=src,
        dst_ref=dst,
        send_sem=send_sem,
        recv_sem=recv_sem,
        device_id=target,
        device_id_type=MESH,
    )


def greet_line(chips):
    rank = lax.axis_index("ctx")
    chip, core = rank // 2, rank % 2
    barrier = pltpu.get_barrier_semaphore()
    pl.semaphore_signal(barrier, 1, device_id={"ctx": rank + 1 - 2 * core}, device_id_type=MESH)

    @pl.when(chip > 0)
    def _():
        pl.semaphore_signal(barrier, 1, device_id={"ctx": rank - 2}, device_id_type=MESH)

    @pl.when(chip < chips - 1)
    def _():
        pl.semaphore_signal(barrier, 1, device_id={"ctx": rank + 2}, device_id_type=MESH)

    sides = (chip > 0).astype(jnp.int32) + (chip < chips - 1).astype(jnp.int32)
    pl.semaphore_wait(barrier, 1 + sides)


class LineGather:
    def __init__(self, blocks, send_sems, recv_sems):
        self.blocks, self.send_sems, self.recv_sems = blocks, send_sems, recv_sems
        self.rank = lax.axis_index("ctx")
        self.chip, self.core = self.rank // 2, self.rank % 2
        self.chips = blocks.shape[0] // 2

    def copy(self, way, origin, target, src=None):
        block = self.blocks.at[origin]
        return send(
            block if src is None else src,
            block,
            self.send_sems.at[way, origin],
            self.recv_sems.at[origin],
            ctx=target,
        )

    def pass_on(self, origin, src=None):
        chip = origin // 2

        @pl.when((chip <= self.chip) & (self.chip < self.chips - 1))
        def _():
            self.copy(0, origin, self.rank + 2, src).start()

        @pl.when((chip >= self.chip) & (self.chip > 0))
        def _():
            self.copy(1, origin, self.rank - 2, src).start()

        self.copy(2, origin, self.rank + 1 - 2 * self.core, src).start()

    def arrive(self, step, part):
        side, other = part % 2, part // 2
        origin_chip = self.chip + jnp.where(side == 0, -step, step)
        origin = 2 * origin_chip + jnp.where(other == 0, self.core, 1 - self.core)
        valid = (origin_chip >= 0) & (origin_chip < self.chips) & ((step > 0) | (side == 0))

        @pl.when(valid & (origin != self.rank))
        def _():
            self.copy(0, origin, self.rank).wait_recv()

            @pl.when(other == 0)
            def _():
                self.pass_on(origin)

        return valid, origin

    def finish(self):
        def one(chip, carry):
            origin = 2 * chip + self.core

            @pl.when((chip <= self.chip) & (self.chip < self.chips - 1))
            def _():
                self.copy(0, origin, self.rank).wait_send()

            @pl.when((chip >= self.chip) & (self.chip > 0))
            def _():
                self.copy(1, origin, self.rank).wait_send()

            self.copy(2, origin, self.rank).wait_send()
            return carry

        lax.fori_loop(0, self.chips, one, 0)

    @staticmethod
    def semaphores(ctx):
        return [pltpu.SemaphoreType.DMA((3, ctx)), pltpu.SemaphoreType.DMA((ctx,))]


class LineSum:
    def __init__(self, blocks, pair, passing, sems):
        self.blocks, self.pair, self.passing = blocks, pair, passing
        self.pair_send, self.pair_recv, self.line_send, self.line_recv = sems
        self.rank = lax.axis_index("ctx")
        self.chip, self.core = self.rank // 2, self.rank % 2
        self.chips = blocks.shape[0] // 2
        self.pieces = self.line_recv.shape[2]
        self.piece = blocks.shape[1] // self.pieces

    def pair_copy(self, chip):
        return send(
            self.blocks.at[2 * chip + 1 - self.core],
            self.pair.at[chip],
            self.pair_send.at[chip],
            self.pair_recv.at[chip],
            ctx=self.rank + 1 - 2 * self.core,
        )

    def line_copy(self, way, chip, piece, target):
        rows = pl.ds(piece * self.piece, self.piece)
        return send(
            self.blocks.at[2 * chip + self.core, rows],
            self.passing.at[way, chip, rows],
            self.line_send.at[chip, piece],
            self.line_recv.at[way, chip, piece],
            ctx=target,
        )

    def both(self, chip, rows):
        mine = self.blocks[2 * chip + self.core, rows].astype(WIDE)
        return mine + self.pair[chip, rows].astype(WIDE)

    def forward(self, way, chip, valid):
        behind = jnp.where(way == 0, self.chip > 0, self.chip < self.chips - 1)
        target = self.rank + jnp.where(way == 0, 2, -2)

        @pl.when(valid)
        def _():
            self.pair_copy(chip).wait_recv()

            def one(piece, carry):
                rows = pl.ds(pl.multiple_of(piece * self.piece, self.piece), self.piece)
                total = self.both(chip, rows)

                @pl.when(behind)
                def _():
                    self.line_copy(way, chip, piece, target).wait_recv()
                    passing = self.passing[way, chip, rows].astype(WIDE)
                    self.blocks[2 * chip + self.core, rows] = (total + passing).astype(LOW)

                @pl.when(jnp.logical_not(behind))
                def _():
                    self.blocks[2 * chip + self.core, rows] = total.astype(LOW)

                self.line_copy(way, chip, piece, target).start()
                return carry

            lax.fori_loop(0, self.pieces, one, 0)

    def near_first(self, step, way):
        last = self.chips - 1
        chip = jnp.where(way == 0, step - self.chip, 2 * last - self.chip - step)
        ahead = jnp.where(way == 0, (chip > self.chip) & (chip <= last), (chip >= 0) & (chip < self.chip))
        self.forward(way, chip, ahead)

    def far_first(self, step, way):
        last = self.chips - 1
        chip = jnp.where(way == 0, last + self.chip - step, step - last + self.chip)
        ahead = jnp.where(way == 0, (chip > self.chip) & (chip <= last), (chip >= 0) & (chip < self.chip))
        self.forward(way, chip, ahead)

    def finish(self, out):
        self.pair_copy(self.chip).wait_recv()

        def one(piece, carry):
            rows = pl.ds(pl.multiple_of(piece * self.piece, self.piece), self.piece)
            out[rows] = self.both(self.chip, rows)

            @pl.when(self.chip > 0)
            def _():
                self.line_copy(0, self.chip, piece, self.rank).wait_recv()
                out[rows] = out[rows] + self.passing[0, self.chip, rows].astype(WIDE)

            @pl.when(self.chip < self.chips - 1)
            def _():
                self.line_copy(1, self.chip, piece, self.rank).wait_recv()
                out[rows] = out[rows] + self.passing[1, self.chip, rows].astype(WIDE)

            return carry

        lax.fori_loop(0, self.pieces, one, 0)

        def sent(chip, carry):
            self.pair_copy(chip).wait_send()

            @pl.when(chip != self.chip)
            def _():
                for piece in range(self.pieces):
                    self.line_copy(0, chip, piece, self.rank).wait_send()

            return carry

        lax.fori_loop(0, self.chips, sent, 0)

    @staticmethod
    def scratch(ctx, rows, columns, pieces):
        chips = ctx // 2
        return [
            pltpu.VMEM((ctx, rows, columns), LOW),
            pltpu.VMEM((chips, rows, columns), LOW),
            pltpu.VMEM((2, chips, rows, columns), LOW),
            pltpu.SemaphoreType.DMA((chips,)),
            pltpu.SemaphoreType.DMA((chips,)),
            pltpu.SemaphoreType.DMA((chips, pieces)),
            pltpu.SemaphoreType.DMA((2, chips, pieces)),
        ]


def feed_kernel(
    mixed_ref,
    in_ref,
    vectors_ref,
    bias_ref,
    proj_ref,
    fc_ref,
    out_ref,
    cot_ref,
    resid_ref,
    grad_ref,
    ffn_ref,
    act_ref,
    pre_ref,
    part_ref,
    gather_send,
    gather_recv,
    blocks,
    pair,
    passing,
    *sems,
):
    gather = LineGather(ffn_ref, gather_send, gather_recv)
    total = LineSum(blocks, pair, passing, sems)
    chips = gather.chips
    greet_line(chips)
    resid = in_ref[...].astype(WIDE) + dot(mixed_ref[:, 0:D], proj_ref[...]) + vectors_ref[0:1]
    resid_ref[...] = resid
    normed, _ = normalize(resid)
    ffn_ref[gather.rank] = (normed * vectors_ref[1:2] + vectors_ref[2:3]).astype(LOW)
    gather.pass_on(gather.rank)

    def work(origin):
        pre = dot(ffn_ref[origin], fc_ref[...]) + bias_ref[0:1]
        bend = jnp.tanh(0.7978845608028654 * (pre + 0.044715 * pre * pre * pre))
        act = (0.5 * pre * (1.0 + bend)).astype(LOW)
        act_ref[origin] = act
        slope = 0.5 * (1.0 + bend) + 0.5 * pre * (1.0 - bend * bend) * 0.7978845608028654 * (
            1.0 + 3 * 0.044715 * pre * pre
        )
        grad_pre = (slope * dot(cot_ref[origin], out_ref[...], 1, 1)).astype(LOW)
        pre_ref[origin] = grad_pre
        blocks[origin] = dot(grad_pre, fc_ref[...], 1, 1).astype(LOW)

        @pl.when(origin % 2 != gather.core)
        def _():
            total.pair_copy(origin // 2).start()

        part_ref[origin] = dot(act, out_ref[...]).astype(LOW)

    def step(index, carry):
        distance, part = index // 4, index % 4

        @pl.when(distance < chips)
        def _():
            valid, origin = gather.arrive(distance, part)

            @pl.when(valid)
            def _():
                work(origin)

        @pl.when(part == 3)
        def _():
            def way(index, carry):
                total.near_first(distance, index)
                return carry

            lax.fori_loop(0, 2, way, 0)

        return carry

    lax.fori_loop(0, 4 * (2 * chips - 1), step, 0)
    total.finish(grad_ref)
    gather.finish()


def feed(mixed, own_in, vectors, bias, proj, fc, out, cot):
    ctx, tokens, _ = cot.shape
    width = fc.shape[1]
    return pl.pallas_call(
        feed_kernel,
        out_shape=(
            jax.ShapeDtypeStruct((tokens, D), WIDE),
            jax.ShapeDtypeStruct((tokens, D), WIDE),
            jax.ShapeDtypeStruct((ctx, tokens, D), LOW),
            jax.ShapeDtypeStruct((ctx, tokens, width), LOW),
            jax.ShapeDtypeStruct((ctx, tokens, width), LOW),
            jax.ShapeDtypeStruct((ctx, tokens, D), LOW),
        ),
        in_specs=[pl.BlockSpec(memory_space=pltpu.VMEM)] * 8,
        out_specs=[pl.BlockSpec(memory_space=pltpu.VMEM)] * 6,
        scratch_shapes=LineGather.semaphores(ctx) + LineSum.scratch(ctx, tokens, D, 4),
        compiler_params=pltpu.CompilerParams(
            vmem_limit_bytes=60 * MIB, collective_id=2, has_side_effects=True
        ),
        name="feed",
    )(mixed, own_in, vectors, bias, proj, fc, out, cot)


def gather_rows(block):
    return lax.all_gather(block, ("dp", "ctx"), axis=0, tiled=True)


def swap_rows(blocks):
    swapped = lax.all_to_all(blocks, "ctx", 0, 0, tiled=True)
    swapped = swapped.reshape(-1, blocks.shape[-1])
    return lax.all_gather(swapped, "dp", axis=0, tiled=True)


def swap_back(rows, ctx):
    mine = lax.psum_scatter(rows.astype(LOW), "dp", scatter_dimension=0, tiled=True)
    blocks = mine.reshape(ctx, -1, rows.shape[-1])
    return lax.all_to_all(blocks, "ctx", 0, 0, tiled=True)


def by_rank_heads(rows, ctx, slots):
    count = rows.shape[0]
    split = rows.reshape(count, 3, D)
    split = jnp.pad(split, ((0, 0), (0, 0), (0, (ctx * slots - HEADS) * HEAD_DIM)))
    split = split.reshape(count, 3, ctx, slots * HEAD_DIM)
    return split.transpose(2, 0, 1, 3).reshape(ctx, count, 3 * slots * HEAD_DIM)


def from_rank_heads(blocks, slots):
    ctx, count = blocks.shape[:2]
    split = blocks.reshape(ctx, count, 3, slots * HEAD_DIM).transpose(1, 2, 0, 3)
    return split.reshape(count, 3, ctx * slots * HEAD_DIM)[:, :, :D].reshape(count, 3 * D)


def by_rank_units(rows, ctx, dp):
    count = rows.shape[0]
    split = rows.reshape(count, dp, ctx, FF // (dp * ctx)).transpose(2, 0, 1, 3)
    return split.reshape(ctx, count, FF // ctx)


def from_rank_units(blocks, dp):
    ctx, count = blocks.shape[:2]
    split = blocks.reshape(ctx, count, dp, FF // (dp * ctx)).transpose(1, 2, 0, 3)
    return split.reshape(count, FF)


def rank_vector(vector, ctx, slots, rank):
    padded = jnp.pad(vector, (0, (ctx * slots - HEADS) * HEAD_DIM))
    width = slots * HEAD_DIM
    return lax.dynamic_slice_in_dim(padded, rank * width, width, 0)


def shards(
    hidden_in, qkv_weight, proj_weight, fc_weight, out_weight, small_params, segments, cotangent
):
    tokens = hidden_in.shape[1]
    length = segments.shape[1]
    ctx = lax.axis_size("ctx")
    dp = lax.axis_size("dp")
    owners = dp * ctx
    rank = lax.axis_index("ctx")
    slots = -(-HEADS // ctx)
    width = slots * HEAD_DIM
    units = FF // owners
    whole_rows = D % owners == 0
    block = min(256, length)

    vec_count = small_params.shape[0]
    vec_pad = -(-vec_count // 1024) * 1024
    small = lax.all_gather(
        jnp.pad(small_params, (0, vec_pad - vec_count)).reshape(1, -1, 128),
        ("dp", "ctx"),
        axis=0,
        tiled=True,
    )
    small = small.reshape(owners, vec_pad)[:, :vec_count].reshape(-1).astype(WIDE)
    gain_one, shift_one, bias_query, bias_value, bias_proj, gain_two, shift_two = [
        small[i * D : (i + 1) * D] for i in range(7)
    ]
    bias_fc = small[7 * D : 7 * D + FF]
    bias_out = small[7 * D + FF :]
    bias_units = lax.dynamic_index_in_dim(
        bias_fc.reshape(dp, ctx, units), rank, 1, keepdims=False
    ).reshape(-1)
    if whole_rows:
        mat_qkv = swap_rows(by_rank_heads(qkv_weight.reshape(-1, 3 * D), ctx, slots))
        mat_fc = swap_rows(by_rank_units(fc_weight.reshape(-1, FF), ctx, dp))
        mat_proj = gather_rows(proj_weight.reshape(1, -1, D)).reshape(D, D)
    else:
        mat_qkv = by_rank_heads(gather_rows(qkv_weight).reshape(D, 3 * D), ctx, slots)
        mat_qkv = lax.dynamic_index_in_dim(mat_qkv, rank, 0, keepdims=False)
        mat_fc = by_rank_units(gather_rows(fc_weight).reshape(D, FF), ctx, dp)
        mat_fc = lax.dynamic_index_in_dim(mat_fc, rank, 0, keepdims=False)
        mat_proj = gather_rows(proj_weight).reshape(D, D)
    mat_out = lax.all_gather(
        out_weight.reshape(1, units, D), "dp", axis=0, tiled=True
    ).reshape(dp * units, D)

    own_in = hidden_in[0].astype(WIDE)
    normed_one, scale_one = normalize(own_in)
    attn_in = lax.all_gather(
        (normed_one * gain_one + shift_one).astype(LOW), "ctx", axis=0, tiled=True
    )
    cot = lax.all_gather(cotangent[0], "ctx", axis=0, tiled=True)
    zeros = jnp.zeros((width,), WIDE)
    bias_qkv = jnp.concatenate(
        [
            rank_vector(bias_query, ctx, slots, rank),
            zeros,
            rank_vector(bias_value, ctx, slots, rank),
        ]
    )
    qkv = (dot(attn_in, mat_qkv) + bias_qkv).astype(LOW)
    docs = segments[0]
    doc_start = jnp.sum((docs[:, None] < docs[None, :]).astype(jnp.int32), 0)[None]
    mixed, stats = attend(qkv, doc_start, block)
    own_mixed = lax.all_to_all(mixed.reshape(ctx, tokens, width), "ctx", 0, 0, tiled=True)
    own_mixed = own_mixed.transpose(1, 0, 2).reshape(tokens, ctx * width)[:, :D]

    vectors = jnp.stack([bias_proj, gain_two, shift_two])
    cot_blocks = cot.reshape(ctx, tokens, D)
    resid, grad_normed_two, ffn_in, act, grad_pre, out_part = feed(
        own_mixed, hidden_in[0], vectors, bias_units[None], mat_proj, mat_fc, mat_out, cot_blocks
    )
    ffn_in, act, grad_pre, out_part = [
        rows.reshape(length, -1) for rows in (ffn_in, act, grad_pre, out_part)
    ]
    output = (
        resid
        + lax.psum_scatter(out_part, "ctx", scatter_dimension=0, tiled=True).astype(WIDE)
        + bias_out
    )
    normed_two, scale_two = normalize(resid)
    grad_out = lax.psum_scatter(
        dot(act, cot, 0, 0).astype(LOW).reshape(dp, units, D), "dp", scatter_dimension=0, tiled=True
    )
    grad_fc = dot(ffn_in, grad_pre, 0, 0)

    own_cot = cotangent[0].astype(WIDE)
    grad_resid = own_cot + norm_back(normed_two, scale_two, gain_two, grad_normed_two)
    resid_low = grad_resid.astype(LOW)
    grad_mixed = dot(resid_low, mat_proj, 1, 1).astype(LOW)
    grad_mixed = jnp.pad(grad_mixed, ((0, 0), (0, ctx * width - D)))
    grad_mixed = grad_mixed.reshape(tokens, ctx, width).transpose(1, 0, 2)
    grad_mixed = lax.all_to_all(grad_mixed, "ctx", 0, 0, tiled=True).reshape(length, width)
    grad_rows = attend_back(qkv, doc_start, stats, mixed, grad_mixed, block)
    grad_normed_one = lax.psum_scatter(
        dot(grad_rows, mat_qkv, 1, 1).astype(LOW), "ctx", scatter_dimension=0, tiled=True
    ).astype(WIDE)
    grad_input = grad_resid + norm_back(normed_one, scale_one, gain_one, grad_normed_one)
    grad_qkv = dot(attn_in, grad_rows, 0, 0)
    grad_proj = dot(own_mixed, resid_low, 0, 0)

    if whole_rows:
        share_fc = from_rank_units(swap_back(grad_fc, ctx), dp)
        share_qkv = from_rank_heads(swap_back(grad_qkv, ctx), slots)
        part = lax.psum_scatter(grad_proj.astype(LOW), "dp", scatter_dimension=0, tiled=True)
        part = part.reshape(ctx, D // owners, D)
        share_proj = lax.psum_scatter(part, "ctx", scatter_dimension=0, tiled=True)
    else:
        here = (jnp.arange(ctx) == rank)[:, None, None]
        full_fc = from_rank_units(jnp.where(here, grad_fc[None], 0.0), dp).reshape(-1)
        full_qkv = from_rank_heads(jnp.where(here, grad_qkv[None], 0.0), slots).reshape(-1)
        both = ("dp", "ctx")
        share_fc = lax.psum_scatter(full_fc, both, scatter_dimension=0, tiled=True)
        share_qkv = lax.psum_scatter(full_qkv, both, scatter_dimension=0, tiled=True)
        share_proj = lax.psum_scatter(
            grad_proj.reshape(-1), both, scatter_dimension=0, tiled=True
        )

    def column_sum(values):
        return jnp.sum(values.astype(WIDE), 0)

    def spread_heads(part):
        padded = jnp.zeros((ctx * width,), WIDE)
        return lax.dynamic_update_slice_in_dim(padded, part, rank * width, 0)[:D]

    grads = column_sum(grad_rows)
    pre_sum = column_sum(grad_pre).reshape(dp, 1, units)
    pre_sum = lax.dynamic_update_slice_in_dim(
        jnp.zeros((dp, ctx, units), WIDE), pre_sum, rank, 1
    ).reshape(FF)
    vector = jnp.concatenate(
        [
            column_sum(grad_normed_one * normed_one),
            column_sum(grad_normed_one),
            spread_heads(grads[:width]),
            spread_heads(grads[2 * width :]),
            column_sum(grad_resid),
            column_sum(grad_normed_two * normed_two),
            column_sum(grad_normed_two),
            pre_sum,
            column_sum(own_cot),
        ]
    ).reshape(owners, vec_count)
    vector = jnp.pad(vector, ((0, 0), (0, vec_pad - vec_count))).reshape(owners, -1, 128)
    share_vector = lax.psum_scatter(vector, ("dp", "ctx"), scatter_dimension=0, tiled=True)
    return (
        output[None],
        grad_input[None],
        share_qkv.astype(WIDE).reshape(-1),
        share_proj.astype(WIDE).reshape(-1),
        share_fc.astype(WIDE).reshape(-1),
        grad_out.astype(WIDE).reshape(-1),
        share_vector.reshape(-1)[:vec_count],
    )


def solution(mesh):
    flat = P(("dp", "ctx"))
    rows = P("dp", "ctx", None)
    return jax.shard_map(
        shards,
        mesh=mesh,
        in_specs=(rows, flat, flat, flat, flat, flat, P("dp", None), rows),
        out_specs=(rows, rows, flat, flat, flat, flat, flat),
        check_vma=False,
    )
```

```python
import functools

import jax
import jax.numpy as jnp
from jax import lax
from jax.experimental import pallas as pl
from jax.experimental.pallas import tpu as pltpu
from jax.sharding import PartitionSpec as P

D = 1600
HEADS = 25
HEAD_DIM = 64
FF = 6400
EPSILON = 1e-05
LOW = jnp.bfloat16
WIDE = jnp.float32
MIB = 1024 * 1024


def dot(left, right, left_dim=1, right_dim=0):
    return lax.dot_general(
        left, right, (((left_dim,), (right_dim,)), ((), ())), preferred_element_type=WIDE
    )


def normalize(rows):
    centre = rows - jnp.mean(rows, -1, keepdims=True)
    spread = jnp.mean(centre * centre, -1, keepdims=True)
    scale = lax.rsqrt(spread + EPSILON)
    return centre * scale, scale


def norm_back(normed, scale, gain, incoming):
    scaled = gain * incoming
    return scale * (
        scaled
        - jnp.mean(scaled, -1, keepdims=True)
        - normed * jnp.mean(scaled * normed, -1, keepdims=True)
    )


def head_lanes(head, width):
    lane = lax.broadcasted_iota(jnp.int32, (1, width), 1)
    return (lane // HEAD_DIM) == head


def allowed_scores(scores, doc_start, first_query, keys, block):
    key_pos = lax.broadcasted_iota(jnp.int32, (keys, block), 0)
    query_pos = first_query + lax.broadcasted_iota(jnp.int32, (keys, block), 1)
    seen = (key_pos >= doc_start) & (key_pos <= query_pos)
    return jnp.where(seen, scores, -1e30)


def attend_body(block, qkv_ref, start_ref, mixed_ref, stat_ref, value_t):
    length = qkv_ref.shape[0]
    width = mixed_ref.shape[1]
    slots = width // HEAD_DIM
    value_t[...] = qkv_ref[:, 2 * width : 3 * width].astype(WIDE).T.astype(LOW)
    stat_ref[...] = jnp.zeros_like(stat_ref)
    for index in range(length // block):
        keys = (index + 1) * block
        rows = pl.ds(index * block, block)
        key_rows = qkv_ref[0:keys, width : 2 * width]
        doc_start = start_ref[0:1, rows]
        outs = []
        for head in range(slots):
            query = jnp.where(
                head_lanes(head, width), qkv_ref[rows, 0:width] * LOW(HEAD_DIM**-0.5), LOW(0)
            )
            scores = dot(key_rows, query, 1, 1)
            scores = allowed_scores(scores, doc_start, index * block, keys, block)
            top = jnp.max(scores, 0, keepdims=True)
            expo = jnp.exp(scores - top)
            total = jnp.sum(expo, 0, keepdims=True)
            head_rows = slice(head * HEAD_DIM, (head + 1) * HEAD_DIM)
            out = dot(value_t[head_rows, 0:keys], expo.astype(LOW))
            outs.append(out / total)
            stat_ref[head : head + 1, rows] = top + jnp.log(total)
        mixed_ref[rows, :] = jnp.concatenate(outs, 0).T.astype(LOW)


def attend_back_body(
    block, qkv_ref, start_ref, stat_ref, grad_ref, out_ref, key_t, key_grad, value_grad
):
    length = qkv_ref.shape[0]
    width = grad_ref.shape[1]
    slots = width // HEAD_DIM
    scale = HEAD_DIM**-0.5
    key_t[...] = qkv_ref[:, width : 2 * width].astype(WIDE).T.astype(LOW)
    key_grad[...] = jnp.zeros_like(key_grad)
    value_grad[...] = jnp.zeros_like(value_grad)
    for index in range(length // block):
        keys = (index + 1) * block
        rows = pl.ds(index * block, block)
        key_rows = qkv_ref[0:keys, width : 2 * width]
        value_rows = qkv_ref[0:keys, 2 * width : 3 * width]
        doc_start = start_ref[0:1, rows]
        outs = []
        for head in range(slots):
            lanes = head_lanes(head, width)
            head_rows = slice(head * HEAD_DIM, (head + 1) * HEAD_DIM)
            query = jnp.where(lanes, qkv_ref[rows, 0:width] * LOW(scale), LOW(0))
            grad = jnp.where(lanes, grad_ref[rows, :], LOW(0))
            scores = dot(key_rows, query, 1, 1)
            scores = allowed_scores(scores, doc_start, index * block, keys, block)
            probs = jnp.exp(scores - stat_ref[head : head + 1, rows])
            grad_probs = dot(value_rows, grad, 1, 1)
            delta = jnp.sum(probs * grad_probs, 0, keepdims=True)
            grad_scores = (probs * (grad_probs - delta)).astype(LOW)
            value_grad[0:keys, :] += dot(probs.astype(LOW), grad)
            key_grad[0:keys, :] += dot(grad_scores, query)
            outs.append(dot(key_t[head_rows, 0:keys], grad_scores))
        out_ref[rows, 0:width] = (jnp.concatenate(outs, 0).T * scale).astype(LOW)
    out_ref[:, width : 2 * width] = key_grad[...].astype(LOW)
    out_ref[:, 2 * width : 3 * width] = value_grad[...].astype(LOW)


MESH = pl.DeviceIdType.MESH


def send(src, dst, send_sem, recv_sem, **target):
    return pltpu.make_async_remote_copy(
        src_ref=src,
        dst_ref=dst,
        send_sem=send_sem,
        recv_sem=recv_sem,
        device_id=target,
        device_id_type=MESH,
    )


def greet_line(chips):
    rank = lax.axis_index("ctx")
    chip, core = rank // 2, rank % 2
    barrier = pltpu.get_barrier_semaphore()
    pl.semaphore_signal(barrier, 1, device_id={"ctx": rank + 1 - 2 * core}, device_id_type=MESH)

    @pl.when(chip > 0)
    def _():
        pl.semaphore_signal(barrier, 1, device_id={"ctx": rank - 2}, device_id_type=MESH)

    @pl.when(chip < chips - 1)
    def _():
        pl.semaphore_signal(barrier, 1, device_id={"ctx": rank + 2}, device_id_type=MESH)

    sides = (chip > 0).astype(jnp.int32) + (chip < chips - 1).astype(jnp.int32)
    pl.semaphore_wait(barrier, 1 + sides)


def greet_all():
    barrier = pltpu.get_barrier_semaphore()
    count = 0
    for axis in ("ctx", "dp"):
        size = lax.axis_size(axis)
        here = lax.axis_index(axis)

        def one(off, carry, axis=axis, size=size, here=here):
            peer = lax.rem(here + off, size)
            pl.semaphore_signal(barrier, 1, device_id={axis: peer}, device_id_type=MESH)
            return carry

        lax.fori_loop(1, size, one, 0)
        count += size - 1
    pl.semaphore_wait(barrier, count)


class Swap:
    def __init__(self, axis, source, target, sems):
        self.axis, self.source, self.target = axis, source, target
        self.send_sems, self.recv_sems = sems
        self.rank = lax.axis_index(axis)
        self.size = lax.axis_size(axis)

    def copy(self, peer, origin, target):
        return send(
            self.source(peer),
            self.target(origin),
            self.send_sems.at[peer],
            self.recv_sems.at[origin],
            **{self.axis: target},
        )

    def every(self, act):
        def one(off, carry):
            act(lax.rem(self.rank + off, self.size))
            return carry

        lax.fori_loop(1, self.size, one, 0)

    def start(self):
        self.every(lambda peer: self.copy(peer, self.rank, peer).start())

    def wait(self):
        self.every(lambda peer: self.copy(peer, peer, self.rank).wait_recv())

    def drain(self):
        self.every(lambda peer: self.copy(peer, self.rank, peer).wait_send())

    @staticmethod
    def semaphores(size):
        return [pltpu.SemaphoreType.DMA((size,)), pltpu.SemaphoreType.DMA((size,))]


class PlaneGather:
    def __init__(self, blocks, sems):
        self.blocks = blocks
        self.size = blocks.shape[0]
        self.rank = lax.axis_index("dp")
        self.square = self.size == 4
        self.send_sems, self.recv_sems = sems
        if self.square:
            self.beside = self.rank + 1 - 2 * (self.rank % 2)
            self.above = self.rank + 2 - 4 * (self.rank // 2)
            half = blocks.shape[1] // 32 * 16
            self.low, self.high = pl.ds(0, half), pl.ds(half, blocks.shape[1] - half)
        else:
            self.swap = Swap("dp", lambda peer: blocks.at[self.rank], blocks.at.__getitem__, sems)

    def copy(self, index, ref, target):
        return send(ref, ref, self.send_sems.at[index], self.recv_sems.at[index], dp=target)

    def start(self):
        if not self.square:
            self.swap.start()
            return
        own = self.blocks.at[self.rank]
        self.copy(0, own, self.beside).start()
        self.copy(1, own, self.above).start()

    def relay(self):
        if not self.square:
            return
        self.copy(0, self.blocks.at[self.beside], self.beside).wait_recv()
        self.copy(2, self.blocks.at[self.beside, self.low], self.above).start()
        self.copy(1, self.blocks.at[self.above], self.above).wait_recv()
        self.copy(3, self.blocks.at[self.above, self.high], self.beside).start()

    def wait(self):
        if not self.square:
            self.swap.wait()
            self.swap.drain()
            return
        far = 3 - self.rank
        own = self.blocks.at[self.rank]
        self.copy(2, self.blocks.at[far, self.low], self.above).wait_recv()
        self.copy(3, self.blocks.at[far, self.high], self.beside).wait_recv()
        self.copy(0, own, self.beside).wait_send()
        self.copy(1, own, self.above).wait_send()
        self.copy(2, self.blocks.at[self.beside, self.low], self.above).wait_send()
        self.copy(3, self.blocks.at[self.above, self.high], self.beside).wait_send()

    semaphores = staticmethod(Swap.semaphores)


class PlaneSum:
    def __init__(self, blocks, landed, sems):
        self.blocks, self.landed = blocks, landed
        self.rank = lax.axis_index("dp")
        self.swap = Swap("dp", blocks.at.__getitem__, landed.at.__getitem__, sems)

    def start(self):
        self.swap.start()

    def total(self):
        self.swap.wait()
        total = self.blocks[self.rank].astype(WIDE)
        for off in range(1, self.swap.size):
            total = total + self.landed[lax.rem(self.rank + off, self.swap.size)].astype(WIDE)
        return total


class LineGather:
    def __init__(self, blocks, send_sems, recv_sems):
        self.blocks, self.send_sems, self.recv_sems = blocks, send_sems, recv_sems
        self.rank = lax.axis_index("ctx")
        self.chip, self.core = self.rank // 2, self.rank % 2
        self.chips = blocks.shape[0] // 2

    def copy(self, way, origin, target, src=None):
        block = self.blocks.at[origin]
        return send(
            block if src is None else src,
            block,
            self.send_sems.at[way, origin],
            self.recv_sems.at[origin],
            ctx=target,
        )

    def pass_on(self, origin, src=None):
        chip = origin // 2

        @pl.when((chip <= self.chip) & (self.chip < self.chips - 1))
        def _():
            self.copy(0, origin, self.rank + 2, src).start()

        @pl.when((chip >= self.chip) & (self.chip > 0))
        def _():
            self.copy(1, origin, self.rank - 2, src).start()

        self.copy(2, origin, self.rank + 1 - 2 * self.core, src).start()

    def arrive(self, step, part):
        side, other = part % 2, part // 2
        origin_chip = self.chip + jnp.where(side == 0, -step, step)
        origin = 2 * origin_chip + jnp.where(other == 0, self.core, 1 - self.core)
        valid = (origin_chip >= 0) & (origin_chip < self.chips) & ((step > 0) | (side == 0))

        @pl.when(valid & (origin != self.rank))
        def _():
            self.copy(0, origin, self.rank).wait_recv()

            @pl.when(other == 0)
            def _():
                self.pass_on(origin)

        return valid, origin

    def finish(self):
        def one(chip, carry):
            origin = 2 * chip + self.core

            @pl.when((chip <= self.chip) & (self.chip < self.chips - 1))
            def _():
                self.copy(0, origin, self.rank).wait_send()

            @pl.when((chip >= self.chip) & (self.chip > 0))
            def _():
                self.copy(1, origin, self.rank).wait_send()

            self.copy(2, origin, self.rank).wait_send()
            return carry

        lax.fori_loop(0, self.chips, one, 0)

    @staticmethod
    def semaphores(ctx):
        return [pltpu.SemaphoreType.DMA((3, ctx)), pltpu.SemaphoreType.DMA((ctx,))]


class LineSum:
    def __init__(self, blocks, pair, passing, sems):
        self.blocks, self.pair, self.passing = blocks, pair, passing
        self.pair_send, self.pair_recv, self.line_send, self.line_recv = sems
        self.rank = lax.axis_index("ctx")
        self.chip, self.core = self.rank // 2, self.rank % 2
        self.chips = blocks.shape[0] // 2
        self.pieces = self.line_recv.shape[2]
        self.piece = blocks.shape[1] // self.pieces

    def pair_copy(self, chip):
        return send(
            self.blocks.at[2 * chip + 1 - self.core],
            self.pair.at[chip],
            self.pair_send.at[chip],
            self.pair_recv.at[chip],
            ctx=self.rank + 1 - 2 * self.core,
        )

    def line_copy(self, way, chip, piece, target):
        rows = pl.ds(piece * self.piece, self.piece)
        return send(
            self.blocks.at[2 * chip + self.core, rows],
            self.passing.at[way, chip, rows],
            self.line_send.at[chip, piece],
            self.line_recv.at[way, chip, piece],
            ctx=target,
        )

    def both(self, chip, rows):
        mine = self.blocks[2 * chip + self.core, rows].astype(WIDE)
        return mine + self.pair[chip, rows].astype(WIDE)

    def forward(self, way, chip, valid):
        behind = jnp.where(way == 0, self.chip > 0, self.chip < self.chips - 1)
        target = self.rank + jnp.where(way == 0, 2, -2)

        @pl.when(valid)
        def _():
            self.pair_copy(chip).wait_recv()

            def one(piece, carry):
                rows = pl.ds(pl.multiple_of(piece * self.piece, self.piece), self.piece)
                total = self.both(chip, rows)

                @pl.when(behind)
                def _():
                    self.line_copy(way, chip, piece, target).wait_recv()
                    passing = self.passing[way, chip, rows].astype(WIDE)
                    self.blocks[2 * chip + self.core, rows] = (total + passing).astype(LOW)

                @pl.when(jnp.logical_not(behind))
                def _():
                    self.blocks[2 * chip + self.core, rows] = total.astype(LOW)

                self.line_copy(way, chip, piece, target).start()
                return carry

            lax.fori_loop(0, self.pieces, one, 0)

    def near_first(self, step, way):
        last = self.chips - 1
        chip = jnp.where(way == 0, step - self.chip, 2 * last - self.chip - step)
        ahead = jnp.where(way == 0, (chip > self.chip) & (chip <= last), (chip >= 0) & (chip < self.chip))
        self.forward(way, chip, ahead)

    def far_first(self, step, way):
        last = self.chips - 1
        chip = jnp.where(way == 0, last + self.chip - step, step - last + self.chip)
        ahead = jnp.where(way == 0, (chip > self.chip) & (chip <= last), (chip >= 0) & (chip < self.chip))
        self.forward(way, chip, ahead)

    def finish(self, out):
        self.pair_copy(self.chip).wait_recv()

        def one(piece, carry):
            rows = pl.ds(pl.multiple_of(piece * self.piece, self.piece), self.piece)
            out[rows] = self.both(self.chip, rows)

            @pl.when(self.chip > 0)
            def _():
                self.line_copy(0, self.chip, piece, self.rank).wait_recv()
                out[rows] = out[rows] + self.passing[0, self.chip, rows].astype(WIDE)

            @pl.when(self.chip < self.chips - 1)
            def _():
                self.line_copy(1, self.chip, piece, self.rank).wait_recv()
                out[rows] = out[rows] + self.passing[1, self.chip, rows].astype(WIDE)

            return carry

        lax.fori_loop(0, self.pieces, one, 0)

        def sent(chip, carry):
            self.pair_copy(chip).wait_send()

            @pl.when(chip != self.chip)
            def _():
                for piece in range(self.pieces):
                    self.line_copy(0, chip, piece, self.rank).wait_send()

            return carry

        lax.fori_loop(0, self.chips, sent, 0)

    @staticmethod
    def scratch(ctx, rows, columns, pieces):
        chips = ctx // 2
        return [
            pltpu.VMEM((ctx, rows, columns), LOW),
            pltpu.VMEM((chips, rows, columns), LOW),
            pltpu.VMEM((2, chips, rows, columns), LOW),
            pltpu.SemaphoreType.DMA((chips,)),
            pltpu.SemaphoreType.DMA((chips,)),
            pltpu.SemaphoreType.DMA((chips, pieces)),
            pltpu.SemaphoreType.DMA((2, chips, pieces)),
        ]


def feed_kernel(
    mixed_ref,
    in_ref,
    vectors_ref,
    bias_ref,
    proj_ref,
    fc_ref,
    out_ref,
    cot_ref,
    resid_ref,
    grad_ref,
    ffn_ref,
    act_ref,
    pre_ref,
    part_ref,
    gather_send,
    gather_recv,
    blocks,
    pair,
    passing,
    *sems,
):
    gather = LineGather(ffn_ref, gather_send, gather_recv)
    total = LineSum(blocks, pair, passing, sems)
    chips = gather.chips
    greet_line(chips)
    resid = in_ref[...].astype(WIDE) + dot(mixed_ref[:, 0:D], proj_ref[...]) + vectors_ref[0:1]
    resid_ref[...] = resid
    normed, _ = normalize(resid)
    ffn_ref[gather.rank] = (normed * vectors_ref[1:2] + vectors_ref[2:3]).astype(LOW)
    gather.pass_on(gather.rank)

    tokens = ffn_ref.shape[1]

    def work(chip):
        both = pl.ds(2 * chip, 2)
        pre = dot(ffn_ref[both].reshape(2 * tokens, D), fc_ref[...]) + bias_ref[0:1]
        bend = jnp.tanh(0.7978845608028654 * (pre + 0.044715 * pre * pre * pre))
        act = (0.5 * pre * (1.0 + bend)).astype(LOW)
        act_ref[both] = act.reshape(2, tokens, -1)
        slope = 0.5 * (1.0 + bend) + 0.5 * pre * (1.0 - bend * bend) * 0.7978845608028654 * (
            1.0 + 3 * 0.044715 * pre * pre
        )
        grad_act = dot(cot_ref[both].reshape(2 * tokens, D), out_ref[...], 1, 1)
        grad_pre = (slope * grad_act).astype(LOW)
        pre_ref[both] = grad_pre.reshape(2, tokens, -1)
        blocks[both] = dot(grad_pre, fc_ref[...], 1, 1).astype(LOW).reshape(2, tokens, D)
        total.pair_copy(chip).start()
        part_ref[both] = dot(act, out_ref[...]).astype(LOW).reshape(2, tokens, D)

    def step(index, carry):
        distance, side = index // 2, index % 2

        @pl.when(distance < chips)
        def _():
            @pl.when(side == 0)
            def _():
                gather.arrive(distance, 0)
                gather.arrive(distance, 1)

            valid, origin = gather.arrive(distance, 2 + side)

            @pl.when(valid)
            def _():
                work(origin // 2)

        @pl.when(side == 1)
        def _():
            def way(index, carry):
                total.near_first(distance, index)
                return carry

            lax.fori_loop(0, 2, way, 0)

        return carry

    lax.fori_loop(0, 2 * (2 * chips - 1), step, 0)
    total.finish(grad_ref)
    gather.finish()


def feed(mixed, own_in, vectors, bias, proj, fc, out, cot):
    ctx, tokens, _ = cot.shape
    width = fc.shape[1]
    return pl.pallas_call(
        feed_kernel,
        out_shape=(
            jax.ShapeDtypeStruct((tokens, D), WIDE),
            jax.ShapeDtypeStruct((tokens, D), WIDE),
            jax.ShapeDtypeStruct((ctx, tokens, D), LOW),
            jax.ShapeDtypeStruct((ctx, tokens, width), LOW),
            jax.ShapeDtypeStruct((ctx, tokens, width), LOW),
            jax.ShapeDtypeStruct((ctx, tokens, D), LOW),
        ),
        in_specs=[pl.BlockSpec(memory_space=pltpu.VMEM)] * 8,
        out_specs=[pl.BlockSpec(memory_space=pltpu.VMEM)] * 6,
        scratch_shapes=LineGather.semaphores(ctx) + LineSum.scratch(ctx, tokens, D, 4),
        compiler_params=pltpu.CompilerParams(
            vmem_limit_bytes=60 * MIB, collective_id=2, has_side_effects=True
        ),
        name="feed",
    )(mixed, own_in, vectors, bias, proj, fc, out, cot)


VMEM = pl.BlockSpec(memory_space=pltpu.VMEM)
HBM = pl.BlockSpec(memory_space=pl.ANY)
PAD = 64


def params(number):
    return pltpu.CompilerParams(
        vmem_limit_bytes=60 * MIB, collective_id=number, has_side_effects=True
    )


class Spread:
    def __init__(self, blocks, landed, wide, out, sems):
        self.blocks, self.landed, self.wide, self.out = blocks, landed, wide, out
        self.swap = Swap("ctx", blocks.at.__getitem__, landed.at.__getitem__, sems[:2])
        self.plane = PlaneGather(out, sems[2:])

    def start(self):
        self.swap.start()
        self.landed[self.swap.rank] = self.blocks[self.swap.rank]

    def cross(self):
        self.swap.wait()
        count = self.out.shape[1] // self.swap.size
        for index in range(self.swap.size):
            self.wide[index * count : index * count + PAD] = self.landed[index].astype(WIDE)
        self.out[self.plane.rank] = self.wide[0 : self.out.shape[1]].astype(LOW)
        self.plane.start()

    def wait(self):
        self.plane.wait()
        self.swap.drain()

    @staticmethod
    def scratch(ctx, dp, rows, columns):
        return [
            pltpu.VMEM((ctx, PAD, columns), LOW),
            pltpu.VMEM((rows + PAD, columns), WIDE),
            *Swap.semaphores(ctx),
            *PlaneGather.semaphores(dp),
        ]


class Collect:
    def __init__(self, parts, landed, wide, blocks, out, sems):
        self.parts, self.wide, self.blocks, self.out = parts, wide, blocks, out
        self.plane = PlaneSum(parts, landed, sems[:2])
        self.swap = Swap("ctx", blocks.at.__getitem__, out.at.__getitem__, sems[2:])

    def cross(self):
        rows = self.parts.shape[1]
        self.wide[0:rows] = self.plane.total()
        self.wide[rows:] = jnp.zeros((PAD, self.wide.shape[1]), WIDE)
        count = rows // self.swap.size
        for index in range(self.swap.size):
            self.blocks[index] = self.wide[index * count : index * count + PAD].astype(LOW)
        self.swap.start()
        self.out[self.swap.rank] = self.blocks[self.swap.rank]

    def wait(self):
        self.swap.wait()
        self.swap.drain()
        self.plane.swap.drain()

    @staticmethod
    def scratch(ctx, dp, rows, columns):
        return [
            pltpu.VMEM((dp, rows, columns), LOW),
            pltpu.VMEM((dp, rows, columns), LOW),
            pltpu.VMEM((rows + PAD, columns), WIDE),
            pltpu.VMEM((ctx, PAD, columns), LOW),
            *Swap.semaphores(dp),
            *Swap.semaphores(ctx),
        ]


def start_kernel(whole, small_ref, rows_ref, *refs):
    if whole:
        blocks_ref, small_out, rows_out, mat_out, *refs = refs
    else:
        small_out, rows_out, *refs = refs
    gather = LineGather(rows_out, *refs[:2])
    seq = lax.axis_index("dp")
    rank = gather.rank
    line = Swap("ctx", lambda peer: small_ref, lambda origin: small_out.at[seq, origin], refs[2:4])
    plane = Swap("dp", lambda peer: small_out.at[seq], small_out.at.__getitem__, refs[4:6])
    spread = Spread(blocks_ref, refs[6], refs[7], mat_out, refs[8:]) if whole else None
    greet_all()
    line.start()
    if whole:
        spread.start()
    gather.pass_on(rank, rows_ref)
    rows_out[rank] = rows_ref[...]
    small_out[seq, rank] = small_ref[...]
    line.wait()
    plane.start()
    if whole:
        spread.cross()

    def arrive(index, carry):
        gather.arrive(1 + index // 4, index % 4)
        return carry

    gather.arrive(0, 2)
    lax.fori_loop(0, 4, arrive, 0)
    if whole:
        spread.plane.relay()
    lax.fori_loop(4, 4 * (gather.chips - 1), arrive, 0)
    plane.wait()
    plane.drain()
    line.drain()
    gather.finish()
    if whole:
        spread.wait()


def start(small, rows, blocks):
    ctx, dp = lax.axis_size("ctx"), lax.axis_size("dp")
    tokens = rows.shape[0]
    whole = blocks is not None
    shapes = [
        jax.ShapeDtypeStruct((dp, ctx, *small.shape), WIDE),
        jax.ShapeDtypeStruct((ctx, tokens, D), LOW),
    ]
    scratch = LineGather.semaphores(ctx) + Swap.semaphores(ctx) + Swap.semaphores(dp)
    given = [small, rows]
    if whole:
        columns = blocks.shape[2]
        given.append(blocks)
        shapes.append(jax.ShapeDtypeStruct((dp, D // dp, columns), LOW))
        scratch += Spread.scratch(ctx, dp, D // dp, columns)
    return pl.pallas_call(
        functools.partial(start_kernel, whole),
        out_shape=shapes,
        in_specs=[VMEM] * len(given),
        out_specs=[VMEM] * len(shapes),
        scratch_shapes=scratch,
        compiler_params=params(0),
        name="start",
    )(*given)


def attend_kernel(
    block, whole, rows_ref, vectors_ref, bias_ref, mat_ref, start_ref, cot_ref, *refs
):
    if whole:
        blocks_ref, *refs = refs
    in_ref, qkv_ref, stat_ref, own_ref, cot_out, *refs = refs
    if whole:
        mat_out, *refs = refs
    mixed, value_t, *refs = refs
    gather = LineGather(cot_out, *refs[:2])
    ctx, tokens, _ = rows_ref.shape
    width = mixed.shape[1]
    swap = Swap(
        "ctx",
        lambda peer: mixed.at[pl.ds(pl.multiple_of(peer * tokens, tokens), tokens)],
        lambda origin: own_ref.at[:, pl.ds(pl.multiple_of(origin * width, width), width)],
        refs[2:4],
    )
    spread = Spread(blocks_ref, refs[4], refs[5], mat_out, refs[6:]) if whole else None
    greet_all()
    if whole:
        spread.start()
    gather.pass_on(gather.rank, cot_ref)
    cot_out[gather.rank] = cot_ref[...]

    def project(index, carry):
        both = pl.ds(2 * index, 2)
        rows = pl.ds(pl.multiple_of(2 * index * tokens, 2 * tokens), 2 * tokens)
        normed, _ = normalize(rows_ref[both].reshape(2 * tokens, D).astype(WIDE))
        attn_in = (normed * vectors_ref[0:1] + vectors_ref[1:2]).astype(LOW)
        in_ref[rows] = attn_in
        qkv_ref[rows] = (dot(attn_in, mat_ref[...]) + bias_ref[0:1]).astype(LOW)
        return carry

    lax.fori_loop(0, ctx // 2, project, 0)
    attend_body(block, qkv_ref, start_ref, mixed, stat_ref, value_t)
    swap.start()
    own_ref[:, pl.ds(pl.multiple_of(swap.rank * width, width), width)] = mixed[
        pl.ds(pl.multiple_of(swap.rank * tokens, tokens), tokens)
    ]
    if whole:
        spread.cross()

    def arrive(index, carry):
        gather.arrive(1 + index // 4, index % 4)
        return carry

    gather.arrive(0, 2)
    lax.fori_loop(0, 4, arrive, 0)
    if whole:
        spread.plane.relay()
    lax.fori_loop(4, 4 * (gather.chips - 1), arrive, 0)
    swap.wait()
    swap.drain()
    gather.finish()
    if whole:
        spread.wait()


def attend(rows, vectors, bias, mat, doc_start, cot, blocks, block):
    ctx, tokens, _ = rows.shape
    dp = lax.axis_size("dp")
    length = ctx * tokens
    width = mat.shape[1] // 3
    whole = blocks is not None
    given = [rows, vectors, bias, mat, doc_start, cot]
    shapes = [
        jax.ShapeDtypeStruct((length, D), LOW),
        jax.ShapeDtypeStruct((length, 3 * width), LOW),
        jax.ShapeDtypeStruct((8, length), WIDE),
        jax.ShapeDtypeStruct((tokens, ctx * width), LOW),
        jax.ShapeDtypeStruct((ctx, tokens, D), LOW),
    ]
    scratch = [pltpu.VMEM((length, width), LOW), pltpu.VMEM((width, length), LOW)]
    scratch += LineGather.semaphores(ctx) + Swap.semaphores(ctx)
    if whole:
        columns = blocks.shape[2]
        given.append(blocks)
        shapes.append(jax.ShapeDtypeStruct((dp, D // dp, columns), LOW))
        scratch += Spread.scratch(ctx, dp, D // dp, columns)
    return pl.pallas_call(
        functools.partial(attend_kernel, block, whole),
        out_shape=shapes,
        in_specs=[VMEM] * len(given),
        out_specs=[VMEM] * len(shapes),
        scratch_shapes=scratch,
        compiler_params=params(1),
        name="attend",
    )(*given)


def back_kernel(
    block,
    whole,
    grad_ref,
    resid_ref,
    own_cot,
    vectors_ref,
    proj_ref,
    qkv_ref,
    start_ref,
    stat_ref,
    ffn_hbm,
    pre_hbm,
    act_hbm,
    cot_hbm,
    resid_out,
    low_out,
    vector_out,
    units_out,
    rows_out,
    share_out,
    fc_out,
    ffn,
    pre,
    act,
    cot,
    load_sems,
    own_grad,
    head_grad,
    key_t,
    key_grad,
    value_grad,
    wide,
    *refs,
):
    loads = [
        pltpu.make_async_copy(src, dst, load_sems.at[index])
        for index, (src, dst) in enumerate(
            ((act_hbm, act), (cot_hbm, cot), (ffn_hbm, ffn), (pre_hbm, pre))
        )
    ]
    for load in loads:
        load.start()
    tokens = own_cot.shape[0]
    length, width = head_grad.shape
    units = share_out.shape[0]
    swap = Swap(
        "ctx",
        lambda peer: own_grad.at[:, pl.ds(pl.multiple_of(peer * width, width), width)],
        lambda origin: head_grad.at[pl.ds(pl.multiple_of(origin * tokens, tokens), tokens)],
        refs[:2],
    )
    share = PlaneSum(refs[2], refs[3], refs[4:6])
    if whole:
        collect = Collect(*refs[6:10], fc_out, refs[10:])
    dp = share.swap.size
    greet_all()
    grad = grad_ref[...]
    normed, scale = normalize(resid_ref[...])
    grad_resid = own_cot[...].astype(WIDE) + norm_back(normed, scale, vectors_ref[0:1], grad)
    resid_out[...] = grad_resid
    low = grad_resid.astype(LOW)
    low_out[...] = low
    own_grad[:, 0:D] = dot(low, proj_ref[...], 1, 1).astype(LOW)
    own_grad[:, D:] = jnp.zeros((tokens, own_grad.shape[1] - D), LOW)
    swap.start()
    head_grad[pl.ds(pl.multiple_of(swap.rank * tokens, tokens), tokens)] = own_grad[
        :, pl.ds(pl.multiple_of(swap.rank * width, width), width)
    ]
    vector_out[0:1] = jnp.sum(grad_resid, 0, keepdims=True)
    vector_out[1:2] = jnp.sum(grad * normed, 0, keepdims=True)
    vector_out[2:3] = jnp.sum(grad, 0, keepdims=True)
    vector_out[3:4] = jnp.sum(own_cot[...].astype(WIDE), 0, keepdims=True)
    vector_out[4:8] = jnp.zeros((4, D), WIDE)
    loads[0].wait()
    loads[1].wait()
    wide[...] = dot(act[...].reshape(length, -1), cot[...].reshape(length, D), 0, 0)
    for index in range(dp):
        share.blocks[index, 0:units] = wide[index * units : (index + 1) * units].astype(LOW)
        if share.blocks.shape[1] > units:
            share.blocks[index, units:] = jnp.zeros((share.blocks.shape[1] - units, D), LOW)
    share.start()
    loads[2].wait()
    loads[3].wait()
    grad_pre = pre[...].reshape(length, -1)
    units_out[...] = dot(jnp.ones((8, length), LOW), grad_pre)
    for index in range(dp):
        rows = slice(index * (D // dp), (index + 1) * (D // dp))
        part = dot(ffn[:, :, rows].reshape(length, D // dp), grad_pre, 0, 0)
        if whole:
            collect.parts[index] = part.astype(LOW)
        else:
            fc_out[rows] = part
    if whole:
        collect.plane.start()
    swap.wait()
    attend_back_body(
        block, qkv_ref, start_ref, stat_ref, head_grad, rows_out, key_t, key_grad, value_grad
    )
    if whole:
        collect.cross()
    share_out[...] = share.total()[0:units]
    swap.drain()
    share.swap.drain()
    if whole:
        collect.wait()


def back(grad, resid, own_cot, vectors, proj, qkv, doc_start, stats, ffn, pre, act, cot, block, whole):
    ctx, tokens, _ = cot.shape
    dp = lax.axis_size("dp")
    length = ctx * tokens
    width = qkv.shape[1] // 3
    columns = act.shape[2]
    units = columns // dp
    padded = -(-units // 16) * 16
    rows = D // dp
    shapes = [
        jax.ShapeDtypeStruct((tokens, D), WIDE),
        jax.ShapeDtypeStruct((tokens, D), LOW),
        jax.ShapeDtypeStruct((8, D), WIDE),
        jax.ShapeDtypeStruct((8, columns), WIDE),
        jax.ShapeDtypeStruct((length, 3 * width), LOW),
        jax.ShapeDtypeStruct((units, D), WIDE),
        jax.ShapeDtypeStruct((ctx, PAD, columns), LOW)
        if whole
        else jax.ShapeDtypeStruct((D, columns), WIDE),
    ]
    scratch = [
        pltpu.VMEM(ffn.shape, LOW),
        pltpu.VMEM(pre.shape, LOW),
        pltpu.VMEM(act.shape, LOW),
        pltpu.VMEM(cot.shape, LOW),
        pltpu.SemaphoreType.DMA((4,)),
        pltpu.VMEM((tokens, ctx * width), LOW),
        pltpu.VMEM((length, width), LOW),
        pltpu.VMEM((width, length), LOW),
        pltpu.VMEM((length, width), WIDE),
        pltpu.VMEM((length, width), WIDE),
        pltpu.VMEM((columns, D), WIDE),
        *Swap.semaphores(ctx),
        pltpu.VMEM((dp, padded, D), LOW),
        pltpu.VMEM((dp, padded, D), LOW),
        *Swap.semaphores(dp),
    ]
    if whole:
        scratch += Collect.scratch(ctx, dp, rows, columns)
    return pl.pallas_call(
        functools.partial(back_kernel, block, whole),
        out_shape=shapes,
        in_specs=[VMEM] * 8 + [HBM] * 4,
        out_specs=[VMEM] * 7,
        scratch_shapes=scratch,
        compiler_params=params(3),
        name="back",
    )(grad, resid, own_cot, vectors, proj, qkv, doc_start, stats, ffn, pre, act, cot)


def last_kernel(
    whole,
    rows_ref,
    mat_ref,
    in_ref,
    own_ref,
    resid_ref,
    vectors_ref,
    grad_out,
    vector_out,
    heads_out,
    mat_out,
    grad,
    *refs,
):
    total = LineSum(*refs[:3], refs[3:7])
    if whole:
        collect = Collect(*refs[7:11], mat_out, refs[11:])
    chips, core = total.chips, total.core
    tokens = own_ref.shape[0]
    dp = lax.axis_size("dp")
    if whole:
        greet_all()
    else:
        greet_line(chips)

    def partial_sum(index, carry):
        chip = lax.rem(chips - 1 - index // 2 + jnp.where(index % 2 == 0, 0, 2 * (index // 2) + 1), chips)
        rows = pl.ds(pl.multiple_of(2 * chip * tokens, 2 * tokens), 2 * tokens)
        part = dot(rows_ref[rows], mat_ref[...], 1, 1).astype(LOW)
        total.blocks[pl.ds(2 * chip, 2)] = part.reshape(2, tokens, D)
        total.pair_copy(chip).start()
        return carry

    lax.fori_loop(0, chips, partial_sum, 0)

    def forward(index, carry):
        total.far_first(index // 2, index % 2)
        return carry

    lax.fori_loop(0, 2, forward, 0)
    for index in range(dp):
        rows = slice(index * (D // dp), (index + 1) * (D // dp))
        part = dot(in_ref[:, rows], rows_ref[...], 0, 0)
        if whole:
            collect.parts[index] = part.astype(LOW)
        else:
            mat_out[rows] = part
    if whole:
        collect.plane.start()
    lax.fori_loop(2, 2 * (2 * chips - 1), forward, 0)
    heads_out[...] = dot(jnp.ones((8, rows_ref.shape[0]), LOW), rows_ref[...])
    if whole:
        collect.cross()
    total.finish(grad)
    normed, scale = normalize(own_ref[...].astype(WIDE))
    incoming = grad[...]
    grad_out[...] = resid_ref[...] + norm_back(normed, scale, vectors_ref[0:1], incoming)
    vector_out[0:1] = jnp.sum(incoming * normed, 0, keepdims=True)
    vector_out[1:2] = jnp.sum(incoming, 0, keepdims=True)
    vector_out[2:8] = jnp.zeros((6, D), WIDE)
    if whole:
        collect.wait()


def last(rows, mat, attn_in, own_in, resid, vectors, whole):
    ctx, dp = lax.axis_size("ctx"), lax.axis_size("dp")
    tokens = own_in.shape[0]
    columns = rows.shape[1]
    shapes = [
        jax.ShapeDtypeStruct((tokens, D), WIDE),
        jax.ShapeDtypeStruct((8, D), WIDE),
        jax.ShapeDtypeStruct((8, columns), WIDE),
        jax.ShapeDtypeStruct((ctx, PAD, columns), LOW)
        if whole
        else jax.ShapeDtypeStruct((D, columns), WIDE),
    ]
    scratch = [pltpu.VMEM((tokens, D), WIDE), *LineSum.scratch(ctx, tokens, D, 4)]
    if whole:
        scratch += Collect.scratch(ctx, dp, D // dp, columns)
    return pl.pallas_call(
        functools.partial(last_kernel, whole),
        out_shape=shapes,
        in_specs=[VMEM] * 6,
        out_specs=[VMEM] * 4,
        scratch_shapes=scratch,
        compiler_params=params(4),
        name="last",
    )(rows, mat, attn_in, own_in, resid, vectors)


def vector_kernel(parts_ref, out_ref, plane_landed, line_parts, line_landed, *sems):
    plane = PlaneSum(parts_ref, plane_landed, sems[:2])
    line = Swap("ctx", line_parts.at.__getitem__, line_landed.at.__getitem__, sems[2:])
    greet_all()
    plane.start()
    line_parts[...] = plane.total()
    line.start()
    line.wait()
    total = line_parts[line.rank]
    for off in range(1, line.size):
        total = total + line_landed[lax.rem(line.rank + off, line.size)]
    out_ref[...] = total
    plane.swap.drain()
    line.drain()


def sum_vector(parts):
    dp, ctx = parts.shape[:2]
    return pl.pallas_call(
        vector_kernel,
        out_shape=jax.ShapeDtypeStruct(parts.shape[2:], WIDE),
        in_specs=[VMEM],
        out_specs=VMEM,
        scratch_shapes=[
            pltpu.VMEM(parts.shape, WIDE),
            pltpu.VMEM(parts.shape[1:], WIDE),
            pltpu.VMEM(parts.shape[1:], WIDE),
            *Swap.semaphores(dp),
            *Swap.semaphores(ctx),
        ],
        compiler_params=params(5),
        name="sum_vector",
    )(parts)


def gather_rows(block):
    return lax.all_gather(block, ("dp", "ctx"), axis=0, tiled=True)


def by_rank_heads(rows, ctx, slots):
    count = rows.shape[0]
    split = rows.reshape(count, 3, D)
    split = jnp.pad(split, ((0, 0), (0, 0), (0, (ctx * slots - HEADS) * HEAD_DIM)))
    split = split.reshape(count, 3, ctx, slots * HEAD_DIM)
    return split.transpose(2, 0, 1, 3).reshape(ctx, count, 3 * slots * HEAD_DIM)


def from_rank_heads(blocks, slots):
    ctx, count = blocks.shape[:2]
    split = blocks.reshape(ctx, count, 3, slots * HEAD_DIM).transpose(1, 2, 0, 3)
    return split.reshape(count, 3, ctx * slots * HEAD_DIM)[:, :, :D].reshape(count, 3 * D)


def by_rank_units(rows, ctx, dp):
    count = rows.shape[0]
    split = rows.reshape(count, dp, ctx, FF // (dp * ctx)).transpose(2, 0, 1, 3)
    return split.reshape(ctx, count, FF // ctx)


def from_rank_units(blocks, dp):
    ctx, count = blocks.shape[:2]
    split = blocks.reshape(ctx, count, dp, FF // (dp * ctx)).transpose(1, 2, 0, 3)
    return split.reshape(count, FF)


def rank_vector(vector, ctx, slots, rank):
    padded = jnp.pad(vector, (0, (ctx * slots - HEADS) * HEAD_DIM))
    width = slots * HEAD_DIM
    return lax.dynamic_slice_in_dim(padded, rank * width, width, 0)


def pad_rows(blocks):
    return jnp.pad(blocks, ((0, 0), (0, PAD - blocks.shape[1]), (0, 0)))


def shards(
    hidden_in, qkv_weight, proj_weight, fc_weight, out_weight, small_params, segments, cotangent
):
    tokens = hidden_in.shape[1]
    length = segments.shape[1]
    ctx = lax.axis_size("ctx")
    dp = lax.axis_size("dp")
    owners = dp * ctx
    rank = lax.axis_index("ctx")
    slots = -(-HEADS // ctx)
    width = slots * HEAD_DIM
    units = FF // owners
    rows = D // owners
    whole = D % owners == 0
    block = min(256, length)
    both = ("dp", "ctx")

    vec_count = small_params.shape[0]
    vec_pad = -(-vec_count // 1024) * 1024
    small = jnp.pad(small_params.astype(WIDE), (0, vec_pad - vec_count)).reshape(-1, 128)
    if whole:
        qkv_blocks = pad_rows(by_rank_heads(qkv_weight.reshape(rows, 3 * D), ctx, slots))
        small, rows_in, mat_qkv = start(small, hidden_in[0], qkv_blocks)
        mat_qkv = mat_qkv.reshape(D, 3 * width)
        fc_blocks = pad_rows(by_rank_units(fc_weight.reshape(rows, FF), ctx, dp))
        mat_proj = gather_rows(proj_weight.reshape(1, rows, D)).reshape(D, D)
    else:
        small, rows_in = start(small, hidden_in[0], None)
        fc_blocks = None
        mat_qkv = by_rank_heads(gather_rows(qkv_weight).reshape(D, 3 * D), ctx, slots)
        mat_qkv = lax.dynamic_index_in_dim(mat_qkv, rank, 0, keepdims=False)
        mat_fc = by_rank_units(gather_rows(fc_weight).reshape(D, FF), ctx, dp)
        mat_fc = lax.dynamic_index_in_dim(mat_fc, rank, 0, keepdims=False)
        mat_proj = gather_rows(proj_weight).reshape(D, D)
    mat_out = lax.all_gather(
        out_weight.reshape(1, units, D), "dp", axis=0, tiled=True
    ).reshape(dp * units, D)
    small = small.reshape(owners, vec_pad)[:, :vec_count].reshape(-1)
    gain_one, shift_one, bias_query, bias_value, bias_proj, gain_two, shift_two = [
        small[i * D : (i + 1) * D] for i in range(7)
    ]
    bias_fc = small[7 * D : 7 * D + FF]
    bias_out = small[7 * D + FF :]
    bias_units = lax.dynamic_index_in_dim(
        bias_fc.reshape(dp, ctx, units), rank, 1, keepdims=False
    ).reshape(-1)
    bias_qkv = jnp.concatenate(
        [
            rank_vector(bias_query, ctx, slots, rank),
            jnp.zeros((width,), WIDE),
            rank_vector(bias_value, ctx, slots, rank),
        ]
    )

    docs = segments[0]
    doc_start = jnp.sum((docs[:, None] < docs[None, :]).astype(jnp.int32), 0)[None]
    attn_in, qkv, stats, own_mixed, cot, *rest = attend(
        rows_in,
        jnp.stack([gain_one, shift_one]),
        bias_qkv[None],
        mat_qkv,
        doc_start,
        cotangent[0],
        fc_blocks,
        block,
    )
    if whole:
        mat_fc = rest[0].reshape(D, FF // ctx)
    resid, grad_normed_two, ffn_in, act, grad_pre, out_part = feed(
        own_mixed,
        hidden_in[0],
        jnp.stack([bias_proj, gain_two, shift_two]),
        bias_units[None],
        mat_proj,
        mat_fc,
        mat_out,
        cot,
    )
    output = (
        resid
        + lax.psum_scatter(
            out_part.reshape(length, D), "ctx", scatter_dimension=0, tiled=True
        ).astype(WIDE)
        + bias_out
    )

    grad_resid, resid_low, sums_two, sums_units, grad_rows, grad_out, grad_fc = back(
        grad_normed_two,
        resid,
        cotangent[0],
        gain_two[None],
        mat_proj,
        qkv,
        doc_start,
        stats,
        ffn_in,
        grad_pre,
        act,
        cot,
        block,
        whole,
    )
    grad_proj = dot(own_mixed[:, :D], resid_low, 0, 0).astype(LOW)
    if whole:
        part = lax.psum_scatter(grad_proj, "dp", scatter_dimension=0, tiled=True)
        share_proj = lax.psum_scatter(
            part.reshape(ctx, rows, D), "ctx", scatter_dimension=0, tiled=True
        )
    else:
        share_proj = lax.psum_scatter(grad_proj.reshape(-1), both, scatter_dimension=0, tiled=True)
    grad_input, sums_one, sums_heads, grad_qkv = last(
        grad_rows, mat_qkv, attn_in, hidden_in[0], grad_resid, gain_one[None], whole
    )
    if whole:
        share_fc = from_rank_units(grad_fc[:, :rows], dp)
        share_qkv = from_rank_heads(grad_qkv[:, :rows], slots)
    else:
        here = (jnp.arange(ctx) == rank)[:, None, None]
        full_fc = from_rank_units(jnp.where(here, grad_fc[None], 0.0), dp).reshape(-1)
        full_qkv = from_rank_heads(jnp.where(here, grad_qkv[None], 0.0), slots).reshape(-1)
        share_fc = lax.psum_scatter(full_fc, both, scatter_dimension=0, tiled=True)
        share_qkv = lax.psum_scatter(full_qkv, both, scatter_dimension=0, tiled=True)

    def spread_heads(part):
        padded = jnp.zeros((ctx * width,), WIDE)
        return lax.dynamic_update_slice_in_dim(padded, part, rank * width, 0)[:D]

    sums_units = lax.dynamic_update_slice_in_dim(
        jnp.zeros((dp, ctx, units), WIDE), sums_units[0].reshape(dp, 1, units), rank, 1
    ).reshape(FF)
    vector = jnp.concatenate(
        [
            sums_one[0],
            sums_one[1],
            spread_heads(sums_heads[0, :width]),
            spread_heads(sums_heads[0, 2 * width :]),
            sums_two[0],
            sums_two[1],
            sums_two[2],
            sums_units,
            sums_two[3],
        ]
    ).reshape(owners, vec_count)
    vector = jnp.pad(vector, ((0, 0), (0, vec_pad - vec_count))).reshape(dp, ctx, -1, 128)
    share_vector = sum_vector(vector)
    return (
        output[None],
        grad_input[None],
        share_qkv.astype(WIDE).reshape(-1),
        share_proj.astype(WIDE).reshape(-1),
        share_fc.astype(WIDE).reshape(-1),
        grad_out.reshape(-1),
        share_vector.reshape(-1)[:vec_count],
    )


def solution(mesh):
    flat = P(("dp", "ctx"))
    rows = P("dp", "ctx", None)
    return jax.shard_map(
        shards,
        mesh=mesh,
        in_specs=(rows, flat, flat, flat, flat, flat, P("dp", None), rows),
        out_specs=(rows, rows, flat, flat, flat, flat, flat),
        check_vma=False,
    )
```

```python
import functools

import jax
import jax.numpy as jnp
from jax import lax
from jax.experimental import pallas as pl
from jax.experimental.pallas import tpu as pltpu
from jax.sharding import PartitionSpec as P

D = 1600
HEADS = 25
HEAD_DIM = 64
FF = 6400
EPSILON = 1e-05
LOW = jnp.bfloat16
WIDE = jnp.float32
MIB = 1024 * 1024


def dot(left, right, left_dim=1, right_dim=0):
    return lax.dot_general(
        left, right, (((left_dim,), (right_dim,)), ((), ())), preferred_element_type=WIDE
    )


def normalize(rows):
    centre = rows - jnp.mean(rows, -1, keepdims=True)
    spread = jnp.mean(centre * centre, -1, keepdims=True)
    scale = lax.rsqrt(spread + EPSILON)
    return centre * scale, scale


def norm_back(normed, scale, gain, incoming):
    scaled = gain * incoming
    return scale * (
        scaled
        - jnp.mean(scaled, -1, keepdims=True)
        - normed * jnp.mean(scaled * normed, -1, keepdims=True)
    )


def head_lanes(head, width):
    lane = lax.broadcasted_iota(jnp.int32, (1, width), 1)
    return (lane // HEAD_DIM) == head


def allowed_scores(scores, doc_start, first_query, keys, block):
    key_pos = lax.broadcasted_iota(jnp.int32, (keys, block), 0)
    query_pos = first_query + lax.broadcasted_iota(jnp.int32, (keys, block), 1)
    seen = (key_pos >= doc_start) & (key_pos <= query_pos)
    return jnp.where(seen, scores, -1e30)


def attend_body(block, qkv_ref, start_ref, mixed_ref, stat_ref, value_t):
    length = qkv_ref.shape[0]
    width = mixed_ref.shape[1]
    slots = width // HEAD_DIM
    value_t[...] = qkv_ref[:, 2 * width : 3 * width].astype(WIDE).T.astype(LOW)
    stat_ref[...] = jnp.zeros_like(stat_ref)
    for index in range(length // block):
        keys = (index + 1) * block
        rows = pl.ds(index * block, block)
        key_rows = qkv_ref[0:keys, width : 2 * width]
        doc_start = start_ref[0:1, rows]
        outs = []
        for head in range(slots):
            query = jnp.where(
                head_lanes(head, width), qkv_ref[rows, 0:width] * LOW(HEAD_DIM**-0.5), LOW(0)
            )
            scores = dot(key_rows, query, 1, 1)
            scores = allowed_scores(scores, doc_start, index * block, keys, block)
            top = jnp.max(scores, 0, keepdims=True)
            expo = jnp.exp(scores - top)
            total = jnp.sum(expo, 0, keepdims=True)
            head_rows = slice(head * HEAD_DIM, (head + 1) * HEAD_DIM)
            out = dot(value_t[head_rows, 0:keys], expo.astype(LOW))
            outs.append(out / total)
            stat_ref[head : head + 1, rows] = top + jnp.log(total)
        mixed_ref[rows, :] = jnp.concatenate(outs, 0).T.astype(LOW)


def attend_back_body(
    block, qkv_ref, start_ref, stat_ref, grad_ref, out_ref, key_t, key_grad, value_grad, after
):
    length = qkv_ref.shape[0]
    width = grad_ref.shape[1]
    slots = width // HEAD_DIM
    scale = HEAD_DIM**-0.5
    key_t[...] = qkv_ref[:, width : 2 * width].astype(WIDE).T.astype(LOW)
    key_grad[...] = jnp.zeros_like(key_grad)
    value_grad[...] = jnp.zeros_like(value_grad)
    for index in range(length // block):
        keys = (index + 1) * block
        rows = pl.ds(index * block, block)
        key_rows = qkv_ref[0:keys, width : 2 * width]
        value_rows = qkv_ref[0:keys, 2 * width : 3 * width]
        doc_start = start_ref[0:1, rows]
        outs = []
        for head in range(slots):
            lanes = head_lanes(head, width)
            head_rows = slice(head * HEAD_DIM, (head + 1) * HEAD_DIM)
            query = jnp.where(lanes, qkv_ref[rows, 0:width] * LOW(scale), LOW(0))
            grad = jnp.where(lanes, grad_ref[rows, :], LOW(0))
            scores = dot(key_rows, query, 1, 1)
            scores = allowed_scores(scores, doc_start, index * block, keys, block)
            probs = jnp.exp(scores - stat_ref[head : head + 1, rows])
            grad_probs = dot(value_rows, grad, 1, 1)
            delta = jnp.sum(probs * grad_probs, 0, keepdims=True)
            grad_scores = (probs * (grad_probs - delta)).astype(LOW)
            value_grad[0:keys, :] += dot(probs.astype(LOW), grad)
            key_grad[0:keys, :] += dot(grad_scores, query)
            outs.append(dot(key_t[head_rows, 0:keys], grad_scores))
        out_ref[rows, 0:width] = (jnp.concatenate(outs, 0).T * scale).astype(LOW)
        if index in after:
            after[index]()
    out_ref[:, width : 2 * width] = key_grad[...].astype(LOW)
    out_ref[:, 2 * width : 3 * width] = value_grad[...].astype(LOW)


MESH = pl.DeviceIdType.MESH


def send(src, dst, send_sem, recv_sem, **target):
    return pltpu.make_async_remote_copy(
        src_ref=src,
        dst_ref=dst,
        send_sem=send_sem,
        recv_sem=recv_sem,
        device_id=target,
        device_id_type=MESH,
    )


def greet_line(chips):
    rank = lax.axis_index("ctx")
    chip, core = rank // 2, rank % 2
    barrier = pltpu.get_barrier_semaphore()
    pl.semaphore_signal(barrier, 1, device_id={"ctx": rank + 1 - 2 * core}, device_id_type=MESH)

    @pl.when(chip > 0)
    def _():
        pl.semaphore_signal(barrier, 1, device_id={"ctx": rank - 2}, device_id_type=MESH)

    @pl.when(chip < chips - 1)
    def _():
        pl.semaphore_signal(barrier, 1, device_id={"ctx": rank + 2}, device_id_type=MESH)

    sides = (chip > 0).astype(jnp.int32) + (chip < chips - 1).astype(jnp.int32)
    pl.semaphore_wait(barrier, 1 + sides)


def greet_all():
    barrier = pltpu.get_barrier_semaphore()
    count = 0
    for axis in ("ctx", "dp"):
        size = lax.axis_size(axis)
        here = lax.axis_index(axis)

        def one(off, carry, axis=axis, size=size, here=here):
            peer = lax.rem(here + off, size)
            pl.semaphore_signal(barrier, 1, device_id={axis: peer}, device_id_type=MESH)
            return carry

        lax.fori_loop(1, size, one, 0)
        count += size - 1
    pl.semaphore_wait(barrier, count)


class Swap:
    def __init__(self, axis, source, target, sems):
        self.axis, self.source, self.target = axis, source, target
        self.send_sems, self.recv_sems = sems
        self.rank = lax.axis_index(axis)
        self.size = lax.axis_size(axis)

    def copy(self, peer, origin, target):
        return send(
            self.source(peer),
            self.target(origin),
            self.send_sems.at[peer],
            self.recv_sems.at[origin],
            **{self.axis: target},
        )

    def every(self, act):
        def one(off, carry):
            act(lax.rem(self.rank + off, self.size))
            return carry

        lax.fori_loop(1, self.size, one, 0)

    def start(self):
        self.every(lambda peer: self.copy(peer, self.rank, peer).start())

    def wait(self):
        self.every(lambda peer: self.copy(peer, peer, self.rank).wait_recv())

    def drain(self):
        self.every(lambda peer: self.copy(peer, self.rank, peer).wait_send())

    @staticmethod
    def semaphores(size):
        return [pltpu.SemaphoreType.DMA((size,)), pltpu.SemaphoreType.DMA((size,))]


class ChipSwap(Swap):
    def __init__(self, source, target, sems):
        super().__init__("ctx", source, target, sems)
        self.core = self.rank % 2
        self.rank, self.size = self.rank // 2, self.size // 2

    def copy(self, peer, origin, target):
        return send(
            self.source(peer),
            self.target(origin),
            self.send_sems.at[peer],
            self.recv_sems.at[origin],
            ctx=2 * target + self.core,
        )


class PlaneGather:
    def __init__(self, blocks, sems):
        self.blocks = blocks
        self.size = blocks.shape[0]
        self.rank = lax.axis_index("dp")
        self.square = self.size == 4
        self.send_sems, self.recv_sems = sems
        if self.square:
            self.beside = self.rank + 1 - 2 * (self.rank % 2)
            self.above = self.rank + 2 - 4 * (self.rank // 2)
            half = blocks.shape[1] // 32 * 16
            self.low, self.high = pl.ds(0, half), pl.ds(half, blocks.shape[1] - half)
        else:
            self.swap = Swap("dp", lambda peer: blocks.at[self.rank], blocks.at.__getitem__, sems)

    def copy(self, index, ref, target):
        return send(ref, ref, self.send_sems.at[index], self.recv_sems.at[index], dp=target)

    def start(self):
        if not self.square:
            self.swap.start()
            return
        own = self.blocks.at[self.rank]
        self.copy(0, own, self.beside).start()
        self.copy(1, own, self.above).start()

    def relay(self):
        if not self.square:
            return
        self.copy(0, self.blocks.at[self.beside], self.beside).wait_recv()
        self.copy(2, self.blocks.at[self.beside, self.low], self.above).start()
        self.copy(1, self.blocks.at[self.above], self.above).wait_recv()
        self.copy(3, self.blocks.at[self.above, self.high], self.beside).start()

    def wait(self):
        if not self.square:
            self.swap.wait()
            self.swap.drain()
            return
        far = 3 - self.rank
        own = self.blocks.at[self.rank]
        self.copy(2, self.blocks.at[far, self.low], self.above).wait_recv()
        self.copy(3, self.blocks.at[far, self.high], self.beside).wait_recv()
        self.copy(0, own, self.beside).wait_send()
        self.copy(1, own, self.above).wait_send()
        self.copy(2, self.blocks.at[self.beside, self.low], self.above).wait_send()
        self.copy(3, self.blocks.at[self.above, self.high], self.beside).wait_send()

    semaphores = staticmethod(Swap.semaphores)


class PlaneSum:
    def __init__(self, blocks, landed, sems):
        self.blocks, self.landed = blocks, landed
        self.rank = lax.axis_index("dp")
        self.send_sems, self.recv_sems = sems
        self.swap = Swap("dp", blocks.at.__getitem__, landed.at.__getitem__, sems)
        self.square = blocks.shape[0] == 4
        if self.square:
            self.beside = self.rank + 1 - 2 * (self.rank % 2)
            self.above = self.rank + 2 - 4 * (self.rank // 2)
            half = blocks.shape[1] // 32 * 16
            self.low, self.high = pl.ds(0, half), pl.ds(half, blocks.shape[1] - half)

    def copy(self, index):
        far = 3 - self.rank
        block, slot, rows, target = (
            (far, 0, self.low, self.beside),
            (self.beside, 1, self.low, self.beside),
            (far, 0, self.high, self.above),
            (self.above, 1, self.high, self.above),
            (self.above, 2, self.low, self.above),
            (self.beside, 2, self.high, self.beside),
        )[index]
        return send(
            self.blocks.at[block, rows],
            self.landed.at[slot, rows],
            self.send_sems.at[index],
            self.recv_sems.at[index],
            dp=target,
        )

    def start(self):
        if not self.square:
            self.swap.start()
            return
        for index in range(4):
            self.copy(index).start()

    def relay(self):
        if not self.square:
            return
        for index, block, rows in ((0, self.above, self.low), (2, self.beside, self.high)):
            self.copy(index).wait_recv()
            total = self.blocks[block, rows].astype(WIDE) + self.landed[0, rows].astype(WIDE)
            self.blocks[block, rows] = total.astype(self.blocks.dtype)
            self.copy(4 + index // 2).start()

    def total(self):
        total = self.blocks[self.rank].astype(WIDE)
        if not self.square:
            self.swap.wait()
            for off in range(1, self.swap.size):
                total = total + self.landed[lax.rem(self.rank + off, self.swap.size)].astype(WIDE)
            return total
        for index in (1, 3, 4, 5):
            self.copy(index).wait_recv()
        return total + self.landed[1].astype(WIDE) + self.landed[2].astype(WIDE)

    def drain(self):
        if not self.square:
            self.swap.drain()
            return
        for index in range(6):
            self.copy(index).wait_send()

    @staticmethod
    def semaphores(size):
        return Swap.semaphores(max(size, 6))


class LineGather:
    def __init__(self, blocks, send_sems, recv_sems):
        self.blocks, self.send_sems, self.recv_sems = blocks, send_sems, recv_sems
        self.rank = lax.axis_index("ctx")
        self.chip, self.core = self.rank // 2, self.rank % 2
        self.chips = blocks.shape[0] // 2

    def copy(self, way, origin, target, src=None):
        block = self.blocks.at[origin]
        return send(
            block if src is None else src,
            block,
            self.send_sems.at[way, origin],
            self.recv_sems.at[origin],
            ctx=target,
        )

    def pass_on(self, origin, src=None):
        chip = origin // 2

        @pl.when((chip <= self.chip) & (self.chip < self.chips - 1))
        def _():
            self.copy(0, origin, self.rank + 2, src).start()

        @pl.when((chip >= self.chip) & (self.chip > 0))
        def _():
            self.copy(1, origin, self.rank - 2, src).start()

        self.copy(2, origin, self.rank + 1 - 2 * self.core, src).start()

    def arrive(self, step, part):
        side, other = part % 2, part // 2
        origin_chip = self.chip + jnp.where(side == 0, -step, step)
        origin = 2 * origin_chip + jnp.where(other == 0, self.core, 1 - self.core)
        valid = (origin_chip >= 0) & (origin_chip < self.chips) & ((step > 0) | (side == 0))

        @pl.when(valid & (origin != self.rank))
        def _():
            self.copy(0, origin, self.rank).wait_recv()

            @pl.when(other == 0)
            def _():
                self.pass_on(origin)

        return valid, origin

    def finish(self):
        def one(chip, carry):
            origin = 2 * chip + self.core

            @pl.when((chip <= self.chip) & (self.chip < self.chips - 1))
            def _():
                self.copy(0, origin, self.rank).wait_send()

            @pl.when((chip >= self.chip) & (self.chip > 0))
            def _():
                self.copy(1, origin, self.rank).wait_send()

            self.copy(2, origin, self.rank).wait_send()
            return carry

        lax.fori_loop(0, self.chips, one, 0)

    @staticmethod
    def semaphores(ctx):
        return [pltpu.SemaphoreType.DMA((3, ctx)), pltpu.SemaphoreType.DMA((ctx,))]


class LineSum:
    def __init__(self, blocks, pair, passing, sems):
        self.blocks, self.pair, self.passing = blocks, pair, passing
        self.pair_send, self.pair_recv, self.line_send, self.line_recv = sems
        self.rank = lax.axis_index("ctx")
        self.chip, self.core = self.rank // 2, self.rank % 2
        self.chips = blocks.shape[0] // 2
        self.pieces = self.line_recv.shape[2]
        self.piece = blocks.shape[1] // self.pieces

    def pair_copy(self, chip):
        return send(
            self.blocks.at[2 * chip + 1 - self.core],
            self.pair.at[chip],
            self.pair_send.at[chip],
            self.pair_recv.at[chip],
            ctx=self.rank + 1 - 2 * self.core,
        )

    def line_copy(self, way, chip, piece, target):
        rows = pl.ds(piece * self.piece, self.piece)
        return send(
            self.blocks.at[2 * chip + self.core, rows],
            self.passing.at[way, chip, rows],
            self.line_send.at[chip, piece],
            self.line_recv.at[way, chip, piece],
            ctx=target,
        )

    def both(self, chip, rows):
        mine = self.blocks[2 * chip + self.core, rows].astype(WIDE)
        return mine + self.pair[chip, rows].astype(WIDE)

    def forward(self, way, chip, valid):
        behind = jnp.where(way == 0, self.chip > 0, self.chip < self.chips - 1)
        target = self.rank + jnp.where(way == 0, 2, -2)

        @pl.when(valid)
        def _():
            self.pair_copy(chip).wait_recv()

            def one(piece, carry):
                rows = pl.ds(pl.multiple_of(piece * self.piece, self.piece), self.piece)
                total = self.both(chip, rows)

                @pl.when(behind)
                def _():
                    self.line_copy(way, chip, piece, target).wait_recv()
                    passing = self.passing[way, chip, rows].astype(WIDE)
                    self.blocks[2 * chip + self.core, rows] = (total + passing).astype(LOW)

                @pl.when(jnp.logical_not(behind))
                def _():
                    self.blocks[2 * chip + self.core, rows] = total.astype(LOW)

                self.line_copy(way, chip, piece, target).start()
                return carry

            lax.fori_loop(0, self.pieces, one, 0)

    def near_first(self, step, way):
        last = self.chips - 1
        chip = jnp.where(way == 0, step - self.chip, 2 * last - self.chip - step)
        ahead = jnp.where(way == 0, (chip > self.chip) & (chip <= last), (chip >= 0) & (chip < self.chip))
        self.forward(way, chip, ahead)

    def far_first(self, step, way):
        last = self.chips - 1
        chip = jnp.where(way == 0, last + self.chip - step, step - last + self.chip)
        ahead = jnp.where(way == 0, (chip > self.chip) & (chip <= last), (chip >= 0) & (chip < self.chip))
        self.forward(way, chip, ahead)

    def send_pairs(self):
        def one(chip, carry):
            self.pair_copy(chip).start()
            return carry

        lax.fori_loop(0, self.chips, one, 0)

    def far_steps(self, begin, end):
        def one(index, carry):
            self.far_first(index // 2, index % 2)
            return carry

        lax.fori_loop(2 * begin, 2 * end, one, 0)

    def finish(self, out):
        self.pair_copy(self.chip).wait_recv()

        def one(piece, carry):
            rows = pl.ds(pl.multiple_of(piece * self.piece, self.piece), self.piece)
            out[rows] = self.both(self.chip, rows)

            @pl.when(self.chip > 0)
            def _():
                self.line_copy(0, self.chip, piece, self.rank).wait_recv()
                out[rows] = out[rows] + self.passing[0, self.chip, rows].astype(WIDE)

            @pl.when(self.chip < self.chips - 1)
            def _():
                self.line_copy(1, self.chip, piece, self.rank).wait_recv()
                out[rows] = out[rows] + self.passing[1, self.chip, rows].astype(WIDE)

            return carry

        lax.fori_loop(0, self.pieces, one, 0)

        def sent(chip, carry):
            self.pair_copy(chip).wait_send()

            @pl.when(chip != self.chip)
            def _():
                for piece in range(self.pieces):
                    self.line_copy(0, chip, piece, self.rank).wait_send()

            return carry

        lax.fori_loop(0, self.chips, sent, 0)

    @staticmethod
    def scratch(ctx, rows, columns, pieces):
        chips = ctx // 2
        return [
            pltpu.VMEM((ctx, rows, columns), LOW),
            pltpu.VMEM((chips, rows, columns), LOW),
            pltpu.VMEM((2, chips, rows, columns), LOW),
            pltpu.SemaphoreType.DMA((chips,)),
            pltpu.SemaphoreType.DMA((chips,)),
            pltpu.SemaphoreType.DMA((chips, pieces)),
            pltpu.SemaphoreType.DMA((2, chips, pieces)),
        ]


def feed_kernel(
    mixed_ref,
    in_ref,
    vectors_ref,
    bias_ref,
    proj_ref,
    fc_ref,
    out_ref,
    cot_ref,
    resid_ref,
    grad_ref,
    ffn_ref,
    act_ref,
    pre_ref,
    part_ref,
    gather_send,
    gather_recv,
    blocks,
    pair,
    passing,
    *sems,
):
    gather = LineGather(ffn_ref, gather_send, gather_recv)
    total = LineSum(blocks, pair, passing, sems)
    chips = gather.chips
    greet_line(chips)
    resid = in_ref[...].astype(WIDE) + dot(mixed_ref[:, 0:D], proj_ref[...]) + vectors_ref[0:1]
    resid_ref[...] = resid
    normed, _ = normalize(resid)
    ffn_ref[gather.rank] = (normed * vectors_ref[1:2] + vectors_ref[2:3]).astype(LOW)
    gather.pass_on(gather.rank)

    tokens = ffn_ref.shape[1]

    def work(chip):
        both = pl.ds(2 * chip, 2)
        pre = dot(ffn_ref[both].reshape(2 * tokens, D), fc_ref[...]) + bias_ref[0:1]
        bend = jnp.tanh(0.7978845608028654 * (pre + 0.044715 * pre * pre * pre))
        act = (0.5 * pre * (1.0 + bend)).astype(LOW)
        act_ref[both] = act.reshape(2, tokens, -1)
        slope = 0.5 * (1.0 + bend) + 0.5 * pre * (1.0 - bend * bend) * 0.7978845608028654 * (
            1.0 + 3 * 0.044715 * pre * pre
        )
        grad_act = dot(cot_ref[both].reshape(2 * tokens, D), out_ref[...], 1, 1)
        grad_pre = (slope * grad_act).astype(LOW)
        pre_ref[both] = grad_pre.reshape(2, tokens, -1)
        blocks[both] = dot(grad_pre, fc_ref[...], 1, 1).astype(LOW).reshape(2, tokens, D)
        total.pair_copy(chip).start()
        part_ref[both] = dot(act, out_ref[...]).astype(LOW).reshape(2, tokens, D)

    def step(index, carry):
        distance, side = index // 2, index % 2

        @pl.when(distance < chips)
        def _():
            @pl.when(side == 0)
            def _():
                gather.arrive(distance, 0)
                gather.arrive(distance, 1)

            valid, origin = gather.arrive(distance, 2 + side)

            @pl.when(valid)
            def _():
                work(origin // 2)

        @pl.when(side == 1)
        def _():
            def way(index, carry):
                total.near_first(distance, index)
                return carry

            lax.fori_loop(0, 2, way, 0)

        return carry

    lax.fori_loop(0, 2 * (2 * chips - 1), step, 0)
    total.finish(grad_ref)
    gather.finish()


def feed(mixed, own_in, vectors, bias, proj, fc, out, cot):
    ctx, tokens, _ = cot.shape
    width = fc.shape[1]
    return pl.pallas_call(
        feed_kernel,
        out_shape=(
            jax.ShapeDtypeStruct((tokens, D), WIDE),
            jax.ShapeDtypeStruct((tokens, D), WIDE),
            jax.ShapeDtypeStruct((ctx, tokens, D), LOW),
            jax.ShapeDtypeStruct((ctx, tokens, width), LOW),
            jax.ShapeDtypeStruct((ctx, tokens, width), LOW),
            jax.ShapeDtypeStruct((ctx, tokens, D), LOW),
        ),
        in_specs=[pl.BlockSpec(memory_space=pltpu.VMEM)] * 8,
        out_specs=[pl.BlockSpec(memory_space=pltpu.VMEM)] * 6,
        scratch_shapes=LineGather.semaphores(ctx) + LineSum.scratch(ctx, tokens, D, 4),
        compiler_params=pltpu.CompilerParams(
            vmem_limit_bytes=60 * MIB, collective_id=2, has_side_effects=True
        ),
        name="feed",
    )(mixed, own_in, vectors, bias, proj, fc, out, cot)


VMEM = pl.BlockSpec(memory_space=pltpu.VMEM)
HBM = pl.BlockSpec(memory_space=pl.ANY)
PAD = 64


def params(number):
    return pltpu.CompilerParams(
        vmem_limit_bytes=63 * MIB, collective_id=number, has_side_effects=True
    )


class Spread:
    def __init__(self, blocks, landed, wide, out, sems):
        self.blocks, self.landed, self.wide, self.out = blocks, landed, wide, out
        self.swap = Swap("ctx", blocks.at.__getitem__, landed.at.__getitem__, sems[:2])
        self.plane = PlaneGather(out, sems[2:])

    def start(self):
        self.swap.start()
        self.landed[self.swap.rank] = self.blocks[self.swap.rank]

    def cross(self):
        self.swap.wait()
        count = self.out.shape[1] // self.swap.size
        for index in range(self.swap.size):
            self.wide[index * count : index * count + PAD] = self.landed[index].astype(WIDE)
        self.out[self.plane.rank] = self.wide[0 : self.out.shape[1]].astype(LOW)
        self.plane.start()

    def wait(self):
        self.plane.wait()
        self.swap.drain()

    @staticmethod
    def scratch(ctx, dp, rows, columns):
        return [
            pltpu.VMEM((ctx, PAD, columns), LOW),
            pltpu.VMEM((rows + PAD, columns), WIDE),
            *Swap.semaphores(ctx),
            *PlaneGather.semaphores(dp),
        ]


class Collect:
    def __init__(self, parts, landed, wide, blocks, out, sems):
        self.parts, self.wide, self.blocks, self.out = parts, wide, blocks, out
        self.plane = PlaneSum(parts, landed, sems[:2])
        self.swap = Swap("ctx", blocks.at.__getitem__, out.at.__getitem__, sems[2:])

    def cross(self):
        rows = self.parts.shape[1]
        self.wide[0:rows] = self.plane.total()
        self.wide[rows:] = jnp.zeros((PAD, self.wide.shape[1]), WIDE)
        count = rows // self.swap.size
        for index in range(self.swap.size):
            self.blocks[index] = self.wide[index * count : index * count + PAD].astype(LOW)
        self.swap.start()
        self.out[self.swap.rank] = self.blocks[self.swap.rank]

    def wait(self):
        self.swap.wait()
        self.swap.drain()
        self.plane.drain()

    @staticmethod
    def scratch(ctx, dp, rows, columns):
        return [
            pltpu.VMEM((dp, rows, columns), LOW),
            pltpu.VMEM((dp, rows, columns), LOW),
            pltpu.VMEM((rows + PAD, columns), WIDE),
            pltpu.VMEM((ctx, PAD, columns), LOW),
            *PlaneSum.semaphores(dp),
            *Swap.semaphores(ctx),
        ]


def start_kernel(whole, small_ref, rows_ref, unit_rows_ref, *refs):
    if whole:
        blocks_ref, proj_ref, *refs = refs
    small_out, rows_out, units_out, *refs = refs
    if whole:
        mat_out, proj_out, *refs = refs
    gather = LineGather(rows_out, *refs[:2])
    seq = lax.axis_index("dp")
    rank = gather.rank
    line = Swap("ctx", lambda peer: small_ref, lambda origin: small_out.at[seq, origin], refs[2:4])
    plane = Swap("dp", lambda peer: small_out.at[seq], small_out.at.__getitem__, refs[4:6])
    units = PlaneGather(units_out, refs[6:8])
    if whole:
        spread = Spread(blocks_ref, refs[8], refs[9], mat_out, refs[10:14])
        proj = ChipSwap(
            lambda peer: proj_ref,
            lambda origin: proj_out.at[pl.ds(pl.multiple_of(origin * PAD, PAD), PAD)],
            refs[14:16],
        )
    greet_all()
    line.start()
    if whole:
        spread.start()
    gather.pass_on(rank, rows_ref)
    units_out[seq] = unit_rows_ref[...]
    units.start()
    if whole:
        proj.start()
        proj_out[pl.ds(pl.multiple_of(proj.rank * PAD, PAD), PAD)] = proj_ref[...]
    rows_out[rank] = rows_ref[...]
    small_out[seq, rank] = small_ref[...]
    line.wait()
    plane.start()
    if whole:
        spread.cross()

    def arrive(index, carry):
        gather.arrive(1 + index // 4, index % 4)
        return carry

    gather.arrive(0, 2)
    lax.fori_loop(0, 4, arrive, 0)
    units.relay()
    lax.fori_loop(4, 8, arrive, 0)
    if whole:
        spread.plane.relay()
    lax.fori_loop(8, 4 * (gather.chips - 1), arrive, 0)
    plane.wait()
    plane.drain()
    line.drain()
    gather.finish()
    units.wait()
    if whole:
        spread.wait()
        proj.wait()
        proj.drain()


def start(small, rows, unit_rows, blocks, proj):
    ctx, dp = lax.axis_size("ctx"), lax.axis_size("dp")
    tokens = rows.shape[0]
    whole = blocks is not None
    shapes = [
        jax.ShapeDtypeStruct((dp, ctx, *small.shape), WIDE),
        jax.ShapeDtypeStruct((ctx, tokens, D), LOW),
        jax.ShapeDtypeStruct((dp, *unit_rows.shape), LOW),
    ]
    scratch = LineGather.semaphores(ctx) + Swap.semaphores(ctx) + Swap.semaphores(dp)
    scratch += PlaneGather.semaphores(dp)
    given = [small, rows, unit_rows]
    if whole:
        columns = blocks.shape[2]
        given += [blocks, proj]
        shapes.append(jax.ShapeDtypeStruct((dp, D // dp, columns), LOW))
        shapes.append(jax.ShapeDtypeStruct((ctx // 2 * PAD, D), LOW))
        scratch += Spread.scratch(ctx, dp, D // dp, columns) + Swap.semaphores(ctx // 2)
    return pl.pallas_call(
        functools.partial(start_kernel, whole),
        out_shape=shapes,
        in_specs=[VMEM] * len(given),
        out_specs=[VMEM] * len(shapes),
        scratch_shapes=scratch,
        compiler_params=params(0),
        name="start",
    )(*given)


class Projection:
    def __init__(self, blocks, wide, out, sems):
        self.blocks, self.wide, self.out = blocks, wide, out
        self.rank = lax.axis_index("ctx")
        self.core = self.rank % 2
        self.plane = PlaneGather(blocks.at[self.core], sems[:2])
        self.send_sems, self.recv_sems = sems[2:]

    def start(self, rows):
        self.blocks[self.core, self.plane.rank] = rows
        self.plane.start()
        self.to_other(self.plane.rank).start()

    def to_other(self, seq):
        block = self.blocks.at[self.core, seq]
        return send(
            block,
            block,
            self.send_sems.at[seq],
            self.recv_sems.at[seq],
            ctx=self.rank + 1 - 2 * self.core,
        )

    def wait(self):
        self.plane.wait()

        def others(off, carry):
            self.to_other(lax.rem(self.plane.rank + off, self.plane.size)).start()
            return carry

        lax.fori_loop(1, self.plane.size, others, 0)
        ctx = 2 * (self.blocks.shape[2] // PAD)
        count = self.out.shape[1] // ctx

        def order(off, carry):
            seq = lax.rem(self.plane.rank + off, self.plane.size)
            self.to_other(seq).wait_recv()
            for rank in range(ctx):
                rows = self.blocks[rank % 2, seq, rank // 2 * PAD : rank // 2 * PAD + PAD]
                self.wide[rank * count : rank * count + PAD] = rows.astype(WIDE)
            self.out[seq] = self.wide[0 : self.out.shape[1]].astype(LOW)
            return carry

        lax.fori_loop(0, self.plane.size, order, 0)

        def sent(seq, carry):
            self.to_other(seq).wait_send()
            return carry

        lax.fori_loop(0, self.plane.size, sent, 0)

    @staticmethod
    def scratch(ctx, dp):
        return [
            pltpu.VMEM((2, dp, ctx // 2 * PAD, D), LOW),
            pltpu.VMEM((D // dp + PAD, D), WIDE),
            *PlaneGather.semaphores(dp),
            *Swap.semaphores(dp),
        ]


def attend_kernel(
    block, whole, rows_ref, vectors_ref, bias_ref, mat_ref, start_ref, cot_ref, *refs
):
    if whole:
        blocks_ref, proj_ref, *refs = refs
    in_ref, qkv_ref, stat_ref, own_ref, cot_out, *refs = refs
    if whole:
        mat_out, proj_out, *refs = refs
    mixed, value_t, *refs = refs
    gather = LineGather(cot_out, *refs[:2])
    ctx, tokens, _ = rows_ref.shape
    width = mixed.shape[1]
    swap = Swap(
        "ctx",
        lambda peer: mixed.at[pl.ds(pl.multiple_of(peer * tokens, tokens), tokens)],
        lambda origin: own_ref.at[:, pl.ds(pl.multiple_of(origin * width, width), width)],
        refs[2:4],
    )
    if whole:
        spread = Spread(blocks_ref, refs[4], refs[5], mat_out, refs[6:10])
        proj = Projection(refs[10], refs[11], proj_out, refs[12:])
    greet_all()
    if whole:
        spread.start()
    gather.pass_on(gather.rank, cot_ref)
    if whole:
        proj.start(proj_ref[...])
    cot_out[gather.rank] = cot_ref[...]

    def project(index, carry):
        both = pl.ds(2 * index, 2)
        rows = pl.ds(pl.multiple_of(2 * index * tokens, 2 * tokens), 2 * tokens)
        normed, _ = normalize(rows_ref[both].reshape(2 * tokens, D).astype(WIDE))
        attn_in = (normed * vectors_ref[0:1] + vectors_ref[1:2]).astype(LOW)
        in_ref[rows] = attn_in
        qkv_ref[rows] = (dot(attn_in, mat_ref[...]) + bias_ref[0:1]).astype(LOW)
        return carry

    lax.fori_loop(0, ctx // 2, project, 0)
    attend_body(block, qkv_ref, start_ref, mixed, stat_ref, value_t)
    swap.start()
    own_ref[:, pl.ds(pl.multiple_of(swap.rank * width, width), width)] = mixed[
        pl.ds(pl.multiple_of(swap.rank * tokens, tokens), tokens)
    ]
    if whole:
        spread.cross()
        proj.plane.relay()

    def arrive(index, carry):
        gather.arrive(1 + index // 4, index % 4)
        return carry

    gather.arrive(0, 2)
    lax.fori_loop(0, 4, arrive, 0)
    if whole:
        spread.plane.relay()
    lax.fori_loop(4, 8, arrive, 0)
    if whole:
        proj.wait()
    lax.fori_loop(8, 4 * (gather.chips - 1), arrive, 0)
    swap.wait()
    swap.drain()
    gather.finish()
    if whole:
        spread.wait()


def attend(rows, vectors, bias, mat, doc_start, cot, blocks, proj, block):
    ctx, tokens, _ = rows.shape
    dp = lax.axis_size("dp")
    length = ctx * tokens
    width = mat.shape[1] // 3
    whole = blocks is not None
    given = [rows, vectors, bias, mat, doc_start, cot]
    shapes = [
        jax.ShapeDtypeStruct((length, D), LOW),
        jax.ShapeDtypeStruct((length, 3 * width), LOW),
        jax.ShapeDtypeStruct((8, length), WIDE),
        jax.ShapeDtypeStruct((tokens, ctx * width), LOW),
        jax.ShapeDtypeStruct((ctx, tokens, D), LOW),
    ]
    scratch = [pltpu.VMEM((length, width), LOW), pltpu.VMEM((width, length), LOW)]
    scratch += LineGather.semaphores(ctx) + Swap.semaphores(ctx)
    if whole:
        columns = blocks.shape[2]
        given += [blocks, proj]
        shapes.append(jax.ShapeDtypeStruct((dp, D // dp, columns), LOW))
        shapes.append(jax.ShapeDtypeStruct((dp, D // dp, D), LOW))
        scratch += Spread.scratch(ctx, dp, D // dp, columns) + Projection.scratch(ctx, dp)
    return pl.pallas_call(
        functools.partial(attend_kernel, block, whole),
        out_shape=shapes,
        in_specs=[VMEM] * len(given),
        out_specs=[VMEM] * len(shapes),
        scratch_shapes=scratch,
        compiler_params=params(1),
        name="attend",
    )(*given)


def back_kernel(
    block,
    whole,
    grad_ref,
    resid_ref,
    own_cot,
    vectors_ref,
    proj_ref,
    qkv_ref,
    start_ref,
    stat_ref,
    ffn_hbm,
    pre_hbm,
    act_hbm,
    cot_hbm,
    part_hbm,
    resid_out,
    low_out,
    vector_out,
    units_out,
    rows_out,
    share_out,
    output_ref,
    fc_out,
    ffn,
    pre,
    act,
    cot,
    load_sems,
    own_grad,
    head_grad,
    key_t,
    key_grad,
    value_grad,
    *refs,
):
    total = LineSum(*refs[:3], refs[3:7])
    loads = [
        pltpu.make_async_copy(src, dst, load_sems.at[index])
        for index, (src, dst) in enumerate(
            (
                (part_hbm, total.blocks),
                (ffn_hbm, ffn),
                (pre_hbm, pre),
                (act_hbm, act),
                (cot_hbm, cot),
            )
        )
    ]
    for load in loads:
        load.start()
    tokens = own_cot.shape[0]
    length, width = head_grad.shape
    units = share_out.shape[0]
    swap = Swap(
        "ctx",
        lambda peer: own_grad.at[:, pl.ds(pl.multiple_of(peer * width, width), width)],
        lambda origin: head_grad.at[pl.ds(pl.multiple_of(origin * tokens, tokens), tokens)],
        refs[7:9],
    )
    share = PlaneSum(refs[9], refs[10], refs[11:13])
    if whole:
        collect = Collect(*refs[13:17], fc_out, refs[17:])
    dp = share.swap.size
    greet_all()
    loads[0].wait()
    total.send_pairs()
    grad = grad_ref[...]
    normed, scale = normalize(resid_ref[...])
    grad_resid = own_cot[...].astype(WIDE) + norm_back(normed, scale, vectors_ref[0:1], grad)
    resid_out[...] = grad_resid
    low = grad_resid.astype(LOW)
    low_out[...] = low
    own_grad[:, 0:D] = dot(low, proj_ref[...], 1, 1).astype(LOW)
    own_grad[:, D:] = jnp.zeros((tokens, own_grad.shape[1] - D), LOW)
    swap.start()
    head_grad[pl.ds(pl.multiple_of(swap.rank * tokens, tokens), tokens)] = own_grad[
        :, pl.ds(pl.multiple_of(swap.rank * width, width), width)
    ]
    vector_out[0:1] = jnp.sum(grad_resid, 0, keepdims=True)
    vector_out[1:2] = jnp.sum(grad * normed, 0, keepdims=True)
    vector_out[2:3] = jnp.sum(grad, 0, keepdims=True)
    vector_out[3:4] = jnp.sum(own_cot[...].astype(WIDE), 0, keepdims=True)
    vector_out[4:8] = jnp.zeros((4, D), WIDE)
    loads[1].wait()
    loads[2].wait()
    grad_pre = pre[...].reshape(length, -1)
    units_out[...] = dot(jnp.ones((8, length), LOW), grad_pre)
    for index in range(dp):
        rows = slice(index * (D // dp), (index + 1) * (D // dp))
        part = dot(ffn[:, :, rows].reshape(length, D // dp), grad_pre, 0, 0)
        if whole:
            collect.parts[index] = part.astype(LOW)
        else:
            fc_out[rows] = part
    if whole:
        collect.plane.start()
    total.far_steps(0, 1)
    loads[3].wait()
    loads[4].wait()
    for index in range(dp):
        rows = slice(index * units, (index + 1) * units)
        part = dot(act[:, :, rows].reshape(length, units), cot[...].reshape(length, D), 0, 0)
        share.blocks[index] = part.astype(LOW)
    share.start()
    swap.wait()
    chips = total.chips

    def first():
        total.far_steps(1, 2)
        if whole:
            collect.plane.relay()

    def second():
        total.far_steps(2, 3)
        share.relay()

    attend_back_body(
        block,
        qkv_ref,
        start_ref,
        stat_ref,
        head_grad,
        rows_out,
        key_t,
        key_grad,
        value_grad,
        {1: first, 2: second},
    )
    if whole:
        collect.cross()
    total.far_steps(3, 2 * chips - 1)
    total.finish(output_ref)
    output_ref[...] = output_ref[...] + resid_ref[...] + vectors_ref[1:2]
    share_out[...] = share.total()
    swap.drain()
    share.drain()
    if whole:
        collect.wait()


def back(
    grad, resid, own_cot, vectors, proj, qkv, doc_start, stats, ffn, pre, act, cot, part, block, whole
):
    ctx, tokens, _ = cot.shape
    dp = lax.axis_size("dp")
    length = ctx * tokens
    width = qkv.shape[1] // 3
    columns = act.shape[2]
    units = columns // dp
    rows = D // dp
    shapes = [
        jax.ShapeDtypeStruct((tokens, D), WIDE),
        jax.ShapeDtypeStruct((tokens, D), LOW),
        jax.ShapeDtypeStruct((8, D), WIDE),
        jax.ShapeDtypeStruct((8, columns), WIDE),
        jax.ShapeDtypeStruct((length, 3 * width), LOW),
        jax.ShapeDtypeStruct((units, D), WIDE),
        jax.ShapeDtypeStruct((tokens, D), WIDE),
        jax.ShapeDtypeStruct((ctx, PAD, columns), LOW)
        if whole
        else jax.ShapeDtypeStruct((D, columns), WIDE),
    ]
    scratch = [
        pltpu.VMEM(ffn.shape, LOW),
        pltpu.VMEM(pre.shape, LOW),
        pltpu.VMEM(act.shape, LOW),
        pltpu.VMEM(cot.shape, LOW),
        pltpu.SemaphoreType.DMA((5,)),
        pltpu.VMEM((tokens, ctx * width), LOW),
        pltpu.VMEM((length, width), LOW),
        pltpu.VMEM((width, length), LOW),
        pltpu.VMEM((length, width), WIDE),
        pltpu.VMEM((length, width), WIDE),
        *LineSum.scratch(ctx, tokens, D, 4),
        *Swap.semaphores(ctx),
        pltpu.VMEM((dp, units, D), LOW),
        pltpu.VMEM((dp, units, D), LOW),
        *PlaneSum.semaphores(dp),
    ]
    if whole:
        scratch += Collect.scratch(ctx, dp, rows, columns)
    return pl.pallas_call(
        functools.partial(back_kernel, block, whole),
        out_shape=shapes,
        in_specs=[VMEM] * 8 + [HBM] * 5,
        out_specs=[VMEM] * 8,
        scratch_shapes=scratch,
        compiler_params=params(3),
        name="back",
    )(grad, resid, own_cot, vectors, proj, qkv, doc_start, stats, ffn, pre, act, cot, part)


class ProjectionSum:
    def __init__(self, out, refs):
        self.out = out
        self.mixed, self.low, self.parts, landed, self.blocks, self.came = refs[:6]
        self.send_sems, self.recv_sems = refs[6:8]
        self.plane = PlaneSum(self.parts, landed, refs[8:10])
        self.rank = lax.axis_index("ctx")
        self.core = self.rank % 2
        self.swap = ChipSwap(self.blocks.at.__getitem__, self.came.at.__getitem__, refs[10:12])

    def pair_copies(self):
        return [
            send(
                ref.at[self.core],
                ref.at[self.core],
                self.send_sems.at[index],
                self.recv_sems.at[index],
                ctx=self.rank + 1 - 2 * self.core,
            )
            for index, ref in enumerate((self.mixed, self.low))
        ]

    def start(self, mixed, low):
        self.mixed[self.core] = mixed
        self.low[self.core] = low
        for copy in self.pair_copies():
            copy.start()

    def multiply(self):
        for copy in self.pair_copies():
            copy.wait_recv()
        dp, rows = self.parts.shape[:2]
        chips = rows // PAD
        tokens = 2 * self.low.shape[1]
        count = D // (2 * chips * dp)
        mixed = self.mixed[...].reshape(tokens, -1)[:, 0:D]
        low = self.low[...].reshape(tokens, D)
        feature = lax.broadcasted_iota(jnp.int32, (D, rows), 0)
        column = lax.broadcasted_iota(jnp.int32, (1, rows), 1)
        place = column % PAD
        for index in range(dp):
            owner = index * 2 * chips + column // PAD * 2 + self.core
            wanted = jnp.where(place < count, owner * count + place, -1)
            chosen = jnp.where(feature == wanted, 1.0, 0.0).astype(LOW)
            picked = dot(mixed, chosen).astype(LOW)
            self.parts[index] = dot(picked, low, 0, 0).astype(LOW)
        self.plane.start()

    def cross(self):
        total = self.plane.total().astype(LOW)
        self.blocks[...] = total.reshape(self.blocks.shape)
        self.swap.start()

    def wait(self):
        self.swap.wait()
        total = self.blocks[self.swap.rank].astype(WIDE)
        for off in range(1, self.swap.size):
            total = total + self.came[lax.rem(self.swap.rank + off, self.swap.size)].astype(WIDE)
        self.out[...] = total
        for copy in self.pair_copies():
            copy.wait_send()
        self.plane.drain()
        self.swap.drain()

    @staticmethod
    def scratch(ctx, dp, tokens, width):
        chips = ctx // 2
        return [
            pltpu.VMEM((2, tokens, ctx * width), LOW),
            pltpu.VMEM((2, tokens, D), LOW),
            pltpu.VMEM((dp, chips * PAD, D), LOW),
            pltpu.VMEM((dp, chips * PAD, D), LOW),
            pltpu.VMEM((chips, PAD, D), LOW),
            pltpu.VMEM((chips, PAD, D), LOW),
            *Swap.semaphores(2),
            *PlaneSum.semaphores(dp),
            *Swap.semaphores(chips),
        ]


def last_kernel(
    whole,
    rows_ref,
    mat_ref,
    in_ref,
    own_ref,
    resid_ref,
    vectors_ref,
    mixed_ref,
    low_ref,
    grad_out,
    vector_out,
    heads_out,
    mat_out,
    *refs,
):
    if whole:
        proj_out, *refs = refs
    grad, *refs = refs
    total = LineSum(*refs[:3], refs[3:7])
    if whole:
        collect = Collect(*refs[7:11], mat_out, refs[11:15])
        proj = ProjectionSum(proj_out, refs[15:])
    chips = total.chips
    tokens = own_ref.shape[0]
    dp = lax.axis_size("dp")
    if whole:
        greet_all()
        proj.start(mixed_ref[...], low_ref[...])
    else:
        greet_line(chips)

    def partial_sum(index, carry):
        off = jnp.where(index % 2 == 0, -(index // 2), index // 2 + 1)
        chip = lax.rem(chips - 1 + off, chips)
        rows = pl.ds(pl.multiple_of(2 * chip * tokens, 2 * tokens), 2 * tokens)
        part = dot(rows_ref[rows], mat_ref[...], 1, 1).astype(LOW)
        total.blocks[pl.ds(2 * chip, 2)] = part.reshape(2, tokens, D)
        total.pair_copy(chip).start()
        return carry

    lax.fori_loop(0, chips, partial_sum, 0)
    total.far_steps(0, 1)
    for index in range(dp):
        rows = slice(index * (D // dp), (index + 1) * (D // dp))
        part = dot(in_ref[:, rows], rows_ref[...], 0, 0)
        if whole:
            collect.parts[index] = part.astype(LOW)
        else:
            mat_out[rows] = part
    if whole:
        collect.plane.start()
    total.far_steps(1, 2)
    if whole:
        proj.multiply()
    total.far_steps(2, 3)
    heads_out[...] = dot(jnp.ones((8, rows_ref.shape[0]), LOW), rows_ref[...])
    if whole:
        collect.plane.relay()
    total.far_steps(3, 4)
    if whole:
        proj.plane.relay()
        collect.cross()
    total.far_steps(4, 2 * chips - 1)
    total.finish(grad)
    if whole:
        proj.cross()
    normed, scale = normalize(own_ref[...].astype(WIDE))
    incoming = grad[...]
    grad_out[...] = resid_ref[...] + norm_back(normed, scale, vectors_ref[0:1], incoming)
    vector_out[0:1] = jnp.sum(incoming * normed, 0, keepdims=True)
    vector_out[1:2] = jnp.sum(incoming, 0, keepdims=True)
    vector_out[2:8] = jnp.zeros((6, D), WIDE)
    if whole:
        collect.wait()
        proj.wait()


def last(rows, mat, attn_in, own_in, resid, vectors, mixed, low, whole):
    ctx, dp = lax.axis_size("ctx"), lax.axis_size("dp")
    tokens = own_in.shape[0]
    columns = rows.shape[1]
    shapes = [
        jax.ShapeDtypeStruct((tokens, D), WIDE),
        jax.ShapeDtypeStruct((8, D), WIDE),
        jax.ShapeDtypeStruct((8, columns), WIDE),
        jax.ShapeDtypeStruct((ctx, PAD, columns), LOW)
        if whole
        else jax.ShapeDtypeStruct((D, columns), WIDE),
    ]
    scratch = [pltpu.VMEM((tokens, D), WIDE), *LineSum.scratch(ctx, tokens, D, 4)]
    if whole:
        shapes.append(jax.ShapeDtypeStruct((PAD, D), WIDE))
        scratch += Collect.scratch(ctx, dp, D // dp, columns)
        scratch += ProjectionSum.scratch(ctx, dp, tokens, columns // 3)
    return pl.pallas_call(
        functools.partial(last_kernel, whole),
        out_shape=shapes,
        in_specs=[VMEM] * 8,
        out_specs=[VMEM] * len(shapes),
        scratch_shapes=scratch,
        compiler_params=params(4),
        name="last",
    )(rows, mat, attn_in, own_in, resid, vectors, mixed, low)


def vector_kernel(parts_ref, out_ref, plane_landed, line_parts, line_landed, *sems):
    seq = lax.axis_index("dp")
    swap = Swap("dp", parts_ref.at.__getitem__, plane_landed.at.__getitem__, sems[:2])
    line = Swap("ctx", line_parts.at.__getitem__, line_landed.at.__getitem__, sems[2:])
    greet_all()
    swap.start()
    swap.wait()
    total = parts_ref[seq]
    for off in range(1, swap.size):
        total = total + plane_landed[lax.rem(seq + off, swap.size)]
    line_parts[...] = total
    line.start()
    line.wait()
    total = line_parts[line.rank]
    for off in range(1, line.size):
        total = total + line_landed[lax.rem(line.rank + off, line.size)]
    out_ref[...] = total
    swap.drain()
    line.drain()


def sum_vector(parts):
    dp, ctx = parts.shape[:2]
    return pl.pallas_call(
        vector_kernel,
        out_shape=jax.ShapeDtypeStruct(parts.shape[2:], WIDE),
        in_specs=[VMEM],
        out_specs=VMEM,
        scratch_shapes=[
            pltpu.VMEM(parts.shape, WIDE),
            pltpu.VMEM(parts.shape[1:], WIDE),
            pltpu.VMEM(parts.shape[1:], WIDE),
            *PlaneSum.semaphores(dp),
            *Swap.semaphores(ctx),
        ],
        compiler_params=params(5),
        name="sum_vector",
    )(parts)


def gather_rows(block):
    return lax.all_gather(block, ("dp", "ctx"), axis=0, tiled=True)


def by_rank_heads(rows, ctx, slots):
    count = rows.shape[0]
    split = rows.reshape(count, 3, D)
    split = jnp.pad(split, ((0, 0), (0, 0), (0, (ctx * slots - HEADS) * HEAD_DIM)))
    split = split.reshape(count, 3, ctx, slots * HEAD_DIM)
    return split.transpose(2, 0, 1, 3).reshape(ctx, count, 3 * slots * HEAD_DIM)


def from_rank_heads(blocks, slots):
    ctx, count = blocks.shape[:2]
    split = blocks.reshape(ctx, count, 3, slots * HEAD_DIM).transpose(1, 2, 0, 3)
    return split.reshape(count, 3, ctx * slots * HEAD_DIM)[:, :, :D].reshape(count, 3 * D)


def padded_units(units):
    return -(-units // 16) * 16


def by_rank_units(rows, ctx, dp):
    count = rows.shape[0]
    units = FF // (dp * ctx)
    split = rows.reshape(count, dp, ctx, units).transpose(2, 0, 1, 3)
    split = jnp.pad(split, ((0, 0), (0, 0), (0, 0), (0, padded_units(units) - units)))
    return split.reshape(ctx, count, dp * padded_units(units))


def from_rank_units(blocks, dp):
    ctx, count = blocks.shape[:2]
    units = FF // (dp * ctx)
    split = blocks.reshape(ctx, count, dp, padded_units(units))[..., :units]
    return split.transpose(1, 2, 0, 3).reshape(count, FF)


def rank_vector(vector, ctx, slots, rank):
    padded = jnp.pad(vector, (0, (ctx * slots - HEADS) * HEAD_DIM))
    width = slots * HEAD_DIM
    return lax.dynamic_slice_in_dim(padded, rank * width, width, 0)


def pad_rows(blocks, rows=PAD):
    return jnp.pad(blocks, ((0, 0), (0, rows - blocks.shape[1]), (0, 0)))


def shards(
    hidden_in, qkv_weight, proj_weight, fc_weight, out_weight, small_params, segments, cotangent
):
    tokens = hidden_in.shape[1]
    length = segments.shape[1]
    ctx = lax.axis_size("ctx")
    dp = lax.axis_size("dp")
    owners = dp * ctx
    rank = lax.axis_index("ctx")
    slots = -(-HEADS // ctx)
    width = slots * HEAD_DIM
    units = FF // owners
    rows = D // owners
    whole = D % owners == 0
    block = min(256, length)
    both = ("dp", "ctx")

    vec_count = small_params.shape[0]
    vec_pad = -(-vec_count // 1024) * 1024
    small = jnp.pad(small_params.astype(WIDE), (0, vec_pad - vec_count)).reshape(-1, 128)
    more = padded_units(units) - units
    unit_rows = jnp.pad(out_weight.reshape(units, D), ((0, more), (0, 0)))
    if whole:
        qkv_blocks = pad_rows(by_rank_heads(qkv_weight.reshape(rows, 3 * D), ctx, slots))
        proj_rows = pad_rows(proj_weight.reshape(1, rows, D))[0]
        small, rows_in, mat_out, mat_qkv, proj_rows = start(
            small, hidden_in[0], unit_rows, qkv_blocks, proj_rows
        )
        mat_qkv = mat_qkv.reshape(D, 3 * width)
        fc_blocks = pad_rows(by_rank_units(fc_weight.reshape(rows, FF), ctx, dp))
    else:
        small, rows_in, mat_out = start(small, hidden_in[0], unit_rows, None, None)
        fc_blocks = proj_rows = None
        mat_qkv = by_rank_heads(gather_rows(qkv_weight).reshape(D, 3 * D), ctx, slots)
        mat_qkv = lax.dynamic_index_in_dim(mat_qkv, rank, 0, keepdims=False)
        mat_fc = by_rank_units(gather_rows(fc_weight).reshape(D, FF), ctx, dp)
        mat_fc = lax.dynamic_index_in_dim(mat_fc, rank, 0, keepdims=False)
        mat_proj = gather_rows(proj_weight).reshape(D, D)
    mat_out = mat_out.reshape(-1, D)
    small = small.reshape(owners, vec_pad)[:, :vec_count].reshape(-1)
    gain_one, shift_one, bias_query, bias_value, bias_proj, gain_two, shift_two = [
        small[i * D : (i + 1) * D] for i in range(7)
    ]
    bias_fc = small[7 * D : 7 * D + FF]
    bias_out = small[7 * D + FF :]
    bias_units = lax.dynamic_index_in_dim(
        bias_fc.reshape(dp, ctx, units), rank, 1, keepdims=False
    )
    bias_units = jnp.pad(bias_units, ((0, 0), (0, more))).reshape(-1)
    bias_qkv = jnp.concatenate(
        [
            rank_vector(bias_query, ctx, slots, rank),
            jnp.zeros((width,), WIDE),
            rank_vector(bias_value, ctx, slots, rank),
        ]
    )

    docs = segments[0]
    doc_start = jnp.sum((docs[:, None] < docs[None, :]).astype(jnp.int32), 0)[None]
    attn_in, qkv, stats, own_mixed, cot, *rest = attend(
        rows_in,
        jnp.stack([gain_one, shift_one]),
        bias_qkv[None],
        mat_qkv,
        doc_start,
        cotangent[0],
        fc_blocks,
        proj_rows,
        block,
    )
    if whole:
        mat_fc, mat_proj = rest[0].reshape(D, -1), rest[1].reshape(D, D)
    resid, grad_normed_two, ffn_in, act, grad_pre, out_part = feed(
        own_mixed,
        hidden_in[0],
        jnp.stack([bias_proj, gain_two, shift_two]),
        bias_units[None],
        mat_proj,
        mat_fc,
        mat_out,
        cot,
    )
    grad_resid, resid_low, sums_two, sums_units, grad_rows, grad_out, output, grad_fc = back(
        grad_normed_two,
        resid,
        cotangent[0],
        jnp.stack([gain_two, bias_out]),
        mat_proj,
        qkv,
        doc_start,
        stats,
        ffn_in,
        grad_pre,
        act,
        cot,
        out_part,
        block,
        whole,
    )
    grad_input, sums_one, sums_heads, grad_qkv, *rest = last(
        grad_rows,
        mat_qkv,
        attn_in,
        hidden_in[0],
        grad_resid,
        gain_one[None],
        own_mixed,
        resid_low,
        whole,
    )
    if whole:
        share_fc = from_rank_units(grad_fc[:, :rows], dp)
        share_qkv = from_rank_heads(grad_qkv[:, :rows], slots)
        share_proj = rest[0][:rows]
    else:
        grad_proj = dot(own_mixed[:, :D], resid_low, 0, 0).reshape(-1)
        share_proj = lax.psum_scatter(grad_proj, both, scatter_dimension=0, tiled=True)
        here = (jnp.arange(ctx) == rank)[:, None, None]
        full_fc = from_rank_units(jnp.where(here, grad_fc[None], 0.0), dp).reshape(-1)
        full_qkv = from_rank_heads(jnp.where(here, grad_qkv[None], 0.0), slots).reshape(-1)
        share_fc = lax.psum_scatter(full_fc, both, scatter_dimension=0, tiled=True)
        share_qkv = lax.psum_scatter(full_qkv, both, scatter_dimension=0, tiled=True)

    def spread_heads(part):
        padded = jnp.zeros((ctx * width,), WIDE)
        return lax.dynamic_update_slice_in_dim(padded, part, rank * width, 0)[:D]

    sums_units = sums_units[0].reshape(dp, 1, -1)[:, :, :units]
    sums_units = lax.dynamic_update_slice_in_dim(
        jnp.zeros((dp, ctx, units), WIDE), sums_units, rank, 1
    ).reshape(FF)
    vector = jnp.concatenate(
        [
            sums_one[0],
            sums_one[1],
            spread_heads(sums_heads[0, :width]),
            spread_heads(sums_heads[0, 2 * width :]),
            sums_two[0],
            sums_two[1],
            sums_two[2],
            sums_units,
            sums_two[3],
        ]
    ).reshape(owners, vec_count)
    vector = jnp.pad(vector, ((0, 0), (0, vec_pad - vec_count))).reshape(dp, ctx, -1, 128)
    share_vector = sum_vector(vector)
    return (
        output[None],
        grad_input[None],
        share_qkv.astype(WIDE).reshape(-1),
        share_proj.astype(WIDE).reshape(-1),
        share_fc.astype(WIDE).reshape(-1),
        grad_out[:units].reshape(-1),
        share_vector.reshape(-1)[:vec_count],
    )


def solution(mesh):
    flat = P(("dp", "ctx"))
    rows = P("dp", "ctx", None)
    return jax.shard_map(
        shards,
        mesh=mesh,
        in_specs=(rows, flat, flat, flat, flat, flat, P("dp", None), rows),
        out_specs=(rows, rows, flat, flat, flat, flat, flat),
        check_vma=False,
    )
```

```python
import functools

import jax
import jax.numpy as jnp
from jax import lax
from jax.experimental import pallas as pl
from jax.experimental.pallas import tpu as pltpu
from jax.sharding import PartitionSpec as P

D = 1600
HEADS = 25
HEAD_DIM = 64
FF = 6400
EPSILON = 1e-05
LOW = jnp.bfloat16
WIDE = jnp.float32
MIB = 1024 * 1024


def dot(left, right, left_dim=1, right_dim=0):
    return lax.dot_general(
        left, right, (((left_dim,), (right_dim,)), ((), ())), preferred_element_type=WIDE
    )


def normalize(rows):
    centre = rows - jnp.mean(rows, -1, keepdims=True)
    spread = jnp.mean(centre * centre, -1, keepdims=True)
    scale = lax.rsqrt(spread + EPSILON)
    return centre * scale, scale


def norm_back(normed, scale, gain, incoming):
    scaled = gain * incoming
    return scale * (
        scaled
        - jnp.mean(scaled, -1, keepdims=True)
        - normed * jnp.mean(scaled * normed, -1, keepdims=True)
    )


def head_lanes(head, width):
    lane = lax.broadcasted_iota(jnp.int32, (1, width), 1)
    return (lane // HEAD_DIM) == head


def allowed_scores(scores, doc_start, first_query, keys, block):
    key_pos = lax.broadcasted_iota(jnp.int32, (keys, block), 0)
    query_pos = first_query + lax.broadcasted_iota(jnp.int32, (keys, block), 1)
    seen = (key_pos >= doc_start) & (key_pos <= query_pos)
    return jnp.where(seen, scores, -1e30)


def attend_body(block, qkv_ref, start_ref, mixed_ref, stat_ref, value_t):
    length = qkv_ref.shape[0]
    width = mixed_ref.shape[1]
    slots = width // HEAD_DIM
    value_t[...] = qkv_ref[:, 2 * width : 3 * width].astype(WIDE).T.astype(LOW)
    stat_ref[...] = jnp.zeros_like(stat_ref)
    for index in range(length // block):
        keys = (index + 1) * block
        rows = pl.ds(index * block, block)
        key_rows = qkv_ref[0:keys, width : 2 * width]
        doc_start = start_ref[0:1, rows]
        outs = []
        for head in range(slots):
            query = jnp.where(
                head_lanes(head, width), qkv_ref[rows, 0:width] * LOW(HEAD_DIM**-0.5), LOW(0)
            )
            scores = dot(key_rows, query, 1, 1)
            scores = allowed_scores(scores, doc_start, index * block, keys, block)
            top = jnp.max(scores, 0, keepdims=True)
            expo = jnp.exp(scores - top)
            total = jnp.sum(expo, 0, keepdims=True)
            head_rows = slice(head * HEAD_DIM, (head + 1) * HEAD_DIM)
            out = dot(value_t[head_rows, 0:keys], expo.astype(LOW))
            outs.append(out / total)
            stat_ref[head : head + 1, rows] = top + jnp.log(total)
        mixed_ref[rows, :] = jnp.concatenate(outs, 0).T.astype(LOW)


def attend_back_body(
    block, qkv_ref, start_ref, stat_ref, grad_ref, out_ref, key_t, key_grad, value_grad, after
):
    length = qkv_ref.shape[0]
    width = grad_ref.shape[1]
    slots = width // HEAD_DIM
    scale = HEAD_DIM**-0.5
    key_t[...] = qkv_ref[:, width : 2 * width].astype(WIDE).T.astype(LOW)
    key_grad[...] = jnp.zeros_like(key_grad)
    value_grad[...] = jnp.zeros_like(value_grad)
    for index in range(length // block):
        keys = (index + 1) * block
        rows = pl.ds(index * block, block)
        key_rows = qkv_ref[0:keys, width : 2 * width]
        value_rows = qkv_ref[0:keys, 2 * width : 3 * width]
        doc_start = start_ref[0:1, rows]
        outs = []
        for head in range(slots):
            lanes = head_lanes(head, width)
            head_rows = slice(head * HEAD_DIM, (head + 1) * HEAD_DIM)
            query = jnp.where(lanes, qkv_ref[rows, 0:width] * LOW(scale), LOW(0))
            grad = jnp.where(lanes, grad_ref[rows, :], LOW(0))
            scores = dot(key_rows, query, 1, 1)
            scores = allowed_scores(scores, doc_start, index * block, keys, block)
            probs = jnp.exp(scores - stat_ref[head : head + 1, rows])
            grad_probs = dot(value_rows, grad, 1, 1)
            delta = jnp.sum(probs * grad_probs, 0, keepdims=True)
            grad_scores = (probs * (grad_probs - delta)).astype(LOW)
            value_grad[0:keys, :] += dot(probs.astype(LOW), grad)
            key_grad[0:keys, :] += dot(grad_scores, query)
            outs.append(dot(key_t[head_rows, 0:keys], grad_scores))
        out_ref[rows, 0:width] = (jnp.concatenate(outs, 0).T * scale).astype(LOW)
        if index in after:
            after[index]()
    out_ref[:, width : 2 * width] = key_grad[...].astype(LOW)
    out_ref[:, 2 * width : 3 * width] = value_grad[...].astype(LOW)


MESH = pl.DeviceIdType.MESH


def send(src, dst, send_sem, recv_sem, **target):
    return pltpu.make_async_remote_copy(
        src_ref=src,
        dst_ref=dst,
        send_sem=send_sem,
        recv_sem=recv_sem,
        device_id=target,
        device_id_type=MESH,
    )


def greet_line(chips):
    rank = lax.axis_index("ctx")
    chip, core = rank // 2, rank % 2
    barrier = pltpu.get_barrier_semaphore()
    pl.semaphore_signal(barrier, 1, device_id={"ctx": rank + 1 - 2 * core}, device_id_type=MESH)

    @pl.when(chip > 0)
    def _():
        pl.semaphore_signal(barrier, 1, device_id={"ctx": rank - 2}, device_id_type=MESH)

    @pl.when(chip < chips - 1)
    def _():
        pl.semaphore_signal(barrier, 1, device_id={"ctx": rank + 2}, device_id_type=MESH)

    sides = (chip > 0).astype(jnp.int32) + (chip < chips - 1).astype(jnp.int32)
    pl.semaphore_wait(barrier, 1 + sides)


def greet_all():
    barrier = pltpu.get_barrier_semaphore()
    count = 0
    for axis in ("ctx", "dp"):
        size = lax.axis_size(axis)
        here = lax.axis_index(axis)

        def one(off, carry, axis=axis, size=size, here=here):
            peer = lax.rem(here + off, size)
            pl.semaphore_signal(barrier, 1, device_id={axis: peer}, device_id_type=MESH)
            return carry

        lax.fori_loop(1, size, one, 0)
        count += size - 1
    pl.semaphore_wait(barrier, count)


class Swap:
    def __init__(self, axis, source, target, sems):
        self.axis, self.source, self.target = axis, source, target
        self.send_sems, self.recv_sems = sems
        self.rank = lax.axis_index(axis)
        self.size = lax.axis_size(axis)

    def copy(self, peer, origin, target):
        return send(
            self.source(peer),
            self.target(origin),
            self.send_sems.at[peer],
            self.recv_sems.at[origin],
            **{self.axis: target},
        )

    def every(self, act):
        def one(off, carry):
            act(lax.rem(self.rank + off, self.size))
            return carry

        lax.fori_loop(1, self.size, one, 0)

    def start(self):
        self.every(lambda peer: self.copy(peer, self.rank, peer).start())

    def wait(self):
        self.every(lambda peer: self.copy(peer, peer, self.rank).wait_recv())

    def drain(self):
        self.every(lambda peer: self.copy(peer, self.rank, peer).wait_send())

    @staticmethod
    def semaphores(size):
        return [pltpu.SemaphoreType.DMA((size,)), pltpu.SemaphoreType.DMA((size,))]


class ChipSwap(Swap):
    def __init__(self, source, target, sems):
        super().__init__("ctx", source, target, sems)
        self.core = self.rank % 2
        self.rank, self.size = self.rank // 2, self.size // 2

    def copy(self, peer, origin, target):
        return send(
            self.source(peer),
            self.target(origin),
            self.send_sems.at[peer],
            self.recv_sems.at[origin],
            ctx=2 * target + self.core,
        )


class PlaneGather:
    def __init__(self, blocks, sems):
        self.blocks = blocks
        self.size = blocks.shape[0]
        self.rank = lax.axis_index("dp")
        self.square = self.size == 4
        self.send_sems, self.recv_sems = sems
        if self.square:
            self.beside = self.rank + 1 - 2 * (self.rank % 2)
            self.above = self.rank + 2 - 4 * (self.rank // 2)
            half = blocks.shape[1] // 32 * 16
            self.low, self.high = pl.ds(0, half), pl.ds(half, blocks.shape[1] - half)
        else:
            self.swap = Swap("dp", lambda peer: blocks.at[self.rank], blocks.at.__getitem__, sems)

    def copy(self, index, ref, target):
        return send(ref, ref, self.send_sems.at[index], self.recv_sems.at[index], dp=target)

    def start(self):
        if not self.square:
            self.swap.start()
            return
        own = self.blocks.at[self.rank]
        self.copy(0, own, self.beside).start()
        self.copy(1, own, self.above).start()

    def relay(self):
        if not self.square:
            return
        self.copy(0, self.blocks.at[self.beside], self.beside).wait_recv()
        self.copy(2, self.blocks.at[self.beside, self.low], self.above).start()
        self.copy(1, self.blocks.at[self.above], self.above).wait_recv()
        self.copy(3, self.blocks.at[self.above, self.high], self.beside).start()

    def wait(self):
        if not self.square:
            self.swap.wait()
            self.swap.drain()
            return
        far = 3 - self.rank
        own = self.blocks.at[self.rank]
        self.copy(2, self.blocks.at[far, self.low], self.above).wait_recv()
        self.copy(3, self.blocks.at[far, self.high], self.beside).wait_recv()
        self.copy(0, own, self.beside).wait_send()
        self.copy(1, own, self.above).wait_send()
        self.copy(2, self.blocks.at[self.beside, self.low], self.above).wait_send()
        self.copy(3, self.blocks.at[self.above, self.high], self.beside).wait_send()

    semaphores = staticmethod(Swap.semaphores)


class PlaneSum:
    def __init__(self, blocks, landed, sems):
        self.blocks, self.landed = blocks, landed
        self.rank = lax.axis_index("dp")
        self.send_sems, self.recv_sems = sems
        self.swap = Swap("dp", blocks.at.__getitem__, landed.at.__getitem__, sems)
        self.square = blocks.shape[0] == 4
        if self.square:
            self.beside = self.rank + 1 - 2 * (self.rank % 2)
            self.above = self.rank + 2 - 4 * (self.rank // 2)
            half = blocks.shape[1] // 32 * 16
            self.low, self.high = pl.ds(0, half), pl.ds(half, blocks.shape[1] - half)

    def copy(self, index):
        far = 3 - self.rank
        block, slot, rows, target = (
            (far, 0, self.low, self.beside),
            (self.beside, 1, self.low, self.beside),
            (far, 0, self.high, self.above),
            (self.above, 1, self.high, self.above),
            (self.above, 2, self.low, self.above),
            (self.beside, 2, self.high, self.beside),
        )[index]
        return send(
            self.blocks.at[block, rows],
            self.landed.at[slot, rows],
            self.send_sems.at[index],
            self.recv_sems.at[index],
            dp=target,
        )

    def start(self):
        if not self.square:
            self.swap.start()
            return
        for index in range(4):
            self.copy(index).start()

    def relay(self):
        if not self.square:
            return
        for index, block, rows in ((0, self.above, self.low), (2, self.beside, self.high)):
            self.copy(index).wait_recv()
            total = self.blocks[block, rows].astype(WIDE) + self.landed[0, rows].astype(WIDE)
            self.blocks[block, rows] = total.astype(self.blocks.dtype)
            self.copy(4 + index // 2).start()

    def total(self):
        total = self.blocks[self.rank].astype(WIDE)
        if not self.square:
            self.swap.wait()
            for off in range(1, self.swap.size):
                total = total + self.landed[lax.rem(self.rank + off, self.swap.size)].astype(WIDE)
            return total
        for index in (1, 3, 4, 5):
            self.copy(index).wait_recv()
        return total + self.landed[1].astype(WIDE) + self.landed[2].astype(WIDE)

    def drain(self):
        if not self.square:
            self.swap.drain()
            return
        for index in range(6):
            self.copy(index).wait_send()

    @staticmethod
    def semaphores(size):
        return Swap.semaphores(max(size, 6))


class LineGather:
    def __init__(self, blocks, send_sems, recv_sems):
        self.blocks, self.send_sems, self.recv_sems = blocks, send_sems, recv_sems
        self.rank = lax.axis_index("ctx")
        self.chip, self.core = self.rank // 2, self.rank % 2
        self.chips = blocks.shape[0] // 2

    def copy(self, way, origin, target, src=None):
        block = self.blocks.at[origin]
        return send(
            block if src is None else src,
            block,
            self.send_sems.at[way, origin],
            self.recv_sems.at[origin],
            ctx=target,
        )

    def pass_on(self, origin, src=None):
        chip = origin // 2

        @pl.when((chip <= self.chip) & (self.chip < self.chips - 1))
        def _():
            self.copy(0, origin, self.rank + 2, src).start()

        @pl.when((chip >= self.chip) & (self.chip > 0))
        def _():
            self.copy(1, origin, self.rank - 2, src).start()

        self.copy(2, origin, self.rank + 1 - 2 * self.core, src).start()

    def arrive(self, step, part):
        side, other = part % 2, part // 2
        origin_chip = self.chip + jnp.where(side == 0, -step, step)
        origin = 2 * origin_chip + jnp.where(other == 0, self.core, 1 - self.core)
        valid = (origin_chip >= 0) & (origin_chip < self.chips) & ((step > 0) | (side == 0))

        @pl.when(valid & (origin != self.rank))
        def _():
            self.copy(0, origin, self.rank).wait_recv()

            @pl.when(other == 0)
            def _():
                self.pass_on(origin)

        return valid, origin

    def finish(self):
        def one(chip, carry):
            origin = 2 * chip + self.core

            @pl.when((chip <= self.chip) & (self.chip < self.chips - 1))
            def _():
                self.copy(0, origin, self.rank).wait_send()

            @pl.when((chip >= self.chip) & (self.chip > 0))
            def _():
                self.copy(1, origin, self.rank).wait_send()

            self.copy(2, origin, self.rank).wait_send()
            return carry

        lax.fori_loop(0, self.chips, one, 0)

    @staticmethod
    def semaphores(ctx):
        return [pltpu.SemaphoreType.DMA((3, ctx)), pltpu.SemaphoreType.DMA((ctx,))]


class LineSum:
    def __init__(self, blocks, pair, passing, sems):
        self.blocks, self.pair, self.passing = blocks, pair, passing
        self.pair_send, self.pair_recv, self.line_send, self.line_recv = sems
        self.rank = lax.axis_index("ctx")
        self.chip, self.core = self.rank // 2, self.rank % 2
        self.chips = blocks.shape[0] // 2
        self.pieces = self.line_recv.shape[2]
        self.piece = blocks.shape[1] // self.pieces

    def pair_copy(self, chip):
        return send(
            self.blocks.at[2 * chip + 1 - self.core],
            self.pair.at[chip],
            self.pair_send.at[chip],
            self.pair_recv.at[chip],
            ctx=self.rank + 1 - 2 * self.core,
        )

    def line_copy(self, way, chip, piece, target):
        rows = pl.ds(piece * self.piece, self.piece)
        return send(
            self.blocks.at[2 * chip + self.core, rows],
            self.passing.at[way, chip, rows],
            self.line_send.at[chip, piece],
            self.line_recv.at[way, chip, piece],
            ctx=target,
        )

    def both(self, chip, rows):
        mine = self.blocks[2 * chip + self.core, rows].astype(WIDE)
        return mine + self.pair[chip, rows].astype(WIDE)

    def forward(self, way, chip, valid):
        behind = jnp.where(way == 0, self.chip > 0, self.chip < self.chips - 1)
        target = self.rank + jnp.where(way == 0, 2, -2)

        @pl.when(valid)
        def _():
            self.pair_copy(chip).wait_recv()

            def one(piece, carry):
                rows = pl.ds(pl.multiple_of(piece * self.piece, self.piece), self.piece)
                total = self.both(chip, rows)

                @pl.when(behind)
                def _():
                    self.line_copy(way, chip, piece, target).wait_recv()
                    passing = self.passing[way, chip, rows].astype(WIDE)
                    self.blocks[2 * chip + self.core, rows] = (total + passing).astype(LOW)

                @pl.when(jnp.logical_not(behind))
                def _():
                    self.blocks[2 * chip + self.core, rows] = total.astype(LOW)

                self.line_copy(way, chip, piece, target).start()
                return carry

            lax.fori_loop(0, self.pieces, one, 0)

    def near_first(self, step, way):
        last = self.chips - 1
        chip = jnp.where(way == 0, step - self.chip, 2 * last - self.chip - step)
        ahead = jnp.where(way == 0, (chip > self.chip) & (chip <= last), (chip >= 0) & (chip < self.chip))
        self.forward(way, chip, ahead)

    def far_first(self, step, way):
        last = self.chips - 1
        chip = jnp.where(way == 0, last + self.chip - step, step - last + self.chip)
        ahead = jnp.where(way == 0, (chip > self.chip) & (chip <= last), (chip >= 0) & (chip < self.chip))
        self.forward(way, chip, ahead)

    def send_pairs(self):
        def one(chip, carry):
            self.pair_copy(chip).start()
            return carry

        lax.fori_loop(0, self.chips, one, 0)

    def far_steps(self, begin, end):
        def one(index, carry):
            self.far_first(index // 2, index % 2)
            return carry

        lax.fori_loop(2 * begin, 2 * end, one, 0)

    def finish(self, out):
        self.pair_copy(self.chip).wait_recv()

        def one(piece, carry):
            rows = pl.ds(pl.multiple_of(piece * self.piece, self.piece), self.piece)
            out[rows] = self.both(self.chip, rows)

            @pl.when(self.chip > 0)
            def _():
                self.line_copy(0, self.chip, piece, self.rank).wait_recv()
                out[rows] = out[rows] + self.passing[0, self.chip, rows].astype(WIDE)

            @pl.when(self.chip < self.chips - 1)
            def _():
                self.line_copy(1, self.chip, piece, self.rank).wait_recv()
                out[rows] = out[rows] + self.passing[1, self.chip, rows].astype(WIDE)

            return carry

        lax.fori_loop(0, self.pieces, one, 0)

        def sent(chip, carry):
            self.pair_copy(chip).wait_send()

            @pl.when(chip != self.chip)
            def _():
                for piece in range(self.pieces):
                    self.line_copy(0, chip, piece, self.rank).wait_send()

            return carry

        lax.fori_loop(0, self.chips, sent, 0)

    @staticmethod
    def scratch(ctx, rows, columns, pieces):
        chips = ctx // 2
        return [
            pltpu.VMEM((ctx, rows, columns), LOW),
            pltpu.VMEM((chips, rows, columns), LOW),
            pltpu.VMEM((2, chips, rows, columns), LOW),
            pltpu.SemaphoreType.DMA((chips,)),
            pltpu.SemaphoreType.DMA((chips,)),
            pltpu.SemaphoreType.DMA((chips, pieces)),
            pltpu.SemaphoreType.DMA((2, chips, pieces)),
        ]


def feed_kernel(
    mixed_ref,
    in_ref,
    vectors_ref,
    bias_ref,
    proj_ref,
    fc_ref,
    out_ref,
    cot_ref,
    resid_ref,
    grad_ref,
    ffn_ref,
    act_ref,
    pre_ref,
    part_ref,
    gather_send,
    gather_recv,
    blocks,
    pair,
    passing,
    *sems,
):
    gather = LineGather(ffn_ref, gather_send, gather_recv)
    total = LineSum(blocks, pair, passing, sems)
    chips = gather.chips
    greet_line(chips)
    resid = in_ref[...].astype(WIDE) + dot(mixed_ref[:, 0:D], proj_ref[...]) + vectors_ref[0:1]
    resid_ref[...] = resid
    normed, _ = normalize(resid)
    ffn_ref[gather.rank] = (normed * vectors_ref[1:2] + vectors_ref[2:3]).astype(LOW)
    gather.pass_on(gather.rank)

    tokens = ffn_ref.shape[1]

    def work(chip):
        both = pl.ds(2 * chip, 2)
        pre = dot(ffn_ref[both].reshape(2 * tokens, D), fc_ref[...]) + bias_ref[0:1]
        bend = jnp.tanh(0.7978845608028654 * (pre + 0.044715 * pre * pre * pre))
        act = (0.5 * pre * (1.0 + bend)).astype(LOW)
        act_ref[both] = act.reshape(2, tokens, -1)
        slope = 0.5 * (1.0 + bend) + 0.5 * pre * (1.0 - bend * bend) * 0.7978845608028654 * (
            1.0 + 3 * 0.044715 * pre * pre
        )
        grad_act = dot(cot_ref[both].reshape(2 * tokens, D), out_ref[...], 1, 1)
        grad_pre = (slope * grad_act).astype(LOW)
        pre_ref[both] = grad_pre.reshape(2, tokens, -1)
        blocks[both] = dot(grad_pre, fc_ref[...], 1, 1).astype(LOW).reshape(2, tokens, D)
        total.pair_copy(chip).start()
        part_ref[both] = dot(act, out_ref[...]).astype(LOW).reshape(2, tokens, D)

    def step(index, carry):
        distance, side = index // 2, index % 2

        @pl.when(distance < chips)
        def _():
            @pl.when(side == 0)
            def _():
                gather.arrive(distance, 0)
                gather.arrive(distance, 1)

            valid, origin = gather.arrive(distance, 2 + side)

            @pl.when(valid)
            def _():
                work(origin // 2)

        @pl.when(side == 1)
        def _():
            def way(index, carry):
                total.near_first(distance, index)
                return carry

            lax.fori_loop(0, 2, way, 0)

        return carry

    lax.fori_loop(0, 2 * (2 * chips - 1), step, 0)
    total.finish(grad_ref)
    gather.finish()


def feed(mixed, own_in, vectors, bias, proj, fc, out, cot):
    ctx, tokens, _ = cot.shape
    width = fc.shape[1]
    return pl.pallas_call(
        feed_kernel,
        out_shape=(
            jax.ShapeDtypeStruct((tokens, D), WIDE),
            jax.ShapeDtypeStruct((tokens, D), WIDE),
            jax.ShapeDtypeStruct((ctx, tokens, D), LOW),
            jax.ShapeDtypeStruct((ctx, tokens, width), LOW),
            jax.ShapeDtypeStruct((ctx, tokens, width), LOW),
            jax.ShapeDtypeStruct((ctx, tokens, D), LOW),
        ),
        in_specs=[pl.BlockSpec(memory_space=pltpu.VMEM)] * 8,
        out_specs=[pl.BlockSpec(memory_space=pltpu.VMEM)] * 6,
        scratch_shapes=LineGather.semaphores(ctx) + LineSum.scratch(ctx, tokens, D, 4),
        compiler_params=pltpu.CompilerParams(
            vmem_limit_bytes=60 * MIB, collective_id=2, has_side_effects=True
        ),
        name="feed",
    )(mixed, own_in, vectors, bias, proj, fc, out, cot)


VMEM = pl.BlockSpec(memory_space=pltpu.VMEM)
HBM = pl.BlockSpec(memory_space=pl.ANY)


def params(number):
    return pltpu.CompilerParams(
        vmem_limit_bytes=63 * MIB, collective_id=number, has_side_effects=True
    )


def packed_rows(count, columns):
    tiles = -(-columns // 128)
    main = count // 16 * 16
    return tiles * main + -(-(tiles * (count - main)) // 16) * 16


def pack(out, index, rows, first, count, lane, columns):
    tiles = -(-columns // 128)
    main = count // 16 * 16
    for tile in range(tiles):
        lanes = slice(lane + tile * 128, lane + tile * 128 + 128)
        part = rows[first : first + main, lanes]
        out[index, tile * main : (tile + 1) * main] = part.astype(LOW)
    left = [
        rows[first + row : first + row + 1, lane + tile * 128 : lane + tile * 128 + 128]
        for row in range(main, count)
        for tile in range(tiles)
    ]
    space = out.shape[1] - tiles * main
    if space:
        left.append(jnp.zeros((space - len(left), 128), WIDE))
        out[index, tiles * main :] = jnp.concatenate(left, 0).astype(LOW)


def unpack(packed, rows, first, count, columns):
    tiles = -(-columns // 128)
    main = count // 16 * 16
    for tile in range(tiles):
        lanes = slice(tile * 128, tile * 128 + 128)
        rows[first : first + main, lanes] = packed[tile * main : (tile + 1) * main].astype(WIDE)
    left = packed[tiles * main :].astype(WIDE)
    for row in range(main, count):
        for tile in range(tiles):
            place = (row - main) * tiles + tile
            lanes = slice(tile * 128, tile * 128 + 128)
            rows[first + row : first + row + 1, lanes] = left[place : place + 1]


def full_lanes(columns):
    return -(-columns // 128) * 128


def head_pieces(ctx, slots):
    width = slots * HEAD_DIM
    pieces = []
    for rank in range(ctx):
        count = min(width, D - rank * width)
        if count > 0:
            for part in range(3):
                pieces.append((rank, part * width, part * D + rank * width, count))
    return pieces


def unit_pieces(ctx, dp):
    units = FF // (ctx * dp)
    return [
        (rank, seq * padded_units(units), (seq * ctx + rank) * units, units)
        for rank in range(ctx)
        for seq in range(dp)
    ]


def divide(rows_ref, wide, blocks, pieces, columns):
    count = rows_ref.shape[0]
    lanes = full_lanes(columns)
    for rank in range(blocks.shape[0]):
        wide[...] = jnp.zeros_like(wide)
        for owner, here, there, size in pieces:
            if owner == rank:
                wide[0:count, here : here + size] = rows_ref[:, there : there + size].astype(WIDE)
        pack(blocks, rank, wide, 0, count, 0, lanes)


class Spread:
    def __init__(self, blocks, landed, wide, out, sems):
        self.blocks, self.landed, self.wide, self.out = blocks, landed, wide, out
        self.swap = Swap("ctx", blocks.at.__getitem__, landed.at.__getitem__, sems[:2])
        self.plane = PlaneGather(out, sems[2:])

    def start(self):
        self.swap.start()
        self.landed[self.swap.rank] = self.blocks[self.swap.rank]

    def cross(self):
        self.swap.wait()
        count = self.out.shape[1] // self.swap.size
        columns = self.out.shape[2]
        for index in range(self.swap.size):
            unpack(self.landed[index], self.wide, index * count, count, columns)
        self.out[self.plane.rank] = self.wide[:, 0:columns].astype(LOW)
        self.plane.start()

    def wait(self):
        self.plane.wait()

    @staticmethod
    def scratch(ctx, dp, rows, columns):
        return [
            pltpu.VMEM((ctx, packed_rows(rows // ctx, columns), 128), LOW),
            pltpu.VMEM((rows, full_lanes(columns)), WIDE),
            *Swap.semaphores(ctx),
            *PlaneGather.semaphores(dp),
        ]


class Collect:
    def __init__(self, pieces, parts, landed, wide, blocks, came, one, out, sems):
        self.pieces, self.parts, self.wide, self.blocks = pieces, parts, wide, blocks
        self.came, self.one, self.out = came, one, out
        self.plane = PlaneSum(parts, landed, sems[:2])
        self.swap = Swap("ctx", blocks.at.__getitem__, came.at.__getitem__, sems[2:])

    def cross(self):
        rows, columns = self.parts.shape[1:]
        self.wide[:, 0:columns] = self.plane.total()
        if self.wide.shape[1] > columns:
            more = (rows, self.wide.shape[1] - columns)
            self.wide[:, columns:] = jnp.zeros(more, WIDE)
        count = rows // self.swap.size
        for index in range(self.swap.size):
            pack(self.blocks, index, self.wide, index * count, count, 0, columns)
        self.swap.start()
        self.came[self.swap.rank] = self.blocks[self.swap.rank]

    def wait(self):
        self.swap.wait()
        count = self.out.shape[0]
        for rank in range(self.swap.size):
            unpack(self.came[rank], self.one, 0, count, self.parts.shape[2])
            for owner, here, there, size in self.pieces:
                if owner == rank:
                    self.out[:, there : there + size] = self.one[0:count, here : here + size]
        self.swap.drain()
        self.plane.drain()

    @staticmethod
    def scratch(ctx, dp, rows, columns):
        count = rows // ctx
        packed = packed_rows(count, columns)
        return [
            pltpu.VMEM((dp, rows, columns), LOW),
            pltpu.VMEM((dp, rows, columns), LOW),
            pltpu.VMEM((rows, full_lanes(columns)), WIDE),
            pltpu.VMEM((ctx, packed, 128), LOW),
            pltpu.VMEM((ctx, packed, 128), LOW),
            pltpu.VMEM((-(-count // 8) * 8, full_lanes(columns)), WIDE),
            *PlaneSum.semaphores(dp),
            *Swap.semaphores(ctx),
        ]


def start_kernel(whole, slots, small_ref, rows_ref, unit_rows_ref, *refs):
    if whole:
        qkv_ref, fc_ref, proj_ref, *refs = refs
    small_out, rows_out, units_out, *refs = refs
    if whole:
        mat_out, fc_blocks, proj_blocks, *refs = refs
    gather = LineGather(rows_out, *refs[:2])
    seq = lax.axis_index("dp")
    rank = gather.rank
    ctx, dp = 2 * gather.chips, units_out.shape[0]
    line = Swap("ctx", lambda peer: small_ref, lambda origin: small_out.at[seq, origin], refs[2:4])
    plane = Swap("dp", lambda peer: small_out.at[seq], small_out.at.__getitem__, refs[4:6])
    units = PlaneGather(units_out, refs[6:8])
    if whole:
        qkv_blocks, wide_one, wide_two, *refs = refs[8:]
        spread = Spread(qkv_blocks, refs[0], refs[1], mat_out, refs[2:6])
    units_out[seq] = unit_rows_ref[...]
    rows_out[rank] = rows_ref[...]
    small_out[seq, rank] = small_ref[...]
    if whole:
        width = slots * HEAD_DIM
        divide(qkv_ref, wide_one, qkv_blocks, head_pieces(ctx, slots), 3 * width)
    greet_all()
    if whole:
        spread.start()
    line.start()
    units.start()
    if whole:
        spread.swap.drain()
    gather.pass_on(rank, rows_ref)
    line.wait()
    plane.start()
    if whole:
        spread.cross()

    def arrive(index, carry):
        gather.arrive(1 + index // 4, index % 4)
        return carry

    gather.arrive(0, 2)
    lax.fori_loop(0, 4, arrive, 0)
    units.relay()
    if whole:
        columns = dp * padded_units(FF // (ctx * dp))
        divide(fc_ref, wide_two, fc_blocks, unit_pieces(ctx, dp), columns)
        count = proj_ref.shape[0]
        wide_three = refs[6]
        wide_three[0:count, 0:D] = proj_ref[...].astype(WIDE)
        wide_three[0:count, D:] = jnp.zeros((count, full_lanes(D) - D), WIDE)
        pack(proj_blocks, 0, wide_three, 0, count, 0, D)
    lax.fori_loop(4, 8, arrive, 0)
    if whole:
        spread.plane.relay()
    lax.fori_loop(8, 4 * (gather.chips - 1), arrive, 0)
    plane.wait()
    plane.drain()
    line.drain()
    gather.finish()
    units.wait()
    if whole:
        spread.wait()


def start(small, rows, unit_rows, slots, mats):
    ctx, dp = lax.axis_size("ctx"), lax.axis_size("dp")
    tokens = rows.shape[0]
    whole = mats is not None
    shapes = [
        jax.ShapeDtypeStruct((dp, ctx, *small.shape), WIDE),
        jax.ShapeDtypeStruct((ctx, tokens, D), LOW),
        jax.ShapeDtypeStruct((dp, *unit_rows.shape), LOW),
    ]
    scratch = LineGather.semaphores(ctx) + Swap.semaphores(ctx) + Swap.semaphores(dp)
    scratch += PlaneGather.semaphores(dp)
    given = [small, rows, unit_rows]
    if whole:
        given += mats
        columns = 3 * slots * HEAD_DIM
        units = dp * unit_rows.shape[0]
        count = D // (dp * ctx)
        high = -(-count // 8) * 8
        shapes.append(jax.ShapeDtypeStruct((dp, D // dp, columns), LOW))
        shapes.append(jax.ShapeDtypeStruct((ctx, packed_rows(count, units), 128), LOW))
        shapes.append(jax.ShapeDtypeStruct((1, packed_rows(count, D), 128), LOW))
        scratch.append(pltpu.VMEM((ctx, packed_rows(count, columns), 128), LOW))
        scratch.append(pltpu.VMEM((high, full_lanes(columns)), WIDE))
        scratch.append(pltpu.VMEM((high, full_lanes(units)), WIDE))
        scratch += Spread.scratch(ctx, dp, D // dp, columns)
        scratch.append(pltpu.VMEM((high, full_lanes(D)), WIDE))
    return pl.pallas_call(
        functools.partial(start_kernel, whole, slots),
        out_shape=shapes,
        in_specs=[VMEM] * len(given),
        out_specs=[VMEM] * len(shapes),
        scratch_shapes=scratch,
        compiler_params=params(0),
        name="start",
    )(*given)


class Projection:
    def __init__(self, rows, blocks, wide, out, sems):
        self.rows, self.blocks, self.wide, self.out = rows, blocks, wide, out
        self.rank = lax.axis_index("ctx")
        self.core = self.rank % 2
        self.packed = rows.shape[1]
        self.plane = PlaneGather(blocks.at[self.core], sems[:2])
        self.send_sems, self.recv_sems = sems[2:4]
        self.swap = ChipSwap(lambda peer: rows.at[0], self.place, sems[4:])

    def place(self, chip):
        rows = pl.ds(pl.multiple_of(chip * self.packed, self.packed), self.packed)
        return self.blocks.at[self.core, self.plane.rank, rows]

    def start(self):
        self.swap.start()
        rows = pl.ds(pl.multiple_of(self.swap.rank * self.packed, self.packed), self.packed)
        self.blocks[self.core, self.plane.rank, rows] = self.rows[0]

    def cross(self):
        self.swap.wait()
        self.plane.start()
        self.to_other(self.plane.rank).start()

    def to_other(self, seq):
        block = self.blocks.at[self.core, seq]
        return send(
            block,
            block,
            self.send_sems.at[seq],
            self.recv_sems.at[seq],
            ctx=self.rank + 1 - 2 * self.core,
        )

    def wait(self):
        self.plane.wait()

        def others(off, carry):
            self.to_other(lax.rem(self.plane.rank + off, self.plane.size)).start()
            return carry

        lax.fori_loop(1, self.plane.size, others, 0)
        ctx = 2 * self.swap.size
        count = self.out.shape[1] // ctx

        def order(off, carry):
            seq = lax.rem(self.plane.rank + off, self.plane.size)
            self.to_other(seq).wait_recv()
            for rank in range(ctx):
                first = rank // 2 * self.packed
                rows = self.blocks[rank % 2, seq, first : first + self.packed]
                unpack(rows, self.wide, rank * count, count, D)
            self.out[seq] = self.wide[:, 0:D].astype(LOW)
            return carry

        lax.fori_loop(0, self.plane.size, order, 0)

        def sent(seq, carry):
            self.to_other(seq).wait_send()
            return carry

        lax.fori_loop(0, self.plane.size, sent, 0)
        self.swap.drain()

    @staticmethod
    def scratch(ctx, dp):
        packed = packed_rows(D // (dp * ctx), D)
        return [
            pltpu.VMEM((2, dp, ctx // 2 * packed, 128), LOW),
            pltpu.VMEM((D // dp, full_lanes(D)), WIDE),
            *PlaneGather.semaphores(dp),
            *Swap.semaphores(dp),
            *Swap.semaphores(ctx // 2),
        ]


def attend_kernel(
    block, whole, rows_ref, vectors_ref, bias_ref, mat_ref, start_ref, cot_ref, *refs
):
    if whole:
        blocks_ref, proj_ref, *refs = refs
    in_ref, qkv_ref, stat_ref, own_ref, cot_out, *refs = refs
    if whole:
        mat_out, proj_out, *refs = refs
    mixed, value_t, *refs = refs
    gather = LineGather(cot_out, *refs[:2])
    ctx, tokens, _ = rows_ref.shape
    width = mixed.shape[1]
    swap = Swap(
        "ctx",
        lambda peer: mixed.at[pl.ds(pl.multiple_of(peer * tokens, tokens), tokens)],
        lambda origin: own_ref.at[:, pl.ds(pl.multiple_of(origin * width, width), width)],
        refs[2:4],
    )
    if whole:
        spread = Spread(blocks_ref, refs[4], refs[5], mat_out, refs[6:10])
        proj = Projection(proj_ref, refs[10], refs[11], proj_out, refs[12:])
    greet_all()
    if whole:
        spread.start()
        proj.start()
    cot_out[gather.rank] = cot_ref[...]

    def project(index, carry):
        both = pl.ds(2 * index, 2)
        rows = pl.ds(pl.multiple_of(2 * index * tokens, 2 * tokens), 2 * tokens)
        normed, _ = normalize(rows_ref[both].reshape(2 * tokens, D).astype(WIDE))
        attn_in = (normed * vectors_ref[0:1] + vectors_ref[1:2]).astype(LOW)
        in_ref[rows] = attn_in
        qkv_ref[rows] = (dot(attn_in, mat_ref[...]) + bias_ref[0:1]).astype(LOW)
        return carry

    lax.fori_loop(0, ctx // 2, project, 0)
    attend_body(block, qkv_ref, start_ref, mixed, stat_ref, value_t)
    swap.start()
    own_ref[:, pl.ds(pl.multiple_of(swap.rank * width, width), width)] = mixed[
        pl.ds(pl.multiple_of(swap.rank * tokens, tokens), tokens)
    ]
    gather.pass_on(gather.rank, cot_ref)
    if whole:
        spread.cross()
        spread.swap.drain()
        proj.cross()

    def arrive(index, carry):
        gather.arrive(1 + index // 4, index % 4)
        return carry

    gather.arrive(0, 2)
    lax.fori_loop(0, 4, arrive, 0)
    if whole:
        spread.plane.relay()
        proj.plane.relay()
    lax.fori_loop(4, 4 * (gather.chips - 1), arrive, 0)
    if whole:
        proj.wait()
        spread.wait()
    swap.wait()
    swap.drain()
    gather.finish()


def attend(rows, vectors, bias, mat, doc_start, cot, blocks, proj, columns, block):
    ctx, tokens, _ = rows.shape
    dp = lax.axis_size("dp")
    length = ctx * tokens
    width = mat.shape[1] // 3
    whole = blocks is not None
    given = [rows, vectors, bias, mat, doc_start, cot]
    shapes = [
        jax.ShapeDtypeStruct((length, D), LOW),
        jax.ShapeDtypeStruct((length, 3 * width), LOW),
        jax.ShapeDtypeStruct((8, length), WIDE),
        jax.ShapeDtypeStruct((tokens, ctx * width), LOW),
        jax.ShapeDtypeStruct((ctx, tokens, D), LOW),
    ]
    scratch = [pltpu.VMEM((length, width), LOW), pltpu.VMEM((width, length), LOW)]
    scratch += LineGather.semaphores(ctx) + Swap.semaphores(ctx)
    if whole:
        given += [blocks, proj]
        shapes.append(jax.ShapeDtypeStruct((dp, D // dp, columns), LOW))
        shapes.append(jax.ShapeDtypeStruct((dp, D // dp, D), LOW))
        scratch += Spread.scratch(ctx, dp, D // dp, columns) + Projection.scratch(ctx, dp)
    return pl.pallas_call(
        functools.partial(attend_kernel, block, whole),
        out_shape=shapes,
        in_specs=[VMEM] * len(given),
        out_specs=[VMEM] * len(shapes),
        scratch_shapes=scratch,
        compiler_params=params(1),
        name="attend",
    )(*given)


def back_kernel(
    block,
    whole,
    grad_ref,
    resid_ref,
    own_cot,
    vectors_ref,
    proj_ref,
    qkv_ref,
    start_ref,
    stat_ref,
    ffn_hbm,
    pre_hbm,
    act_hbm,
    cot_hbm,
    part_hbm,
    resid_out,
    low_out,
    vector_out,
    units_out,
    rows_out,
    share_out,
    output_ref,
    fc_out,
    ffn,
    pre,
    act,
    cot,
    load_sems,
    own_grad,
    head_grad,
    key_t,
    key_grad,
    value_grad,
    *refs,
):
    total = LineSum(*refs[:3], refs[3:7])
    loads = [
        pltpu.make_async_copy(src, dst, load_sems.at[index])
        for index, (src, dst) in enumerate(
            (
                (part_hbm, total.blocks),
                (ffn_hbm, ffn),
                (pre_hbm, pre),
                (act_hbm, act),
                (cot_hbm, cot),
            )
        )
    ]
    for load in loads:
        load.start()
    tokens = own_cot.shape[0]
    length, width = head_grad.shape
    units = share_out.shape[0]
    swap = Swap(
        "ctx",
        lambda peer: own_grad.at[:, pl.ds(pl.multiple_of(peer * width, width), width)],
        lambda origin: head_grad.at[pl.ds(pl.multiple_of(origin * tokens, tokens), tokens)],
        refs[7:9],
    )
    share = PlaneSum(refs[9], refs[10], refs[11:13])
    if whole:
        pieces = unit_pieces(2 * total.chips, refs[9].shape[0])
        collect = Collect(pieces, *refs[13:19], fc_out, refs[19:])
    dp = share.swap.size
    greet_all()
    loads[0].wait()
    total.send_pairs()
    grad = grad_ref[...]
    normed, scale = normalize(resid_ref[...])
    grad_resid = own_cot[...].astype(WIDE) + norm_back(normed, scale, vectors_ref[0:1], grad)
    resid_out[...] = grad_resid
    low = grad_resid.astype(LOW)
    low_out[...] = low
    own_grad[:, 0:D] = dot(low, proj_ref[...], 1, 1).astype(LOW)
    own_grad[:, D:] = jnp.zeros((tokens, own_grad.shape[1] - D), LOW)
    swap.start()
    head_grad[pl.ds(pl.multiple_of(swap.rank * tokens, tokens), tokens)] = own_grad[
        :, pl.ds(pl.multiple_of(swap.rank * width, width), width)
    ]
    vector_out[0:1] = jnp.sum(grad_resid, 0, keepdims=True)
    vector_out[1:2] = jnp.sum(grad * normed, 0, keepdims=True)
    vector_out[2:3] = jnp.sum(grad, 0, keepdims=True)
    vector_out[3:4] = jnp.sum(own_cot[...].astype(WIDE), 0, keepdims=True)
    vector_out[4:8] = jnp.zeros((4, D), WIDE)
    loads[1].wait()
    loads[2].wait()
    grad_pre = pre[...].reshape(length, -1)
    units_out[...] = dot(jnp.ones((8, length), LOW), grad_pre)
    for index in range(dp):
        rows = slice(index * (D // dp), (index + 1) * (D // dp))
        part = dot(ffn[:, :, rows].reshape(length, D // dp), grad_pre, 0, 0)
        if whole:
            collect.parts[index] = part.astype(LOW)
        else:
            fc_out[rows] = part
    if whole:
        collect.plane.start()
    total.far_steps(0, 1)
    loads[3].wait()
    loads[4].wait()
    for index in range(dp):
        rows = slice(index * units, (index + 1) * units)
        part = dot(act[:, :, rows].reshape(length, units), cot[...].reshape(length, D), 0, 0)
        share.blocks[index] = part.astype(LOW)
    share.start()
    swap.wait()
    chips = total.chips

    def first():
        total.far_steps(1, 2)
        if whole:
            collect.plane.relay()

    def second():
        total.far_steps(2, 3)
        share.relay()

    attend_back_body(
        block,
        qkv_ref,
        start_ref,
        stat_ref,
        head_grad,
        rows_out,
        key_t,
        key_grad,
        value_grad,
        {1: first, 2: second},
    )
    if whole:
        collect.cross()
    total.far_steps(3, 2 * chips - 1)
    total.finish(output_ref)
    output_ref[...] = output_ref[...] + resid_ref[...] + vectors_ref[1:2]
    share_out[...] = share.total()
    swap.drain()
    share.drain()
    if whole:
        collect.wait()


def back(
    grad, resid, own_cot, vectors, proj, qkv, doc_start, stats, ffn, pre, act, cot, part, block, whole
):
    ctx, tokens, _ = cot.shape
    dp = lax.axis_size("dp")
    length = ctx * tokens
    width = qkv.shape[1] // 3
    columns = act.shape[2]
    units = columns // dp
    rows = D // dp
    shapes = [
        jax.ShapeDtypeStruct((tokens, D), WIDE),
        jax.ShapeDtypeStruct((tokens, D), LOW),
        jax.ShapeDtypeStruct((8, D), WIDE),
        jax.ShapeDtypeStruct((8, columns), WIDE),
        jax.ShapeDtypeStruct((length, 3 * width), LOW),
        jax.ShapeDtypeStruct((units, D), WIDE),
        jax.ShapeDtypeStruct((tokens, D), WIDE),
        jax.ShapeDtypeStruct((rows // ctx, FF) if whole else (D, columns), WIDE),
    ]
    scratch = [
        pltpu.VMEM(ffn.shape, LOW),
        pltpu.VMEM(pre.shape, LOW),
        pltpu.VMEM(act.shape, LOW),
        pltpu.VMEM(cot.shape, LOW),
        pltpu.SemaphoreType.DMA((5,)),
        pltpu.VMEM((tokens, ctx * width), LOW),
        pltpu.VMEM((length, width), LOW),
        pltpu.VMEM((width, length), LOW),
        pltpu.VMEM((length, width), WIDE),
        pltpu.VMEM((length, width), WIDE),
        *LineSum.scratch(ctx, tokens, D, 4),
        *Swap.semaphores(ctx),
        pltpu.VMEM((dp, units, D), LOW),
        pltpu.VMEM((dp, units, D), LOW),
        *PlaneSum.semaphores(dp),
    ]
    if whole:
        scratch += Collect.scratch(ctx, dp, rows, columns)
    return pl.pallas_call(
        functools.partial(back_kernel, block, whole),
        out_shape=shapes,
        in_specs=[VMEM] * 8 + [HBM] * 5,
        out_specs=[VMEM] * 8,
        scratch_shapes=scratch,
        compiler_params=params(3),
        name="back",
    )(grad, resid, own_cot, vectors, proj, qkv, doc_start, stats, ffn, pre, act, cot, part)


class ProjectionSum:
    def __init__(self, out, refs):
        self.out = out
        self.mixed, self.low, self.parts, landed, self.wide, self.blocks, self.came = refs[:7]
        self.send_sems, self.recv_sems = refs[7:9]
        self.plane = PlaneSum(self.parts, landed, refs[9:11])
        self.rank = lax.axis_index("ctx")
        self.core = self.rank % 2
        self.swap = ChipSwap(self.blocks.at.__getitem__, self.came.at.__getitem__, refs[11:13])

    def pair_copies(self):
        return [
            send(
                ref.at[self.core],
                ref.at[self.core],
                self.send_sems.at[index],
                self.recv_sems.at[index],
                ctx=self.rank + 1 - 2 * self.core,
            )
            for index, ref in enumerate((self.mixed, self.low))
        ]

    def start(self, mixed, low):
        self.mixed[self.core] = mixed
        self.low[self.core] = low
        for copy in self.pair_copies():
            copy.start()

    def multiply(self):
        for copy in self.pair_copies():
            copy.wait_recv()
        dp, rows = self.parts.shape[:2]
        chips = self.swap.size
        tokens = 2 * self.low.shape[1]
        count = self.out.shape[0]
        mixed = self.mixed[...].reshape(tokens, -1)[:, 0:D]
        low = self.low[...].reshape(tokens, D)
        feature = lax.broadcasted_iota(jnp.int32, (D, rows), 0)
        column = lax.broadcasted_iota(jnp.int32, (1, rows), 1)
        for index in range(dp):
            owner = index * 2 * chips + column // count * 2 + self.core
            wanted = jnp.where(column < chips * count, owner * count + column % count, -1)
            chosen = jnp.where(feature == wanted, 1.0, 0.0).astype(LOW)
            picked = dot(mixed, chosen).astype(LOW)
            self.parts[index] = dot(picked, low, 0, 0).astype(LOW)
        self.plane.start()

    def cross(self):
        count = self.out.shape[0]
        self.wide[:, 0:D] = self.plane.total()
        self.wide[:, D:] = jnp.zeros((self.wide.shape[0], self.wide.shape[1] - D), WIDE)
        for chip in range(self.swap.size):
            pack(self.blocks, chip, self.wide, chip * count, count, 0, D)
        self.swap.start()

    def wait(self):
        self.swap.wait()
        total = self.blocks[self.swap.rank].astype(WIDE)
        for off in range(1, self.swap.size):
            total = total + self.came[lax.rem(self.swap.rank + off, self.swap.size)].astype(WIDE)
        count = self.out.shape[0]
        unpack(total, self.wide, 0, count, D)
        self.out[...] = self.wide[0:count, 0:D]
        for copy in self.pair_copies():
            copy.wait_send()
        self.plane.drain()
        self.swap.drain()

    @staticmethod
    def scratch(ctx, dp, tokens, width):
        chips = ctx // 2
        count = D // (dp * ctx)
        rows = -(-(chips * count) // 16) * 16
        packed = packed_rows(count, D)
        return [
            pltpu.VMEM((2, tokens, ctx * width), LOW),
            pltpu.VMEM((2, tokens, D), LOW),
            pltpu.VMEM((dp, rows, D), LOW),
            pltpu.VMEM((dp, rows, D), LOW),
            pltpu.VMEM((rows, full_lanes(D)), WIDE),
            pltpu.VMEM((chips, packed, 128), LOW),
            pltpu.VMEM((chips, packed, 128), LOW),
            *Swap.semaphores(2),
            *PlaneSum.semaphores(dp),
            *Swap.semaphores(chips),
        ]


def last_kernel(
    whole,
    slots,
    rows_ref,
    mat_ref,
    in_ref,
    own_ref,
    resid_ref,
    vectors_ref,
    mixed_ref,
    low_ref,
    grad_out,
    vector_out,
    heads_out,
    mat_out,
    *refs,
):
    if whole:
        proj_out, *refs = refs
    grad, *refs = refs
    total = LineSum(*refs[:3], refs[3:7])
    if whole:
        collect = Collect(
            head_pieces(2 * total.chips, slots), *refs[7:13], mat_out, refs[13:17]
        )
        proj = ProjectionSum(proj_out, refs[17:])
    chips = total.chips
    tokens = own_ref.shape[0]
    dp = lax.axis_size("dp")
    if whole:
        greet_all()
        proj.start(mixed_ref[...], low_ref[...])
    else:
        greet_line(chips)

    def partial_sum(index, carry):
        off = jnp.where(index % 2 == 0, -(index // 2), index // 2 + 1)
        chip = lax.rem(chips - 1 + off, chips)
        rows = pl.ds(pl.multiple_of(2 * chip * tokens, 2 * tokens), 2 * tokens)
        part = dot(rows_ref[rows], mat_ref[...], 1, 1).astype(LOW)
        total.blocks[pl.ds(2 * chip, 2)] = part.reshape(2, tokens, D)
        total.pair_copy(chip).start()
        return carry

    lax.fori_loop(0, chips, partial_sum, 0)
    total.far_steps(0, 1)
    for index in range(dp):
        rows = slice(index * (D // dp), (index + 1) * (D // dp))
        part = dot(in_ref[:, rows], rows_ref[...], 0, 0)
        if whole:
            collect.parts[index] = part.astype(LOW)
        else:
            mat_out[rows] = part
    if whole:
        collect.plane.start()
    total.far_steps(1, 2)
    if whole:
        proj.multiply()
    total.far_steps(2, 3)
    heads_out[...] = dot(jnp.ones((8, rows_ref.shape[0]), LOW), rows_ref[...])
    if whole:
        collect.plane.relay()
    total.far_steps(3, 4)
    if whole:
        proj.plane.relay()
        collect.cross()
    total.far_steps(4, 2 * chips - 1)
    total.finish(grad)
    if whole:
        proj.cross()
    normed, scale = normalize(own_ref[...].astype(WIDE))
    incoming = grad[...]
    grad_out[...] = resid_ref[...] + norm_back(normed, scale, vectors_ref[0:1], incoming)
    vector_out[0:1] = jnp.sum(incoming * normed, 0, keepdims=True)
    vector_out[1:2] = jnp.sum(incoming, 0, keepdims=True)
    vector_out[2:8] = jnp.zeros((6, D), WIDE)
    if whole:
        collect.wait()
        proj.wait()


def last(rows, mat, attn_in, own_in, resid, vectors, mixed, low, whole):
    ctx, dp = lax.axis_size("ctx"), lax.axis_size("dp")
    tokens = own_in.shape[0]
    columns = rows.shape[1]
    shapes = [
        jax.ShapeDtypeStruct((tokens, D), WIDE),
        jax.ShapeDtypeStruct((8, D), WIDE),
        jax.ShapeDtypeStruct((8, columns), WIDE),
        jax.ShapeDtypeStruct((D // (ctx * dp), 3 * D) if whole else (D, columns), WIDE),
    ]
    scratch = [pltpu.VMEM((tokens, D), WIDE), *LineSum.scratch(ctx, tokens, D, 4)]
    if whole:
        shapes.append(jax.ShapeDtypeStruct((D // (ctx * dp), D), WIDE))
        scratch += Collect.scratch(ctx, dp, D // dp, columns)
        scratch += ProjectionSum.scratch(ctx, dp, tokens, columns // 3)
    return pl.pallas_call(
        functools.partial(last_kernel, whole, columns // (3 * HEAD_DIM)),
        out_shape=shapes,
        in_specs=[VMEM] * 8,
        out_specs=[VMEM] * len(shapes),
        scratch_shapes=scratch,
        compiler_params=params(4),
        name="last",
    )(rows, mat, attn_in, own_in, resid, vectors, mixed, low)


def vector_kernel(parts_ref, out_ref, plane_landed, line_parts, line_landed, *sems):
    seq = lax.axis_index("dp")
    swap = Swap("dp", parts_ref.at.__getitem__, plane_landed.at.__getitem__, sems[:2])
    line = Swap("ctx", line_parts.at.__getitem__, line_landed.at.__getitem__, sems[2:])
    greet_all()
    swap.start()
    swap.wait()
    total = parts_ref[seq]
    for off in range(1, swap.size):
        total = total + plane_landed[lax.rem(seq + off, swap.size)]
    line_parts[...] = total
    line.start()
    line.wait()
    total = line_parts[line.rank]
    for off in range(1, line.size):
        total = total + line_landed[lax.rem(line.rank + off, line.size)]
    out_ref[...] = total
    swap.drain()
    line.drain()


def sum_vector(parts):
    dp, ctx = parts.shape[:2]
    return pl.pallas_call(
        vector_kernel,
        out_shape=jax.ShapeDtypeStruct(parts.shape[2:], WIDE),
        in_specs=[VMEM],
        out_specs=VMEM,
        scratch_shapes=[
            pltpu.VMEM(parts.shape, WIDE),
            pltpu.VMEM(parts.shape[1:], WIDE),
            pltpu.VMEM(parts.shape[1:], WIDE),
            *PlaneSum.semaphores(dp),
            *Swap.semaphores(ctx),
        ],
        compiler_params=params(5),
        name="sum_vector",
    )(parts)


def gather_rows(block):
    return lax.all_gather(block, ("dp", "ctx"), axis=0, tiled=True)


def by_rank_heads(rows, ctx, slots):
    count = rows.shape[0]
    split = rows.reshape(count, 3, D)
    split = jnp.pad(split, ((0, 0), (0, 0), (0, (ctx * slots - HEADS) * HEAD_DIM)))
    split = split.reshape(count, 3, ctx, slots * HEAD_DIM)
    return split.transpose(2, 0, 1, 3).reshape(ctx, count, 3 * slots * HEAD_DIM)


def from_rank_heads(blocks, slots):
    ctx, count = blocks.shape[:2]
    split = blocks.reshape(ctx, count, 3, slots * HEAD_DIM).transpose(1, 2, 0, 3)
    return split.reshape(count, 3, ctx * slots * HEAD_DIM)[:, :, :D].reshape(count, 3 * D)


def padded_units(units):
    return -(-units // 16) * 16


def by_rank_units(rows, ctx, dp):
    count = rows.shape[0]
    units = FF // (dp * ctx)
    split = rows.reshape(count, dp, ctx, units).transpose(2, 0, 1, 3)
    split = jnp.pad(split, ((0, 0), (0, 0), (0, 0), (0, padded_units(units) - units)))
    return split.reshape(ctx, count, dp * padded_units(units))


def from_rank_units(blocks, dp):
    ctx, count = blocks.shape[:2]
    units = FF // (dp * ctx)
    split = blocks.reshape(ctx, count, dp, padded_units(units))[..., :units]
    return split.transpose(1, 2, 0, 3).reshape(count, FF)


def rank_vector(vector, ctx, slots, rank):
    padded = jnp.pad(vector, (0, (ctx * slots - HEADS) * HEAD_DIM))
    width = slots * HEAD_DIM
    return lax.dynamic_slice_in_dim(padded, rank * width, width, 0)


def shards(
    hidden_in, qkv_weight, proj_weight, fc_weight, out_weight, small_params, segments, cotangent
):
    tokens = hidden_in.shape[1]
    length = segments.shape[1]
    ctx = lax.axis_size("ctx")
    dp = lax.axis_size("dp")
    owners = dp * ctx
    rank = lax.axis_index("ctx")
    slots = -(-HEADS // ctx)
    width = slots * HEAD_DIM
    units = FF // owners
    rows = D // owners
    whole = D % owners == 0
    block = min(256, length)
    both = ("dp", "ctx")

    vec_count = small_params.shape[0]
    vec_pad = -(-vec_count // 1024) * 1024
    small = jnp.pad(small_params.astype(WIDE), (0, vec_pad - vec_count)).reshape(-1, 128)
    more = padded_units(units) - units
    unit_rows = jnp.pad(out_weight.reshape(units, D), ((0, more), (0, 0)))
    if whole:
        mats = [
            qkv_weight.reshape(rows, 3 * D),
            fc_weight.reshape(rows, FF),
            proj_weight.reshape(rows, D),
        ]
        small, rows_in, mat_out, mat_qkv, fc_blocks, proj_rows = start(
            small, hidden_in[0], unit_rows, slots, mats
        )
        mat_qkv = mat_qkv.reshape(D, 3 * width)
    else:
        small, rows_in, mat_out = start(small, hidden_in[0], unit_rows, slots, None)
        fc_blocks = proj_rows = None
        mat_qkv = by_rank_heads(gather_rows(qkv_weight).reshape(D, 3 * D), ctx, slots)
        mat_qkv = lax.dynamic_index_in_dim(mat_qkv, rank, 0, keepdims=False)
        mat_fc = by_rank_units(gather_rows(fc_weight).reshape(D, FF), ctx, dp)
        mat_fc = lax.dynamic_index_in_dim(mat_fc, rank, 0, keepdims=False)
        mat_proj = gather_rows(proj_weight).reshape(D, D)
    mat_out = mat_out.reshape(-1, D)
    small = small.reshape(owners, vec_pad)[:, :vec_count].reshape(-1)
    gain_one, shift_one, bias_query, bias_value, bias_proj, gain_two, shift_two = [
        small[i * D : (i + 1) * D] for i in range(7)
    ]
    bias_fc = small[7 * D : 7 * D + FF]
    bias_out = small[7 * D + FF :]
    bias_units = lax.dynamic_index_in_dim(
        bias_fc.reshape(dp, ctx, units), rank, 1, keepdims=False
    )
    bias_units = jnp.pad(bias_units, ((0, 0), (0, more))).reshape(-1)
    bias_qkv = jnp.concatenate(
        [
            rank_vector(bias_query, ctx, slots, rank),
            jnp.zeros((width,), WIDE),
            rank_vector(bias_value, ctx, slots, rank),
        ]
    )

    docs = segments[0]
    doc_start = jnp.sum((docs[:, None] < docs[None, :]).astype(jnp.int32), 0)[None]
    attn_in, qkv, stats, own_mixed, cot, *rest = attend(
        rows_in,
        jnp.stack([gain_one, shift_one]),
        bias_qkv[None],
        mat_qkv,
        doc_start,
        cotangent[0],
        fc_blocks,
        proj_rows,
        mat_out.shape[0],
        block,
    )
    if whole:
        mat_fc, mat_proj = rest[0].reshape(D, -1), rest[1].reshape(D, D)
    resid, grad_normed_two, ffn_in, act, grad_pre, out_part = feed(
        own_mixed,
        hidden_in[0],
        jnp.stack([bias_proj, gain_two, shift_two]),
        bias_units[None],
        mat_proj,
        mat_fc,
        mat_out,
        cot,
    )
    grad_resid, resid_low, sums_two, sums_units, grad_rows, grad_out, output, grad_fc = back(
        grad_normed_two,
        resid,
        cotangent[0],
        jnp.stack([gain_two, bias_out]),
        mat_proj,
        qkv,
        doc_start,
        stats,
        ffn_in,
        grad_pre,
        act,
        cot,
        out_part,
        block,
        whole,
    )
    grad_input, sums_one, sums_heads, grad_qkv, *rest = last(
        grad_rows,
        mat_qkv,
        attn_in,
        hidden_in[0],
        grad_resid,
        gain_one[None],
        own_mixed,
        resid_low,
        whole,
    )
    if whole:
        share_fc, share_qkv, share_proj = grad_fc, grad_qkv, rest[0]
    else:
        grad_proj = dot(own_mixed[:, :D], resid_low, 0, 0).reshape(-1)
        share_proj = lax.psum_scatter(grad_proj, both, scatter_dimension=0, tiled=True)
        here = (jnp.arange(ctx) == rank)[:, None, None]
        full_fc = from_rank_units(jnp.where(here, grad_fc[None], 0.0), dp).reshape(-1)
        full_qkv = from_rank_heads(jnp.where(here, grad_qkv[None], 0.0), slots).reshape(-1)
        share_fc = lax.psum_scatter(full_fc, both, scatter_dimension=0, tiled=True)
        share_qkv = lax.psum_scatter(full_qkv, both, scatter_dimension=0, tiled=True)

    def spread_heads(part):
        padded = jnp.zeros((ctx * width,), WIDE)
        return lax.dynamic_update_slice_in_dim(padded, part, rank * width, 0)[:D]

    sums_units = sums_units[0].reshape(dp, 1, -1)[:, :, :units]
    sums_units = lax.dynamic_update_slice_in_dim(
        jnp.zeros((dp, ctx, units), WIDE), sums_units, rank, 1
    ).reshape(FF)
    vector = jnp.concatenate(
        [
            sums_one[0],
            sums_one[1],
            spread_heads(sums_heads[0, :width]),
            spread_heads(sums_heads[0, 2 * width :]),
            sums_two[0],
            sums_two[1],
            sums_two[2],
            sums_units,
            sums_two[3],
        ]
    ).reshape(owners, vec_count)
    vector = jnp.pad(vector, ((0, 0), (0, vec_pad - vec_count))).reshape(dp, ctx, -1, 128)
    share_vector = sum_vector(vector)
    return (
        output[None],
        grad_input[None],
        share_qkv.astype(WIDE).reshape(-1),
        share_proj.astype(WIDE).reshape(-1),
        share_fc.astype(WIDE).reshape(-1),
        grad_out[:units].reshape(-1),
        share_vector.reshape(-1)[:vec_count],
    )


def solution(mesh):
    flat = P(("dp", "ctx"))
    rows = P("dp", "ctx", None)
    return jax.shard_map(
        shards,
        mesh=mesh,
        in_specs=(rows, flat, flat, flat, flat, flat, P("dp", None), rows),
        out_specs=(rows, rows, flat, flat, flat, flat, flat),
        check_vma=False,
    )
```

```python
import functools

import jax
import jax.numpy as jnp
from jax import lax
from jax.experimental import pallas as pl
from jax.experimental.pallas import tpu as pltpu
from jax.sharding import PartitionSpec as P

D = 1600
HEADS = 25
HEAD_DIM = 64
FF = 6400
EPSILON = 1e-05
LOW = jnp.bfloat16
WIDE = jnp.float32
MIB = 1024 * 1024


def dot(left, right, left_dim=1, right_dim=0):
    return lax.dot_general(
        left, right, (((left_dim,), (right_dim,)), ((), ())), preferred_element_type=WIDE
    )


def normalize(rows):
    centre = rows - jnp.mean(rows, -1, keepdims=True)
    spread = jnp.mean(centre * centre, -1, keepdims=True)
    scale = lax.rsqrt(spread + EPSILON)
    return centre * scale, scale


def norm_back(normed, scale, gain, incoming):
    scaled = gain * incoming
    return scale * (
        scaled
        - jnp.mean(scaled, -1, keepdims=True)
        - normed * jnp.mean(scaled * normed, -1, keepdims=True)
    )


def head_lanes(head, width):
    lane = lax.broadcasted_iota(jnp.int32, (1, width), 1)
    return (lane // HEAD_DIM) == head


def allowed_scores(scores, doc_start, first_query, keys, block):
    key_pos = lax.broadcasted_iota(jnp.int32, (keys, block), 0)
    query_pos = first_query + lax.broadcasted_iota(jnp.int32, (keys, block), 1)
    seen = (key_pos >= doc_start) & (key_pos <= query_pos)
    return jnp.where(seen, scores, -1e30)


def attend_body(block, qkv_ref, start_ref, mixed_ref, stat_ref, value_t):
    length = qkv_ref.shape[0]
    width = mixed_ref.shape[1]
    slots = width // HEAD_DIM
    value_t[...] = qkv_ref[:, 2 * width : 3 * width].astype(WIDE).T.astype(LOW)
    stat_ref[...] = jnp.zeros_like(stat_ref)
    for index in range(length // block):
        keys = (index + 1) * block
        rows = pl.ds(index * block, block)
        key_rows = qkv_ref[0:keys, width : 2 * width]
        doc_start = start_ref[0:1, rows]
        outs = []
        for head in range(slots):
            query = jnp.where(
                head_lanes(head, width), qkv_ref[rows, 0:width] * LOW(HEAD_DIM**-0.5), LOW(0)
            )
            scores = dot(key_rows, query, 1, 1)
            scores = allowed_scores(scores, doc_start, index * block, keys, block)
            top = jnp.max(scores, 0, keepdims=True)
            expo = jnp.exp(scores - top)
            total = jnp.sum(expo, 0, keepdims=True)
            head_rows = slice(head * HEAD_DIM, (head + 1) * HEAD_DIM)
            out = dot(value_t[head_rows, 0:keys], expo.astype(LOW))
            outs.append(out / total)
            stat_ref[head : head + 1, rows] = top + jnp.log(total)
        mixed_ref[rows, :] = jnp.concatenate(outs, 0).T.astype(LOW)


def attend_back_body(
    block, qkv_ref, start_ref, stat_ref, grad_ref, out_ref, key_t, key_grad, value_grad, after
):
    length = qkv_ref.shape[0]
    width = grad_ref.shape[1]
    slots = width // HEAD_DIM
    scale = HEAD_DIM**-0.5
    key_t[...] = qkv_ref[:, width : 2 * width].astype(WIDE).T.astype(LOW)
    key_grad[...] = jnp.zeros_like(key_grad)
    value_grad[...] = jnp.zeros_like(value_grad)
    for index in range(length // block):
        keys = (index + 1) * block
        rows = pl.ds(index * block, block)
        key_rows = qkv_ref[0:keys, width : 2 * width]
        value_rows = qkv_ref[0:keys, 2 * width : 3 * width]
        doc_start = start_ref[0:1, rows]
        outs = []
        for head in range(slots):
            lanes = head_lanes(head, width)
            head_rows = slice(head * HEAD_DIM, (head + 1) * HEAD_DIM)
            query = jnp.where(lanes, qkv_ref[rows, 0:width] * LOW(scale), LOW(0))
            grad = jnp.where(lanes, grad_ref[rows, :], LOW(0))
            scores = dot(key_rows, query, 1, 1)
            scores = allowed_scores(scores, doc_start, index * block, keys, block)
            probs = jnp.exp(scores - stat_ref[head : head + 1, rows])
            grad_probs = dot(value_rows, grad, 1, 1)
            delta = jnp.sum(probs * grad_probs, 0, keepdims=True)
            grad_scores = (probs * (grad_probs - delta)).astype(LOW)
            value_grad[0:keys, :] += dot(probs.astype(LOW), grad)
            key_grad[0:keys, :] += dot(grad_scores, query)
            outs.append(dot(key_t[head_rows, 0:keys], grad_scores))
        out_ref[rows, 0:width] = (jnp.concatenate(outs, 0).T * scale).astype(LOW)
        if index in after:
            after[index]()
    out_ref[:, width : 2 * width] = key_grad[...].astype(LOW)
    out_ref[:, 2 * width : 3 * width] = value_grad[...].astype(LOW)


MESH = pl.DeviceIdType.MESH


def send(src, dst, send_sem, recv_sem, **target):
    return pltpu.make_async_remote_copy(
        src_ref=src,
        dst_ref=dst,
        send_sem=send_sem,
        recv_sem=recv_sem,
        device_id=target,
        device_id_type=MESH,
    )


def greet_line(chips):
    rank = lax.axis_index("ctx")
    chip, core = rank // 2, rank % 2
    barrier = pltpu.get_barrier_semaphore()
    pl.semaphore_signal(barrier, 1, device_id={"ctx": rank + 1 - 2 * core}, device_id_type=MESH)

    @pl.when(chip > 0)
    def _():
        pl.semaphore_signal(barrier, 1, device_id={"ctx": rank - 2}, device_id_type=MESH)

    @pl.when(chip < chips - 1)
    def _():
        pl.semaphore_signal(barrier, 1, device_id={"ctx": rank + 2}, device_id_type=MESH)

    sides = (chip > 0).astype(jnp.int32) + (chip < chips - 1).astype(jnp.int32)
    pl.semaphore_wait(barrier, 1 + sides)


def greet_all():
    barrier = pltpu.get_barrier_semaphore()
    count = 0
    for axis in ("ctx", "dp"):
        size = lax.axis_size(axis)
        here = lax.axis_index(axis)

        def one(off, carry, axis=axis, size=size, here=here):
            peer = lax.rem(here + off, size)
            pl.semaphore_signal(barrier, 1, device_id={axis: peer}, device_id_type=MESH)
            return carry

        lax.fori_loop(1, size, one, 0)
        count += size - 1
    pl.semaphore_wait(barrier, count)


class Swap:
    def __init__(self, axis, source, target, sems):
        self.axis, self.source, self.target = axis, source, target
        self.send_sems, self.recv_sems = sems
        self.rank = lax.axis_index(axis)
        self.size = lax.axis_size(axis)

    def copy(self, peer, origin, target):
        return send(
            self.source(peer),
            self.target(origin),
            self.send_sems.at[peer],
            self.recv_sems.at[origin],
            **{self.axis: target},
        )

    def every(self, act):
        def one(off, carry):
            act(lax.rem(self.rank + off, self.size))
            return carry

        lax.fori_loop(1, self.size, one, 0)

    def start(self):
        self.every(lambda peer: self.copy(peer, self.rank, peer).start())

    def wait(self):
        self.every(lambda peer: self.copy(peer, peer, self.rank).wait_recv())

    def drain(self):
        self.every(lambda peer: self.copy(peer, self.rank, peer).wait_send())

    @staticmethod
    def semaphores(size):
        return [pltpu.SemaphoreType.DMA((size,)), pltpu.SemaphoreType.DMA((size,))]


class ChipSwap(Swap):
    def __init__(self, source, target, sems):
        super().__init__("ctx", source, target, sems)
        self.core = self.rank % 2
        self.rank, self.size = self.rank // 2, self.size // 2

    def copy(self, peer, origin, target):
        return send(
            self.source(peer),
            self.target(origin),
            self.send_sems.at[peer],
            self.recv_sems.at[origin],
            ctx=2 * target + self.core,
        )


class PlaneGather:
    def __init__(self, blocks, sems):
        self.blocks = blocks
        self.size = blocks.shape[0]
        self.rank = lax.axis_index("dp")
        self.square = self.size == 4
        self.send_sems, self.recv_sems = sems
        if self.square:
            self.beside = self.rank + 1 - 2 * (self.rank % 2)
            self.above = self.rank + 2 - 4 * (self.rank // 2)
            half = blocks.shape[1] // 32 * 16
            self.low, self.high = pl.ds(0, half), pl.ds(half, blocks.shape[1] - half)
        else:
            self.swap = Swap("dp", lambda peer: blocks.at[self.rank], blocks.at.__getitem__, sems)

    def copy(self, index, ref, target):
        return send(ref, ref, self.send_sems.at[index], self.recv_sems.at[index], dp=target)

    def start(self):
        if not self.square:
            self.swap.start()
            return
        own = self.blocks.at[self.rank]
        self.copy(0, own, self.beside).start()
        self.copy(1, own, self.above).start()

    def relay(self):
        if not self.square:
            return
        self.copy(0, self.blocks.at[self.beside], self.beside).wait_recv()
        self.copy(2, self.blocks.at[self.beside, self.low], self.above).start()
        self.copy(1, self.blocks.at[self.above], self.above).wait_recv()
        self.copy(3, self.blocks.at[self.above, self.high], self.beside).start()

    def wait(self):
        if not self.square:
            self.swap.wait()
            self.swap.drain()
            return
        far = 3 - self.rank
        own = self.blocks.at[self.rank]
        self.copy(2, self.blocks.at[far, self.low], self.above).wait_recv()
        self.copy(3, self.blocks.at[far, self.high], self.beside).wait_recv()
        self.copy(0, own, self.beside).wait_send()
        self.copy(1, own, self.above).wait_send()
        self.copy(2, self.blocks.at[self.beside, self.low], self.above).wait_send()
        self.copy(3, self.blocks.at[self.above, self.high], self.beside).wait_send()

    semaphores = staticmethod(Swap.semaphores)


class PlaneSum:
    def __init__(self, blocks, landed, sems):
        self.blocks, self.landed = blocks, landed
        self.rank = lax.axis_index("dp")
        self.send_sems, self.recv_sems = sems
        self.swap = Swap("dp", blocks.at.__getitem__, landed.at.__getitem__, sems)
        self.square = blocks.shape[0] == 4
        if self.square:
            self.beside = self.rank + 1 - 2 * (self.rank % 2)
            self.above = self.rank + 2 - 4 * (self.rank // 2)
            half = blocks.shape[1] // 32 * 16
            self.low, self.high = pl.ds(0, half), pl.ds(half, blocks.shape[1] - half)

    def copy(self, index):
        far = 3 - self.rank
        block, slot, rows, target = (
            (far, 0, self.low, self.beside),
            (self.beside, 1, self.low, self.beside),
            (far, 0, self.high, self.above),
            (self.above, 1, self.high, self.above),
            (self.above, 2, self.low, self.above),
            (self.beside, 2, self.high, self.beside),
        )[index]
        return send(
            self.blocks.at[block, rows],
            self.landed.at[slot, rows],
            self.send_sems.at[index],
            self.recv_sems.at[index],
            dp=target,
        )

    def start(self):
        if not self.square:
            self.swap.start()
            return
        for index in range(4):
            self.copy(index).start()

    def relay(self):
        if not self.square:
            return
        for index, block, rows in ((0, self.above, self.low), (2, self.beside, self.high)):
            self.copy(index).wait_recv()
            total = self.blocks[block, rows].astype(WIDE) + self.landed[0, rows].astype(WIDE)
            self.blocks[block, rows] = total.astype(self.blocks.dtype)
            self.copy(4 + index // 2).start()

    def total(self):
        total = self.blocks[self.rank].astype(WIDE)
        if not self.square:
            self.swap.wait()
            for off in range(1, self.swap.size):
                total = total + self.landed[lax.rem(self.rank + off, self.swap.size)].astype(WIDE)
            return total
        for index in (1, 3, 4, 5):
            self.copy(index).wait_recv()
        return total + self.landed[1].astype(WIDE) + self.landed[2].astype(WIDE)

    def drain(self):
        if not self.square:
            self.swap.drain()
            return
        for index in range(6):
            self.copy(index).wait_send()

    @staticmethod
    def semaphores(size):
        return Swap.semaphores(max(size, 6))


class LineGather:
    def __init__(self, blocks, send_sems, recv_sems):
        self.blocks, self.send_sems, self.recv_sems = blocks, send_sems, recv_sems
        self.rank = lax.axis_index("ctx")
        self.chip, self.core = self.rank // 2, self.rank % 2
        self.chips = blocks.shape[0] // 2

    def copy(self, way, origin, target, src=None):
        block = self.blocks.at[origin]
        return send(
            block if src is None else src,
            block,
            self.send_sems.at[way, origin],
            self.recv_sems.at[origin],
            ctx=target,
        )

    def pass_on(self, origin, src=None):
        chip = origin // 2

        @pl.when((chip <= self.chip) & (self.chip < self.chips - 1))
        def _():
            self.copy(0, origin, self.rank + 2, src).start()

        @pl.when((chip >= self.chip) & (self.chip > 0))
        def _():
            self.copy(1, origin, self.rank - 2, src).start()

        self.copy(2, origin, self.rank + 1 - 2 * self.core, src).start()

    def arrive(self, step, part):
        side, other = part % 2, part // 2
        origin_chip = self.chip + jnp.where(side == 0, -step, step)
        origin = 2 * origin_chip + jnp.where(other == 0, self.core, 1 - self.core)
        valid = (origin_chip >= 0) & (origin_chip < self.chips) & ((step > 0) | (side == 0))

        @pl.when(valid & (origin != self.rank))
        def _():
            self.copy(0, origin, self.rank).wait_recv()

            @pl.when(other == 0)
            def _():
                self.pass_on(origin)

        return valid, origin

    def finish(self):
        def one(chip, carry):
            origin = 2 * chip + self.core

            @pl.when((chip <= self.chip) & (self.chip < self.chips - 1))
            def _():
                self.copy(0, origin, self.rank).wait_send()

            @pl.when((chip >= self.chip) & (self.chip > 0))
            def _():
                self.copy(1, origin, self.rank).wait_send()

            self.copy(2, origin, self.rank).wait_send()
            return carry

        lax.fori_loop(0, self.chips, one, 0)

    @staticmethod
    def semaphores(ctx):
        return [pltpu.SemaphoreType.DMA((3, ctx)), pltpu.SemaphoreType.DMA((ctx,))]


class LineSum:
    def __init__(self, blocks, pair, passing, sems):
        self.blocks, self.pair, self.passing = blocks, pair, passing
        self.pair_send, self.pair_recv, self.line_send, self.line_recv = sems
        self.rank = lax.axis_index("ctx")
        self.chip, self.core = self.rank // 2, self.rank % 2
        self.chips = blocks.shape[0] // 2
        self.pieces = self.line_recv.shape[2]
        self.piece = blocks.shape[1] // self.pieces

    def pair_copy(self, chip):
        return send(
            self.blocks.at[2 * chip + 1 - self.core],
            self.pair.at[chip],
            self.pair_send.at[chip],
            self.pair_recv.at[chip],
            ctx=self.rank + 1 - 2 * self.core,
        )

    def line_copy(self, way, chip, piece, target):
        rows = pl.ds(piece * self.piece, self.piece)
        return send(
            self.blocks.at[2 * chip + self.core, rows],
            self.passing.at[way, chip, rows],
            self.line_send.at[chip, piece],
            self.line_recv.at[way, chip, piece],
            ctx=target,
        )

    def both(self, chip, rows):
        mine = self.blocks[2 * chip + self.core, rows].astype(WIDE)
        return mine + self.pair[chip, rows].astype(WIDE)

    def forward(self, way, chip, valid):
        behind = jnp.where(way == 0, self.chip > 0, self.chip < self.chips - 1)
        target = self.rank + jnp.where(way == 0, 2, -2)

        @pl.when(valid)
        def _():
            self.pair_copy(chip).wait_recv()

            def one(piece, carry):
                rows = pl.ds(pl.multiple_of(piece * self.piece, self.piece), self.piece)
                total = self.both(chip, rows)

                @pl.when(behind)
                def _():
                    self.line_copy(way, chip, piece, target).wait_recv()
                    passing = self.passing[way, chip, rows].astype(WIDE)
                    self.blocks[2 * chip + self.core, rows] = (total + passing).astype(LOW)

                @pl.when(jnp.logical_not(behind))
                def _():
                    self.blocks[2 * chip + self.core, rows] = total.astype(LOW)

                self.line_copy(way, chip, piece, target).start()
                return carry

            lax.fori_loop(0, self.pieces, one, 0)

    def near_first(self, step, way):
        last = self.chips - 1
        chip = jnp.where(way == 0, step - self.chip, 2 * last - self.chip - step)
        ahead = jnp.where(way == 0, (chip > self.chip) & (chip <= last), (chip >= 0) & (chip < self.chip))
        self.forward(way, chip, ahead)

    def far_first(self, step, way):
        last = self.chips - 1
        chip = jnp.where(way == 0, last + self.chip - step, step - last + self.chip)
        ahead = jnp.where(way == 0, (chip > self.chip) & (chip <= last), (chip >= 0) & (chip < self.chip))
        self.forward(way, chip, ahead)

    def send_pairs(self):
        def one(chip, carry):
            self.pair_copy(chip).start()
            return carry

        lax.fori_loop(0, self.chips, one, 0)

    def far_steps(self, begin, end):
        def one(index, carry):
            self.far_first(index // 2, index % 2)
            return carry

        lax.fori_loop(2 * begin, 2 * end, one, 0)

    def finish(self, out):
        self.pair_copy(self.chip).wait_recv()

        def one(piece, carry):
            rows = pl.ds(pl.multiple_of(piece * self.piece, self.piece), self.piece)
            out[rows] = self.both(self.chip, rows)

            @pl.when(self.chip > 0)
            def _():
                self.line_copy(0, self.chip, piece, self.rank).wait_recv()
                out[rows] = out[rows] + self.passing[0, self.chip, rows].astype(WIDE)

            @pl.when(self.chip < self.chips - 1)
            def _():
                self.line_copy(1, self.chip, piece, self.rank).wait_recv()
                out[rows] = out[rows] + self.passing[1, self.chip, rows].astype(WIDE)

            return carry

        lax.fori_loop(0, self.pieces, one, 0)

        def sent(chip, carry):
            self.pair_copy(chip).wait_send()

            @pl.when(chip != self.chip)
            def _():
                for piece in range(self.pieces):
                    self.line_copy(0, chip, piece, self.rank).wait_send()

            return carry

        lax.fori_loop(0, self.chips, sent, 0)

    @staticmethod
    def scratch(ctx, rows, columns, pieces):
        chips = ctx // 2
        return [
            pltpu.VMEM((ctx, rows, columns), LOW),
            pltpu.VMEM((chips, rows, columns), LOW),
            pltpu.VMEM((2, chips, rows, columns), LOW),
            pltpu.SemaphoreType.DMA((chips,)),
            pltpu.SemaphoreType.DMA((chips,)),
            pltpu.SemaphoreType.DMA((chips, pieces)),
            pltpu.SemaphoreType.DMA((2, chips, pieces)),
        ]


VMEM = pl.BlockSpec(memory_space=pltpu.VMEM)
HBM = pl.BlockSpec(memory_space=pl.ANY)


def params(number):
    return pltpu.CompilerParams(
        vmem_limit_bytes=63 * MIB, collective_id=number, has_side_effects=True
    )


def packed_rows(count, columns):
    tiles = -(-columns // 128)
    main = count // 16 * 16
    return tiles * main + -(-(tiles * (count - main)) // 16) * 16


def pack(out, index, rows, first, count, lane, columns):
    tiles = -(-columns // 128)
    main = count // 16 * 16
    for tile in range(tiles):
        lanes = slice(lane + tile * 128, lane + tile * 128 + 128)
        part = rows[first : first + main, lanes]
        out[index, tile * main : (tile + 1) * main] = part.astype(LOW)
    left = [
        rows[first + row : first + row + 1, lane + tile * 128 : lane + tile * 128 + 128]
        for row in range(main, count)
        for tile in range(tiles)
    ]
    space = out.shape[1] - tiles * main
    if space:
        left.append(jnp.zeros((space - len(left), 128), WIDE))
        out[index, tiles * main :] = jnp.concatenate(left, 0).astype(LOW)


def unpack(packed, rows, first, count, columns):
    tiles = -(-columns // 128)
    main = count // 16 * 16
    for tile in range(tiles):
        lanes = slice(tile * 128, tile * 128 + 128)
        rows[first : first + main, lanes] = packed[tile * main : (tile + 1) * main].astype(WIDE)
    left = packed[tiles * main :].astype(WIDE)
    for row in range(main, count):
        for tile in range(tiles):
            place = (row - main) * tiles + tile
            lanes = slice(tile * 128, tile * 128 + 128)
            rows[first + row : first + row + 1, lanes] = left[place : place + 1]


def full_lanes(columns):
    return -(-columns // 128) * 128


def head_pieces(ctx, slots):
    width = slots * HEAD_DIM
    pieces = []
    for rank in range(ctx):
        count = min(width, D - rank * width)
        if count > 0:
            for part in range(3):
                pieces.append((rank, part * width, part * D + rank * width, count))
    return pieces


def unit_pieces(ctx, dp):
    units = FF // (ctx * dp)
    return [
        (rank, seq * padded_units(units), (seq * ctx + rank) * units, units)
        for rank in range(ctx)
        for seq in range(dp)
    ]


def divide(rows_ref, wide, blocks, pieces, columns):
    count = rows_ref.shape[0]
    lanes = full_lanes(columns)
    for rank in range(blocks.shape[0]):
        wide[...] = jnp.zeros_like(wide)
        for owner, here, there, size in pieces:
            if owner == rank:
                wide[0:count, here : here + size] = rows_ref[:, there : there + size].astype(WIDE)
        pack(blocks, rank, wide, 0, count, 0, lanes)


class Spread:
    def __init__(self, blocks, landed, wide, out, sems):
        self.blocks, self.landed, self.wide, self.out = blocks, landed, wide, out
        self.swap = Swap("ctx", blocks.at.__getitem__, landed.at.__getitem__, sems[:2])
        self.plane = PlaneGather(out, sems[2:])

    def start(self):
        self.swap.start()
        self.landed[self.swap.rank] = self.blocks[self.swap.rank]

    def cross(self):
        self.swap.wait()
        count = self.out.shape[1] // self.swap.size
        columns = self.out.shape[2]
        for index in range(self.swap.size):
            unpack(self.landed[index], self.wide, index * count, count, columns)
        self.out[self.plane.rank] = self.wide[:, 0:columns].astype(LOW)
        self.plane.start()

    def wait(self):
        self.plane.wait()

    @staticmethod
    def scratch(ctx, dp, rows, columns):
        return [
            pltpu.VMEM((ctx, packed_rows(rows // ctx, columns), 128), LOW),
            pltpu.VMEM((rows, full_lanes(columns)), WIDE),
            *Swap.semaphores(ctx),
            *PlaneGather.semaphores(dp),
        ]


class Collect:
    def __init__(self, pieces, parts, landed, wide, blocks, came, one, out, sems):
        self.pieces, self.parts, self.wide, self.blocks = pieces, parts, wide, blocks
        self.came, self.one, self.out = came, one, out
        self.plane = PlaneSum(parts, landed, sems[:2])
        self.swap = Swap("ctx", blocks.at.__getitem__, came.at.__getitem__, sems[2:])

    def cross(self):
        rows, columns = self.parts.shape[1:]
        self.wide[:, 0:columns] = self.plane.total()
        if self.wide.shape[1] > columns:
            more = (rows, self.wide.shape[1] - columns)
            self.wide[:, columns:] = jnp.zeros(more, WIDE)
        count = rows // self.swap.size
        for index in range(self.swap.size):
            pack(self.blocks, index, self.wide, index * count, count, 0, columns)
        self.swap.start()
        self.came[self.swap.rank] = self.blocks[self.swap.rank]

    def wait(self):
        self.swap.wait()
        count = self.out.shape[0]
        for rank in range(self.swap.size):
            unpack(self.came[rank], self.one, 0, count, self.parts.shape[2])
            for owner, here, there, size in self.pieces:
                if owner == rank:
                    self.out[:, there : there + size] = self.one[0:count, here : here + size]
        self.swap.drain()
        self.plane.drain()

    @staticmethod
    def scratch(ctx, dp, rows, columns):
        count = rows // ctx
        packed = packed_rows(count, columns)
        return [
            pltpu.VMEM((dp, rows, columns), LOW),
            pltpu.VMEM((dp, rows, columns), LOW),
            pltpu.VMEM((rows, full_lanes(columns)), WIDE),
            pltpu.VMEM((ctx, packed, 128), LOW),
            pltpu.VMEM((ctx, packed, 128), LOW),
            pltpu.VMEM((-(-count // 8) * 8, full_lanes(columns)), WIDE),
            *PlaneSum.semaphores(dp),
            *Swap.semaphores(ctx),
        ]


class Projection:
    def __init__(self, rows, blocks, wide, out, sems):
        self.rows, self.blocks, self.wide, self.out = rows, blocks, wide, out
        self.rank = lax.axis_index("ctx")
        self.core = self.rank % 2
        self.packed = rows.shape[1]
        self.plane = PlaneGather(blocks.at[self.core], sems[:2])
        self.send_sems, self.recv_sems = sems[2:4]
        self.swap = ChipSwap(lambda peer: rows.at[0], self.place, sems[4:])

    def place(self, chip):
        rows = pl.ds(pl.multiple_of(chip * self.packed, self.packed), self.packed)
        return self.blocks.at[self.core, self.plane.rank, rows]

    def start(self):
        self.swap.start()
        rows = pl.ds(pl.multiple_of(self.swap.rank * self.packed, self.packed), self.packed)
        self.blocks[self.core, self.plane.rank, rows] = self.rows[0]

    def cross(self):
        self.swap.wait()
        self.plane.start()
        self.to_other(self.plane.rank).start()

    def to_other(self, seq):
        block = self.blocks.at[self.core, seq]
        return send(
            block,
            block,
            self.send_sems.at[seq],
            self.recv_sems.at[seq],
            ctx=self.rank + 1 - 2 * self.core,
        )

    def wait(self):
        self.plane.wait()

        def others(off, carry):
            self.to_other(lax.rem(self.plane.rank + off, self.plane.size)).start()
            return carry

        lax.fori_loop(1, self.plane.size, others, 0)
        ctx = 2 * self.swap.size
        count = self.out.shape[1] // ctx

        def order(off, carry):
            seq = lax.rem(self.plane.rank + off, self.plane.size)
            self.to_other(seq).wait_recv()
            for rank in range(ctx):
                first = rank // 2 * self.packed
                rows = self.blocks[rank % 2, seq, first : first + self.packed]
                unpack(rows, self.wide, rank * count, count, D)
            self.out[seq] = self.wide[:, 0:D].astype(LOW)
            return carry

        lax.fori_loop(0, self.plane.size, order, 0)

        def sent(seq, carry):
            self.to_other(seq).wait_send()
            return carry

        lax.fori_loop(0, self.plane.size, sent, 0)
        self.swap.drain()

    @staticmethod
    def scratch(ctx, dp):
        packed = packed_rows(D // (dp * ctx), D)
        return [
            pltpu.VMEM((2, dp, ctx // 2 * packed, 128), LOW),
            pltpu.VMEM((D // dp, full_lanes(D)), WIDE),
            *PlaneGather.semaphores(dp),
            *Swap.semaphores(dp),
            *Swap.semaphores(ctx // 2),
        ]


def vector_pieces(owners, count):
    pieces = []
    for owner in range(owners):
        begin = 0
        while begin < count:
            place = owner * count + begin
            size = min(count - begin, D - place % D)
            pieces.append((owner, begin, place // D, place % D, size))
            begin += size
    return pieces


def unit_bias_pieces(rank, ctx, dp):
    units = FF // (ctx * dp)
    pieces = []
    for seq in range(dp):
        begin = 0
        while begin < units:
            place = (seq * ctx + rank) * units + begin
            size = min(units - begin, D - place % D)
            pieces.append((seq * padded_units(units) + begin, 7 + place // D, place % D, size))
            begin += size
    return pieces


GAIN_ONE, SHIFT_ONE, BIAS_QUERY, BIAS_VALUE, BIAS_PROJ, GAIN_TWO, SHIFT_TWO = range(7)
BIAS_OUT = 11
ROWS = 16


class Names:
    def __init__(self, names, refs):
        self.__dict__.update(zip(names, refs, strict=True))


def forward_kernel(block, names, whole, *refs):
    r = Names(names, refs)
    seq, rank = lax.axis_index("dp"), lax.axis_index("ctx")
    ctx, tokens, _ = r.rows.shape
    dp, units = r.units.shape[:2]
    width = r.mixed.shape[1]
    vec_count = 12 * D // (ctx * dp)

    def out(ref, target, index):
        return pltpu.make_async_copy(ref, target, r.out_sems.at[index])

    rows_in = LineGather(r.rows, r.rows_send, r.rows_recv)
    cots = LineGather(r.cots, r.cots_send, r.cots_recv)
    feed = LineGather(r.rows, r.feed_send, r.feed_recv)
    total = LineSum(
        r.sum_blocks,
        r.sum_pair,
        r.sum_passing,
        (r.sum_pair_send, r.sum_pair_recv, r.sum_line_send, r.sum_line_recv),
    )
    chips = feed.chips
    line = Swap(
        "ctx",
        lambda peer: r.small,
        lambda origin: r.smalls.at[seq, origin],
        (r.line_send, r.line_recv),
    )
    plane = Swap(
        "dp",
        lambda peer: r.smalls.at[seq],
        r.smalls.at.__getitem__,
        (r.plane_send, r.plane_recv),
    )
    unit_rows = PlaneGather(r.units, (r.units_send, r.units_recv))
    to_tokens = Swap(
        "ctx",
        lambda peer: r.mixed.at[pl.ds(pl.multiple_of(peer * tokens, tokens), tokens)],
        lambda origin: r.own_mixed.at[:, pl.ds(pl.multiple_of(origin * width, width), width)],
        (r.mixed_send, r.mixed_recv),
    )
    if whole:
        heads = Spread(
            r.qkv_blocks,
            r.qkv_landed,
            r.qkv_wide,
            r.qkv_mat,
            (r.qkv_send, r.qkv_recv, r.qkv_plane_send, r.qkv_plane_recv),
        )
        columns = Spread(
            r.fc_blocks,
            r.fc_landed,
            r.fc_wide,
            r.fc_mat,
            (r.fc_send, r.fc_recv, r.fc_plane_send, r.fc_plane_recv),
        )
        proj = Projection(
            r.proj_packed,
            r.proj_blocks,
            r.proj_wide,
            r.proj_mat,
            (
                r.proj_plane_send,
                r.proj_plane_recv,
                r.proj_pair_send,
                r.proj_pair_recv,
                r.proj_send,
                r.proj_recv,
            ),
        )
        divide(r.qkv_rows, r.qkv_lanes, r.qkv_blocks, head_pieces(ctx, width // HEAD_DIM), 3 * width)
    r.rows[rank] = r.own_in[...]
    r.cots[rank] = r.own_cot[...]
    r.units[seq] = r.own_units[...]
    r.smalls[seq, rank] = r.small[...]
    greet_all()

    line.start()
    if whole:
        heads.start()
    unit_rows.start()
    if whole:
        count = r.proj_rows.shape[0]
        r.proj_lanes[0:count, 0:D] = r.proj_rows[...].astype(WIDE)
        r.proj_lanes[0:count, D:] = jnp.zeros((count, full_lanes(D) - D), WIDE)
        pack(r.proj_packed, 0, r.proj_lanes, 0, count, 0, D)
        heads.swap.drain()
        proj.start()
    rows_in.pass_on(rank)
    line.wait()
    plane.start()
    if whole:
        heads.cross()
        divide(r.fc_rows, r.fc_lanes, r.fc_blocks, unit_pieces(ctx, dp), dp * units)

    def arrivals(gather):
        def arrive(index, carry):
            gather.arrive(1 + index // 4, index % 4)
            return carry

        return arrive

    rows_in.arrive(0, 2)
    lax.fori_loop(0, 4, arrivals(rows_in), 0)
    unit_rows.relay()
    if whole:
        proj.cross()
    lax.fori_loop(4, 8, arrivals(rows_in), 0)
    if whole:
        heads.plane.relay()
        columns.start()
    lax.fori_loop(8, 4 * (chips - 1), arrivals(rows_in), 0)
    rows_in.finish()
    plane.wait()
    r.vectors[...] = jnp.zeros_like(r.vectors)
    for owner, begin, row, lane, size in vector_pieces(ctx * dp, vec_count):
        r.vectors[row : row + 1, lane : lane + size] = r.smalls[
            owner // ctx, owner % ctx, 0:1, begin : begin + size
        ]
    r.bias_units[...] = jnp.zeros_like(r.bias_units)
    for owner in range(ctx):

        @pl.when(rank == owner)
        def _(owner=owner):
            for here, row, lane, size in unit_bias_pieces(owner, ctx, dp):
                r.bias_units[0:1, here : here + size] = r.vectors[row : row + 1, lane : lane + size]

    if whole:
        heads.wait()
        out(r.qkv_mat, r.qkv_mat_out, 0).start()
    mine = pl.ds(pl.multiple_of(rank * width, width), width)
    bias = jnp.concatenate(
        [
            r.vectors[BIAS_QUERY : BIAS_QUERY + 1, mine],
            jnp.zeros((1, width), WIDE),
            r.vectors[BIAS_VALUE : BIAS_VALUE + 1, mine],
        ],
        1,
    )

    def project(index, carry):
        both = pl.ds(2 * index, 2)
        normed, _ = normalize(r.rows[both].reshape(2 * tokens, D).astype(WIDE))
        attn_in = normed * r.vectors[GAIN_ONE : GAIN_ONE + 1, 0:D]
        attn_in = (attn_in + r.vectors[SHIFT_ONE : SHIFT_ONE + 1, 0:D]).astype(LOW)
        r.rows[both] = attn_in.reshape(2, tokens, D)
        rows = pl.ds(pl.multiple_of(2 * index * tokens, 2 * tokens), 2 * tokens)
        r.qkv[rows] = (dot(attn_in, r.qkv_mat[...].reshape(D, 3 * width)) + bias).astype(LOW)
        return carry

    lax.fori_loop(0, chips, project, 0)
    out(r.rows, r.attn_in_out, 1).start()
    out(r.qkv, r.qkv_out, 2).start()
    if whole:
        proj.plane.relay()
        columns.cross()
    cots.pass_on(rank)
    attend_body(block, r.qkv, r.doc_start, r.mixed, r.stats, r.value_t)
    out(r.rows, r.attn_in_out, 1).wait()
    to_tokens.start()
    r.own_mixed[:, mine] = r.mixed[pl.ds(pl.multiple_of(rank * tokens, tokens), tokens)]
    if whole:
        proj.wait()
        out(r.proj_mat, r.proj_mat_out, 3).start()
        columns.plane.relay()
    cots.arrive(0, 2)
    lax.fori_loop(0, 4, arrivals(cots), 0)
    to_tokens.wait()
    resid = dot(r.own_mixed[:, 0:D], r.proj_mat[...].reshape(D, D))
    resid = resid + r.own_in[...].astype(WIDE) + r.vectors[BIAS_PROJ : BIAS_PROJ + 1, 0:D]
    r.resid[...] = resid
    normed, _ = normalize(resid)
    ffn_in = normed * r.vectors[GAIN_TWO : GAIN_TWO + 1, 0:D]
    r.rows[rank] = (ffn_in + r.vectors[SHIFT_TWO : SHIFT_TWO + 1, 0:D]).astype(LOW)
    feed.pass_on(rank)
    unit_rows.wait()
    if whole:
        columns.wait()

    def keep(chip, slot):
        both = pl.ds(2 * chip, 2)
        return [
            pltpu.make_async_copy(ref.at[slot], target.at[both], r.keep_sems.at[index, slot])
            for index, (ref, target) in enumerate(
                ((r.act, r.act_out), (r.pre, r.pre_out), (r.part, r.part_out))
            )
        ]

    def pass_rows(chip):
        both = pl.ds(2 * chip, 2)
        return [
            pltpu.make_async_copy(ref.at[both], target.at[both], r.pass_sems.at[index, chip])
            for index, (ref, target) in enumerate(((r.rows, r.ffn_out), (r.cots, r.cots_out)))
        ]

    def work(chip, done):
        both = pl.ds(2 * chip, 2)
        slot = done % 2

        @pl.when(done >= 2)
        def _():
            for copy in keep(chip, slot):
                copy.wait()

        for copy in pass_rows(chip):
            copy.start()
        fc = r.fc_mat[...].reshape(D, dp * units)
        mat = r.units[...].reshape(dp * units, D)
        pre = dot(r.rows[both].reshape(2 * tokens, D), fc) + r.bias_units[0:1]
        bend = jnp.tanh(0.7978845608028654 * (pre + 0.044715 * pre * pre * pre))
        act = (0.5 * pre * (1.0 + bend)).astype(LOW)
        r.act[slot] = act.reshape(2, tokens, -1)
        slope = 0.5 * (1.0 + bend) + 0.5 * pre * (1.0 - bend * bend) * 0.7978845608028654 * (
            1.0 + 3 * 0.044715 * pre * pre
        )
        grad_act = dot(r.cots[both].reshape(2 * tokens, D), mat, 1, 1)
        grad_pre = (slope * grad_act).astype(LOW)
        r.pre[slot] = grad_pre.reshape(2, tokens, -1)
        r.sum_blocks[both] = dot(grad_pre, fc, 1, 1).astype(LOW).reshape(2, tokens, D)
        total.pair_copy(chip).start()
        r.part[slot] = dot(act, mat).astype(LOW).reshape(2, tokens, D)
        for copy in keep(chip, slot):
            copy.start()

    def step(index, done):
        distance, side = index // 2, index % 2
        near = distance < chips
        origin_chip = rank // 2 + jnp.where(side == 0, -distance, distance)
        valid = near & (origin_chip >= 0) & (origin_chip < chips) & ((distance > 0) | (side == 0))

        @pl.when(near)
        def _():
            @pl.when(side == 0)
            def _():
                @pl.when(distance > 1)
                def _():
                    cots.arrive(distance, 0)
                    cots.arrive(distance, 1)

                feed.arrive(distance, 0)
                feed.arrive(distance, 1)

            @pl.when(distance > 1)
            def _():
                cots.arrive(distance, 2 + side)

            feed.arrive(distance, 2 + side)

            @pl.when(valid)
            def _():
                work(origin_chip, done)

        @pl.when(side == 1)
        def _():
            def way(index, carry):
                total.near_first(distance, index)
                return carry

            lax.fori_loop(0, 2, way, 0)

        return done + valid.astype(jnp.int32)

    lax.fori_loop(0, 2 * (2 * chips - 1), step, jnp.int32(0))
    total.finish(r.grad)

    feed.finish()
    cots.finish()
    line.drain()
    plane.drain()
    to_tokens.drain()
    for slot in range(2):
        for copy in keep(0, slot):
            copy.wait()

    def passed(chip, carry):
        for copy in pass_rows(chip):
            copy.wait()
        return carry

    lax.fori_loop(0, chips, passed, 0)
    out(r.qkv, r.qkv_out, 2).wait()
    if whole:
        out(r.qkv_mat, r.qkv_mat_out, 0).wait()
        out(r.proj_mat, r.proj_mat_out, 3).wait()
        columns.swap.drain()


def forward(small, own_in, own_cot, unit_rows, doc_start, mats, slots, whole, block):
    ctx, dp = lax.axis_size("ctx"), lax.axis_size("dp")
    tokens = own_in.shape[0]
    length = ctx * tokens
    width = slots * HEAD_DIM
    units = unit_rows.shape[0]
    columns = dp * units
    chips = ctx // 2
    count = D // (dp * ctx)
    high = -(-count // 8) * 8
    names, given, in_specs = [], [], []
    shapes, out_specs, scratch = [], [], []
    in_names, out_names, scratch_names = [], [], []

    def take(name, value):
        in_names.append(name)
        given.append(value)

    def give(name, shape, kind=LOW, spec=HBM):
        out_names.append(name)
        shapes.append(jax.ShapeDtypeStruct(shape, kind))
        out_specs.append(spec)

    def hold(name, *what):
        scratch_names.append(name)
        scratch.append(pltpu.VMEM(what[0], what[1] if len(what) > 1 else LOW))

    def sems(*pairs):
        for name, shape in pairs:
            scratch_names.append(name)
            scratch.append(pltpu.SemaphoreType.DMA(shape))

    def both(name, size):
        sems((name + "_send", (size,)), (name + "_recv", (size,)))

    take("small", small)
    take("own_in", own_in)
    take("own_cot", own_cot)
    take("own_units", unit_rows)
    take("doc_start", doc_start)
    for name, value in zip(
        ("qkv_rows", "fc_rows", "proj_rows") if whole else ("qkv_mat", "fc_mat", "proj_mat"),
        mats,
        strict=True,
    ):
        take(name, value)
    give("vectors", (ROWS, max(full_lanes(D), ctx * width)), WIDE, VMEM)
    give("attn_in_out", (ctx, tokens, D))
    give("qkv_out", (length, 3 * width))
    give("stats", (8, length), WIDE, VMEM)
    give("own_mixed", (tokens, ctx * width), LOW, VMEM)
    give("cots_out", (ctx, tokens, D))
    give("resid", (tokens, D), WIDE, VMEM)
    give("grad", (tokens, D), WIDE, VMEM)
    give("ffn_out", (ctx, tokens, D))
    give("act_out", (ctx, tokens, columns))
    give("pre_out", (ctx, tokens, columns))
    give("part_out", (ctx, tokens, D))
    if whole:
        give("qkv_mat_out", (dp, D // dp, 3 * width))
        give("proj_mat_out", (dp, D // dp, D))
    hold("rows", (ctx, tokens, D))
    hold("cots", (ctx, tokens, D))
    hold("units", (dp, units, D))
    hold("smalls", (dp, ctx, *small.shape), WIDE)
    hold("bias_units", (8, columns), WIDE)
    hold("qkv", (length, 3 * width))
    hold("mixed", (length, width))
    hold("value_t", (width, length))
    hold("act", (2, 2, tokens, columns))
    hold("pre", (2, 2, tokens, columns))
    hold("part", (2, 2, tokens, D))
    hold("sum_blocks", (ctx, tokens, D))
    hold("sum_pair", (chips, tokens, D))
    hold("sum_passing", (2, chips, tokens, D))
    sems(
        ("sum_pair_send", (chips,)),
        ("sum_pair_recv", (chips,)),
        ("sum_line_send", (chips, 4)),
        ("sum_line_recv", (2, chips, 4)),
        ("out_sems", (4,)),
        ("keep_sems", (3, 2)),
        ("pass_sems", (2, chips)),
    )
    for name in ("rows", "cots", "feed"):
        sems((name + "_send", (3, ctx)), (name + "_recv", (ctx,)))
    both("line", ctx)
    both("plane", dp)
    both("units", max(dp, 4))
    both("mixed", ctx)
    if whole:
        for name, lanes in (("qkv", 3 * width), ("fc", columns)):
            packed = (ctx, packed_rows(count, lanes), 128)
            hold(name + "_lanes", (high, full_lanes(lanes)), WIDE)
            hold(name + "_blocks", packed)
            hold(name + "_landed", packed)
            hold(name + "_wide", (D // dp, full_lanes(lanes)), WIDE)
            hold(name + "_mat", (dp, D // dp, lanes))
            both(name, ctx)
            both(name + "_plane", max(dp, 4))
        packed = packed_rows(count, D)
        hold("proj_lanes", (high, full_lanes(D)), WIDE)
        hold("proj_packed", (1, packed, 128))
        hold("proj_blocks", (2, dp, chips * packed, 128))
        hold("proj_wide", (D // dp, full_lanes(D)), WIDE)
        hold("proj_mat", (dp, D // dp, D))
        both("proj_plane", max(dp, 4))
        both("proj_pair", dp)
        both("proj", chips)
    names = tuple(in_names + out_names + scratch_names)
    results = pl.pallas_call(
        functools.partial(forward_kernel, block, names, whole),
        out_shape=shapes,
        in_specs=[VMEM] * len(given),
        out_specs=out_specs,
        scratch_shapes=scratch,
        compiler_params=params(0),
        name="forward",
    )(*given)
    return Names(tuple(out_names), results)


def back_kernel(
    block,
    whole,
    grad_ref,
    resid_ref,
    own_cot,
    vectors_ref,
    proj_ref,
    qkv_ref,
    start_ref,
    stat_ref,
    ffn_hbm,
    pre_hbm,
    act_hbm,
    cot_hbm,
    part_hbm,
    resid_out,
    low_out,
    vector_out,
    units_out,
    rows_out,
    share_out,
    output_ref,
    fc_out,
    ffn,
    pre,
    act,
    cot,
    load_sems,
    own_grad,
    head_grad,
    key_t,
    key_grad,
    value_grad,
    *refs,
):
    total = LineSum(*refs[:3], refs[3:7])
    loads = [
        pltpu.make_async_copy(src, dst, load_sems.at[index])
        for index, (src, dst) in enumerate(
            (
                (part_hbm, total.blocks),
                (ffn_hbm, ffn),
                (pre_hbm, pre),
                (act_hbm, act),
                (cot_hbm, cot),
            )
        )
    ]
    for load in loads:
        load.start()
    tokens = own_cot.shape[0]
    length, width = head_grad.shape
    units = share_out.shape[0]
    swap = Swap(
        "ctx",
        lambda peer: own_grad.at[:, pl.ds(pl.multiple_of(peer * width, width), width)],
        lambda origin: head_grad.at[pl.ds(pl.multiple_of(origin * tokens, tokens), tokens)],
        refs[7:9],
    )
    share = PlaneSum(refs[9], refs[10], refs[11:13])
    if whole:
        pieces = unit_pieces(2 * total.chips, refs[9].shape[0])
        collect = Collect(pieces, *refs[13:19], fc_out, refs[19:])
    dp = share.swap.size
    greet_all()
    loads[0].wait()
    total.send_pairs()
    grad = grad_ref[...]
    normed, scale = normalize(resid_ref[...])
    grad_resid = own_cot[...].astype(WIDE) + norm_back(normed, scale, vectors_ref[GAIN_TWO : GAIN_TWO + 1, 0:D], grad)
    resid_out[...] = grad_resid
    low = grad_resid.astype(LOW)
    low_out[...] = low
    own_grad[:, 0:D] = dot(low, proj_ref[...], 1, 1).astype(LOW)
    own_grad[:, D:] = jnp.zeros((tokens, own_grad.shape[1] - D), LOW)
    swap.start()
    head_grad[pl.ds(pl.multiple_of(swap.rank * tokens, tokens), tokens)] = own_grad[
        :, pl.ds(pl.multiple_of(swap.rank * width, width), width)
    ]
    vector_out[0:1] = jnp.sum(grad_resid, 0, keepdims=True)
    vector_out[1:2] = jnp.sum(grad * normed, 0, keepdims=True)
    vector_out[2:3] = jnp.sum(grad, 0, keepdims=True)
    vector_out[3:4] = jnp.sum(own_cot[...].astype(WIDE), 0, keepdims=True)
    vector_out[4:8] = jnp.zeros((4, D), WIDE)
    loads[1].wait()
    loads[2].wait()
    grad_pre = pre[...].reshape(length, -1)
    units_out[...] = dot(jnp.ones((8, length), LOW), grad_pre)
    for index in range(dp):
        rows = slice(index * (D // dp), (index + 1) * (D // dp))
        part = dot(ffn[:, :, rows].reshape(length, D // dp), grad_pre, 0, 0)
        if whole:
            collect.parts[index] = part.astype(LOW)
        else:
            fc_out[rows] = part
    if whole:
        collect.plane.start()
    total.far_steps(0, 1)
    loads[3].wait()
    loads[4].wait()
    for index in range(dp):
        rows = slice(index * units, (index + 1) * units)
        part = dot(act[:, :, rows].reshape(length, units), cot[...].reshape(length, D), 0, 0)
        share.blocks[index] = part.astype(LOW)
    share.start()
    swap.wait()
    chips = total.chips

    def first():
        total.far_steps(1, 2)
        if whole:
            collect.plane.relay()

    def second():
        total.far_steps(2, 3)
        share.relay()

    attend_back_body(
        block,
        qkv_ref,
        start_ref,
        stat_ref,
        head_grad,
        rows_out,
        key_t,
        key_grad,
        value_grad,
        {1: first, 2: second},
    )
    if whole:
        collect.cross()
    total.far_steps(3, 2 * chips - 1)
    total.finish(output_ref)
    bias = vectors_ref[BIAS_OUT : BIAS_OUT + 1, 0:D]
    output_ref[...] = output_ref[...] + resid_ref[...] + bias
    share_out[...] = share.total()
    swap.drain()
    share.drain()
    if whole:
        collect.wait()


def back(
    grad, resid, own_cot, vectors, proj, qkv, doc_start, stats, ffn, pre, act, cot, part, block, whole
):
    ctx, tokens, _ = cot.shape
    dp = lax.axis_size("dp")
    length = ctx * tokens
    width = qkv.shape[1] // 3
    columns = act.shape[2]
    units = columns // dp
    rows = D // dp
    shapes = [
        jax.ShapeDtypeStruct((tokens, D), WIDE),
        jax.ShapeDtypeStruct((tokens, D), LOW),
        jax.ShapeDtypeStruct((8, D), WIDE),
        jax.ShapeDtypeStruct((8, columns), WIDE),
        jax.ShapeDtypeStruct((length, 3 * width), LOW),
        jax.ShapeDtypeStruct((units, D), WIDE),
        jax.ShapeDtypeStruct((tokens, D), WIDE),
        jax.ShapeDtypeStruct((rows // ctx, FF) if whole else (D, columns), WIDE),
    ]
    scratch = [
        pltpu.VMEM(ffn.shape, LOW),
        pltpu.VMEM(pre.shape, LOW),
        pltpu.VMEM(act.shape, LOW),
        pltpu.VMEM(cot.shape, LOW),
        pltpu.SemaphoreType.DMA((5,)),
        pltpu.VMEM((tokens, ctx * width), LOW),
        pltpu.VMEM((length, width), LOW),
        pltpu.VMEM((width, length), LOW),
        pltpu.VMEM((length, width), WIDE),
        pltpu.VMEM((length, width), WIDE),
        *LineSum.scratch(ctx, tokens, D, 4),
        *Swap.semaphores(ctx),
        pltpu.VMEM((dp, units, D), LOW),
        pltpu.VMEM((dp, units, D), LOW),
        *PlaneSum.semaphores(dp),
    ]
    if whole:
        scratch += Collect.scratch(ctx, dp, rows, columns)
    return pl.pallas_call(
        functools.partial(back_kernel, block, whole),
        out_shape=shapes,
        in_specs=[VMEM] * 8 + [HBM] * 5,
        out_specs=[VMEM] * 8,
        scratch_shapes=scratch,
        compiler_params=params(3),
        name="back",
    )(grad, resid, own_cot, vectors, proj, qkv, doc_start, stats, ffn, pre, act, cot, part)


class ProjectionSum:
    def __init__(self, out, refs):
        self.out = out
        self.mixed, self.low, self.parts, landed, self.wide, self.blocks, self.came = refs[:7]
        self.send_sems, self.recv_sems = refs[7:9]
        self.plane = PlaneSum(self.parts, landed, refs[9:11])
        self.rank = lax.axis_index("ctx")
        self.core = self.rank % 2
        self.swap = ChipSwap(self.blocks.at.__getitem__, self.came.at.__getitem__, refs[11:13])

    def pair_copies(self):
        return [
            send(
                ref.at[self.core],
                ref.at[self.core],
                self.send_sems.at[index],
                self.recv_sems.at[index],
                ctx=self.rank + 1 - 2 * self.core,
            )
            for index, ref in enumerate((self.mixed, self.low))
        ]

    def start(self, mixed, low):
        self.mixed[self.core] = mixed
        self.low[self.core] = low
        for copy in self.pair_copies():
            copy.start()

    def multiply(self):
        for copy in self.pair_copies():
            copy.wait_recv()
        dp, rows = self.parts.shape[:2]
        chips = self.swap.size
        tokens = 2 * self.low.shape[1]
        count = self.out.shape[0]
        mixed = self.mixed[...].reshape(tokens, -1)[:, 0:D]
        low = self.low[...].reshape(tokens, D)
        feature = lax.broadcasted_iota(jnp.int32, (D, rows), 0)
        column = lax.broadcasted_iota(jnp.int32, (1, rows), 1)
        for index in range(dp):
            owner = index * 2 * chips + column // count * 2 + self.core
            wanted = jnp.where(column < chips * count, owner * count + column % count, -1)
            chosen = jnp.where(feature == wanted, 1.0, 0.0).astype(LOW)
            picked = dot(mixed, chosen).astype(LOW)
            self.parts[index] = dot(picked, low, 0, 0).astype(LOW)
        self.plane.start()

    def cross(self):
        count = self.out.shape[0]
        self.wide[:, 0:D] = self.plane.total()
        self.wide[:, D:] = jnp.zeros((self.wide.shape[0], self.wide.shape[1] - D), WIDE)
        for chip in range(self.swap.size):
            pack(self.blocks, chip, self.wide, chip * count, count, 0, D)
        self.swap.start()

    def wait(self):
        self.swap.wait()
        total = self.blocks[self.swap.rank].astype(WIDE)
        for off in range(1, self.swap.size):
            total = total + self.came[lax.rem(self.swap.rank + off, self.swap.size)].astype(WIDE)
        count = self.out.shape[0]
        unpack(total, self.wide, 0, count, D)
        self.out[...] = self.wide[0:count, 0:D]
        for copy in self.pair_copies():
            copy.wait_send()
        self.plane.drain()
        self.swap.drain()

    @staticmethod
    def scratch(ctx, dp, tokens, width):
        chips = ctx // 2
        count = D // (dp * ctx)
        rows = -(-(chips * count) // 16) * 16
        packed = packed_rows(count, D)
        return [
            pltpu.VMEM((2, tokens, ctx * width), LOW),
            pltpu.VMEM((2, tokens, D), LOW),
            pltpu.VMEM((dp, rows, D), LOW),
            pltpu.VMEM((dp, rows, D), LOW),
            pltpu.VMEM((rows, full_lanes(D)), WIDE),
            pltpu.VMEM((chips, packed, 128), LOW),
            pltpu.VMEM((chips, packed, 128), LOW),
            *Swap.semaphores(2),
            *PlaneSum.semaphores(dp),
            *Swap.semaphores(chips),
        ]


def last_kernel(
    whole,
    slots,
    rows_ref,
    mat_ref,
    in_ref,
    own_ref,
    resid_ref,
    vectors_ref,
    mixed_ref,
    low_ref,
    grad_out,
    vector_out,
    heads_out,
    mat_out,
    *refs,
):
    if whole:
        proj_out, *refs = refs
    grad, *refs = refs
    total = LineSum(*refs[:3], refs[3:7])
    if whole:
        collect = Collect(
            head_pieces(2 * total.chips, slots), *refs[7:13], mat_out, refs[13:17]
        )
        proj = ProjectionSum(proj_out, refs[17:])
    chips = total.chips
    tokens = own_ref.shape[0]
    dp = lax.axis_size("dp")
    if whole:
        greet_all()
        proj.start(mixed_ref[...], low_ref[...])
    else:
        greet_line(chips)

    def partial_sum(index, carry):
        off = jnp.where(index % 2 == 0, -(index // 2), index // 2 + 1)
        chip = lax.rem(chips - 1 + off, chips)
        rows = pl.ds(pl.multiple_of(2 * chip * tokens, 2 * tokens), 2 * tokens)
        part = dot(rows_ref[rows], mat_ref[...], 1, 1).astype(LOW)
        total.blocks[pl.ds(2 * chip, 2)] = part.reshape(2, tokens, D)
        total.pair_copy(chip).start()
        return carry

    lax.fori_loop(0, chips, partial_sum, 0)
    total.far_steps(0, 1)
    for index in range(dp):
        rows = slice(index * (D // dp), (index + 1) * (D // dp))
        part = dot(in_ref[:, rows], rows_ref[...], 0, 0)
        if whole:
            collect.parts[index] = part.astype(LOW)
        else:
            mat_out[rows] = part
    if whole:
        collect.plane.start()
    total.far_steps(1, 2)
    if whole:
        proj.multiply()
    total.far_steps(2, 3)
    heads_out[...] = dot(jnp.ones((8, rows_ref.shape[0]), LOW), rows_ref[...])
    if whole:
        collect.plane.relay()
    total.far_steps(3, 4)
    if whole:
        proj.plane.relay()
        collect.cross()
    total.far_steps(4, 2 * chips - 1)
    total.finish(grad)
    if whole:
        proj.cross()
    normed, scale = normalize(own_ref[...].astype(WIDE))
    incoming = grad[...]
    gain = vectors_ref[GAIN_ONE : GAIN_ONE + 1, 0:D]
    grad_out[...] = resid_ref[...] + norm_back(normed, scale, gain, incoming)
    vector_out[0:1] = jnp.sum(incoming * normed, 0, keepdims=True)
    vector_out[1:2] = jnp.sum(incoming, 0, keepdims=True)
    vector_out[2:8] = jnp.zeros((6, D), WIDE)
    if whole:
        collect.wait()
        proj.wait()


def last(rows, mat, attn_in, own_in, resid, vectors, mixed, low, whole):
    ctx, dp = lax.axis_size("ctx"), lax.axis_size("dp")
    tokens = own_in.shape[0]
    columns = rows.shape[1]
    shapes = [
        jax.ShapeDtypeStruct((tokens, D), WIDE),
        jax.ShapeDtypeStruct((8, D), WIDE),
        jax.ShapeDtypeStruct((8, columns), WIDE),
        jax.ShapeDtypeStruct((D // (ctx * dp), 3 * D) if whole else (D, columns), WIDE),
    ]
    scratch = [pltpu.VMEM((tokens, D), WIDE), *LineSum.scratch(ctx, tokens, D, 4)]
    if whole:
        shapes.append(jax.ShapeDtypeStruct((D // (ctx * dp), D), WIDE))
        scratch += Collect.scratch(ctx, dp, D // dp, columns)
        scratch += ProjectionSum.scratch(ctx, dp, tokens, columns // 3)
    return pl.pallas_call(
        functools.partial(last_kernel, whole, columns // (3 * HEAD_DIM)),
        out_shape=shapes,
        in_specs=[VMEM] * 8,
        out_specs=[VMEM] * len(shapes),
        scratch_shapes=scratch,
        compiler_params=params(4),
        name="last",
    )(rows, mat, attn_in, own_in, resid, vectors, mixed, low)


def vector_kernel(parts_ref, out_ref, plane_landed, line_parts, line_landed, *sems):
    seq = lax.axis_index("dp")
    swap = Swap("dp", parts_ref.at.__getitem__, plane_landed.at.__getitem__, sems[:2])
    line = Swap("ctx", line_parts.at.__getitem__, line_landed.at.__getitem__, sems[2:])
    greet_all()
    swap.start()
    swap.wait()
    total = parts_ref[seq]
    for off in range(1, swap.size):
        total = total + plane_landed[lax.rem(seq + off, swap.size)]
    line_parts[...] = total
    line.start()
    line.wait()
    total = line_parts[line.rank]
    for off in range(1, line.size):
        total = total + line_landed[lax.rem(line.rank + off, line.size)]
    out_ref[...] = total
    swap.drain()
    line.drain()


def sum_vector(parts):
    dp, ctx = parts.shape[:2]
    return pl.pallas_call(
        vector_kernel,
        out_shape=jax.ShapeDtypeStruct(parts.shape[2:], WIDE),
        in_specs=[VMEM],
        out_specs=VMEM,
        scratch_shapes=[
            pltpu.VMEM(parts.shape, WIDE),
            pltpu.VMEM(parts.shape[1:], WIDE),
            pltpu.VMEM(parts.shape[1:], WIDE),
            *PlaneSum.semaphores(dp),
            *Swap.semaphores(ctx),
        ],
        compiler_params=params(5),
        name="sum_vector",
    )(parts)


def gather_rows(block):
    return lax.all_gather(block, ("dp", "ctx"), axis=0, tiled=True)


def by_rank_heads(rows, ctx, slots):
    count = rows.shape[0]
    split = rows.reshape(count, 3, D)
    split = jnp.pad(split, ((0, 0), (0, 0), (0, (ctx * slots - HEADS) * HEAD_DIM)))
    split = split.reshape(count, 3, ctx, slots * HEAD_DIM)
    return split.transpose(2, 0, 1, 3).reshape(ctx, count, 3 * slots * HEAD_DIM)


def from_rank_heads(blocks, slots):
    ctx, count = blocks.shape[:2]
    split = blocks.reshape(ctx, count, 3, slots * HEAD_DIM).transpose(1, 2, 0, 3)
    return split.reshape(count, 3, ctx * slots * HEAD_DIM)[:, :, :D].reshape(count, 3 * D)


def padded_units(units):
    return -(-units // 16) * 16


def by_rank_units(rows, ctx, dp):
    count = rows.shape[0]
    units = FF // (dp * ctx)
    split = rows.reshape(count, dp, ctx, units).transpose(2, 0, 1, 3)
    split = jnp.pad(split, ((0, 0), (0, 0), (0, 0), (0, padded_units(units) - units)))
    return split.reshape(ctx, count, dp * padded_units(units))


def from_rank_units(blocks, dp):
    ctx, count = blocks.shape[:2]
    units = FF // (dp * ctx)
    split = blocks.reshape(ctx, count, dp, padded_units(units))[..., :units]
    return split.transpose(1, 2, 0, 3).reshape(count, FF)


def shards(
    hidden_in, qkv_weight, proj_weight, fc_weight, out_weight, small_params, segments, cotangent
):
    tokens = hidden_in.shape[1]
    length = segments.shape[1]
    ctx = lax.axis_size("ctx")
    dp = lax.axis_size("dp")
    owners = dp * ctx
    rank = lax.axis_index("ctx")
    slots = -(-HEADS // ctx)
    width = slots * HEAD_DIM
    units = FF // owners
    rows = D // owners
    whole = D % owners == 0
    block = min(256, length)
    both = ("dp", "ctx")

    vec_count = small_params.shape[0]
    small = jnp.pad(small_params.astype(WIDE), (0, full_lanes(vec_count) - vec_count))[None]
    unit_rows = jnp.pad(out_weight.reshape(units, D), ((0, padded_units(units) - units), (0, 0)))
    docs = segments[0]
    doc_start = jnp.sum((docs[:, None] < docs[None, :]).astype(jnp.int32), 0)[None]
    if whole:
        mats = (
            qkv_weight.reshape(rows, 3 * D),
            fc_weight.reshape(rows, FF),
            proj_weight.reshape(rows, D),
        )
    else:
        mat_qkv = by_rank_heads(gather_rows(qkv_weight).reshape(D, 3 * D), ctx, slots)
        mat_qkv = lax.dynamic_index_in_dim(mat_qkv, rank, 0, keepdims=False)
        mat_fc = by_rank_units(gather_rows(fc_weight).reshape(D, FF), ctx, dp)
        mat_fc = lax.dynamic_index_in_dim(mat_fc, rank, 0, keepdims=False)
        mat_proj = gather_rows(proj_weight).reshape(D, D)
        mats = (mat_qkv, mat_fc, mat_proj)
    made = forward(
        small, hidden_in[0], cotangent[0], unit_rows, doc_start, mats, slots, whole, block
    )
    if whole:
        mat_qkv = made.qkv_mat_out.reshape(D, 3 * width)
        mat_proj = made.proj_mat_out.reshape(D, D)
    vectors = made.vectors

    grad_resid, resid_low, sums_two, sums_units, grad_rows, grad_out, output, grad_fc = back(
        made.grad,
        made.resid,
        cotangent[0],
        vectors,
        mat_proj,
        made.qkv_out,
        doc_start,
        made.stats,
        made.ffn_out,
        made.pre_out,
        made.act_out,
        made.cots_out,
        made.part_out,
        block,
        whole,
    )
    grad_input, sums_one, sums_heads, grad_qkv, *rest = last(
        grad_rows,
        mat_qkv,
        made.attn_in_out.reshape(length, D),
        hidden_in[0],
        grad_resid,
        vectors,
        made.own_mixed,
        resid_low,
        whole,
    )
    if whole:
        share_fc, share_qkv, share_proj = grad_fc, grad_qkv, rest[0]
    else:
        grad_proj = dot(made.own_mixed[:, :D], resid_low, 0, 0).reshape(-1)
        share_proj = lax.psum_scatter(grad_proj, both, scatter_dimension=0, tiled=True)
        here = (jnp.arange(ctx) == rank)[:, None, None]
        full_fc = from_rank_units(jnp.where(here, grad_fc[None], 0.0), dp).reshape(-1)
        full_qkv = from_rank_heads(jnp.where(here, grad_qkv[None], 0.0), slots).reshape(-1)
        share_fc = lax.psum_scatter(full_fc, both, scatter_dimension=0, tiled=True)
        share_qkv = lax.psum_scatter(full_qkv, both, scatter_dimension=0, tiled=True)

    def spread_heads(part):
        padded = jnp.zeros((ctx * width,), WIDE)
        return lax.dynamic_update_slice_in_dim(padded, part, rank * width, 0)[:D]

    sums_units = sums_units[0].reshape(dp, 1, -1)[:, :, :units]
    sums_units = lax.dynamic_update_slice_in_dim(
        jnp.zeros((dp, ctx, units), WIDE), sums_units, rank, 1
    ).reshape(FF)
    vector = jnp.concatenate(
        [
            sums_one[0],
            sums_one[1],
            spread_heads(sums_heads[0, :width]),
            spread_heads(sums_heads[0, 2 * width :]),
            sums_two[0],
            sums_two[1],
            sums_two[2],
            sums_units,
            sums_two[3],
        ]
    ).reshape(owners, vec_count)
    vec_pad = -(-vec_count // 1024) * 1024
    vector = jnp.pad(vector, ((0, 0), (0, vec_pad - vec_count))).reshape(dp, ctx, -1, 128)
    share_vector = sum_vector(vector)
    return (
        output[None],
        grad_input[None],
        share_qkv.astype(WIDE).reshape(-1),
        share_proj.astype(WIDE).reshape(-1),
        share_fc.astype(WIDE).reshape(-1),
        grad_out[:units].reshape(-1),
        share_vector.reshape(-1)[:vec_count],
    )


def solution(mesh):
    flat = P(("dp", "ctx"))
    rows = P("dp", "ctx", None)
    return jax.shard_map(
        shards,
        mesh=mesh,
        in_specs=(rows, flat, flat, flat, flat, flat, P("dp", None), rows),
        out_specs=(rows, rows, flat, flat, flat, flat, flat),
        check_vma=False,
    )
```

```python
import functools

import jax
import jax.numpy as jnp
from jax import lax
from jax.experimental import pallas as pl
from jax.experimental.pallas import tpu as pltpu
from jax.sharding import PartitionSpec as P

D = 1600
HEADS = 25
HEAD_DIM = 64
FF = 6400
EPSILON = 1e-05
LOW = jnp.bfloat16
WIDE = jnp.float32
MIB = 1024 * 1024


def dot(left, right, left_dim=1, right_dim=0):
    return lax.dot_general(
        left, right, (((left_dim,), (right_dim,)), ((), ())), preferred_element_type=WIDE
    )


def normalize(rows):
    centre = rows - jnp.mean(rows, -1, keepdims=True)
    spread = jnp.mean(centre * centre, -1, keepdims=True)
    scale = lax.rsqrt(spread + EPSILON)
    return centre * scale, scale


def norm_back(normed, scale, gain, incoming):
    scaled = gain * incoming
    return scale * (
        scaled
        - jnp.mean(scaled, -1, keepdims=True)
        - normed * jnp.mean(scaled * normed, -1, keepdims=True)
    )


def head_lanes(head, width):
    lane = lax.broadcasted_iota(jnp.int32, (1, width), 1)
    return (lane // HEAD_DIM) == head


def allowed_scores(scores, doc_start, first_query, keys, block):
    key_pos = lax.broadcasted_iota(jnp.int32, (keys, block), 0)
    query_pos = first_query + lax.broadcasted_iota(jnp.int32, (keys, block), 1)
    seen = (key_pos >= doc_start) & (key_pos <= query_pos)
    return jnp.where(seen, scores, -1e30)


def attend_body(block, qkv_ref, start_ref, mixed_ref, stat_ref, value_t):
    length = qkv_ref.shape[0]
    width = mixed_ref.shape[1]
    slots = width // HEAD_DIM
    value_t[...] = qkv_ref[:, 2 * width : 3 * width].astype(WIDE).T.astype(LOW)
    stat_ref[...] = jnp.zeros_like(stat_ref)
    for index in range(length // block):
        keys = (index + 1) * block
        rows = pl.ds(index * block, block)
        key_rows = qkv_ref[0:keys, width : 2 * width]
        doc_start = start_ref[0:1, rows]
        outs = []
        for head in range(slots):
            query = jnp.where(
                head_lanes(head, width), qkv_ref[rows, 0:width] * LOW(HEAD_DIM**-0.5), LOW(0)
            )
            scores = dot(key_rows, query, 1, 1)
            scores = allowed_scores(scores, doc_start, index * block, keys, block)
            top = jnp.max(scores, 0, keepdims=True)
            expo = jnp.exp(scores - top)
            total = jnp.sum(expo, 0, keepdims=True)
            head_rows = slice(head * HEAD_DIM, (head + 1) * HEAD_DIM)
            out = dot(value_t[head_rows, 0:keys], expo.astype(LOW))
            outs.append(out / total)
            stat_ref[head : head + 1, rows] = top + jnp.log(total)
        mixed_ref[rows, :] = jnp.concatenate(outs, 0).T.astype(LOW)


def attend_back_body(
    block, qkv_ref, start_ref, stat_ref, grad_ref, out_ref, key_t, key_grad, value_grad, after
):
    length = qkv_ref.shape[0]
    width = grad_ref.shape[1]
    slots = width // HEAD_DIM
    scale = HEAD_DIM**-0.5
    key_t[...] = qkv_ref[:, width : 2 * width].astype(WIDE).T.astype(LOW)
    key_grad[...] = jnp.zeros_like(key_grad)
    value_grad[...] = jnp.zeros_like(value_grad)
    for index in range(length // block):
        keys = (index + 1) * block
        rows = pl.ds(index * block, block)
        key_rows = qkv_ref[0:keys, width : 2 * width]
        value_rows = qkv_ref[0:keys, 2 * width : 3 * width]
        doc_start = start_ref[0:1, rows]
        outs = []
        for head in range(slots):
            lanes = head_lanes(head, width)
            head_rows = slice(head * HEAD_DIM, (head + 1) * HEAD_DIM)
            query = jnp.where(lanes, qkv_ref[rows, 0:width] * LOW(scale), LOW(0))
            grad = jnp.where(lanes, grad_ref[rows, :], LOW(0))
            scores = dot(key_rows, query, 1, 1)
            scores = allowed_scores(scores, doc_start, index * block, keys, block)
            probs = jnp.exp(scores - stat_ref[head : head + 1, rows])
            grad_probs = dot(value_rows, grad, 1, 1)
            delta = jnp.sum(probs * grad_probs, 0, keepdims=True)
            grad_scores = (probs * (grad_probs - delta)).astype(LOW)
            value_grad[0:keys, :] += dot(probs.astype(LOW), grad)
            key_grad[0:keys, :] += dot(grad_scores, query)
            outs.append(dot(key_t[head_rows, 0:keys], grad_scores))
        out_ref[rows, 0:width] = (jnp.concatenate(outs, 0).T * scale).astype(LOW)
        if index in after:
            after[index]()
    out_ref[:, width : 2 * width] = key_grad[...].astype(LOW)
    out_ref[:, 2 * width : 3 * width] = value_grad[...].astype(LOW)


MESH = pl.DeviceIdType.MESH


def send(src, dst, send_sem, recv_sem, **target):
    return pltpu.make_async_remote_copy(
        src_ref=src,
        dst_ref=dst,
        send_sem=send_sem,
        recv_sem=recv_sem,
        device_id=target,
        device_id_type=MESH,
    )


def greet_line(chips):
    rank = lax.axis_index("ctx")
    chip, core = rank // 2, rank % 2
    barrier = pltpu.get_barrier_semaphore()
    pl.semaphore_signal(barrier, 1, device_id={"ctx": rank + 1 - 2 * core}, device_id_type=MESH)

    @pl.when(chip > 0)
    def _():
        pl.semaphore_signal(barrier, 1, device_id={"ctx": rank - 2}, device_id_type=MESH)

    @pl.when(chip < chips - 1)
    def _():
        pl.semaphore_signal(barrier, 1, device_id={"ctx": rank + 2}, device_id_type=MESH)

    sides = (chip > 0).astype(jnp.int32) + (chip < chips - 1).astype(jnp.int32)
    pl.semaphore_wait(barrier, 1 + sides)


def greet_all():
    barrier = pltpu.get_barrier_semaphore()
    count = 0
    for axis in ("ctx", "dp"):
        size = lax.axis_size(axis)
        here = lax.axis_index(axis)

        def one(off, carry, axis=axis, size=size, here=here):
            peer = lax.rem(here + off, size)
            pl.semaphore_signal(barrier, 1, device_id={axis: peer}, device_id_type=MESH)
            return carry

        lax.fori_loop(1, size, one, 0)
        count += size - 1
    pl.semaphore_wait(barrier, count)


class Swap:
    def __init__(self, axis, source, target, sems):
        self.axis, self.source, self.target = axis, source, target
        self.send_sems, self.recv_sems = sems
        self.rank = lax.axis_index(axis)
        self.size = lax.axis_size(axis)

    def copy(self, peer, origin, target):
        return send(
            self.source(peer),
            self.target(origin),
            self.send_sems.at[peer],
            self.recv_sems.at[origin],
            **{self.axis: target},
        )

    def every(self, act):
        def one(off, carry):
            act(lax.rem(self.rank + off, self.size))
            return carry

        lax.fori_loop(1, self.size, one, 0)

    def start(self):
        self.every(lambda peer: self.copy(peer, self.rank, peer).start())

    def wait(self):
        self.every(lambda peer: self.copy(peer, peer, self.rank).wait_recv())

    def drain(self):
        self.every(lambda peer: self.copy(peer, self.rank, peer).wait_send())

    @staticmethod
    def semaphores(size):
        return [pltpu.SemaphoreType.DMA((size,)), pltpu.SemaphoreType.DMA((size,))]


class ChipSwap(Swap):
    def __init__(self, source, target, sems):
        super().__init__("ctx", source, target, sems)
        self.core = self.rank % 2
        self.rank, self.size = self.rank // 2, self.size // 2

    def copy(self, peer, origin, target):
        return send(
            self.source(peer),
            self.target(origin),
            self.send_sems.at[peer],
            self.recv_sems.at[origin],
            ctx=2 * target + self.core,
        )


class PlaneGather:
    def __init__(self, blocks, sems):
        self.blocks = blocks
        self.size = blocks.shape[0]
        self.rank = lax.axis_index("dp")
        self.square = self.size == 4
        self.send_sems, self.recv_sems = sems
        if self.square:
            self.beside = self.rank + 1 - 2 * (self.rank % 2)
            self.above = self.rank + 2 - 4 * (self.rank // 2)
            half = blocks.shape[1] // 32 * 16
            self.low, self.high = pl.ds(0, half), pl.ds(half, blocks.shape[1] - half)
        else:
            self.swap = Swap("dp", lambda peer: blocks.at[self.rank], blocks.at.__getitem__, sems)

    def copy(self, index, ref, target):
        return send(ref, ref, self.send_sems.at[index], self.recv_sems.at[index], dp=target)

    def start(self):
        if not self.square:
            self.swap.start()
            return
        own = self.blocks.at[self.rank]
        self.copy(0, own, self.beside).start()
        self.copy(1, own, self.above).start()

    def relay(self):
        if not self.square:
            return
        self.copy(0, self.blocks.at[self.beside], self.beside).wait_recv()
        self.copy(2, self.blocks.at[self.beside, self.low], self.above).start()
        self.copy(1, self.blocks.at[self.above], self.above).wait_recv()
        self.copy(3, self.blocks.at[self.above, self.high], self.beside).start()

    def wait(self):
        if not self.square:
            self.swap.wait()
            self.swap.drain()
            return
        far = 3 - self.rank
        own = self.blocks.at[self.rank]
        self.copy(2, self.blocks.at[far, self.low], self.above).wait_recv()
        self.copy(3, self.blocks.at[far, self.high], self.beside).wait_recv()
        self.copy(0, own, self.beside).wait_send()
        self.copy(1, own, self.above).wait_send()
        self.copy(2, self.blocks.at[self.beside, self.low], self.above).wait_send()
        self.copy(3, self.blocks.at[self.above, self.high], self.beside).wait_send()

    semaphores = staticmethod(Swap.semaphores)


class PlaneSum:
    def __init__(self, blocks, landed, sems):
        self.blocks, self.landed = blocks, landed
        self.rank = lax.axis_index("dp")
        self.send_sems, self.recv_sems = sems
        self.swap = Swap("dp", blocks.at.__getitem__, landed.at.__getitem__, sems)
        self.square = blocks.shape[0] == 4
        if self.square:
            self.beside = self.rank + 1 - 2 * (self.rank % 2)
            self.above = self.rank + 2 - 4 * (self.rank // 2)
            half = blocks.shape[1] // 32 * 16
            self.low, self.high = pl.ds(0, half), pl.ds(half, blocks.shape[1] - half)

    def copy(self, index):
        far = 3 - self.rank
        block, slot, rows, target = (
            (far, 0, self.low, self.beside),
            (self.beside, 1, self.low, self.beside),
            (far, 0, self.high, self.above),
            (self.above, 1, self.high, self.above),
            (self.above, 2, self.low, self.above),
            (self.beside, 2, self.high, self.beside),
        )[index]
        return send(
            self.blocks.at[block, rows],
            self.landed.at[slot, rows],
            self.send_sems.at[index],
            self.recv_sems.at[index],
            dp=target,
        )

    def start(self):
        if not self.square:
            self.swap.start()
            return
        for index in range(4):
            self.copy(index).start()

    def relay(self):
        if not self.square:
            return
        for index, block, rows in ((0, self.above, self.low), (2, self.beside, self.high)):
            self.copy(index).wait_recv()
            total = self.blocks[block, rows].astype(WIDE) + self.landed[0, rows].astype(WIDE)
            self.blocks[block, rows] = total.astype(self.blocks.dtype)
            self.copy(4 + index // 2).start()

    def total(self):
        total = self.blocks[self.rank].astype(WIDE)
        if not self.square:
            self.swap.wait()
            for off in range(1, self.swap.size):
                total = total + self.landed[lax.rem(self.rank + off, self.swap.size)].astype(WIDE)
            return total
        for index in (1, 3, 4, 5):
            self.copy(index).wait_recv()
        return total + self.landed[1].astype(WIDE) + self.landed[2].astype(WIDE)

    def drain(self):
        if not self.square:
            self.swap.drain()
            return
        for index in range(6):
            self.copy(index).wait_send()

    @staticmethod
    def semaphores(size):
        return Swap.semaphores(max(size, 6))


class LineGather:
    def __init__(self, blocks, send_sems, recv_sems):
        self.blocks, self.send_sems, self.recv_sems = blocks, send_sems, recv_sems
        self.rank = lax.axis_index("ctx")
        self.chip, self.core = self.rank // 2, self.rank % 2
        self.chips = blocks.shape[0] // 2

    def copy(self, way, origin, target, src=None):
        block = self.blocks.at[origin]
        return send(
            block if src is None else src,
            block,
            self.send_sems.at[way, origin],
            self.recv_sems.at[origin],
            ctx=target,
        )

    def pass_on(self, origin, src=None):
        chip = origin // 2

        @pl.when((chip <= self.chip) & (self.chip < self.chips - 1))
        def _():
            self.copy(0, origin, self.rank + 2, src).start()

        @pl.when((chip >= self.chip) & (self.chip > 0))
        def _():
            self.copy(1, origin, self.rank - 2, src).start()

        self.copy(2, origin, self.rank + 1 - 2 * self.core, src).start()

    def arrive(self, step, part):
        side, other = part % 2, part // 2
        origin_chip = self.chip + jnp.where(side == 0, -step, step)
        origin = 2 * origin_chip + jnp.where(other == 0, self.core, 1 - self.core)
        valid = (origin_chip >= 0) & (origin_chip < self.chips) & ((step > 0) | (side == 0))

        @pl.when(valid & (origin != self.rank))
        def _():
            self.copy(0, origin, self.rank).wait_recv()

            @pl.when(other == 0)
            def _():
                self.pass_on(origin)

        return valid, origin

    def finish(self):
        def one(chip, carry):
            origin = 2 * chip + self.core

            @pl.when((chip <= self.chip) & (self.chip < self.chips - 1))
            def _():
                self.copy(0, origin, self.rank).wait_send()

            @pl.when((chip >= self.chip) & (self.chip > 0))
            def _():
                self.copy(1, origin, self.rank).wait_send()

            self.copy(2, origin, self.rank).wait_send()
            return carry

        lax.fori_loop(0, self.chips, one, 0)

    @staticmethod
    def semaphores(ctx):
        return [pltpu.SemaphoreType.DMA((3, ctx)), pltpu.SemaphoreType.DMA((ctx,))]


class LineSum:
    def __init__(self, blocks, pair, passing, sems):
        self.blocks, self.pair, self.passing = blocks, pair, passing
        self.pair_send, self.pair_recv, self.line_send, self.line_recv = sems
        self.rank = lax.axis_index("ctx")
        self.chip, self.core = self.rank // 2, self.rank % 2
        self.chips = blocks.shape[0] // 2
        self.pieces = self.line_recv.shape[2]
        self.piece = blocks.shape[1] // self.pieces

    def pair_copy(self, chip):
        return send(
            self.blocks.at[2 * chip + 1 - self.core],
            self.pair.at[chip],
            self.pair_send.at[chip],
            self.pair_recv.at[chip],
            ctx=self.rank + 1 - 2 * self.core,
        )

    def line_copy(self, way, chip, piece, target, at):
        rows = pl.ds(piece * self.piece, self.piece)
        slot = jnp.where((way == 1) & (chip == at), self.chips, chip)
        return send(
            self.blocks.at[2 * chip + self.core, rows],
            self.passing.at[slot, rows],
            self.line_send.at[chip, piece],
            self.line_recv.at[way, chip, piece],
            ctx=target,
        )

    def both(self, chip, rows):
        mine = self.blocks[2 * chip + self.core, rows].astype(WIDE)
        return mine + self.pair[chip, rows].astype(WIDE)

    def forward(self, way, chip, valid):
        behind = jnp.where(way == 0, self.chip > 0, self.chip < self.chips - 1)
        target = self.rank + jnp.where(way == 0, 2, -2)

        @pl.when(valid)
        def _():
            self.pair_copy(chip).wait_recv()

            def one(piece, carry):
                rows = pl.ds(pl.multiple_of(piece * self.piece, self.piece), self.piece)
                total = self.both(chip, rows)

                @pl.when(behind)
                def _():
                    self.line_copy(way, chip, piece, target, self.chip).wait_recv()
                    passing = self.passing[chip, rows].astype(WIDE)
                    self.blocks[2 * chip + self.core, rows] = (total + passing).astype(LOW)

                @pl.when(jnp.logical_not(behind))
                def _():
                    self.blocks[2 * chip + self.core, rows] = total.astype(LOW)

                self.line_copy(way, chip, piece, target, target // 2).start()
                return carry

            lax.fori_loop(0, self.pieces, one, 0)

    def near_first(self, step, way):
        last = self.chips - 1
        chip = jnp.where(way == 0, step - self.chip, 2 * last - self.chip - step)
        ahead = jnp.where(way == 0, (chip > self.chip) & (chip <= last), (chip >= 0) & (chip < self.chip))
        self.forward(way, chip, ahead)

    def far_first(self, step, way):
        last = self.chips - 1
        chip = jnp.where(way == 0, last + self.chip - step, step - last + self.chip)
        ahead = jnp.where(way == 0, (chip > self.chip) & (chip <= last), (chip >= 0) & (chip < self.chip))
        self.forward(way, chip, ahead)

    def send_pairs(self):
        def one(chip, carry):
            self.pair_copy(chip).start()
            return carry

        lax.fori_loop(0, self.chips, one, 0)

    def far_steps(self, begin, end):
        def one(index, carry):
            self.far_first(index // 2, index % 2)
            return carry

        lax.fori_loop(2 * begin, 2 * end, one, 0)

    def finish(self, out):
        self.pair_copy(self.chip).wait_recv()

        def one(piece, carry):
            rows = pl.ds(pl.multiple_of(piece * self.piece, self.piece), self.piece)
            out[rows] = self.both(self.chip, rows)

            @pl.when(self.chip > 0)
            def _():
                self.line_copy(0, self.chip, piece, self.rank, self.chip).wait_recv()
                out[rows] = out[rows] + self.passing[self.chip, rows].astype(WIDE)

            @pl.when(self.chip < self.chips - 1)
            def _():
                self.line_copy(1, self.chip, piece, self.rank, self.chip).wait_recv()
                out[rows] = out[rows] + self.passing[self.chips, rows].astype(WIDE)

            return carry

        lax.fori_loop(0, self.pieces, one, 0)

        def sent(chip, carry):
            self.pair_copy(chip).wait_send()

            @pl.when(chip != self.chip)
            def _():
                for piece in range(self.pieces):
                    self.line_copy(0, chip, piece, self.rank, self.chip).wait_send()

            return carry

        lax.fori_loop(0, self.chips, sent, 0)

    @staticmethod
    def scratch(ctx, rows, columns, pieces):
        chips = ctx // 2
        return [
            pltpu.VMEM((ctx, rows, columns), LOW),
            pltpu.VMEM((chips, rows, columns), LOW),
            pltpu.VMEM((chips + 1, rows, columns), LOW),
            pltpu.SemaphoreType.DMA((chips,)),
            pltpu.SemaphoreType.DMA((chips,)),
            pltpu.SemaphoreType.DMA((chips, pieces)),
            pltpu.SemaphoreType.DMA((2, chips, pieces)),
        ]


VMEM = pl.BlockSpec(memory_space=pltpu.VMEM)
HBM = pl.BlockSpec(memory_space=pl.ANY)


def params(number):
    return pltpu.CompilerParams(
        vmem_limit_bytes=63 * MIB, collective_id=number, has_side_effects=True
    )


def packed_rows(count, columns):
    tiles = -(-columns // 128)
    main = count // 16 * 16
    return tiles * main + -(-(tiles * (count - main)) // 16) * 16


def pack(out, index, rows, first, count, lane, columns):
    tiles = -(-columns // 128)
    main = count // 16 * 16
    for tile in range(tiles):
        lanes = slice(lane + tile * 128, lane + tile * 128 + 128)
        part = rows[first : first + main, lanes]
        out[index, tile * main : (tile + 1) * main] = part.astype(LOW)
    left = [
        rows[first + row : first + row + 1, lane + tile * 128 : lane + tile * 128 + 128]
        for row in range(main, count)
        for tile in range(tiles)
    ]
    space = out.shape[1] - tiles * main
    if space:
        left.append(jnp.zeros((space - len(left), 128), WIDE))
        out[index, tiles * main :] = jnp.concatenate(left, 0).astype(LOW)


def unpack(packed, rows, first, count, columns):
    tiles = -(-columns // 128)
    main = count // 16 * 16
    for tile in range(tiles):
        lanes = slice(tile * 128, tile * 128 + 128)
        rows[first : first + main, lanes] = packed[tile * main : (tile + 1) * main].astype(WIDE)
    left = packed[tiles * main :].astype(WIDE)
    for row in range(main, count):
        for tile in range(tiles):
            place = (row - main) * tiles + tile
            lanes = slice(tile * 128, tile * 128 + 128)
            rows[first + row : first + row + 1, lanes] = left[place : place + 1]


def full_lanes(columns):
    return -(-columns // 128) * 128


def head_pieces(ctx, slots):
    width = slots * HEAD_DIM
    pieces = []
    for rank in range(ctx):
        count = min(width, D - rank * width)
        if count > 0:
            for part in range(3):
                pieces.append((rank, part * width, part * D + rank * width, count))
    return pieces


def unit_pieces(ctx, dp):
    units = FF // (ctx * dp)
    return [
        (rank, seq * padded_units(units), (seq * ctx + rank) * units, units)
        for rank in range(ctx)
        for seq in range(dp)
    ]


def divide(rows_ref, wide, blocks, pieces, columns):
    count = rows_ref.shape[0]
    lanes = full_lanes(columns)
    for rank in range(blocks.shape[0]):
        wide[...] = jnp.zeros_like(wide)
        for owner, here, there, size in pieces:
            if owner == rank:
                wide[0:count, here : here + size] = rows_ref[:, there : there + size].astype(WIDE)
        pack(blocks, rank, wide, 0, count, 0, lanes)


class Spread:
    def __init__(self, blocks, landed, wide, out, sems):
        self.blocks, self.landed, self.wide, self.out = blocks, landed, wide, out
        self.swap = Swap("ctx", blocks.at.__getitem__, landed.at.__getitem__, sems[:2])
        self.plane = PlaneGather(out, sems[2:])

    def start(self):
        self.swap.start()
        self.landed[self.swap.rank] = self.blocks[self.swap.rank]

    def cross(self):
        self.swap.wait()
        count = self.out.shape[1] // self.swap.size
        columns = self.out.shape[2]
        for index in range(self.swap.size):
            unpack(self.landed[index], self.wide, index * count, count, columns)
        self.out[self.plane.rank] = self.wide[:, 0:columns].astype(LOW)
        self.plane.start()

    def wait(self):
        self.plane.wait()

    @staticmethod
    def scratch(ctx, dp, rows, columns):
        return [
            pltpu.VMEM((ctx, packed_rows(rows // ctx, columns), 128), LOW),
            pltpu.VMEM((rows, full_lanes(columns)), WIDE),
            *Swap.semaphores(ctx),
            *PlaneGather.semaphores(dp),
        ]


class StreamSum:
    def __init__(self, parts, landed, stage, stage_sems, sems):
        self.parts, self.landed, self.stage, self.stage_sems = parts, landed, stage, stage_sems
        self.plane = PlaneSum(parts, landed, sems)

    def put(self, index, part):
        if index >= 2:
            self.move(index - 2).wait()
        self.stage[index % 2] = part.astype(LOW)
        self.move(index).start()

    def move(self, index):
        slot = index % 2
        return pltpu.make_async_copy(
            self.stage.at[slot], self.parts.at[index], self.stage_sems.at[slot]
        )

    def start(self):
        self.move(2).wait()
        self.move(3).wait()
        self.plane.start()

    def load(self, source, slot, rows):
        return pltpu.make_async_copy(
            source.at[rows], self.stage.at[slot, rows], self.stage_sems.at[slot]
        )

    def relayed(self, index):
        plane = self.plane
        rows, target = ((plane.low, plane.above), (plane.high, plane.beside))[index]
        return send(
            self.stage.at[2, rows],
            self.landed.at[2, rows],
            plane.send_sems.at[4 + index],
            plane.recv_sems.at[4 + index],
            dp=target,
        )

    def relay(self):
        plane = self.plane
        for index, block, rows in ((0, plane.above, plane.low), (1, plane.beside, plane.high)):
            plane.copy(2 * index).wait_recv()
            loads = (
                self.load(self.parts.at[block], 0, rows),
                self.load(self.landed.at[0], 1, rows),
            )
            for load in loads:
                load.start()
            for load in loads:
                load.wait()
            total = self.stage[0, rows].astype(WIDE) + self.stage[1, rows].astype(WIDE)
            self.stage[2, rows] = total.astype(LOW)
            self.relayed(index).start()

    def total(self):
        plane = self.plane
        for index in range(4):
            plane.copy(index).wait_send()
        plane.copy(1).wait_recv()
        plane.copy(3).wait_recv()
        for index in range(2):
            self.relayed(index).wait_send()
            self.relayed(index).wait_recv()
        every = pl.ds(0, self.parts.shape[1])
        loads = (
            self.load(self.parts.at[plane.rank], 0, every),
            self.load(self.landed.at[1], 1, every),
            self.load(self.landed.at[2], 2, every),
        )
        for load in loads:
            load.start()
        for load in loads:
            load.wait()
        total = self.stage[0].astype(WIDE) + self.stage[1].astype(WIDE)
        return total + self.stage[2].astype(WIDE)


class Collect:
    def __init__(self, pieces, plane, wide, blocks, came, out, sems):
        self.pieces, self.plane, self.wide, self.blocks = pieces, plane, wide, blocks
        self.came, self.out = came, out
        self.swap = Swap("ctx", blocks.at.__getitem__, came.at.__getitem__, sems)

    def cross(self):
        rows, columns = self.plane.parts.shape[1:]
        lanes = full_lanes(columns)
        self.wide[0:rows, 0:columns] = self.plane.total()
        if lanes > columns:
            self.wide[0:rows, columns:lanes] = jnp.zeros((rows, lanes - columns), WIDE)
        count = rows // self.swap.size
        for index in range(self.swap.size):
            pack(self.blocks, index, self.wide, index * count, count, 0, columns)
        self.swap.start()
        self.came[self.swap.rank] = self.blocks[self.swap.rank]

    def wait(self):
        self.swap.wait()
        count = self.out.shape[0]
        for rank in range(self.swap.size):
            unpack(self.came[rank], self.wide, 0, count, self.plane.parts.shape[2])
            for owner, here, there, size in self.pieces:
                if owner == rank:
                    self.out[:, there : there + size] = self.wide[0:count, here : here + size]
        self.swap.drain()


class Projection:
    def __init__(self, rows, blocks, wide, out, sems):
        self.rows, self.blocks, self.wide, self.out = rows, blocks, wide, out
        self.rank = lax.axis_index("ctx")
        self.core = self.rank % 2
        self.packed = rows.shape[1]
        self.plane = PlaneGather(blocks.at[self.core], sems[:2])
        self.send_sems, self.recv_sems = sems[2:4]
        self.swap = ChipSwap(lambda peer: rows.at[0], self.place, sems[4:])

    def place(self, chip):
        rows = pl.ds(pl.multiple_of(chip * self.packed, self.packed), self.packed)
        return self.blocks.at[self.core, self.plane.rank, rows]

    def start(self):
        self.swap.start()
        rows = pl.ds(pl.multiple_of(self.swap.rank * self.packed, self.packed), self.packed)
        self.blocks[self.core, self.plane.rank, rows] = self.rows[0]

    def cross(self):
        self.swap.wait()
        self.plane.start()
        self.to_other(self.plane.rank).start()

    def to_other(self, seq):
        block = self.blocks.at[self.core, seq]
        return send(
            block,
            block,
            self.send_sems.at[seq],
            self.recv_sems.at[seq],
            ctx=self.rank + 1 - 2 * self.core,
        )

    def wait(self):
        self.plane.wait()

        def others(off, carry):
            self.to_other(lax.rem(self.plane.rank + off, self.plane.size)).start()
            return carry

        lax.fori_loop(1, self.plane.size, others, 0)
        ctx = 2 * self.swap.size
        count = self.out.shape[1] // ctx

        def order(off, carry):
            seq = lax.rem(self.plane.rank + off, self.plane.size)
            self.to_other(seq).wait_recv()
            for rank in range(ctx):
                first = rank // 2 * self.packed
                rows = self.blocks[rank % 2, seq, first : first + self.packed]
                unpack(rows, self.wide, rank * count, count, D)
            self.out[seq] = self.wide[:, 0:D].astype(LOW)
            return carry

        lax.fori_loop(0, self.plane.size, order, 0)

        def sent(seq, carry):
            self.to_other(seq).wait_send()
            return carry

        lax.fori_loop(0, self.plane.size, sent, 0)
        self.swap.drain()

    @staticmethod
    def scratch(ctx, dp):
        packed = packed_rows(D // (dp * ctx), D)
        return [
            pltpu.VMEM((2, dp, ctx // 2 * packed, 128), LOW),
            pltpu.VMEM((D // dp, full_lanes(D)), WIDE),
            *PlaneGather.semaphores(dp),
            *Swap.semaphores(dp),
            *Swap.semaphores(ctx // 2),
        ]


def vector_pieces(owners, count):
    pieces = []
    for owner in range(owners):
        begin = 0
        while begin < count:
            place = owner * count + begin
            size = min(count - begin, D - place % D)
            pieces.append((owner, begin, place // D, place % D, size))
            begin += size
    return pieces


def unit_bias_pieces(rank, ctx, dp):
    units = FF // (ctx * dp)
    pieces = []
    for seq in range(dp):
        begin = 0
        while begin < units:
            place = (seq * ctx + rank) * units + begin
            size = min(units - begin, D - place % D)
            pieces.append((seq * padded_units(units) + begin, 7 + place // D, place % D, size))
            begin += size
    return pieces


GAIN_ONE, SHIFT_ONE, BIAS_QUERY, BIAS_VALUE, BIAS_PROJ, GAIN_TWO, SHIFT_TWO = range(7)
BIAS_OUT = 11
ROWS = 16


class Names:
    def __init__(self, names, refs):
        self.__dict__.update(zip(names, refs, strict=True))


def forward_kernel(block, names, whole, *refs):
    r = Names(names, refs)
    seq, rank = lax.axis_index("dp"), lax.axis_index("ctx")
    ctx, tokens, _ = r.rows.shape
    dp, units = r.units.shape[:2]
    width = r.mixed.shape[1]
    vec_count = 12 * D // (ctx * dp)

    def out(ref, target, index):
        return pltpu.make_async_copy(ref, target, r.out_sems.at[index])

    rows_in = LineGather(r.rows, r.rows_send, r.rows_recv)
    cots = LineGather(r.cots, r.cots_send, r.cots_recv)
    feed = LineGather(r.rows, r.feed_send, r.feed_recv)
    total = LineSum(
        r.sum_blocks,
        r.sum_pair,
        r.sum_passing,
        (r.sum_pair_send, r.sum_pair_recv, r.sum_line_send, r.sum_line_recv),
    )
    chips = feed.chips
    line = Swap(
        "ctx",
        lambda peer: r.small,
        lambda origin: r.smalls.at[seq, origin],
        (r.line_send, r.line_recv),
    )
    plane = Swap(
        "dp",
        lambda peer: r.smalls.at[seq],
        r.smalls.at.__getitem__,
        (r.plane_send, r.plane_recv),
    )
    unit_rows = PlaneGather(r.units, (r.units_send, r.units_recv))
    to_tokens = Swap(
        "ctx",
        lambda peer: r.mixed.at[pl.ds(pl.multiple_of(peer * tokens, tokens), tokens)],
        lambda origin: r.own_mixed.at[:, pl.ds(pl.multiple_of(origin * width, width), width)],
        (r.mixed_send, r.mixed_recv),
    )
    if whole:
        heads = Spread(
            r.qkv_blocks,
            r.qkv_landed,
            r.qkv_wide,
            r.qkv_mat,
            (r.qkv_send, r.qkv_recv, r.qkv_plane_send, r.qkv_plane_recv),
        )
        columns = Spread(
            r.fc_blocks,
            r.fc_landed,
            r.fc_wide,
            r.fc_mat,
            (r.fc_send, r.fc_recv, r.fc_plane_send, r.fc_plane_recv),
        )
        proj = Projection(
            r.proj_packed,
            r.proj_blocks,
            r.proj_wide,
            r.proj_mat,
            (
                r.proj_plane_send,
                r.proj_plane_recv,
                r.proj_pair_send,
                r.proj_pair_recv,
                r.proj_send,
                r.proj_recv,
            ),
        )
        divide(r.qkv_rows, r.qkv_lanes, r.qkv_blocks, head_pieces(ctx, width // HEAD_DIM), 3 * width)
    r.rows[rank] = r.own_in[...]
    r.cots[rank] = r.own_cot[...]
    r.units[seq] = r.own_units[...]
    r.smalls[seq, rank] = r.small[...]
    greet_all()

    line.start()
    if whole:
        heads.start()
    unit_rows.start()
    if whole:
        count = r.proj_rows.shape[0]
        r.proj_lanes[0:count, 0:D] = r.proj_rows[...].astype(WIDE)
        r.proj_lanes[0:count, D:] = jnp.zeros((count, full_lanes(D) - D), WIDE)
        pack(r.proj_packed, 0, r.proj_lanes, 0, count, 0, D)
        heads.swap.drain()
        proj.start()
    rows_in.pass_on(rank)
    line.wait()
    plane.start()
    if whole:
        heads.cross()
        divide(r.fc_rows, r.fc_lanes, r.fc_blocks, unit_pieces(ctx, dp), dp * units)

    def arrivals(gather):
        def arrive(index, carry):
            gather.arrive(1 + index // 4, index % 4)
            return carry

        return arrive

    rows_in.arrive(0, 2)
    lax.fori_loop(0, 4, arrivals(rows_in), 0)
    unit_rows.relay()
    if whole:
        proj.cross()
    lax.fori_loop(4, 8, arrivals(rows_in), 0)
    if whole:
        heads.plane.relay()
        columns.start()
    lax.fori_loop(8, 4 * (chips - 1), arrivals(rows_in), 0)
    rows_in.finish()
    plane.wait()
    r.vectors[...] = jnp.zeros_like(r.vectors)
    for owner, begin, row, lane, size in vector_pieces(ctx * dp, vec_count):
        r.vectors[row : row + 1, lane : lane + size] = r.smalls[
            owner // ctx, owner % ctx, 0:1, begin : begin + size
        ]
    r.bias_units[...] = jnp.zeros_like(r.bias_units)
    for owner in range(ctx):

        @pl.when(rank == owner)
        def _(owner=owner):
            for here, row, lane, size in unit_bias_pieces(owner, ctx, dp):
                r.bias_units[0:1, here : here + size] = r.vectors[row : row + 1, lane : lane + size]

    if whole:
        heads.wait()
        out(r.qkv_mat, r.qkv_mat_out, 0).start()
    mine = pl.ds(pl.multiple_of(rank * width, width), width)
    bias = jnp.concatenate(
        [
            r.vectors[BIAS_QUERY : BIAS_QUERY + 1, mine],
            jnp.zeros((1, width), WIDE),
            r.vectors[BIAS_VALUE : BIAS_VALUE + 1, mine],
        ],
        1,
    )

    def project(index, carry):
        both = pl.ds(2 * index, 2)
        normed, _ = normalize(r.rows[both].reshape(2 * tokens, D).astype(WIDE))
        attn_in = normed * r.vectors[GAIN_ONE : GAIN_ONE + 1, 0:D]
        attn_in = (attn_in + r.vectors[SHIFT_ONE : SHIFT_ONE + 1, 0:D]).astype(LOW)
        r.rows[both] = attn_in.reshape(2, tokens, D)
        rows = pl.ds(pl.multiple_of(2 * index * tokens, 2 * tokens), 2 * tokens)
        r.qkv[rows] = (dot(attn_in, r.qkv_mat[...].reshape(D, 3 * width)) + bias).astype(LOW)
        return carry

    lax.fori_loop(0, chips, project, 0)
    out(r.rows, r.attn_in_out, 1).start()
    out(r.qkv, r.qkv_out, 2).start()
    if whole:
        proj.plane.relay()
        columns.cross()
    cots.pass_on(rank)
    attend_body(block, r.qkv, r.doc_start, r.mixed, r.stats, r.value_t)
    out(r.rows, r.attn_in_out, 1).wait()
    to_tokens.start()
    r.own_mixed[:, mine] = r.mixed[pl.ds(pl.multiple_of(rank * tokens, tokens), tokens)]
    if whole:
        proj.wait()
        out(r.proj_mat, r.proj_mat_out, 3).start()
        columns.plane.relay()
    cots.arrive(0, 2)
    lax.fori_loop(0, 4, arrivals(cots), 0)
    to_tokens.wait()
    resid = dot(r.own_mixed[:, 0:D], r.proj_mat[...].reshape(D, D))
    resid = resid + r.own_in[...].astype(WIDE) + r.vectors[BIAS_PROJ : BIAS_PROJ + 1, 0:D]
    r.resid[...] = resid
    normed, _ = normalize(resid)
    ffn_in = normed * r.vectors[GAIN_TWO : GAIN_TWO + 1, 0:D]
    r.rows[rank] = (ffn_in + r.vectors[SHIFT_TWO : SHIFT_TWO + 1, 0:D]).astype(LOW)
    feed.pass_on(rank)
    unit_rows.wait()
    if whole:
        columns.wait()

    def keep(chip, slot):
        both = pl.ds(2 * chip, 2)
        return [
            pltpu.make_async_copy(ref.at[slot], target.at[both], r.keep_sems.at[index, slot])
            for index, (ref, target) in enumerate(
                ((r.act, r.act_out), (r.pre, r.pre_out), (r.part, r.part_out))
            )
        ]

    def pass_rows(chip):
        both = pl.ds(2 * chip, 2)
        return [
            pltpu.make_async_copy(ref.at[both], target.at[both], r.pass_sems.at[index, chip])
            for index, (ref, target) in enumerate(((r.rows, r.ffn_out), (r.cots, r.cots_out)))
        ]

    def work(chip, done):
        both = pl.ds(2 * chip, 2)
        slot = done % 2

        @pl.when(done >= 2)
        def _():
            for copy in keep(chip, slot):
                copy.wait()

        for copy in pass_rows(chip):
            copy.start()
        fc = r.fc_mat[...].reshape(D, dp * units)
        mat = r.units[...].reshape(dp * units, D)
        pre = dot(r.rows[both].reshape(2 * tokens, D), fc) + r.bias_units[0:1]
        bend = jnp.tanh(0.7978845608028654 * (pre + 0.044715 * pre * pre * pre))
        act = (0.5 * pre * (1.0 + bend)).astype(LOW)
        r.act[slot] = act.reshape(2, tokens, -1)
        slope = 0.5 * (1.0 + bend) + 0.5 * pre * (1.0 - bend * bend) * 0.7978845608028654 * (
            1.0 + 3 * 0.044715 * pre * pre
        )
        grad_act = dot(r.cots[both].reshape(2 * tokens, D), mat, 1, 1)
        grad_pre = (slope * grad_act).astype(LOW)
        r.pre[slot] = grad_pre.reshape(2, tokens, -1)
        r.sum_blocks[both] = dot(grad_pre, fc, 1, 1).astype(LOW).reshape(2, tokens, D)
        total.pair_copy(chip).start()
        r.part[slot] = dot(act, mat).astype(LOW).reshape(2, tokens, D)
        for copy in keep(chip, slot):
            copy.start()

    def step(index, done):
        distance, side = index // 2, index % 2
        near = distance < chips
        origin_chip = rank // 2 + jnp.where(side == 0, -distance, distance)
        valid = near & (origin_chip >= 0) & (origin_chip < chips) & ((distance > 0) | (side == 0))

        @pl.when(near)
        def _():
            @pl.when(side == 0)
            def _():
                @pl.when(distance > 1)
                def _():
                    cots.arrive(distance, 0)
                    cots.arrive(distance, 1)

                feed.arrive(distance, 0)
                feed.arrive(distance, 1)

            @pl.when(distance > 1)
            def _():
                cots.arrive(distance, 2 + side)

            feed.arrive(distance, 2 + side)

            @pl.when(valid)
            def _():
                work(origin_chip, done)

        @pl.when(side == 1)
        def _():
            def way(index, carry):
                total.near_first(distance, index)
                return carry

            lax.fori_loop(0, 2, way, 0)

        return done + valid.astype(jnp.int32)

    lax.fori_loop(0, 2 * (2 * chips - 1), step, jnp.int32(0))
    total.finish(r.grad)

    feed.finish()
    cots.finish()
    line.drain()
    plane.drain()
    to_tokens.drain()
    for slot in range(2):
        for copy in keep(0, slot):
            copy.wait()

    def passed(chip, carry):
        for copy in pass_rows(chip):
            copy.wait()
        return carry

    lax.fori_loop(0, chips, passed, 0)
    out(r.qkv, r.qkv_out, 2).wait()
    if whole:
        out(r.qkv_mat, r.qkv_mat_out, 0).wait()
        out(r.proj_mat, r.proj_mat_out, 3).wait()
        columns.swap.drain()


def forward(small, own_in, own_cot, unit_rows, doc_start, mats, slots, whole, block):
    ctx, dp = lax.axis_size("ctx"), lax.axis_size("dp")
    tokens = own_in.shape[0]
    length = ctx * tokens
    width = slots * HEAD_DIM
    units = unit_rows.shape[0]
    columns = dp * units
    chips = ctx // 2
    count = D // (dp * ctx)
    high = -(-count // 8) * 8
    names, given, in_specs = [], [], []
    shapes, out_specs, scratch = [], [], []
    in_names, out_names, scratch_names = [], [], []

    def take(name, value):
        in_names.append(name)
        given.append(value)

    def give(name, shape, kind=LOW, spec=HBM):
        out_names.append(name)
        shapes.append(jax.ShapeDtypeStruct(shape, kind))
        out_specs.append(spec)

    def hold(name, *what):
        scratch_names.append(name)
        scratch.append(pltpu.VMEM(what[0], what[1] if len(what) > 1 else LOW))

    def sems(*pairs):
        for name, shape in pairs:
            scratch_names.append(name)
            scratch.append(pltpu.SemaphoreType.DMA(shape))

    def both(name, size):
        sems((name + "_send", (size,)), (name + "_recv", (size,)))

    take("small", small)
    take("own_in", own_in)
    take("own_cot", own_cot)
    take("own_units", unit_rows)
    take("doc_start", doc_start)
    for name, value in zip(
        ("qkv_rows", "fc_rows", "proj_rows") if whole else ("qkv_mat", "fc_mat", "proj_mat"),
        mats,
        strict=True,
    ):
        take(name, value)
    give("vectors", (ROWS, max(full_lanes(D), ctx * width)), WIDE, VMEM)
    give("attn_in_out", (ctx, tokens, D))
    give("qkv_out", (length, 3 * width))
    give("stats", (8, length), WIDE, VMEM)
    give("own_mixed", (tokens, ctx * width), LOW, VMEM)
    give("cots_out", (ctx, tokens, D))
    give("resid", (tokens, D), WIDE, VMEM)
    give("grad", (tokens, D), WIDE, VMEM)
    give("ffn_out", (ctx, tokens, D))
    give("act_out", (ctx, tokens, columns))
    give("pre_out", (ctx, tokens, columns))
    give("part_out", (ctx, tokens, D))
    if whole:
        give("qkv_mat_out", (dp, D // dp, 3 * width))
        give("proj_mat_out", (dp, D // dp, D))
    hold("rows", (ctx, tokens, D))
    hold("cots", (ctx, tokens, D))
    hold("units", (dp, units, D))
    hold("smalls", (dp, ctx, *small.shape), WIDE)
    hold("bias_units", (8, columns), WIDE)
    hold("qkv", (length, 3 * width))
    hold("mixed", (length, width))
    hold("value_t", (width, length))
    hold("act", (2, 2, tokens, columns))
    hold("pre", (2, 2, tokens, columns))
    hold("part", (2, 2, tokens, D))
    hold("sum_blocks", (ctx, tokens, D))
    hold("sum_pair", (chips, tokens, D))
    hold("sum_passing", (chips + 1, tokens, D))
    sems(
        ("sum_pair_send", (chips,)),
        ("sum_pair_recv", (chips,)),
        ("sum_line_send", (chips, 4)),
        ("sum_line_recv", (2, chips, 4)),
        ("out_sems", (4,)),
        ("keep_sems", (3, 2)),
        ("pass_sems", (2, chips)),
    )
    for name in ("rows", "cots", "feed"):
        sems((name + "_send", (3, ctx)), (name + "_recv", (ctx,)))
    both("line", ctx)
    both("plane", dp)
    both("units", max(dp, 4))
    both("mixed", ctx)
    if whole:
        for name, lanes in (("qkv", 3 * width), ("fc", columns)):
            packed = (ctx, packed_rows(count, lanes), 128)
            hold(name + "_lanes", (high, full_lanes(lanes)), WIDE)
            hold(name + "_blocks", packed)
            hold(name + "_landed", packed)
            hold(name + "_wide", (D // dp, full_lanes(lanes)), WIDE)
            hold(name + "_mat", (dp, D // dp, lanes))
            both(name, ctx)
            both(name + "_plane", max(dp, 4))
        packed = packed_rows(count, D)
        hold("proj_lanes", (high, full_lanes(D)), WIDE)
        hold("proj_packed", (1, packed, 128))
        hold("proj_blocks", (2, dp, chips * packed, 128))
        hold("proj_wide", (D // dp, full_lanes(D)), WIDE)
        hold("proj_mat", (dp, D // dp, D))
        both("proj_plane", max(dp, 4))
        both("proj_pair", dp)
        both("proj", chips)
    names = tuple(in_names + out_names + scratch_names)
    results = pl.pallas_call(
        functools.partial(forward_kernel, block, names, whole),
        out_shape=shapes,
        in_specs=[VMEM] * len(given),
        out_specs=out_specs,
        scratch_shapes=scratch,
        compiler_params=params(0),
        name="forward",
    )(*given)
    return Names(tuple(out_names), results)


def back_kernel(
    block,
    grad_ref,
    resid_ref,
    own_cot,
    vectors_ref,
    proj_ref,
    qkv_ref,
    start_ref,
    stat_ref,
    ffn_hbm,
    pre_hbm,
    act_hbm,
    cot_hbm,
    part_hbm,
    resid_out,
    low_out,
    vector_out,
    units_out,
    rows_out,
    share_out,
    output_ref,
    fc_out,
    ffn,
    pre,
    act,
    cot,
    load_sems,
    own_grad,
    head_grad,
    key_t,
    key_grad,
    value_grad,
    *refs,
):
    total = LineSum(*refs[:3], refs[3:7])
    loads = [
        pltpu.make_async_copy(src, dst, load_sems.at[index])
        for index, (src, dst) in enumerate(
            (
                (part_hbm, total.blocks),
                (ffn_hbm, ffn),
                (pre_hbm, pre),
                (act_hbm, act),
                (cot_hbm, cot),
            )
        )
    ]
    for load in loads:
        load.start()
    tokens = own_cot.shape[0]
    length, width = head_grad.shape
    units = share_out.shape[0]
    swap = Swap(
        "ctx",
        lambda peer: own_grad.at[:, pl.ds(pl.multiple_of(peer * width, width), width)],
        lambda origin: head_grad.at[pl.ds(pl.multiple_of(origin * tokens, tokens), tokens)],
        refs[7:9],
    )
    share = PlaneSum(refs[9], refs[10], refs[11:13])
    dp = share.swap.size
    greet_all()
    loads[0].wait()
    total.send_pairs()
    grad = grad_ref[...]
    normed, scale = normalize(resid_ref[...])
    grad_resid = own_cot[...].astype(WIDE) + norm_back(normed, scale, vectors_ref[GAIN_TWO : GAIN_TWO + 1, 0:D], grad)
    resid_out[...] = grad_resid
    low = grad_resid.astype(LOW)
    low_out[...] = low
    own_grad[:, 0:D] = dot(low, proj_ref[...], 1, 1).astype(LOW)
    own_grad[:, D:] = jnp.zeros((tokens, own_grad.shape[1] - D), LOW)
    swap.start()
    head_grad[pl.ds(pl.multiple_of(swap.rank * tokens, tokens), tokens)] = own_grad[
        :, pl.ds(pl.multiple_of(swap.rank * width, width), width)
    ]
    vector_out[0:1] = jnp.sum(grad_resid, 0, keepdims=True)
    vector_out[1:2] = jnp.sum(grad * normed, 0, keepdims=True)
    vector_out[2:3] = jnp.sum(grad, 0, keepdims=True)
    vector_out[3:4] = jnp.sum(own_cot[...].astype(WIDE), 0, keepdims=True)
    vector_out[4:8] = jnp.zeros((4, D), WIDE)
    loads[1].wait()
    loads[2].wait()
    grad_pre = pre[...].reshape(length, -1)
    units_out[...] = dot(jnp.ones((8, length), LOW), grad_pre)
    for index in range(dp):
        rows = slice(index * (D // dp), (index + 1) * (D // dp))
        fc_out[rows] = dot(ffn[:, :, rows].reshape(length, D // dp), grad_pre, 0, 0)
    total.far_steps(0, 1)
    loads[3].wait()
    loads[4].wait()
    for index in range(dp):
        rows = slice(index * units, (index + 1) * units)
        part = dot(act[:, :, rows].reshape(length, units), cot[...].reshape(length, D), 0, 0)
        share.blocks[index] = part.astype(LOW)
    share.start()
    swap.wait()
    chips = total.chips

    def first():
        total.far_steps(1, 2)

    def second():
        total.far_steps(2, 3)
        share.relay()

    attend_back_body(
        block,
        qkv_ref,
        start_ref,
        stat_ref,
        head_grad,
        rows_out,
        key_t,
        key_grad,
        value_grad,
        {1: first, 2: second},
    )
    total.far_steps(3, 2 * chips - 1)
    total.finish(output_ref)
    bias = vectors_ref[BIAS_OUT : BIAS_OUT + 1, 0:D]
    output_ref[...] = output_ref[...] + resid_ref[...] + bias
    share_out[...] = share.total()
    swap.drain()
    share.drain()


def back(
    grad, resid, own_cot, vectors, proj, qkv, doc_start, stats, ffn, pre, act, cot, part, block
):
    ctx, tokens, _ = cot.shape
    dp = lax.axis_size("dp")
    length = ctx * tokens
    width = qkv.shape[1] // 3
    columns = act.shape[2]
    units = columns // dp
    shapes = [
        jax.ShapeDtypeStruct((tokens, D), WIDE),
        jax.ShapeDtypeStruct((tokens, D), LOW),
        jax.ShapeDtypeStruct((8, D), WIDE),
        jax.ShapeDtypeStruct((8, columns), WIDE),
        jax.ShapeDtypeStruct((length, 3 * width), LOW),
        jax.ShapeDtypeStruct((units, D), WIDE),
        jax.ShapeDtypeStruct((tokens, D), WIDE),
        jax.ShapeDtypeStruct((D, columns), WIDE),
    ]
    scratch = [
        pltpu.VMEM(ffn.shape, LOW),
        pltpu.VMEM(pre.shape, LOW),
        pltpu.VMEM(act.shape, LOW),
        pltpu.VMEM(cot.shape, LOW),
        pltpu.SemaphoreType.DMA((5,)),
        pltpu.VMEM((tokens, ctx * width), LOW),
        pltpu.VMEM((length, width), LOW),
        pltpu.VMEM((width, length), LOW),
        pltpu.VMEM((length, width), WIDE),
        pltpu.VMEM((length, width), WIDE),
        *LineSum.scratch(ctx, tokens, D, 4),
        *Swap.semaphores(ctx),
        pltpu.VMEM((dp, units, D), LOW),
        pltpu.VMEM((dp, units, D), LOW),
        *PlaneSum.semaphores(dp),
    ]
    return pl.pallas_call(
        functools.partial(back_kernel, block),
        out_shape=shapes,
        in_specs=[VMEM] * 8 + [HBM] * 5,
        out_specs=[VMEM] * 8,
        scratch_shapes=scratch,
        compiler_params=params(3),
        name="back",
    )(grad, resid, own_cot, vectors, proj, qkv, doc_start, stats, ffn, pre, act, cot, part)


class ProjectionSum:
    def __init__(self, out, mixed, low, plane, wide, blocks, came, pair_sems, sems):
        self.out, self.mixed, self.low, self.plane = out, mixed, low, plane
        self.wide, self.blocks, self.came = wide, blocks, came
        self.send_sems, self.recv_sems = pair_sems
        self.rank = lax.axis_index("ctx")
        self.core = self.rank % 2
        self.swap = ChipSwap(blocks.at.__getitem__, came.at.__getitem__, sems)

    def pair_copies(self):
        return [
            send(
                ref.at[self.core],
                ref.at[self.core],
                self.send_sems.at[index],
                self.recv_sems.at[index],
                ctx=self.rank + 1 - 2 * self.core,
            )
            for index, ref in enumerate((self.mixed, self.low))
        ]

    def start(self, mixed, low):
        self.mixed[self.core] = mixed
        self.low[self.core] = low
        for copy in self.pair_copies():
            copy.start()

    def multiply(self):
        for copy in self.pair_copies():
            copy.wait_recv()
        dp, rows = self.plane.parts.shape[:2]
        chips = self.swap.size
        tokens = 2 * self.low.shape[1]
        count = self.out.shape[0]
        mixed = self.mixed[...].reshape(tokens, -1)[:, 0:D]
        low = self.low[...].reshape(tokens, D)
        feature = lax.broadcasted_iota(jnp.int32, (D, rows), 0)
        column = lax.broadcasted_iota(jnp.int32, (1, rows), 1)
        for index in range(dp):
            owner = index * 2 * chips + column // count * 2 + self.core
            wanted = jnp.where(column < chips * count, owner * count + column % count, -1)
            chosen = jnp.where(feature == wanted, 1.0, 0.0).astype(LOW)
            picked = dot(mixed, chosen).astype(LOW)
            self.plane.put(index, dot(picked, low, 0, 0))
        self.plane.start()

    def cross(self):
        count = self.out.shape[0]
        rows = self.plane.parts.shape[1]
        lanes = full_lanes(D)
        self.wide[0:rows, 0:D] = self.plane.total()
        self.wide[0:rows, D:lanes] = jnp.zeros((rows, lanes - D), WIDE)
        for chip in range(self.swap.size):
            pack(self.blocks, chip, self.wide, chip * count, count, 0, D)
        self.swap.start()

    def wait(self):
        self.swap.wait()
        total = self.blocks[self.swap.rank].astype(WIDE)
        for off in range(1, self.swap.size):
            total = total + self.came[lax.rem(self.swap.rank + off, self.swap.size)].astype(WIDE)
        count = self.out.shape[0]
        unpack(total, self.wide, 0, count, D)
        self.out[...] = self.wide[0:count, 0:D]
        for copy in self.pair_copies():
            copy.wait_send()
        self.swap.drain()


def partial_sums(total, rows_ref, mat):
    chips, tokens = total.chips, total.blocks.shape[1]

    def one(index, carry):
        off = jnp.where(index % 2 == 0, -(index // 2), index // 2 + 1)
        chip = lax.rem(chips - 1 + off, chips)
        rows = pl.ds(pl.multiple_of(2 * chip * tokens, 2 * tokens), 2 * tokens)
        part = dot(rows_ref[rows], mat[...].reshape(D, -1), 1, 1).astype(LOW)
        total.blocks[pl.ds(2 * chip, 2)] = part.reshape(2, tokens, D)
        total.pair_copy(chip).start()
        return carry

    lax.fori_loop(0, chips, one, 0)


def last_kernel(
    rows_ref,
    mat_ref,
    in_ref,
    own_ref,
    resid_ref,
    vectors_ref,
    grad_out,
    vector_out,
    heads_out,
    mat_out,
    grad,
    *refs,
):
    total = LineSum(*refs[:3], refs[3:7])
    chips = total.chips
    dp = lax.axis_size("dp")
    greet_line(chips)
    partial_sums(total, rows_ref, mat_ref)
    total.far_steps(0, 1)
    for index in range(dp):
        rows = slice(index * (D // dp), (index + 1) * (D // dp))
        mat_out[rows] = dot(in_ref[:, rows], rows_ref[...], 0, 0)
    total.far_steps(1, 2 * chips - 1)
    heads_out[...] = dot(jnp.ones((8, rows_ref.shape[0]), LOW), rows_ref[...])
    total.finish(grad)
    normed, scale = normalize(own_ref[...].astype(WIDE))
    incoming = grad[...]
    gain = vectors_ref[GAIN_ONE : GAIN_ONE + 1, 0:D]
    grad_out[...] = resid_ref[...] + norm_back(normed, scale, gain, incoming)
    vector_out[0:1] = jnp.sum(incoming * normed, 0, keepdims=True)
    vector_out[1:2] = jnp.sum(incoming, 0, keepdims=True)
    vector_out[2:8] = jnp.zeros((6, D), WIDE)


def last(rows, mat, attn_in, own_in, resid, vectors):
    ctx = lax.axis_size("ctx")
    tokens = own_in.shape[0]
    columns = rows.shape[1]
    return pl.pallas_call(
        last_kernel,
        out_shape=[
            jax.ShapeDtypeStruct((tokens, D), WIDE),
            jax.ShapeDtypeStruct((8, D), WIDE),
            jax.ShapeDtypeStruct((8, columns), WIDE),
            jax.ShapeDtypeStruct((D, columns), WIDE),
        ],
        in_specs=[VMEM] * 6,
        out_specs=[VMEM] * 4,
        scratch_shapes=[pltpu.VMEM((tokens, D), WIDE), *LineSum.scratch(ctx, tokens, D, 4)],
        compiler_params=params(4),
        name="last",
    )(rows, mat, attn_in, own_in, resid, vectors)


def vector_kernel(parts_ref, out_ref, plane_landed, line_parts, line_landed, *sems):
    seq = lax.axis_index("dp")
    swap = Swap("dp", parts_ref.at.__getitem__, plane_landed.at.__getitem__, sems[:2])
    line = Swap("ctx", line_parts.at.__getitem__, line_landed.at.__getitem__, sems[2:])
    greet_all()
    swap.start()
    swap.wait()
    total = parts_ref[seq]
    for off in range(1, swap.size):
        total = total + plane_landed[lax.rem(seq + off, swap.size)]
    line_parts[...] = total
    line.start()
    line.wait()
    total = line_parts[line.rank]
    for off in range(1, line.size):
        total = total + line_landed[lax.rem(line.rank + off, line.size)]
    out_ref[...] = total
    swap.drain()
    line.drain()


def sum_vector(parts):
    dp, ctx = parts.shape[:2]
    return pl.pallas_call(
        vector_kernel,
        out_shape=jax.ShapeDtypeStruct(parts.shape[2:], WIDE),
        in_specs=[VMEM],
        out_specs=VMEM,
        scratch_shapes=[
            pltpu.VMEM(parts.shape, WIDE),
            pltpu.VMEM(parts.shape[1:], WIDE),
            pltpu.VMEM(parts.shape[1:], WIDE),
            *PlaneSum.semaphores(dp),
            *Swap.semaphores(ctx),
        ],
        compiler_params=params(5),
        name="sum_vector",
    )(parts)


GRAD_ONE, SUM_ONE, SUM_QUERY, SUM_VALUE, SUM_RESID, GRAD_FFN, SUM_FFN = range(7)
SUM_OUT = 11


def backward_kernel(block, names, *refs):
    r = Names(names, refs)
    seq, rank = lax.axis_index("dp"), lax.axis_index("ctx")
    ctx, tokens, _ = r.big.shape
    length, width = r.head_grad.shape
    dp, owners_rows = r.fc_parts.shape[:2]
    units = r.out_parts.shape[1]
    columns = dp * units
    vec_count = 12 * D // (ctx * dp)

    def load(source, target, index):
        return pltpu.make_async_copy(source, target, r.load_sems.at[index])

    summed = LineSum(
        r.out_blocks,
        r.out_pair,
        r.out_passing,
        (r.out_pair_send, r.out_pair_recv, r.out_line_send, r.out_line_recv),
    )
    total = LineSum(
        r.in_blocks,
        r.in_pair,
        r.in_passing,
        (r.in_pair_send, r.in_pair_recv, r.in_line_send, r.in_line_recv),
    )
    chips = total.chips
    to_heads = Swap(
        "ctx",
        lambda peer: r.own_grad.at[:, pl.ds(pl.multiple_of(peer * width, width), width)],
        lambda origin: r.head_grad.at[pl.ds(pl.multiple_of(origin * tokens, tokens), tokens)],
        (r.heads_send, r.heads_recv),
    )
    some = r.stage_fc.at[:, :, pl.ds(0, 3 * width)]
    fc = Collect(
        unit_pieces(ctx, dp),
        StreamSum(
            r.fc_parts, r.fc_landed, r.stage_fc, r.stage_fc_sems, (r.fc_plane_send, r.fc_plane_recv)
        ),
        r.wide,
        r.fc_blocks,
        r.fc_came,
        r.fc_out,
        (r.fc_send, r.fc_recv),
    )
    qkv = Collect(
        head_pieces(ctx, width // HEAD_DIM),
        StreamSum(
            r.qkv_parts, r.qkv_landed, some, r.stage_fc_sems, (r.qkv_plane_send, r.qkv_plane_recv)
        ),
        r.wide,
        r.qkv_blocks,
        r.qkv_came,
        r.qkv_grad,
        (r.qkv_send, r.qkv_recv),
    )
    share = StreamSum(
        r.out_parts,
        r.out_landed,
        r.stage_out,
        r.stage_out_sems,
        (r.out_plane_send, r.out_plane_recv),
    )
    proj = ProjectionSum(
        r.proj_grad,
        r.mixed_pair,
        r.low_pair,
        StreamSum(
            r.proj_parts,
            r.proj_landed,
            r.stage_out,
            r.stage_out_sems,
            (r.proj_plane_send, r.proj_plane_recv),
        ),
        r.wide,
        r.proj_blocks,
        r.proj_came,
        (r.proj_pair_send, r.proj_pair_recv),
        (r.proj_send, r.proj_recv),
    )
    vec_plane = Swap(
        "dp",
        r.vec_parts.at.__getitem__,
        r.vec_landed.at.__getitem__,
        (r.vec_plane_send, r.vec_plane_recv),
    )
    vec_line = Swap(
        "ctx", r.vec_rows.at.__getitem__, r.vec_came.at.__getitem__, (r.vec_send, r.vec_recv)
    )
    heads_mat = r.mat.at[:, :, pl.ds(0, 3 * width)]
    loads = [
        load(r.proj_mat, r.mat, 0),
        load(r.part, r.out_blocks, 1),
        load(r.ffn, r.big, 2),
        load(r.pre, r.feed, 3),
        load(r.qkv_mat, heads_mat, 0),
        load(r.attn_in, r.big, 2),
        load(r.act, r.feed, 3),
        load(r.cots, r.big, 2),
    ]
    for index in range(4):
        loads[index].start()
    greet_all()

    grad = r.grad[...]
    normed, scale = normalize(r.resid[...])
    gain = r.vectors[GAIN_TWO : GAIN_TWO + 1, 0:D]
    own_cot = r.own_cot[...].astype(WIDE)
    grad_resid = own_cot + norm_back(normed, scale, gain, grad)
    r.grad_resid[...] = grad_resid
    low = grad_resid.astype(LOW)
    loads[0].wait()
    r.own_grad[:, 0:D] = dot(low, r.mat[...].reshape(D, D), 1, 1).astype(LOW)
    r.own_grad[:, D:] = jnp.zeros((tokens, r.own_grad.shape[1] - D), LOW)
    to_heads.start()
    loads[4].start()
    mine = pl.ds(pl.multiple_of(rank * width, width), width)
    here = pl.ds(pl.multiple_of(rank * tokens, tokens), tokens)
    r.head_grad[here] = r.own_grad[:, mine]
    proj.start(r.own_mixed[...], low)
    loads[1].wait()
    summed.send_pairs()
    vec = r.vec
    vec[...] = jnp.zeros_like(vec)

    def note(row, value):
        vec[row : row + 1, 0:D] = jnp.sum(value, 0, keepdims=True)

    note(SUM_RESID, grad_resid)
    note(GRAD_FFN, grad * normed)
    note(SUM_FFN, grad)
    note(SUM_OUT, own_cot)

    loads[2].wait()
    loads[3].wait()
    grad_pre = r.feed[...].reshape(length, columns)
    sums = dot(jnp.ones((8, length), LOW), grad_pre)[0:1]
    for owner in range(ctx):

        @pl.when(rank == owner)
        def _(owner=owner):
            for place, row, lane, size in unit_bias_pieces(owner, ctx, dp):
                vec[row : row + 1, lane : lane + size] = sums[:, place : place + size]

    def by_parts(plane, left, right, count):
        for index in range(dp):
            rows = slice(index * count, (index + 1) * count)
            plane.put(index, dot(left[:, :, rows].reshape(length, count), right, 0, 0))
        plane.start()

    by_parts(fc.plane, r.big, grad_pre, owners_rows)
    loads[5].start()
    loads[6].start()
    summed.far_steps(0, 1)

    to_heads.wait()

    def first():
        summed.far_steps(1, 2)

    def second():
        summed.far_steps(2, 3)
        fc.plane.relay()

    attend_back_body(
        block,
        r.qkv,
        r.doc_start,
        r.stats,
        r.head_grad,
        r.rows,
        r.key_t,
        r.key_grad,
        r.value_grad,
        {1: first, 2: second},
    )
    loads[4].wait()
    partial_sums(total, r.rows, heads_mat)
    total.far_steps(0, 1)
    summed.far_steps(3, 4)
    fc.cross()
    loads[5].wait()
    by_parts(qkv.plane, r.big, r.rows[...], owners_rows)
    loads[7].start()
    total.far_steps(1, 2)
    summed.far_steps(4, 5)
    proj.multiply()
    total.far_steps(2, 3)
    summed.far_steps(5, 2 * chips - 1)
    loads[6].wait()
    loads[7].wait()
    by_parts(share, r.feed, r.big[...].reshape(length, D), units)
    total.far_steps(3, 2 * chips - 1)
    sums = dot(jnp.ones((8, length), LOW), r.rows[...])
    vec[SUM_QUERY : SUM_QUERY + 1, mine] = sums[0:1, 0:width]
    vec[SUM_VALUE : SUM_VALUE + 1, mine] = sums[0:1, 2 * width :]
    qkv.plane.relay()
    total.finish(r.grad_in)

    incoming = r.grad_in[...]
    normed, scale = normalize(r.own_in[...].astype(WIDE))
    gain = r.vectors[GAIN_ONE : GAIN_ONE + 1, 0:D]
    r.grad_in[...] = r.grad_resid[...] + norm_back(normed, scale, gain, incoming)
    note(GRAD_ONE, incoming * normed)
    note(SUM_ONE, incoming)
    for owner, begin, row, lane, size in vector_pieces(ctx * dp, vec_count):
        r.vec_parts[owner // ctx, owner % ctx, 0:1, begin : begin + size] = vec[
            row : row + 1, lane : lane + size
        ]
    vec_plane.start()
    qkv.cross()
    proj.plane.relay()
    vec_plane.wait()
    rows = r.vec_parts[seq]
    for off in range(1, dp):
        rows = rows + r.vec_landed[lax.rem(seq + off, dp)]
    r.vec_rows[...] = rows
    vec_line.start()
    summed.finish(r.output)
    bias = r.vectors[BIAS_OUT : BIAS_OUT + 1, 0:D]
    r.output[...] = r.output[...] + r.resid[...] + bias
    fc.wait()
    proj.cross()
    share.relay()
    vec_line.wait()
    row = r.vec_rows[rank]
    for off in range(1, ctx):
        row = row + r.vec_came[lax.rem(rank + off, ctx)]
    r.vec_out[...] = row
    qkv.wait()
    r.out_grad[...] = share.total()
    proj.wait()
    to_heads.drain()
    vec_plane.drain()
    vec_line.drain()


def backward(made, own_in, own_cot, doc_start, block):
    ctx, dp = lax.axis_size("ctx"), lax.axis_size("dp")
    tokens = own_in.shape[0]
    length = ctx * tokens
    width = made.qkv_out.shape[1] // 3
    columns = made.act_out.shape[2]
    units = columns // dp
    chips = ctx // 2
    rows = D // dp
    count = rows // ctx
    lanes = full_lanes(12 * D // (ctx * dp))
    near = -(-(chips * count) // 16) * 16
    in_names, given, in_specs = [], [], []
    out_names, shapes, out_specs = [], [], []
    scratch_names, scratch = [], []

    def take(name, value, spec=VMEM):
        in_names.append(name)
        given.append(value)
        in_specs.append(spec)

    def give(name, shape, kind=WIDE, spec=VMEM):
        out_names.append(name)
        shapes.append(jax.ShapeDtypeStruct(shape, kind))
        out_specs.append(spec)

    def hold(name, shape, kind=LOW):
        scratch_names.append(name)
        scratch.append(pltpu.VMEM(shape, kind))

    def sems(*pairs):
        for name, shape in pairs:
            scratch_names.append(name)
            scratch.append(pltpu.SemaphoreType.DMA(shape))

    def both(name, size):
        sems((name + "_send", (size,)), (name + "_recv", (size,)))

    take("grad", made.grad)
    take("resid", made.resid)
    take("own_cot", own_cot)
    take("own_in", own_in)
    take("vectors", made.vectors)
    take("own_mixed", made.own_mixed)
    take("qkv", made.qkv_out)
    take("doc_start", doc_start)
    take("stats", made.stats)
    take("proj_mat", made.proj_mat_out, HBM)
    take("qkv_mat", made.qkv_mat_out, HBM)
    take("part", made.part_out, HBM)
    take("ffn", made.ffn_out, HBM)
    take("pre", made.pre_out, HBM)
    take("attn_in", made.attn_in_out, HBM)
    take("act", made.act_out, HBM)
    take("cots", made.cots_out, HBM)
    give("output", (tokens, D))
    give("grad_in", (tokens, D))
    give("qkv_grad", (count, 3 * D))
    give("proj_grad", (count, D))
    give("fc_out", (count, FF))
    give("out_grad", (units, D))
    give("vec_out", (1, lanes))
    for name, shape in (
        ("fc", (rows, columns)),
        ("qkv", (rows, 3 * width)),
        ("out", (units, D)),
        ("proj", (near, D)),
    ):
        give(name + "_parts", (dp, *shape), LOW, HBM)
        give(name + "_landed", (3, *shape), LOW, HBM)
        both(name + "_plane", 6)
    hold("mat", (dp, rows, D))
    hold("big", (ctx, tokens, D))
    hold("feed", (ctx, tokens, columns))
    hold("stage_fc", (3, rows, columns))
    assert near == units
    hold("stage_out", (3, units, D))
    hold("wide", (rows, full_lanes(D)), WIDE)
    for name, lanes_of in (("fc", columns), ("qkv", 3 * width)):
        hold(name + "_blocks", (ctx, packed_rows(count, lanes_of), 128))
        hold(name + "_came", (ctx, packed_rows(count, lanes_of), 128))
        both(name, ctx)
    hold("proj_blocks", (chips, packed_rows(count, D), 128))
    hold("proj_came", (chips, packed_rows(count, D), 128))
    both("proj", chips)
    both("proj_pair", 2)
    hold("mixed_pair", (2, tokens, ctx * width))
    hold("low_pair", (2, tokens, D))
    for name in ("out", "in"):
        hold(name + "_blocks", (ctx, tokens, D))
        hold(name + "_pair", (chips, tokens, D))
        hold(name + "_passing", (chips + 1, tokens, D))
        both(name + "_pair", chips)
        sems((name + "_line_send", (chips, 4)), (name + "_line_recv", (2, chips, 4)))
    hold("own_grad", (tokens, ctx * width))
    hold("head_grad", (length, width))
    hold("rows", (length, 3 * width))
    hold("key_t", (width, length))
    hold("key_grad", (length, width), WIDE)
    hold("value_grad", (length, width), WIDE)
    hold("grad_resid", (tokens, D), WIDE)
    hold("vec", (ROWS, max(full_lanes(D), ctx * width)), WIDE)
    hold("vec_parts", (dp, ctx, 1, lanes), WIDE)
    hold("vec_landed", (dp, ctx, 1, lanes), WIDE)
    hold("vec_rows", (ctx, 1, lanes), WIDE)
    hold("vec_came", (ctx, 1, lanes), WIDE)
    both("heads", ctx)
    both("vec_plane", dp)
    both("vec", ctx)
    sems(
        ("load_sems", (4,)),
        ("stage_fc_sems", (3,)),
        ("stage_out_sems", (3,)),
    )
    names = tuple(in_names + out_names + scratch_names)
    results = pl.pallas_call(
        functools.partial(backward_kernel, block, names),
        out_shape=shapes,
        in_specs=in_specs,
        out_specs=out_specs,
        scratch_shapes=scratch,
        compiler_params=params(6),
        name="backward",
    )(*given)
    return Names(tuple(out_names), results)


def gather_rows(block):
    return lax.all_gather(block, ("dp", "ctx"), axis=0, tiled=True)


def by_rank_heads(rows, ctx, slots):
    count = rows.shape[0]
    split = rows.reshape(count, 3, D)
    split = jnp.pad(split, ((0, 0), (0, 0), (0, (ctx * slots - HEADS) * HEAD_DIM)))
    split = split.reshape(count, 3, ctx, slots * HEAD_DIM)
    return split.transpose(2, 0, 1, 3).reshape(ctx, count, 3 * slots * HEAD_DIM)


def from_rank_heads(blocks, slots):
    ctx, count = blocks.shape[:2]
    split = blocks.reshape(ctx, count, 3, slots * HEAD_DIM).transpose(1, 2, 0, 3)
    return split.reshape(count, 3, ctx * slots * HEAD_DIM)[:, :, :D].reshape(count, 3 * D)


def padded_units(units):
    return -(-units // 16) * 16


def by_rank_units(rows, ctx, dp):
    count = rows.shape[0]
    units = FF // (dp * ctx)
    split = rows.reshape(count, dp, ctx, units).transpose(2, 0, 1, 3)
    split = jnp.pad(split, ((0, 0), (0, 0), (0, 0), (0, padded_units(units) - units)))
    return split.reshape(ctx, count, dp * padded_units(units))


def from_rank_units(blocks, dp):
    ctx, count = blocks.shape[:2]
    units = FF // (dp * ctx)
    split = blocks.reshape(ctx, count, dp, padded_units(units))[..., :units]
    return split.transpose(1, 2, 0, 3).reshape(count, FF)


def shards(
    hidden_in, qkv_weight, proj_weight, fc_weight, out_weight, small_params, segments, cotangent
):
    tokens = hidden_in.shape[1]
    length = segments.shape[1]
    ctx = lax.axis_size("ctx")
    dp = lax.axis_size("dp")
    owners = dp * ctx
    rank = lax.axis_index("ctx")
    slots = -(-HEADS // ctx)
    width = slots * HEAD_DIM
    units = FF // owners
    rows = D // owners
    whole = D % owners == 0 and dp == 4
    block = min(256, length)
    both = ("dp", "ctx")

    vec_count = small_params.shape[0]
    small = jnp.pad(small_params.astype(WIDE), (0, full_lanes(vec_count) - vec_count))[None]
    unit_rows = jnp.pad(out_weight.reshape(units, D), ((0, padded_units(units) - units), (0, 0)))
    docs = segments[0]
    doc_start = jnp.sum((docs[:, None] < docs[None, :]).astype(jnp.int32), 0)[None]
    if whole:
        mats = (
            qkv_weight.reshape(rows, 3 * D),
            fc_weight.reshape(rows, FF),
            proj_weight.reshape(rows, D),
        )
    else:
        mat_qkv = by_rank_heads(gather_rows(qkv_weight).reshape(D, 3 * D), ctx, slots)
        mat_qkv = lax.dynamic_index_in_dim(mat_qkv, rank, 0, keepdims=False)
        mat_fc = by_rank_units(gather_rows(fc_weight).reshape(D, FF), ctx, dp)
        mat_fc = lax.dynamic_index_in_dim(mat_fc, rank, 0, keepdims=False)
        mat_proj = gather_rows(proj_weight).reshape(D, D)
        mats = (mat_qkv, mat_fc, mat_proj)
    made = forward(
        small, hidden_in[0], cotangent[0], unit_rows, doc_start, mats, slots, whole, block
    )
    if whole:
        done = backward(made, hidden_in[0], cotangent[0], doc_start, block)
        return (
            done.output[None],
            done.grad_in[None],
            done.qkv_grad.reshape(-1),
            done.proj_grad.reshape(-1),
            done.fc_out.reshape(-1),
            done.out_grad[:units].reshape(-1),
            done.vec_out[0, :vec_count],
        )
    vectors = made.vectors

    grad_resid, resid_low, sums_two, sums_units, grad_rows, grad_out, output, grad_fc = back(
        made.grad,
        made.resid,
        cotangent[0],
        vectors,
        mat_proj,
        made.qkv_out,
        doc_start,
        made.stats,
        made.ffn_out,
        made.pre_out,
        made.act_out,
        made.cots_out,
        made.part_out,
        block,
    )
    grad_input, sums_one, sums_heads, grad_qkv = last(
        grad_rows,
        mat_qkv,
        made.attn_in_out.reshape(length, D),
        hidden_in[0],
        grad_resid,
        vectors,
    )
    here = (jnp.arange(ctx) == rank)[:, None, None]
    full_fc = from_rank_units(jnp.where(here, grad_fc[None], 0.0), dp).reshape(-1)
    full_qkv = from_rank_heads(jnp.where(here, grad_qkv[None], 0.0), slots).reshape(-1)
    grad_proj = dot(made.own_mixed[:, :D], resid_low, 0, 0).reshape(-1)
    share_fc, share_qkv, share_proj = [
        lax.psum_scatter(full, both, scatter_dimension=0, tiled=True)
        for full in (full_fc, full_qkv, grad_proj)
    ]

    def spread_heads(part):
        padded = jnp.zeros((ctx * width,), WIDE)
        return lax.dynamic_update_slice_in_dim(padded, part, rank * width, 0)[:D]

    sums_units = sums_units[0].reshape(dp, 1, -1)[:, :, :units]
    sums_units = lax.dynamic_update_slice_in_dim(
        jnp.zeros((dp, ctx, units), WIDE), sums_units, rank, 1
    ).reshape(FF)
    vector = jnp.concatenate(
        [
            sums_one[0],
            sums_one[1],
            spread_heads(sums_heads[0, :width]),
            spread_heads(sums_heads[0, 2 * width :]),
            sums_two[0],
            sums_two[1],
            sums_two[2],
            sums_units,
            sums_two[3],
        ]
    ).reshape(owners, vec_count)
    vec_pad = -(-vec_count // 1024) * 1024
    vector = jnp.pad(vector, ((0, 0), (0, vec_pad - vec_count))).reshape(dp, ctx, -1, 128)
    share_vector = sum_vector(vector)
    return (
        output[None],
        grad_input[None],
        share_qkv.astype(WIDE).reshape(-1),
        share_proj.astype(WIDE).reshape(-1),
        share_fc.astype(WIDE).reshape(-1),
        grad_out[:units].reshape(-1),
        share_vector.reshape(-1)[:vec_count],
    )


def solution(mesh):
    flat = P(("dp", "ctx"))
    rows = P("dp", "ctx", None)
    return jax.shard_map(
        shards,
        mesh=mesh,
        in_specs=(rows, flat, flat, flat, flat, flat, P("dp", None), rows),
        out_specs=(rows, rows, flat, flat, flat, flat, flat),
        check_vma=False,
    )
```

```python
import functools

import jax
import jax.numpy as jnp
from jax import lax
from jax.experimental import pallas as pl
from jax.experimental.pallas import tpu as pltpu
from jax.sharding import PartitionSpec as P

D = 1600
HEADS = 25
HEAD_DIM = 64
FF = 6400
EPSILON = 1e-05
LOW = jnp.bfloat16
WIDE = jnp.float32
MIB = 1024 * 1024


def dot(left, right, left_dim=1, right_dim=0):
    return lax.dot_general(
        left, right, (((left_dim,), (right_dim,)), ((), ())), preferred_element_type=WIDE
    )


def normalize(rows):
    centre = rows - jnp.mean(rows, -1, keepdims=True)
    spread = jnp.mean(centre * centre, -1, keepdims=True)
    scale = lax.rsqrt(spread + EPSILON)
    return centre * scale, scale


def norm_back(normed, scale, gain, incoming):
    scaled = gain * incoming
    return scale * (
        scaled
        - jnp.mean(scaled, -1, keepdims=True)
        - normed * jnp.mean(scaled * normed, -1, keepdims=True)
    )


def head_lanes(head, width):
    lane = lax.broadcasted_iota(jnp.int32, (1, width), 1)
    return (lane // HEAD_DIM) == head


def allowed_scores(scores, doc_start, first_query, keys, block):
    key_pos = lax.broadcasted_iota(jnp.int32, (keys, block), 0)
    query_pos = first_query + lax.broadcasted_iota(jnp.int32, (keys, block), 1)
    seen = (key_pos >= doc_start) & (key_pos <= query_pos)
    return jnp.where(seen, scores, -1e30)


def attend_body(block, qkv_ref, start_ref, mixed_ref, stat_ref, value_t):
    length = qkv_ref.shape[0]
    width = mixed_ref.shape[1]
    slots = width // HEAD_DIM
    value_t[...] = qkv_ref[:, 2 * width : 3 * width].astype(WIDE).T.astype(LOW)
    stat_ref[...] = jnp.zeros_like(stat_ref)
    for index in range(length // block):
        keys = (index + 1) * block
        rows = pl.ds(index * block, block)
        key_rows = qkv_ref[0:keys, width : 2 * width]
        doc_start = start_ref[0:1, rows]
        outs = []
        for head in range(slots):
            query = jnp.where(
                head_lanes(head, width), qkv_ref[rows, 0:width] * LOW(HEAD_DIM**-0.5), LOW(0)
            )
            scores = dot(key_rows, query, 1, 1)
            scores = allowed_scores(scores, doc_start, index * block, keys, block)
            top = jnp.max(scores, 0, keepdims=True)
            expo = jnp.exp(scores - top)
            total = jnp.sum(expo, 0, keepdims=True)
            head_rows = slice(head * HEAD_DIM, (head + 1) * HEAD_DIM)
            out = dot(value_t[head_rows, 0:keys], expo.astype(LOW))
            outs.append(out / total)
            stat_ref[head : head + 1, rows] = top + jnp.log(total)
        mixed_ref[rows, :] = jnp.concatenate(outs, 0).T.astype(LOW)


def attend_back_body(
    block, qkv_ref, start_ref, stat_ref, grad_ref, out_ref, key_t, key_grad, value_grad, after
):
    length = qkv_ref.shape[0]
    width = grad_ref.shape[1]
    slots = width // HEAD_DIM
    scale = HEAD_DIM**-0.5
    key_t[...] = qkv_ref[:, width : 2 * width].astype(WIDE).T.astype(LOW)
    key_grad[...] = jnp.zeros_like(key_grad)
    value_grad[...] = jnp.zeros_like(value_grad)
    for index in range(length // block):
        keys = (index + 1) * block
        rows = pl.ds(index * block, block)
        key_rows = qkv_ref[0:keys, width : 2 * width]
        value_rows = qkv_ref[0:keys, 2 * width : 3 * width]
        doc_start = start_ref[0:1, rows]
        outs = []
        for head in range(slots):
            lanes = head_lanes(head, width)
            head_rows = slice(head * HEAD_DIM, (head + 1) * HEAD_DIM)
            query = jnp.where(lanes, qkv_ref[rows, 0:width] * LOW(scale), LOW(0))
            grad = jnp.where(lanes, grad_ref[rows, :], LOW(0))
            scores = dot(key_rows, query, 1, 1)
            scores = allowed_scores(scores, doc_start, index * block, keys, block)
            probs = jnp.exp(scores - stat_ref[head : head + 1, rows])
            grad_probs = dot(value_rows, grad, 1, 1)
            delta = jnp.sum(probs * grad_probs, 0, keepdims=True)
            grad_scores = (probs * (grad_probs - delta)).astype(LOW)
            value_grad[0:keys, :] += dot(probs.astype(LOW), grad)
            key_grad[0:keys, :] += dot(grad_scores, query)
            outs.append(dot(key_t[head_rows, 0:keys], grad_scores))
        out_ref[rows, 0:width] = (jnp.concatenate(outs, 0).T * scale).astype(LOW)
        if index in after:
            after[index]()
    out_ref[:, width : 2 * width] = key_grad[...].astype(LOW)
    out_ref[:, 2 * width : 3 * width] = value_grad[...].astype(LOW)


MESH = pl.DeviceIdType.MESH


def send(src, dst, send_sem, recv_sem, **target):
    return pltpu.make_async_remote_copy(
        src_ref=src,
        dst_ref=dst,
        send_sem=send_sem,
        recv_sem=recv_sem,
        device_id=target,
        device_id_type=MESH,
    )


def greet_line(chips):
    rank = lax.axis_index("ctx")
    chip, core = rank // 2, rank % 2
    barrier = pltpu.get_barrier_semaphore()
    pl.semaphore_signal(barrier, 1, device_id={"ctx": rank + 1 - 2 * core}, device_id_type=MESH)

    @pl.when(chip > 0)
    def _():
        pl.semaphore_signal(barrier, 1, device_id={"ctx": rank - 2}, device_id_type=MESH)

    @pl.when(chip < chips - 1)
    def _():
        pl.semaphore_signal(barrier, 1, device_id={"ctx": rank + 2}, device_id_type=MESH)

    sides = (chip > 0).astype(jnp.int32) + (chip < chips - 1).astype(jnp.int32)
    pl.semaphore_wait(barrier, 1 + sides)


def greet_all(between=lambda: None):
    barrier = pltpu.get_barrier_semaphore()
    count = 0
    for axis in ("ctx", "dp"):
        size = lax.axis_size(axis)
        here = lax.axis_index(axis)

        def one(off, carry, axis=axis, size=size, here=here):
            peer = lax.rem(here + off, size)
            pl.semaphore_signal(barrier, 1, device_id={axis: peer}, device_id_type=MESH)
            return carry

        lax.fori_loop(1, size, one, 0)
        count += size - 1
    between()
    pl.semaphore_wait(barrier, count)


class Swap:
    def __init__(self, axis, source, target, sems):
        self.axis, self.source, self.target = axis, source, target
        self.send_sems, self.recv_sems = sems
        self.rank = lax.axis_index(axis)
        self.size = lax.axis_size(axis)

    def copy(self, peer, origin, target):
        return send(
            self.source(peer),
            self.target(origin),
            self.send_sems.at[peer],
            self.recv_sems.at[origin],
            **{self.axis: target},
        )

    def every(self, act):
        def one(off, carry):
            act(lax.rem(self.rank + off, self.size))
            return carry

        lax.fori_loop(1, self.size, one, 0)

    def start(self):
        self.every(lambda peer: self.copy(peer, self.rank, peer).start())

    def wait(self):
        self.every(lambda peer: self.copy(peer, peer, self.rank).wait_recv())

    def drain(self):
        self.every(lambda peer: self.copy(peer, self.rank, peer).wait_send())

    @staticmethod
    def semaphores(size):
        return [pltpu.SemaphoreType.DMA((size,)), pltpu.SemaphoreType.DMA((size,))]


class ChipSwap(Swap):
    def __init__(self, source, target, sems):
        super().__init__("ctx", source, target, sems)
        self.core = self.rank % 2
        self.rank, self.size = self.rank // 2, self.size // 2

    def copy(self, peer, origin, target):
        return send(
            self.source(peer),
            self.target(origin),
            self.send_sems.at[peer],
            self.recv_sems.at[origin],
            ctx=2 * target + self.core,
        )


class PlaneGather:
    def __init__(self, blocks, sems):
        self.blocks = blocks
        self.size = blocks.shape[0]
        self.rank = lax.axis_index("dp")
        self.square = self.size == 4
        self.send_sems, self.recv_sems = sems
        if self.square:
            self.beside = self.rank + 1 - 2 * (self.rank % 2)
            self.above = self.rank + 2 - 4 * (self.rank // 2)
            half = blocks.shape[1] // 32 * 16
            self.low, self.high = pl.ds(0, half), pl.ds(half, blocks.shape[1] - half)
        else:
            self.swap = Swap("dp", lambda peer: blocks.at[self.rank], blocks.at.__getitem__, sems)

    def copy(self, index, ref, target):
        return send(ref, ref, self.send_sems.at[index], self.recv_sems.at[index], dp=target)

    def start(self):
        if not self.square:
            self.swap.start()
            return
        own = self.blocks.at[self.rank]
        self.copy(0, own, self.beside).start()
        self.copy(1, own, self.above).start()

    def relay(self):
        if not self.square:
            return
        self.copy(0, self.blocks.at[self.beside], self.beside).wait_recv()
        self.copy(2, self.blocks.at[self.beside, self.low], self.above).start()
        self.copy(1, self.blocks.at[self.above], self.above).wait_recv()
        self.copy(3, self.blocks.at[self.above, self.high], self.beside).start()

    def wait(self):
        if not self.square:
            self.swap.wait()
            self.swap.drain()
            return
        far = 3 - self.rank
        own = self.blocks.at[self.rank]
        self.copy(2, self.blocks.at[far, self.low], self.above).wait_recv()
        self.copy(3, self.blocks.at[far, self.high], self.beside).wait_recv()
        self.copy(0, own, self.beside).wait_send()
        self.copy(1, own, self.above).wait_send()
        self.copy(2, self.blocks.at[self.beside, self.low], self.above).wait_send()
        self.copy(3, self.blocks.at[self.above, self.high], self.beside).wait_send()

    semaphores = staticmethod(Swap.semaphores)


class PlaneSum:
    def __init__(self, blocks, landed, sems):
        self.blocks, self.landed = blocks, landed
        self.rank = lax.axis_index("dp")
        self.send_sems, self.recv_sems = sems
        self.swap = Swap("dp", blocks.at.__getitem__, landed.at.__getitem__, sems)
        self.square = blocks.shape[0] == 4
        if self.square:
            self.beside = self.rank + 1 - 2 * (self.rank % 2)
            self.above = self.rank + 2 - 4 * (self.rank // 2)
            half = blocks.shape[1] // 32 * 16
            self.low, self.high = pl.ds(0, half), pl.ds(half, blocks.shape[1] - half)

    def copy(self, index):
        far = 3 - self.rank
        block, slot, rows, target = (
            (far, 0, self.low, self.beside),
            (self.beside, 1, self.low, self.beside),
            (far, 0, self.high, self.above),
            (self.above, 1, self.high, self.above),
            (self.above, 2, self.low, self.above),
            (self.beside, 2, self.high, self.beside),
        )[index]
        return send(
            self.blocks.at[block, rows],
            self.landed.at[slot, rows],
            self.send_sems.at[index],
            self.recv_sems.at[index],
            dp=target,
        )

    def start(self):
        if not self.square:
            self.swap.start()
            return
        for index in range(4):
            self.copy(index).start()

    def relay(self):
        if not self.square:
            return
        for index, block, rows in ((0, self.above, self.low), (2, self.beside, self.high)):
            self.copy(index).wait_recv()
            total = self.blocks[block, rows].astype(WIDE) + self.landed[0, rows].astype(WIDE)
            self.blocks[block, rows] = total.astype(self.blocks.dtype)
            self.copy(4 + index // 2).start()

    def total(self):
        total = self.blocks[self.rank].astype(WIDE)
        if not self.square:
            self.swap.wait()
            for off in range(1, self.swap.size):
                total = total + self.landed[lax.rem(self.rank + off, self.swap.size)].astype(WIDE)
            return total
        for index in (1, 3, 4, 5):
            self.copy(index).wait_recv()
        return total + self.landed[1].astype(WIDE) + self.landed[2].astype(WIDE)

    def drain(self):
        if not self.square:
            self.swap.drain()
            return
        for index in range(6):
            self.copy(index).wait_send()

    @staticmethod
    def semaphores(size):
        return Swap.semaphores(max(size, 6))


class LineGather:
    def __init__(self, blocks, send_sems, recv_sems):
        self.blocks, self.send_sems, self.recv_sems = blocks, send_sems, recv_sems
        self.rank = lax.axis_index("ctx")
        self.chip, self.core = self.rank // 2, self.rank % 2
        self.chips = blocks.shape[0] // 2

    def copy(self, way, origin, target, src=None):
        block = self.blocks.at[origin]
        return send(
            block if src is None else src,
            block,
            self.send_sems.at[way, origin],
            self.recv_sems.at[origin],
            ctx=target,
        )

    def pass_on(self, origin, src=None):
        chip = origin // 2

        @pl.when((chip <= self.chip) & (self.chip < self.chips - 1))
        def _():
            self.copy(0, origin, self.rank + 2, src).start()

        @pl.when((chip >= self.chip) & (self.chip > 0))
        def _():
            self.copy(1, origin, self.rank - 2, src).start()

        self.copy(2, origin, self.rank + 1 - 2 * self.core, src).start()

    def arrive(self, step, part):
        side, other = part % 2, part // 2
        origin_chip = self.chip + jnp.where(side == 0, -step, step)
        origin = 2 * origin_chip + jnp.where(other == 0, self.core, 1 - self.core)
        valid = (origin_chip >= 0) & (origin_chip < self.chips) & ((step > 0) | (side == 0))

        @pl.when(valid & (origin != self.rank))
        def _():
            self.copy(0, origin, self.rank).wait_recv()

            @pl.when(other == 0)
            def _():
                self.pass_on(origin)

        return valid, origin

    def finish(self):
        def one(chip, carry):
            origin = 2 * chip + self.core

            @pl.when((chip <= self.chip) & (self.chip < self.chips - 1))
            def _():
                self.copy(0, origin, self.rank).wait_send()

            @pl.when((chip >= self.chip) & (self.chip > 0))
            def _():
                self.copy(1, origin, self.rank).wait_send()

            self.copy(2, origin, self.rank).wait_send()
            return carry

        lax.fori_loop(0, self.chips, one, 0)

    @staticmethod
    def semaphores(ctx):
        return [pltpu.SemaphoreType.DMA((3, ctx)), pltpu.SemaphoreType.DMA((ctx,))]


class LineSum:
    def __init__(self, blocks, pair, passing, sems):
        self.blocks, self.pair, self.passing = blocks, pair, passing
        self.pair_send, self.pair_recv, self.line_send, self.line_recv = sems
        self.rank = lax.axis_index("ctx")
        self.chip, self.core = self.rank // 2, self.rank % 2
        self.chips = blocks.shape[0] // 2
        self.pieces = self.line_recv.shape[2]
        self.piece = blocks.shape[1] // self.pieces

    def pair_copy(self, chip):
        return send(
            self.blocks.at[2 * chip + 1 - self.core],
            self.pair.at[chip],
            self.pair_send.at[chip],
            self.pair_recv.at[chip],
            ctx=self.rank + 1 - 2 * self.core,
        )

    def line_copy(self, way, chip, piece, target, at):
        rows = pl.ds(piece * self.piece, self.piece)
        slot = jnp.where((way == 1) & (chip == at), self.chips, chip)
        return send(
            self.blocks.at[2 * chip + self.core, rows],
            self.passing.at[slot, rows],
            self.line_send.at[chip, piece],
            self.line_recv.at[way, chip, piece],
            ctx=target,
        )

    def both(self, chip, rows):
        mine = self.blocks[2 * chip + self.core, rows].astype(WIDE)
        return mine + self.pair[chip, rows].astype(WIDE)

    def forward(self, way, chip, valid):
        behind = jnp.where(way == 0, self.chip > 0, self.chip < self.chips - 1)
        target = self.rank + jnp.where(way == 0, 2, -2)

        @pl.when(valid)
        def _():
            self.pair_copy(chip).wait_recv()

            def one(piece, carry):
                rows = pl.ds(pl.multiple_of(piece * self.piece, self.piece), self.piece)
                total = self.both(chip, rows)

                @pl.when(behind)
                def _():
                    self.line_copy(way, chip, piece, target, self.chip).wait_recv()
                    passing = self.passing[chip, rows].astype(WIDE)
                    self.blocks[2 * chip + self.core, rows] = (total + passing).astype(LOW)

                @pl.when(jnp.logical_not(behind))
                def _():
                    self.blocks[2 * chip + self.core, rows] = total.astype(LOW)

                self.line_copy(way, chip, piece, target, target // 2).start()
                return carry

            lax.fori_loop(0, self.pieces, one, 0)

    def near_first(self, step, way):
        last = self.chips - 1
        chip = jnp.where(way == 0, step - self.chip, 2 * last - self.chip - step)
        ahead = jnp.where(way == 0, (chip > self.chip) & (chip <= last), (chip >= 0) & (chip < self.chip))
        self.forward(way, chip, ahead)

    def far_first(self, step, way):
        last = self.chips - 1
        chip = jnp.where(way == 0, last + self.chip - step, step - last + self.chip)
        ahead = jnp.where(way == 0, (chip > self.chip) & (chip <= last), (chip >= 0) & (chip < self.chip))
        self.forward(way, chip, ahead)

    def send_pairs(self):
        def one(chip, carry):
            self.pair_copy(chip).start()
            return carry

        lax.fori_loop(0, self.chips, one, 0)

    def far_steps(self, begin, end):
        def one(index, carry):
            self.far_first(index // 2, index % 2)
            return carry

        lax.fori_loop(2 * begin, 2 * end, one, 0)

    def finish(self, out):
        self.pair_copy(self.chip).wait_recv()

        def one(piece, carry):
            rows = pl.ds(pl.multiple_of(piece * self.piece, self.piece), self.piece)
            out[rows] = self.both(self.chip, rows)

            @pl.when(self.chip > 0)
            def _():
                self.line_copy(0, self.chip, piece, self.rank, self.chip).wait_recv()
                out[rows] = out[rows] + self.passing[self.chip, rows].astype(WIDE)

            @pl.when(self.chip < self.chips - 1)
            def _():
                self.line_copy(1, self.chip, piece, self.rank, self.chip).wait_recv()
                out[rows] = out[rows] + self.passing[self.chips, rows].astype(WIDE)

            return carry

        lax.fori_loop(0, self.pieces, one, 0)

        def sent(chip, carry):
            self.pair_copy(chip).wait_send()

            @pl.when(chip != self.chip)
            def _():
                for piece in range(self.pieces):
                    self.line_copy(0, chip, piece, self.rank, self.chip).wait_send()

            return carry

        lax.fori_loop(0, self.chips, sent, 0)

    @staticmethod
    def scratch(ctx, rows, columns, pieces):
        chips = ctx // 2
        return [
            pltpu.VMEM((ctx, rows, columns), LOW),
            pltpu.VMEM((chips, rows, columns), LOW),
            pltpu.VMEM((chips + 1, rows, columns), LOW),
            pltpu.SemaphoreType.DMA((chips,)),
            pltpu.SemaphoreType.DMA((chips,)),
            pltpu.SemaphoreType.DMA((chips, pieces)),
            pltpu.SemaphoreType.DMA((2, chips, pieces)),
        ]


VMEM = pl.BlockSpec(memory_space=pltpu.VMEM)
HBM = pl.BlockSpec(memory_space=pl.ANY)


def params(number):
    return pltpu.CompilerParams(
        vmem_limit_bytes=63 * MIB, collective_id=number, has_side_effects=True
    )


def packed_rows(count, columns):
    tiles = -(-columns // 128)
    main = count // 16 * 16
    return tiles * main + -(-(tiles * (count - main)) // 16) * 16


def pack(out, index, rows, first, count, lane, columns):
    tiles = -(-columns // 128)
    main = count // 16 * 16
    for tile in range(tiles):
        lanes = slice(lane + tile * 128, lane + tile * 128 + 128)
        part = rows[first : first + main, lanes]
        out[index, tile * main : (tile + 1) * main] = part.astype(LOW)
    left = [
        rows[first + row : first + row + 1, lane + tile * 128 : lane + tile * 128 + 128]
        for row in range(main, count)
        for tile in range(tiles)
    ]
    space = out.shape[1] - tiles * main
    if space:
        left.append(jnp.zeros((space - len(left), 128), WIDE))
        out[index, tiles * main :] = jnp.concatenate(left, 0).astype(LOW)


def unpack(packed, rows, first, count, columns):
    tiles = -(-columns // 128)
    main = count // 16 * 16
    for tile in range(tiles):
        lanes = slice(tile * 128, tile * 128 + 128)
        rows[first : first + main, lanes] = packed[tile * main : (tile + 1) * main].astype(WIDE)
    left = packed[tiles * main :].astype(WIDE)
    for row in range(main, count):
        for tile in range(tiles):
            place = (row - main) * tiles + tile
            lanes = slice(tile * 128, tile * 128 + 128)
            rows[first + row : first + row + 1, lanes] = left[place : place + 1]


def full_lanes(columns):
    return -(-columns // 128) * 128


def head_pieces(ctx, slots):
    width = slots * HEAD_DIM
    pieces = []
    for rank in range(ctx):
        count = min(width, D - rank * width)
        if count > 0:
            for part in range(3):
                pieces.append((rank, part * width, part * D + rank * width, count))
    return pieces


def unit_pieces(ctx, dp):
    units = FF // (ctx * dp)
    return [
        (rank, seq * padded_units(units), (seq * ctx + rank) * units, units)
        for rank in range(ctx)
        for seq in range(dp)
    ]


def divide(rows_ref, wide, blocks, pieces, columns):
    count = rows_ref.shape[0]
    lanes = full_lanes(columns)
    for rank in range(blocks.shape[0]):
        wide[...] = jnp.zeros_like(wide)
        for owner, here, there, size in pieces:
            if owner == rank:
                wide[0:count, here : here + size] = rows_ref[:, there : there + size].astype(WIDE)
        pack(blocks, rank, wide, 0, count, 0, lanes)


class Spread:
    def __init__(self, blocks, landed, wide, out, sems):
        self.blocks, self.landed, self.wide, self.out = blocks, landed, wide, out
        self.swap = Swap("ctx", blocks.at.__getitem__, landed.at.__getitem__, sems[:2])
        self.plane = PlaneGather(out, sems[2:])

    def start(self):
        self.swap.start()
        self.landed[self.swap.rank] = self.blocks[self.swap.rank]

    def cross(self):
        self.swap.wait()
        count = self.out.shape[1] // self.swap.size
        columns = self.out.shape[2]
        for index in range(self.swap.size):
            unpack(self.landed[index], self.wide, index * count, count, columns)
        self.out[self.plane.rank] = self.wide[:, 0:columns].astype(LOW)
        self.plane.start()

    def wait(self):
        self.plane.wait()

    @staticmethod
    def scratch(ctx, dp, rows, columns):
        return [
            pltpu.VMEM((ctx, packed_rows(rows // ctx, columns), 128), LOW),
            pltpu.VMEM((rows, full_lanes(columns)), WIDE),
            *Swap.semaphores(ctx),
            *PlaneGather.semaphores(dp),
        ]


class StreamSum:
    def __init__(self, parts, landed, stage, stage_sems, sems):
        self.parts, self.landed, self.stage, self.stage_sems = parts, landed, stage, stage_sems
        self.plane = PlaneSum(parts, landed, sems)

    def put(self, index, part):
        if index >= 2:
            self.move(index - 2).wait()
        self.stage[index % 2] = part.astype(LOW)
        self.move(index).start()

    def move(self, index):
        slot = index % 2
        return pltpu.make_async_copy(
            self.stage.at[slot], self.parts.at[index], self.stage_sems.at[slot]
        )

    def start(self):
        self.move(2).wait()
        self.move(3).wait()
        self.plane.start()

    def load(self, source, slot, rows):
        return pltpu.make_async_copy(
            source.at[rows], self.stage.at[slot, rows], self.stage_sems.at[slot]
        )

    def relayed(self, index):
        plane = self.plane
        rows, target = ((plane.low, plane.above), (plane.high, plane.beside))[index]
        return send(
            self.stage.at[2, rows],
            self.landed.at[2, rows],
            plane.send_sems.at[4 + index],
            plane.recv_sems.at[4 + index],
            dp=target,
        )

    def relay(self):
        plane = self.plane
        for index, block, rows in ((0, plane.above, plane.low), (1, plane.beside, plane.high)):
            plane.copy(2 * index).wait_recv()
            loads = (
                self.load(self.parts.at[block], 0, rows),
                self.load(self.landed.at[0], 1, rows),
            )
            for load in loads:
                load.start()
            for load in loads:
                load.wait()
            total = self.stage[0, rows].astype(WIDE) + self.stage[1, rows].astype(WIDE)
            self.stage[2, rows] = total.astype(LOW)
            self.relayed(index).start()

    def total(self):
        plane = self.plane
        for index in range(4):
            plane.copy(index).wait_send()
        plane.copy(1).wait_recv()
        plane.copy(3).wait_recv()
        for index in range(2):
            self.relayed(index).wait_send()
            self.relayed(index).wait_recv()
        every = pl.ds(0, self.parts.shape[1])
        loads = (
            self.load(self.parts.at[plane.rank], 0, every),
            self.load(self.landed.at[1], 1, every),
            self.load(self.landed.at[2], 2, every),
        )
        for load in loads:
            load.start()
        for load in loads:
            load.wait()
        total = self.stage[0].astype(WIDE) + self.stage[1].astype(WIDE)
        return total + self.stage[2].astype(WIDE)


class Collect:
    def __init__(self, pieces, plane, wide, blocks, came, out, sems):
        self.pieces, self.plane, self.wide, self.blocks = pieces, plane, wide, blocks
        self.came, self.out = came, out
        self.swap = Swap("ctx", blocks.at.__getitem__, came.at.__getitem__, sems)

    def cross(self):
        rows, columns = self.plane.parts.shape[1:]
        lanes = full_lanes(columns)
        self.wide[0:rows, 0:columns] = self.plane.total()
        if lanes > columns:
            self.wide[0:rows, columns:lanes] = jnp.zeros((rows, lanes - columns), WIDE)
        count = rows // self.swap.size
        for index in range(self.swap.size):
            pack(self.blocks, index, self.wide, index * count, count, 0, columns)
        self.swap.start()
        self.came[self.swap.rank] = self.blocks[self.swap.rank]

    def wait(self):
        self.swap.wait()
        count = self.out.shape[0]
        for rank in range(self.swap.size):
            unpack(self.came[rank], self.wide, 0, count, self.plane.parts.shape[2])
            for owner, here, there, size in self.pieces:
                if owner == rank:
                    self.out[:, there : there + size] = self.wide[0:count, here : here + size]
        self.swap.drain()


class Projection:
    def __init__(self, rows, blocks, wide, out, sems):
        self.rows, self.blocks, self.wide, self.out = rows, blocks, wide, out
        self.rank = lax.axis_index("ctx")
        self.core = self.rank % 2
        self.packed = rows.shape[1]
        self.plane = PlaneGather(blocks.at[self.core], sems[:2])
        self.send_sems, self.recv_sems = sems[2:4]
        self.swap = ChipSwap(lambda peer: rows.at[0], self.place, sems[4:])

    def place(self, chip):
        rows = pl.ds(pl.multiple_of(chip * self.packed, self.packed), self.packed)
        return self.blocks.at[self.core, self.plane.rank, rows]

    def start(self):
        self.swap.start()
        rows = pl.ds(pl.multiple_of(self.swap.rank * self.packed, self.packed), self.packed)
        self.blocks[self.core, self.plane.rank, rows] = self.rows[0]

    def cross(self):
        self.swap.wait()
        self.plane.start()
        self.to_other(self.plane.rank).start()

    def to_other(self, seq):
        block = self.blocks.at[self.core, seq]
        return send(
            block,
            block,
            self.send_sems.at[seq],
            self.recv_sems.at[seq],
            ctx=self.rank + 1 - 2 * self.core,
        )

    def wait(self):
        self.plane.wait()

        def others(off, carry):
            self.to_other(lax.rem(self.plane.rank + off, self.plane.size)).start()
            return carry

        lax.fori_loop(1, self.plane.size, others, 0)
        ctx = 2 * self.swap.size
        count = self.out.shape[1] // ctx

        def order(off, carry):
            seq = lax.rem(self.plane.rank + off, self.plane.size)
            self.to_other(seq).wait_recv()
            for rank in range(ctx):
                first = rank // 2 * self.packed
                rows = self.blocks[rank % 2, seq, first : first + self.packed]
                unpack(rows, self.wide, rank * count, count, D)
            self.out[seq] = self.wide[:, 0:D].astype(LOW)
            return carry

        lax.fori_loop(0, self.plane.size, order, 0)

        def sent(seq, carry):
            self.to_other(seq).wait_send()
            return carry

        lax.fori_loop(0, self.plane.size, sent, 0)
        self.swap.drain()

    @staticmethod
    def scratch(ctx, dp):
        packed = packed_rows(D // (dp * ctx), D)
        return [
            pltpu.VMEM((2, dp, ctx // 2 * packed, 128), LOW),
            pltpu.VMEM((D // dp, full_lanes(D)), WIDE),
            *PlaneGather.semaphores(dp),
            *Swap.semaphores(dp),
            *Swap.semaphores(ctx // 2),
        ]


def vector_pieces(owners, count):
    pieces = []
    for owner in range(owners):
        begin = 0
        while begin < count:
            place = owner * count + begin
            size = min(count - begin, D - place % D)
            pieces.append((owner, begin, place // D, place % D, size))
            begin += size
    return pieces


def unit_bias_pieces(rank, ctx, dp):
    units = FF // (ctx * dp)
    pieces = []
    for seq in range(dp):
        begin = 0
        while begin < units:
            place = (seq * ctx + rank) * units + begin
            size = min(units - begin, D - place % D)
            pieces.append((seq * padded_units(units) + begin, 7 + place // D, place % D, size))
            begin += size
    return pieces


GAIN_ONE, SHIFT_ONE, BIAS_QUERY, BIAS_VALUE, BIAS_PROJ, GAIN_TWO, SHIFT_TWO = range(7)
BIAS_OUT = 11
ROWS = 16


class Build:
    def __init__(self):
        self.ins, self.outs, self.scratch = {}, {}, {}

    def take(self, spec, **values):
        self.ins.update({name: (value, spec) for name, value in values.items()})

    def give(self, kind, spec, **shapes):
        for name, shape in shapes.items():
            self.outs[name] = (jax.ShapeDtypeStruct(shape, kind), spec)

    def hold(self, kind, **shapes):
        self.scratch.update({name: pltpu.VMEM(shape, kind) for name, shape in shapes.items()})

    def sems(self, **shapes):
        self.scratch.update(
            {name: pltpu.SemaphoreType.DMA(shape) for name, shape in shapes.items()}
        )

    def both(self, **sizes):
        for name, size in sizes.items():
            self.sems(**{name + "_send": (size,), name + "_recv": (size,)})

    def line_sum(self, name, ctx, tokens):
        chips = ctx // 2
        shapes = (ctx, tokens, D), (chips, tokens, D), (chips + 1, tokens, D)
        for part, shape in zip(("_blocks", "_pair", "_passing"), shapes, strict=True):
            self.hold(LOW, **{name + part: shape})
        self.both(**{name + "_pair": chips})
        self.sems(
            **{name + "_line_send": (chips, PIECES), name + "_line_recv": (2, chips, PIECES)}
        )

    def call(self, kernel, number, label):
        names = (*self.ins, *self.outs, *self.scratch)
        results = pl.pallas_call(
            functools.partial(kernel, names),
            out_shape=[shape for shape, _ in self.outs.values()],
            in_specs=[spec for _, spec in self.ins.values()],
            out_specs=[spec for _, spec in self.outs.values()],
            scratch_shapes=list(self.scratch.values()),
            compiler_params=params(number),
            name=label,
        )(*[value for value, _ in self.ins.values()])
        return Names(tuple(self.outs), results)


PIECES = 8


class Names:
    def __init__(self, names, refs):
        self.__dict__.update(zip(names, refs, strict=True))


def forward_kernel(block, whole, names, *refs):
    r = Names(names, refs)
    seq, rank = lax.axis_index("dp"), lax.axis_index("ctx")
    ctx, tokens, _ = r.rows.shape
    dp, units = r.units.shape[:2]
    width = r.mixed.shape[1]
    vec_count = 12 * D // (ctx * dp)

    def out(ref, target, index):
        return pltpu.make_async_copy(ref, target, r.out_sems.at[index])

    rows_in = LineGather(r.rows, r.rows_send, r.rows_recv)
    cots = LineGather(r.cots, r.cots_send, r.cots_recv)
    feed = LineGather(r.rows, r.feed_send, r.feed_recv)
    total = LineSum(
        r.sum_blocks,
        r.sum_pair,
        r.sum_passing,
        (r.sum_pair_send, r.sum_pair_recv, r.sum_line_send, r.sum_line_recv),
    )
    chips = feed.chips
    line = Swap(
        "ctx",
        lambda peer: r.small,
        lambda origin: r.smalls.at[seq, origin],
        (r.line_send, r.line_recv),
    )
    plane = Swap(
        "dp",
        lambda peer: r.smalls.at[seq],
        r.smalls.at.__getitem__,
        (r.plane_send, r.plane_recv),
    )
    unit_rows = PlaneGather(r.units, (r.units_send, r.units_recv))
    to_tokens = Swap(
        "ctx",
        lambda peer: r.mixed.at[pl.ds(pl.multiple_of(peer * tokens, tokens), tokens)],
        lambda origin: r.own_mixed.at[:, pl.ds(pl.multiple_of(origin * width, width), width)],
        (r.mixed_send, r.mixed_recv),
    )
    if whole:
        heads = Spread(
            r.qkv_blocks,
            r.qkv_landed,
            r.qkv_wide,
            r.qkv_mat,
            (r.qkv_send, r.qkv_recv, r.qkv_plane_send, r.qkv_plane_recv),
        )
        columns = Spread(
            r.fc_blocks,
            r.fc_landed,
            r.fc_wide,
            r.fc_mat,
            (r.fc_send, r.fc_recv, r.fc_plane_send, r.fc_plane_recv),
        )
        proj = Projection(
            r.proj_packed,
            r.proj_blocks,
            r.proj_wide,
            r.proj_mat,
            (
                r.proj_plane_send,
                r.proj_plane_recv,
                r.proj_pair_send,
                r.proj_pair_recv,
                r.proj_send,
                r.proj_recv,
            ),
        )

    def prepare():
        own = r.in_t[...].astype(WIDE).T.astype(LOW)
        r.own_in[...] = own
        r.rows[rank] = own
        r.smalls[seq, rank] = r.small[...]
        main = r.own_units.shape[0] // 16 * 16
        r.units[seq, 0:main] = r.own_units[0:main]
        if units > main:
            left = r.own_units[main:].astype(WIDE)
            zeros = jnp.zeros((units - r.own_units.shape[0], D), WIDE)
            r.units[seq, main:] = jnp.concatenate([left, zeros], 0).astype(LOW)
        if whole:
            pieces = head_pieces(ctx, width // HEAD_DIM)
            divide(r.qkv_rows, r.qkv_lanes, r.qkv_blocks, pieces, 3 * width)

    greet_all(prepare)

    line.start()
    if whole:
        heads.start()
    unit_rows.start()
    if whole:
        count = r.proj_rows.shape[0]
        r.proj_lanes[0:count, 0:D] = r.proj_rows[...].astype(WIDE)
        r.proj_lanes[0:count, D:] = jnp.zeros((count, full_lanes(D) - D), WIDE)
        pack(r.proj_packed, 0, r.proj_lanes, 0, count, 0, D)
        heads.swap.drain()
        proj.start()
    rows_in.pass_on(rank)
    own_cot = r.cot_t[...].astype(WIDE).T.astype(LOW)
    r.own_cot[...] = own_cot
    r.cots[rank] = own_cot
    line.wait()
    plane.start()
    if whole:
        heads.cross()
        divide(r.fc_rows, r.fc_lanes, r.fc_blocks, unit_pieces(ctx, dp), dp * units)

    def arrivals(gather):
        def arrive(index, carry):
            gather.arrive(1 + index // 4, index % 4)
            return carry

        return arrive

    rows_in.arrive(0, 2)
    lax.fori_loop(0, 4, arrivals(rows_in), 0)
    if whole:
        heads.plane.relay()
        columns.start()
        proj.cross()
    lax.fori_loop(4, 4 * (chips - 1), arrivals(rows_in), 0)
    if whole:
        proj.plane.relay()
    rows_in.finish()
    docs = jnp.broadcast_to(r.docs[...], r.doc_start.shape)
    lane = lax.broadcasted_iota(jnp.int32, docs.shape, 1)
    doc_start = jnp.where(docs != pltpu.roll(docs, 1, 1), lane, 0)
    shift = 1
    while shift < docs.shape[1]:
        earlier = jnp.where(lane >= shift, pltpu.roll(doc_start, shift, 1), 0)
        doc_start = jnp.maximum(doc_start, earlier)
        shift *= 2
    r.doc_start[...] = doc_start
    plane.wait()
    r.vectors[...] = jnp.zeros_like(r.vectors)
    for owner, begin, row, lane, size in vector_pieces(ctx * dp, vec_count):
        r.vectors[row : row + 1, lane : lane + size] = r.smalls[
            owner // ctx, owner % ctx, 0:1, begin : begin + size
        ]
    r.bias_units[...] = jnp.zeros_like(r.bias_units)
    for owner in range(ctx):

        @pl.when(rank == owner)
        def _(owner=owner):
            for here, row, lane, size in unit_bias_pieces(owner, ctx, dp):
                r.bias_units[0:1, here : here + size] = r.vectors[row : row + 1, lane : lane + size]

    if whole:
        heads.wait()
        out(r.qkv_mat, r.qkv_mat_out, 0).start()
    mine = pl.ds(pl.multiple_of(rank * width, width), width)
    bias = jnp.concatenate(
        [
            r.vectors[BIAS_QUERY : BIAS_QUERY + 1, mine],
            jnp.zeros((1, width), WIDE),
            r.vectors[BIAS_VALUE : BIAS_VALUE + 1, mine],
        ],
        1,
    )

    def project(index, carry):
        both = pl.ds(2 * index, 2)
        normed, _ = normalize(r.rows[both].reshape(2 * tokens, D).astype(WIDE))
        attn_in = normed * r.vectors[GAIN_ONE : GAIN_ONE + 1, 0:D]
        attn_in = (attn_in + r.vectors[SHIFT_ONE : SHIFT_ONE + 1, 0:D]).astype(LOW)
        r.rows[both] = attn_in.reshape(2, tokens, D)
        rows = pl.ds(pl.multiple_of(2 * index * tokens, 2 * tokens), 2 * tokens)
        r.qkv[rows] = (dot(attn_in, r.qkv_mat[...].reshape(D, 3 * width)) + bias).astype(LOW)
        return carry

    lax.fori_loop(0, chips, project, 0)
    out(r.rows, r.attn_in_out, 1).start()
    out(r.qkv, r.qkv_out, 2).start()
    cots.pass_on(rank)
    if whole:
        columns.cross()
    attend_body(block, r.qkv, r.doc_start, r.mixed, r.stats, r.value_t)
    out(r.rows, r.attn_in_out, 1).wait()
    to_tokens.start()
    r.own_mixed[:, mine] = r.mixed[pl.ds(pl.multiple_of(rank * tokens, tokens), tokens)]
    if whole:
        proj.wait()
        out(r.proj_mat, r.proj_mat_out, 3).start()
        columns.plane.relay()
    unit_rows.relay()
    to_tokens.wait()
    resid = dot(r.own_mixed[:, 0:D], r.proj_mat[...].reshape(D, D))
    resid = resid + r.own_in[...].astype(WIDE) + r.vectors[BIAS_PROJ : BIAS_PROJ + 1, 0:D]
    r.resid[...] = resid
    normed, _ = normalize(resid)
    ffn_in = normed * r.vectors[GAIN_TWO : GAIN_TWO + 1, 0:D]
    r.rows[rank] = (ffn_in + r.vectors[SHIFT_TWO : SHIFT_TWO + 1, 0:D]).astype(LOW)
    feed.pass_on(rank)
    cots.arrive(0, 2)
    lax.fori_loop(0, 4, arrivals(cots), 0)
    unit_rows.wait()
    if whole:
        columns.wait()

    def keep(chip, slot, which=range(3)):
        both = pl.ds(2 * chip, 2)
        kept = ((r.act, r.act_out), (r.pre, r.pre_out), (r.part, r.part_out))
        return [
            pltpu.make_async_copy(
                kept[index][0].at[slot], kept[index][1].at[both], r.keep_sems.at[index, slot]
            )
            for index in which
        ]

    def pass_rows(chip):
        both = pl.ds(2 * chip, 2)
        return [
            pltpu.make_async_copy(ref.at[both], target.at[both], r.pass_sems.at[index, chip])
            for index, (ref, target) in enumerate(((r.rows, r.ffn_out), (r.cots, r.cots_out)))
        ]

    def work(chip, done):
        both = pl.ds(2 * chip, 2)
        slot = done % 2

        @pl.when(done >= 2)
        def _():
            for copy in keep(chip, slot):
                copy.wait()

        for copy in pass_rows(chip):
            copy.start()
        fc = r.fc_mat[...].reshape(D, dp * units)
        mat = r.units[...].reshape(dp * units, D)
        pre = dot(r.rows[both].reshape(2 * tokens, D), fc) + r.bias_units[0:1]
        bend = jnp.tanh(0.7978845608028654 * (pre + 0.044715 * pre * pre * pre))
        act = (0.5 * pre * (1.0 + bend)).astype(LOW)
        r.act[slot] = act.reshape(2, tokens, -1)
        slope = 0.5 * (1.0 + bend) + 0.5 * pre * (1.0 - bend * bend) * 0.7978845608028654 * (
            1.0 + 3 * 0.044715 * pre * pre
        )
        grad_act = dot(r.cots[both].reshape(2 * tokens, D), mat, 1, 1)
        grad_pre = (slope * grad_act).astype(LOW)
        r.pre[slot] = grad_pre.reshape(2, tokens, -1)
        r.sum_blocks[both] = dot(grad_pre, fc, 1, 1).astype(LOW).reshape(2, tokens, D)
        total.pair_copy(chip).start()
        for copy in keep(chip, slot, (0, 1)):
            copy.start()

    def give_out(chip, done):
        slot = done % 2
        act = r.act[slot].reshape(2 * tokens, dp * units)
        mat = r.units[...].reshape(dp * units, D)
        r.part[slot] = dot(act, mat).astype(LOW).reshape(2, tokens, D)
        keep(chip, slot, (2,))[0].start()

    def step(index, done):
        distance, side = index // 2, index % 2
        near = distance < chips
        origin_chip = rank // 2 + jnp.where(side == 0, -distance, distance)
        valid = near & (origin_chip >= 0) & (origin_chip < chips) & ((distance > 0) | (side == 0))

        @pl.when(near)
        def _():
            @pl.when(side == 0)
            def _():
                @pl.when(distance > 1)
                def _():
                    cots.arrive(distance, 0)
                    cots.arrive(distance, 1)

                feed.arrive(distance, 0)
                feed.arrive(distance, 1)

            @pl.when(distance > 1)
            def _():
                cots.arrive(distance, 2 + side)

            feed.arrive(distance, 2 + side)

            @pl.when(valid)
            def _():
                work(origin_chip, done)

        after = done + valid.astype(jnp.int32)

        @pl.when(side == 1)
        def _():
            def way(index, carry):
                total.near_first(distance, index)
                return carry

            lax.fori_loop(0, 2, way, 0)

            def output(index, carry):
                chip = rank // 2 + jnp.where(index == 0, -distance, distance)
                here = near & (chip >= 0) & (chip < chips) & ((distance > 0) | (index == 0))
                later = (index == 0) & valid & (distance > 0)

                @pl.when(here)
                def _():
                    give_out(chip, after - 1 - later.astype(jnp.int32))

                return carry

            lax.fori_loop(0, 2, output, 0)

        return after

    lax.fori_loop(0, 2 * (2 * chips - 1), step, jnp.int32(0))
    total.finish(r.grad)

    feed.finish()
    cots.finish()
    line.drain()
    plane.drain()
    to_tokens.drain()
    for slot in range(2):
        for copy in keep(0, slot):
            copy.wait()

    def passed(chip, carry):
        for copy in pass_rows(chip):
            copy.wait()
        return carry

    lax.fori_loop(0, chips, passed, 0)
    out(r.qkv, r.qkv_out, 2).wait()
    if whole:
        out(r.qkv_mat, r.qkv_mat_out, 0).wait()
        out(r.proj_mat, r.proj_mat_out, 3).wait()
        columns.swap.drain()


def forward(small, in_t, cot_t, unit_rows, docs, mats, slots, whole, block):
    ctx, dp = lax.axis_size("ctx"), lax.axis_size("dp")
    tokens = in_t.shape[1]
    length = ctx * tokens
    width = slots * HEAD_DIM
    units = padded_units(unit_rows.shape[0])
    columns = dp * units
    chips = ctx // 2
    rows = D // dp
    count = rows // ctx
    high = -(-count // 8) * 8
    b = Build()
    b.take(VMEM, small=small, in_t=in_t, cot_t=cot_t, own_units=unit_rows, docs=docs)
    if whole:
        b.take(VMEM, qkv_rows=mats[0], fc_rows=mats[1], proj_rows=mats[2])
    else:
        b.take(VMEM, qkv_mat=mats[0], fc_mat=mats[1], proj_mat=mats[2])
    b.give(
        WIDE,
        VMEM,
        vectors=(ROWS, max(full_lanes(D), ctx * width)),
        stats=(8, length),
        resid=(tokens, D),
        grad=(tokens, D),
    )
    b.give(
        LOW, VMEM, own_mixed=(tokens, ctx * width), own_in=(tokens, D), own_cot=(tokens, D)
    )
    b.give(jnp.int32, VMEM, doc_start=(8, length))
    b.give(
        LOW,
        HBM,
        attn_in_out=(ctx, tokens, D),
        qkv_out=(length, 3 * width),
        cots_out=(ctx, tokens, D),
        ffn_out=(ctx, tokens, D),
        act_out=(ctx, tokens, columns),
        pre_out=(ctx, tokens, columns),
        part_out=(ctx, tokens, D),
    )
    if whole:
        b.give(LOW, HBM, qkv_mat_out=(dp, rows, 3 * width), proj_mat_out=(dp, rows, D))
    b.hold(
        LOW,
        rows=(ctx, tokens, D),
        cots=(ctx, tokens, D),
        units=(dp, units, D),
        qkv=(length, 3 * width),
        mixed=(length, width),
        value_t=(width, length),
        act=(2, 2, tokens, columns),
        pre=(2, 2, tokens, columns),
        part=(2, 2, tokens, D),
    )
    b.hold(WIDE, smalls=(dp, ctx, *small.shape), bias_units=(8, columns))
    b.line_sum("sum", ctx, tokens)
    b.sems(
        out_sems=(4,),
        keep_sems=(3, 2),
        pass_sems=(2, chips),
        rows_send=(3, ctx),
        rows_recv=(ctx,),
        cots_send=(3, ctx),
        cots_recv=(ctx,),
        feed_send=(3, ctx),
        feed_recv=(ctx,),
    )
    b.both(line=ctx, plane=dp, units=max(dp, 4), mixed=ctx)
    if whole:
        for name, lanes in (("qkv", 3 * width), ("fc", columns)):
            packed = (ctx, packed_rows(count, lanes), 128)
            b.hold(WIDE, **{name + "_lanes": (high, full_lanes(lanes))})
            b.hold(WIDE, **{name + "_wide": (rows, full_lanes(lanes))})
            b.hold(LOW, **{name + "_blocks": packed, name + "_landed": packed})
            b.hold(LOW, **{name + "_mat": (dp, rows, lanes)})
            b.both(**{name: ctx, name + "_plane": max(dp, 4)})
        packed = packed_rows(count, D)
        b.hold(WIDE, proj_lanes=(high, full_lanes(D)), proj_wide=(rows, full_lanes(D)))
        b.hold(
            LOW,
            proj_packed=(1, packed, 128),
            proj_blocks=(2, dp, chips * packed, 128),
            proj_mat=(dp, rows, D),
        )
        b.both(proj_plane=max(dp, 4), proj_pair=dp, proj=chips)
    return b.call(functools.partial(forward_kernel, block, whole), 0, "forward")


def back_kernel(
    block,
    grad_ref,
    resid_ref,
    own_cot,
    vectors_ref,
    proj_ref,
    qkv_ref,
    start_ref,
    stat_ref,
    ffn_hbm,
    pre_hbm,
    act_hbm,
    cot_hbm,
    part_hbm,
    resid_out,
    low_out,
    vector_out,
    units_out,
    rows_out,
    share_out,
    output_ref,
    fc_out,
    ffn,
    pre,
    act,
    cot,
    load_sems,
    own_grad,
    head_grad,
    key_t,
    key_grad,
    value_grad,
    *refs,
):
    total = LineSum(*refs[:3], refs[3:7])
    loads = [
        pltpu.make_async_copy(src, dst, load_sems.at[index])
        for index, (src, dst) in enumerate(
            (
                (part_hbm, total.blocks),
                (ffn_hbm, ffn),
                (pre_hbm, pre),
                (act_hbm, act),
                (cot_hbm, cot),
            )
        )
    ]
    for load in loads:
        load.start()
    tokens = own_cot.shape[0]
    length, width = head_grad.shape
    units = share_out.shape[0]
    swap = Swap(
        "ctx",
        lambda peer: own_grad.at[:, pl.ds(pl.multiple_of(peer * width, width), width)],
        lambda origin: head_grad.at[pl.ds(pl.multiple_of(origin * tokens, tokens), tokens)],
        refs[7:9],
    )
    share = PlaneSum(refs[9], refs[10], refs[11:13])
    dp = share.swap.size
    greet_all()
    loads[0].wait()
    total.send_pairs()
    grad = grad_ref[...]
    normed, scale = normalize(resid_ref[...])
    grad_resid = own_cot[...].astype(WIDE) + norm_back(normed, scale, vectors_ref[GAIN_TWO : GAIN_TWO + 1, 0:D], grad)
    resid_out[...] = grad_resid
    low = grad_resid.astype(LOW)
    low_out[...] = low
    own_grad[:, 0:D] = dot(low, proj_ref[...], 1, 1).astype(LOW)
    own_grad[:, D:] = jnp.zeros((tokens, own_grad.shape[1] - D), LOW)
    swap.start()
    head_grad[pl.ds(pl.multiple_of(swap.rank * tokens, tokens), tokens)] = own_grad[
        :, pl.ds(pl.multiple_of(swap.rank * width, width), width)
    ]
    vector_out[0:1] = jnp.sum(grad_resid, 0, keepdims=True)
    vector_out[1:2] = jnp.sum(grad * normed, 0, keepdims=True)
    vector_out[2:3] = jnp.sum(grad, 0, keepdims=True)
    vector_out[3:4] = jnp.sum(own_cot[...].astype(WIDE), 0, keepdims=True)
    vector_out[4:8] = jnp.zeros((4, D), WIDE)
    loads[1].wait()
    loads[2].wait()
    grad_pre = pre[...].reshape(length, -1)
    units_out[...] = dot(jnp.ones((8, length), LOW), grad_pre)
    for index in range(dp):
        rows = slice(index * (D // dp), (index + 1) * (D // dp))
        fc_out[rows] = dot(ffn[:, :, rows].reshape(length, D // dp), grad_pre, 0, 0)
    total.far_steps(0, 1)
    loads[3].wait()
    loads[4].wait()
    for index in range(dp):
        rows = slice(index * units, (index + 1) * units)
        part = dot(act[:, :, rows].reshape(length, units), cot[...].reshape(length, D), 0, 0)
        share.blocks[index] = part.astype(LOW)
    share.start()
    swap.wait()
    chips = total.chips

    def first():
        total.far_steps(1, 2)

    def second():
        total.far_steps(2, 3)
        share.relay()

    attend_back_body(
        block,
        qkv_ref,
        start_ref,
        stat_ref,
        head_grad,
        rows_out,
        key_t,
        key_grad,
        value_grad,
        {1: first, 2: second},
    )
    total.far_steps(3, 2 * chips - 1)
    total.finish(output_ref)
    bias = vectors_ref[BIAS_OUT : BIAS_OUT + 1, 0:D]
    output_ref[...] = output_ref[...] + resid_ref[...] + bias
    share_out[...] = share.total()
    swap.drain()
    share.drain()


def back(
    grad, resid, own_cot, vectors, proj, qkv, doc_start, stats, ffn, pre, act, cot, part, block
):
    ctx, tokens, _ = cot.shape
    dp = lax.axis_size("dp")
    length = ctx * tokens
    width = qkv.shape[1] // 3
    columns = act.shape[2]
    units = columns // dp
    shapes = [
        jax.ShapeDtypeStruct((tokens, D), WIDE),
        jax.ShapeDtypeStruct((tokens, D), LOW),
        jax.ShapeDtypeStruct((8, D), WIDE),
        jax.ShapeDtypeStruct((8, columns), WIDE),
        jax.ShapeDtypeStruct((length, 3 * width), LOW),
        jax.ShapeDtypeStruct((units, D), WIDE),
        jax.ShapeDtypeStruct((tokens, D), WIDE),
        jax.ShapeDtypeStruct((D, columns), WIDE),
    ]
    scratch = [
        pltpu.VMEM(ffn.shape, LOW),
        pltpu.VMEM(pre.shape, LOW),
        pltpu.VMEM(act.shape, LOW),
        pltpu.VMEM(cot.shape, LOW),
        pltpu.SemaphoreType.DMA((5,)),
        pltpu.VMEM((tokens, ctx * width), LOW),
        pltpu.VMEM((length, width), LOW),
        pltpu.VMEM((width, length), LOW),
        pltpu.VMEM((length, width), WIDE),
        pltpu.VMEM((length, width), WIDE),
        *LineSum.scratch(ctx, tokens, D, 4),
        *Swap.semaphores(ctx),
        pltpu.VMEM((dp, units, D), LOW),
        pltpu.VMEM((dp, units, D), LOW),
        *PlaneSum.semaphores(dp),
    ]
    return pl.pallas_call(
        functools.partial(back_kernel, block),
        out_shape=shapes,
        in_specs=[VMEM] * 8 + [HBM] * 5,
        out_specs=[VMEM] * 8,
        scratch_shapes=scratch,
        compiler_params=params(3),
        name="back",
    )(grad, resid, own_cot, vectors, proj, qkv, doc_start, stats, ffn, pre, act, cot, part)


class ProjectionSum:
    def __init__(self, out, mixed, low, plane, wide, blocks, came, pair_sems, sems):
        self.out, self.mixed, self.low, self.plane = out, mixed, low, plane
        self.wide, self.blocks, self.came = wide, blocks, came
        self.send_sems, self.recv_sems = pair_sems
        self.rank = lax.axis_index("ctx")
        self.core = self.rank % 2
        self.swap = ChipSwap(blocks.at.__getitem__, came.at.__getitem__, sems)

    def pair_copies(self):
        return [
            send(
                ref.at[self.core],
                ref.at[self.core],
                self.send_sems.at[index],
                self.recv_sems.at[index],
                ctx=self.rank + 1 - 2 * self.core,
            )
            for index, ref in enumerate((self.mixed, self.low))
        ]

    def start(self, mixed, low):
        self.mixed[self.core] = mixed
        self.low[self.core] = low
        for copy in self.pair_copies():
            copy.start()

    def multiply(self):
        for copy in self.pair_copies():
            copy.wait_recv()
        dp, rows = self.plane.parts.shape[:2]
        chips = self.swap.size
        tokens = 2 * self.low.shape[1]
        count = self.out.shape[0]
        mixed = self.mixed[...].reshape(tokens, -1)[:, 0:D]
        low = self.low[...].reshape(tokens, D)
        feature = lax.broadcasted_iota(jnp.int32, (D, rows), 0)
        column = lax.broadcasted_iota(jnp.int32, (1, rows), 1)
        for index in range(dp):
            owner = index * 2 * chips + column // count * 2 + self.core
            wanted = jnp.where(column < chips * count, owner * count + column % count, -1)
            chosen = jnp.where(feature == wanted, 1.0, 0.0).astype(LOW)
            picked = dot(mixed, chosen).astype(LOW)
            self.plane.put(index, dot(picked, low, 0, 0))
        self.plane.start()

    def cross(self):
        count = self.out.shape[0]
        rows = self.plane.parts.shape[1]
        lanes = full_lanes(D)
        self.wide[0:rows, 0:D] = self.plane.total()
        self.wide[0:rows, D:lanes] = jnp.zeros((rows, lanes - D), WIDE)
        for chip in range(self.swap.size):
            pack(self.blocks, chip, self.wide, chip * count, count, 0, D)
        self.swap.start()

    def wait(self):
        self.swap.wait()
        total = self.blocks[self.swap.rank].astype(WIDE)
        for off in range(1, self.swap.size):
            total = total + self.came[lax.rem(self.swap.rank + off, self.swap.size)].astype(WIDE)
        count = self.out.shape[0]
        unpack(total, self.wide, 0, count, D)
        self.out[...] = self.wide[0:count, 0:D]
        for copy in self.pair_copies():
            copy.wait_send()
        self.swap.drain()


def partial_sums(total, rows_ref, mat):
    chips, tokens = total.chips, total.blocks.shape[1]

    def one(index, carry):
        off = jnp.where(index % 2 == 0, -(index // 2), index // 2 + 1)
        chip = lax.rem(chips - 1 + off, chips)
        rows = pl.ds(pl.multiple_of(2 * chip * tokens, 2 * tokens), 2 * tokens)
        part = dot(rows_ref[rows], mat[...].reshape(D, -1), 1, 1).astype(LOW)
        total.blocks[pl.ds(2 * chip, 2)] = part.reshape(2, tokens, D)
        total.pair_copy(chip).start()
        return carry

    lax.fori_loop(0, chips, one, 0)


def last_kernel(
    rows_ref,
    mat_ref,
    in_ref,
    own_ref,
    resid_ref,
    vectors_ref,
    grad_out,
    vector_out,
    heads_out,
    mat_out,
    grad,
    *refs,
):
    total = LineSum(*refs[:3], refs[3:7])
    chips = total.chips
    dp = lax.axis_size("dp")
    greet_line(chips)
    partial_sums(total, rows_ref, mat_ref)
    total.far_steps(0, 1)
    for index in range(dp):
        rows = slice(index * (D // dp), (index + 1) * (D // dp))
        mat_out[rows] = dot(in_ref[:, rows], rows_ref[...], 0, 0)
    total.far_steps(1, 2 * chips - 1)
    heads_out[...] = dot(jnp.ones((8, rows_ref.shape[0]), LOW), rows_ref[...])
    total.finish(grad)
    normed, scale = normalize(own_ref[...].astype(WIDE))
    incoming = grad[...]
    gain = vectors_ref[GAIN_ONE : GAIN_ONE + 1, 0:D]
    grad_out[...] = resid_ref[...] + norm_back(normed, scale, gain, incoming)
    vector_out[0:1] = jnp.sum(incoming * normed, 0, keepdims=True)
    vector_out[1:2] = jnp.sum(incoming, 0, keepdims=True)
    vector_out[2:8] = jnp.zeros((6, D), WIDE)


def last(rows, mat, attn_in, own_in, resid, vectors):
    ctx = lax.axis_size("ctx")
    tokens = own_in.shape[0]
    columns = rows.shape[1]
    return pl.pallas_call(
        last_kernel,
        out_shape=[
            jax.ShapeDtypeStruct((tokens, D), WIDE),
            jax.ShapeDtypeStruct((8, D), WIDE),
            jax.ShapeDtypeStruct((8, columns), WIDE),
            jax.ShapeDtypeStruct((D, columns), WIDE),
        ],
        in_specs=[VMEM] * 6,
        out_specs=[VMEM] * 4,
        scratch_shapes=[pltpu.VMEM((tokens, D), WIDE), *LineSum.scratch(ctx, tokens, D, 4)],
        compiler_params=params(4),
        name="last",
    )(rows, mat, attn_in, own_in, resid, vectors)


def vector_kernel(parts_ref, out_ref, plane_landed, line_parts, line_landed, *sems):
    seq = lax.axis_index("dp")
    swap = Swap("dp", parts_ref.at.__getitem__, plane_landed.at.__getitem__, sems[:2])
    line = Swap("ctx", line_parts.at.__getitem__, line_landed.at.__getitem__, sems[2:])
    greet_all()
    swap.start()
    swap.wait()
    total = parts_ref[seq]
    for off in range(1, swap.size):
        total = total + plane_landed[lax.rem(seq + off, swap.size)]
    line_parts[...] = total
    line.start()
    line.wait()
    total = line_parts[line.rank]
    for off in range(1, line.size):
        total = total + line_landed[lax.rem(line.rank + off, line.size)]
    out_ref[...] = total
    swap.drain()
    line.drain()


def sum_vector(parts):
    dp, ctx = parts.shape[:2]
    return pl.pallas_call(
        vector_kernel,
        out_shape=jax.ShapeDtypeStruct(parts.shape[2:], WIDE),
        in_specs=[VMEM],
        out_specs=VMEM,
        scratch_shapes=[
            pltpu.VMEM(parts.shape, WIDE),
            pltpu.VMEM(parts.shape[1:], WIDE),
            pltpu.VMEM(parts.shape[1:], WIDE),
            *PlaneSum.semaphores(dp),
            *Swap.semaphores(ctx),
        ],
        compiler_params=params(5),
        name="sum_vector",
    )(parts)


GRAD_ONE, SUM_ONE, SUM_QUERY, SUM_VALUE, SUM_RESID, GRAD_FFN, SUM_FFN = range(7)
SUM_OUT = 11


def backward_kernel(block, names, *refs):
    r = Names(names, refs)
    seq, rank = lax.axis_index("dp"), lax.axis_index("ctx")
    ctx, tokens, _ = r.big.shape
    length, width = r.head_grad.shape
    dp, owners_rows = r.fc_parts.shape[:2]
    units = r.out_parts.shape[1]
    columns = dp * units
    vec_count = 12 * D // (ctx * dp)

    def load(source, target, index):
        return pltpu.make_async_copy(source, target, r.load_sems.at[index])

    summed = LineSum(
        r.out_blocks,
        r.out_pair,
        r.out_passing,
        (r.out_pair_send, r.out_pair_recv, r.out_line_send, r.out_line_recv),
    )
    total = LineSum(
        r.in_blocks,
        r.in_pair,
        r.in_passing,
        (r.in_pair_send, r.in_pair_recv, r.in_line_send, r.in_line_recv),
    )
    chips = total.chips
    to_heads = Swap(
        "ctx",
        lambda peer: r.own_grad.at[:, pl.ds(pl.multiple_of(peer * width, width), width)],
        lambda origin: r.head_grad.at[pl.ds(pl.multiple_of(origin * tokens, tokens), tokens)],
        (r.heads_send, r.heads_recv),
    )
    some = r.stage_fc.at[:, :, pl.ds(0, 3 * width)]
    fc = Collect(
        unit_pieces(ctx, dp),
        StreamSum(
            r.fc_parts, r.fc_landed, r.stage_fc, r.stage_fc_sems, (r.fc_plane_send, r.fc_plane_recv)
        ),
        r.wide,
        r.fc_blocks,
        r.fc_came,
        r.fc_out,
        (r.fc_send, r.fc_recv),
    )
    qkv = Collect(
        head_pieces(ctx, width // HEAD_DIM),
        StreamSum(
            r.qkv_parts, r.qkv_landed, some, r.stage_fc_sems, (r.qkv_plane_send, r.qkv_plane_recv)
        ),
        r.wide,
        r.qkv_blocks,
        r.qkv_came,
        r.qkv_grad,
        (r.qkv_send, r.qkv_recv),
    )
    share = StreamSum(
        r.out_parts,
        r.out_landed,
        r.stage_out,
        r.stage_out_sems,
        (r.out_plane_send, r.out_plane_recv),
    )
    proj = ProjectionSum(
        r.proj_grad,
        r.mixed_pair,
        r.low_pair,
        StreamSum(
            r.proj_parts,
            r.proj_landed,
            r.stage_out,
            r.stage_out_sems,
            (r.proj_plane_send, r.proj_plane_recv),
        ),
        r.wide,
        r.proj_blocks,
        r.proj_came,
        (r.proj_pair_send, r.proj_pair_recv),
        (r.proj_send, r.proj_recv),
    )
    vec_plane = Swap(
        "dp",
        r.vec_parts.at.__getitem__,
        r.vec_landed.at.__getitem__,
        (r.vec_plane_send, r.vec_plane_recv),
    )
    vec_line = Swap(
        "ctx", r.vec_rows.at.__getitem__, r.vec_came.at.__getitem__, (r.vec_send, r.vec_recv)
    )
    heads_mat = r.mat.at[:, :, pl.ds(0, 3 * width)]
    loads = [
        load(r.proj_mat, r.mat, 0),
        load(r.part, r.out_blocks, 1),
        load(r.ffn, r.big, 2),
        load(r.pre_act, r.feed, 3),
        load(r.qkv_mat, heads_mat, 0),
        load(r.attn_in, r.big, 2),
        load(r.act, r.feed, 3),
        load(r.cots, r.big, 2),
    ]
    for index in range(4):
        loads[index].start()
    greet_all()

    grad = r.grad[...]
    normed, scale = normalize(r.resid[...])
    gain = r.vectors[GAIN_TWO : GAIN_TWO + 1, 0:D]
    own_cot = r.own_cot[...].astype(WIDE)
    grad_resid = own_cot + norm_back(normed, scale, gain, grad)
    r.grad_resid[...] = grad_resid
    low = grad_resid.astype(LOW)
    loads[0].wait()
    r.own_grad[:, 0:D] = dot(low, r.mat[...].reshape(D, D), 1, 1).astype(LOW)
    r.own_grad[:, D:] = jnp.zeros((tokens, r.own_grad.shape[1] - D), LOW)
    to_heads.start()
    loads[4].start()
    mine = pl.ds(pl.multiple_of(rank * width, width), width)
    here = pl.ds(pl.multiple_of(rank * tokens, tokens), tokens)
    r.head_grad[here] = r.own_grad[:, mine]
    proj.start(r.own_mixed[...], low)
    loads[1].wait()
    summed.send_pairs()
    vec = r.vec
    vec[...] = jnp.zeros_like(vec)

    def note(row, value):
        vec[row : row + 1, 0:D] = jnp.sum(value, 0, keepdims=True)

    note(SUM_RESID, grad_resid)
    note(GRAD_FFN, grad * normed)
    note(SUM_FFN, grad)
    note(SUM_OUT, own_cot)

    loads[2].wait()
    loads[3].wait()
    grad_pre = r.feed[...].reshape(length, columns)
    sums = dot(jnp.ones((8, length), LOW), grad_pre)[0:1]
    for owner in range(ctx):

        @pl.when(rank == owner)
        def _(owner=owner):
            for place, row, lane, size in unit_bias_pieces(owner, ctx, dp):
                vec[row : row + 1, lane : lane + size] = sums[:, place : place + size]

    def by_parts(plane, left, right, count):
        for index in range(dp):
            rows = slice(index * count, (index + 1) * count)
            plane.put(index, dot(left[:, :, rows].reshape(length, count), right, 0, 0))
        plane.start()

    by_parts(fc.plane, r.big, grad_pre, owners_rows)
    loads[5].start()
    loads[6].start()
    summed.far_steps(0, 1)

    to_heads.wait()

    def first():
        summed.far_steps(1, 2)

    def second():
        summed.far_steps(2, 3)
        fc.plane.relay()

    attend_back_body(
        block,
        r.qkv,
        r.doc_start,
        r.stats,
        r.head_grad,
        r.rows,
        r.key_t,
        r.key_grad,
        r.value_grad,
        {1: first, 2: second},
    )
    loads[4].wait()
    partial_sums(total, r.rows, heads_mat)
    total.far_steps(0, 1)
    summed.far_steps(3, 4)
    fc.cross()
    loads[5].wait()
    by_parts(qkv.plane, r.big, r.rows[...], owners_rows)
    loads[7].start()
    total.far_steps(1, 2)
    summed.far_steps(4, 5)
    proj.multiply()
    total.far_steps(2, 3)
    summed.far_steps(5, 2 * chips - 1)
    loads[6].wait()
    loads[7].wait()
    by_parts(share, r.feed, r.big[...].reshape(length, D), units)
    total.far_steps(3, 2 * chips - 1)
    sums = dot(jnp.ones((8, length), LOW), r.rows[...])
    vec[SUM_QUERY : SUM_QUERY + 1, mine] = sums[0:1, 0:width]
    vec[SUM_VALUE : SUM_VALUE + 1, mine] = sums[0:1, 2 * width :]
    qkv.plane.relay()
    total.finish(r.came)

    incoming = r.came[...]
    normed, scale = normalize(r.own_in[...].astype(WIDE))
    gain = r.vectors[GAIN_ONE : GAIN_ONE + 1, 0:D]
    grad_in = r.grad_resid[...] + norm_back(normed, scale, gain, incoming)
    r.grad_in_t[...] = grad_in.T
    note(GRAD_ONE, incoming * normed)
    note(SUM_ONE, incoming)
    for owner, begin, row, lane, size in vector_pieces(ctx * dp, vec_count):
        r.vec_parts[owner // ctx, owner % ctx, 0:1, begin : begin + size] = vec[
            row : row + 1, lane : lane + size
        ]
    vec_plane.start()
    qkv.cross()
    proj.plane.relay()
    vec_plane.wait()
    rows = r.vec_parts[seq]
    for off in range(1, dp):
        rows = rows + r.vec_landed[lax.rem(seq + off, dp)]
    r.vec_rows[...] = rows
    vec_line.start()
    summed.finish(r.came)
    bias = r.vectors[BIAS_OUT : BIAS_OUT + 1, 0:D]
    r.output_t[...] = (r.came[...] + r.resid[...] + bias).T
    fc.wait()
    proj.cross()
    share.relay()
    vec_line.wait()
    row = r.vec_rows[rank]
    for off in range(1, ctx):
        row = row + r.vec_came[lax.rem(rank + off, ctx)]
    r.vec_out[...] = row
    qkv.wait()
    r.out_grad[...] = share.total()
    proj.wait()
    to_heads.drain()
    vec_plane.drain()
    vec_line.drain()


def backward(made, block):
    ctx, dp = lax.axis_size("ctx"), lax.axis_size("dp")
    tokens = made.own_in.shape[0]
    length = ctx * tokens
    width = made.qkv_out.shape[1] // 3
    columns = made.act_out.shape[2]
    units = columns // dp
    chips = ctx // 2
    rows = D // dp
    count = rows // ctx
    lanes = full_lanes(12 * D // (ctx * dp))
    b = Build()
    b.take(
        VMEM,
        grad=made.grad,
        resid=made.resid,
        own_cot=made.own_cot,
        own_in=made.own_in,
        vectors=made.vectors,
        own_mixed=made.own_mixed,
        qkv=made.qkv_out,
        doc_start=made.doc_start,
        stats=made.stats,
    )
    b.take(
        HBM,
        proj_mat=made.proj_mat_out,
        qkv_mat=made.qkv_mat_out,
        part=made.part_out,
        ffn=made.ffn_out,
        pre_act=made.pre_out,
        attn_in=made.attn_in_out,
        act=made.act_out,
        cots=made.cots_out,
    )
    b.give(
        WIDE,
        VMEM,
        output_t=(D, tokens),
        grad_in_t=(D, tokens),
        qkv_grad=(count, 3 * D),
        proj_grad=(count, D),
        fc_out=(count, FF),
        out_grad=(units, D),
        vec_out=(1, lanes),
    )
    for name, shape in (
        ("fc", (rows, columns)),
        ("qkv", (rows, 3 * width)),
        ("out", (units, D)),
        ("proj", (units, D)),
    ):
        b.give(LOW, HBM, **{name + "_parts": (dp, *shape), name + "_landed": (3, *shape)})
        b.both(**{name + "_plane": 6})
    b.hold(
        LOW,
        mat=(dp, rows, D),
        big=(ctx, tokens, D),
        feed=(ctx, tokens, columns),
        stage_fc=(3, rows, columns),
        stage_out=(3, units, D),
        proj_blocks=(chips, packed_rows(count, D), 128),
        proj_came=(chips, packed_rows(count, D), 128),
        mixed_pair=(2, tokens, ctx * width),
        low_pair=(2, tokens, D),
        own_grad=(tokens, ctx * width),
        head_grad=(length, width),
        rows=(length, 3 * width),
        key_t=(width, length),
    )
    for name, wide in (("fc", columns), ("qkv", 3 * width)):
        packed = (ctx, packed_rows(count, wide), 128)
        b.hold(LOW, **{name + "_blocks": packed, name + "_came": packed})
    for name in ("out", "in"):
        b.line_sum(name, ctx, tokens)
    b.hold(
        WIDE,
        wide=(rows, full_lanes(D)),
        key_grad=(length, width),
        value_grad=(length, width),
        grad_resid=(tokens, D),
        came=(tokens, D),
        vec=(ROWS, max(full_lanes(D), ctx * width)),
        vec_parts=(dp, ctx, 1, lanes),
        vec_landed=(dp, ctx, 1, lanes),
        vec_rows=(ctx, 1, lanes),
        vec_came=(ctx, 1, lanes),
    )
    b.both(fc=ctx, qkv=ctx, proj=chips, proj_pair=2, heads=ctx, vec_plane=dp, vec=ctx)
    b.sems(load_sems=(4,), stage_fc_sems=(3,), stage_out_sems=(3,))
    assert units == -(-(chips * count) // 16) * 16
    return b.call(functools.partial(backward_kernel, block), 6, "backward")


def gather_rows(block):
    return lax.all_gather(block, ("dp", "ctx"), axis=0, tiled=True)


def by_rank_heads(rows, ctx, slots):
    count = rows.shape[0]
    split = rows.reshape(count, 3, D)
    split = jnp.pad(split, ((0, 0), (0, 0), (0, (ctx * slots - HEADS) * HEAD_DIM)))
    split = split.reshape(count, 3, ctx, slots * HEAD_DIM)
    return split.transpose(2, 0, 1, 3).reshape(ctx, count, 3 * slots * HEAD_DIM)


def from_rank_heads(blocks, slots):
    ctx, count = blocks.shape[:2]
    split = blocks.reshape(ctx, count, 3, slots * HEAD_DIM).transpose(1, 2, 0, 3)
    return split.reshape(count, 3, ctx * slots * HEAD_DIM)[:, :, :D].reshape(count, 3 * D)


def padded_units(units):
    return -(-units // 16) * 16


def by_rank_units(rows, ctx, dp):
    count = rows.shape[0]
    units = FF // (dp * ctx)
    split = rows.reshape(count, dp, ctx, units).transpose(2, 0, 1, 3)
    split = jnp.pad(split, ((0, 0), (0, 0), (0, 0), (0, padded_units(units) - units)))
    return split.reshape(ctx, count, dp * padded_units(units))


def from_rank_units(blocks, dp):
    ctx, count = blocks.shape[:2]
    units = FF // (dp * ctx)
    split = blocks.reshape(ctx, count, dp, padded_units(units))[..., :units]
    return split.transpose(1, 2, 0, 3).reshape(count, FF)


def shards(
    hidden_in, qkv_weight, proj_weight, fc_weight, out_weight, small_params, segments, cotangent
):
    tokens = hidden_in.shape[1]
    length = segments.shape[1]
    ctx = lax.axis_size("ctx")
    dp = lax.axis_size("dp")
    owners = dp * ctx
    rank = lax.axis_index("ctx")
    slots = -(-HEADS // ctx)
    width = slots * HEAD_DIM
    units = FF // owners
    rows = D // owners
    whole = D % owners == 0 and dp == 4
    block = min(256, length)
    both = ("dp", "ctx")

    vec_count = small_params.shape[0]
    small = jnp.pad(small_params.astype(WIDE), (0, full_lanes(vec_count) - vec_count))[None]
    unit_rows = out_weight.reshape(units, D)
    if whole:
        mats = (
            qkv_weight.reshape(rows, 3 * D),
            fc_weight.reshape(rows, FF),
            proj_weight.reshape(rows, D),
        )
    else:
        mat_qkv = by_rank_heads(gather_rows(qkv_weight).reshape(D, 3 * D), ctx, slots)
        mat_qkv = lax.dynamic_index_in_dim(mat_qkv, rank, 0, keepdims=False)
        mat_fc = by_rank_units(gather_rows(fc_weight).reshape(D, FF), ctx, dp)
        mat_fc = lax.dynamic_index_in_dim(mat_fc, rank, 0, keepdims=False)
        mat_proj = gather_rows(proj_weight).reshape(D, D)
        mats = (mat_qkv, mat_fc, mat_proj)
    made = forward(
        small, hidden_in[0].T, cotangent[0].T, unit_rows, segments, mats, slots, whole, block
    )
    if whole:
        done = backward(made, block)
        return (
            done.output_t.T[None],
            done.grad_in_t.T[None],
            done.qkv_grad.reshape(-1),
            done.proj_grad.reshape(-1),
            done.fc_out.reshape(-1),
            done.out_grad[:units].reshape(-1),
            done.vec_out[0, :vec_count],
        )
    vectors = made.vectors

    grad_resid, resid_low, sums_two, sums_units, grad_rows, grad_out, output, grad_fc = back(
        made.grad,
        made.resid,
        cotangent[0],
        vectors,
        mat_proj,
        made.qkv_out,
        made.doc_start,
        made.stats,
        made.ffn_out,
        made.pre_out,
        made.act_out,
        made.cots_out,
        made.part_out,
        block,
    )
    grad_input, sums_one, sums_heads, grad_qkv = last(
        grad_rows,
        mat_qkv,
        made.attn_in_out.reshape(length, D),
        hidden_in[0],
        grad_resid,
        vectors,
    )
    here = (jnp.arange(ctx) == rank)[:, None, None]
    full_fc = from_rank_units(jnp.where(here, grad_fc[None], 0.0), dp).reshape(-1)
    full_qkv = from_rank_heads(jnp.where(here, grad_qkv[None], 0.0), slots).reshape(-1)
    grad_proj = dot(made.own_mixed[:, :D], resid_low, 0, 0).reshape(-1)
    share_fc, share_qkv, share_proj = [
        lax.psum_scatter(full, both, scatter_dimension=0, tiled=True)
        for full in (full_fc, full_qkv, grad_proj)
    ]

    def spread_heads(part):
        padded = jnp.zeros((ctx * width,), WIDE)
        return lax.dynamic_update_slice_in_dim(padded, part, rank * width, 0)[:D]

    sums_units = sums_units[0].reshape(dp, 1, -1)[:, :, :units]
    sums_units = lax.dynamic_update_slice_in_dim(
        jnp.zeros((dp, ctx, units), WIDE), sums_units, rank, 1
    ).reshape(FF)
    vector = jnp.concatenate(
        [
            sums_one[0],
            sums_one[1],
            spread_heads(sums_heads[0, :width]),
            spread_heads(sums_heads[0, 2 * width :]),
            sums_two[0],
            sums_two[1],
            sums_two[2],
            sums_units,
            sums_two[3],
        ]
    ).reshape(owners, vec_count)
    vec_pad = -(-vec_count // 1024) * 1024
    vector = jnp.pad(vector, ((0, 0), (0, vec_pad - vec_count))).reshape(dp, ctx, -1, 128)
    share_vector = sum_vector(vector)
    return (
        output[None],
        grad_input[None],
        share_qkv.astype(WIDE).reshape(-1),
        share_proj.astype(WIDE).reshape(-1),
        share_fc.astype(WIDE).reshape(-1),
        grad_out[:units].reshape(-1),
        share_vector.reshape(-1)[:vec_count],
    )


def solution(mesh):
    flat = P(("dp", "ctx"))
    rows = P("dp", "ctx", None)
    return jax.shard_map(
        shards,
        mesh=mesh,
        in_specs=(rows, flat, flat, flat, flat, flat, P("dp", None), rows),
        out_specs=(rows, rows, flat, flat, flat, flat, flat),
        check_vma=False,
    )
```

```python
import functools

import jax
import jax.numpy as jnp
from jax import lax
from jax.experimental import pallas as pl
from jax.experimental.pallas import tpu as pltpu
from jax.sharding import PartitionSpec as P

D = 1600
HEADS = 25
HEAD_DIM = 64
FF = 6400
EPSILON = 1e-05
LOW = jnp.bfloat16
WIDE = jnp.float32
MIB = 1024 * 1024


def dot(left, right, left_dim=1, right_dim=0):
    return lax.dot_general(
        left, right, (((left_dim,), (right_dim,)), ((), ())), preferred_element_type=WIDE
    )


def normalize(rows):
    centre = rows - jnp.mean(rows, -1, keepdims=True)
    spread = jnp.mean(centre * centre, -1, keepdims=True)
    scale = lax.rsqrt(spread + EPSILON)
    return centre * scale, scale


def norm_back(normed, scale, gain, incoming):
    scaled = gain * incoming
    return scale * (
        scaled
        - jnp.mean(scaled, -1, keepdims=True)
        - normed * jnp.mean(scaled * normed, -1, keepdims=True)
    )


def head_lanes(head, width):
    lane = lax.broadcasted_iota(jnp.int32, (1, width), 1)
    return (lane // HEAD_DIM) == head


def allowed_scores(scores, doc_start, first_query, keys, block):
    key_pos = lax.broadcasted_iota(jnp.int32, (keys, block), 0)
    query_pos = first_query + lax.broadcasted_iota(jnp.int32, (keys, block), 1)
    seen = (key_pos >= doc_start) & (key_pos <= query_pos)
    return jnp.where(seen, scores, -1e30)


def attend_body(block, qkv_ref, start_ref, mixed_ref, stat_ref, value_t):
    length = qkv_ref.shape[0]
    width = mixed_ref.shape[1]
    slots = width // HEAD_DIM
    value_t[...] = qkv_ref[:, 2 * width : 3 * width].astype(WIDE).T.astype(LOW)
    stat_ref[...] = jnp.zeros_like(stat_ref)
    for index in range(length // block):
        keys = (index + 1) * block
        rows = pl.ds(index * block, block)
        key_rows = qkv_ref[0:keys, width : 2 * width]
        doc_start = start_ref[0:1, rows]
        outs = []
        for head in range(slots):
            query = jnp.where(
                head_lanes(head, width), qkv_ref[rows, 0:width] * LOW(HEAD_DIM**-0.5), LOW(0)
            )
            scores = dot(key_rows, query, 1, 1)
            scores = allowed_scores(scores, doc_start, index * block, keys, block)
            top = jnp.max(scores, 0, keepdims=True)
            expo = jnp.exp(scores - top)
            total = jnp.sum(expo, 0, keepdims=True)
            head_rows = slice(head * HEAD_DIM, (head + 1) * HEAD_DIM)
            out = dot(value_t[head_rows, 0:keys], expo.astype(LOW))
            outs.append(out / total)
            stat_ref[head : head + 1, rows] = top + jnp.log(total)
        mixed_ref[rows, :] = jnp.concatenate(outs, 0).T.astype(LOW)


def attend_back_body(
    block, qkv_ref, start_ref, stat_ref, grad_ref, out_ref, key_t, key_grad, value_grad, after
):
    length = qkv_ref.shape[0]
    width = grad_ref.shape[1]
    slots = width // HEAD_DIM
    scale = HEAD_DIM**-0.5
    key_t[...] = qkv_ref[:, width : 2 * width].astype(WIDE).T.astype(LOW)
    key_grad[...] = jnp.zeros_like(key_grad)
    value_grad[...] = jnp.zeros_like(value_grad)
    for index in range(length // block):
        keys = (index + 1) * block
        rows = pl.ds(index * block, block)
        key_rows = qkv_ref[0:keys, width : 2 * width]
        value_rows = qkv_ref[0:keys, 2 * width : 3 * width]
        doc_start = start_ref[0:1, rows]
        outs = []
        for head in range(slots):
            lanes = head_lanes(head, width)
            head_rows = slice(head * HEAD_DIM, (head + 1) * HEAD_DIM)
            query = jnp.where(lanes, qkv_ref[rows, 0:width] * LOW(scale), LOW(0))
            grad = jnp.where(lanes, grad_ref[rows, :], LOW(0))
            scores = dot(key_rows, query, 1, 1)
            scores = allowed_scores(scores, doc_start, index * block, keys, block)
            probs = jnp.exp(scores - stat_ref[head : head + 1, rows])
            grad_probs = dot(value_rows, grad, 1, 1)
            delta = jnp.sum(probs * grad_probs, 0, keepdims=True)
            grad_scores = (probs * (grad_probs - delta)).astype(LOW)
            value_grad[0:keys, :] += dot(probs.astype(LOW), grad)
            key_grad[0:keys, :] += dot(grad_scores, query)
            outs.append(dot(key_t[head_rows, 0:keys], grad_scores))
        out_ref[rows, 0:width] = (jnp.concatenate(outs, 0).T * scale).astype(LOW)
        if index in after:
            after[index]()
    out_ref[:, width : 2 * width] = key_grad[...].astype(LOW)
    out_ref[:, 2 * width : 3 * width] = value_grad[...].astype(LOW)


MESH = pl.DeviceIdType.MESH


def send(src, dst, send_sem, recv_sem, **target):
    return pltpu.make_async_remote_copy(
        src_ref=src,
        dst_ref=dst,
        send_sem=send_sem,
        recv_sem=recv_sem,
        device_id=target,
        device_id_type=MESH,
    )


def greet_line(chips):
    rank = lax.axis_index("ctx")
    chip, core = rank // 2, rank % 2
    barrier = pltpu.get_barrier_semaphore()
    pl.semaphore_signal(barrier, 1, device_id={"ctx": rank + 1 - 2 * core}, device_id_type=MESH)

    @pl.when(chip > 0)
    def _():
        pl.semaphore_signal(barrier, 1, device_id={"ctx": rank - 2}, device_id_type=MESH)

    @pl.when(chip < chips - 1)
    def _():
        pl.semaphore_signal(barrier, 1, device_id={"ctx": rank + 2}, device_id_type=MESH)

    sides = (chip > 0).astype(jnp.int32) + (chip < chips - 1).astype(jnp.int32)
    pl.semaphore_wait(barrier, 1 + sides)


def greet_all(between=lambda: None):
    barrier = pltpu.get_barrier_semaphore()
    count = 0
    for axis in ("ctx", "dp"):
        size = lax.axis_size(axis)
        here = lax.axis_index(axis)

        def one(off, carry, axis=axis, size=size, here=here):
            peer = lax.rem(here + off, size)
            pl.semaphore_signal(barrier, 1, device_id={axis: peer}, device_id_type=MESH)
            return carry

        lax.fori_loop(1, size, one, 0)
        count += size - 1
    between()
    pl.semaphore_wait(barrier, count)


class Swap:
    def __init__(self, axis, source, target, sems):
        self.axis, self.source, self.target = axis, source, target
        self.send_sems, self.recv_sems = sems
        self.rank = lax.axis_index(axis)
        self.size = lax.axis_size(axis)

    def copy(self, peer, origin, target):
        return send(
            self.source(peer),
            self.target(origin),
            self.send_sems.at[peer],
            self.recv_sems.at[origin],
            **{self.axis: target},
        )

    def every(self, act):
        def one(off, carry):
            act(lax.rem(self.rank + off, self.size))
            return carry

        lax.fori_loop(1, self.size, one, 0)

    def start(self):
        self.every(lambda peer: self.copy(peer, self.rank, peer).start())

    def wait(self):
        self.every(lambda peer: self.copy(peer, peer, self.rank).wait_recv())

    def drain(self):
        self.every(lambda peer: self.copy(peer, self.rank, peer).wait_send())

    @staticmethod
    def semaphores(size):
        return [pltpu.SemaphoreType.DMA((size,)), pltpu.SemaphoreType.DMA((size,))]


class ChipSwap(Swap):
    def __init__(self, source, target, sems):
        super().__init__("ctx", source, target, sems)
        self.core = self.rank % 2
        self.rank, self.size = self.rank // 2, self.size // 2

    def copy(self, peer, origin, target):
        return send(
            self.source(peer),
            self.target(origin),
            self.send_sems.at[peer],
            self.recv_sems.at[origin],
            ctx=2 * target + self.core,
        )


class PlaneGather:
    def __init__(self, blocks, sems):
        self.blocks = blocks
        self.size = blocks.shape[0]
        self.rank = lax.axis_index("dp")
        self.square = self.size == 4
        self.send_sems, self.recv_sems = sems
        if self.square:
            self.beside = self.rank + 1 - 2 * (self.rank % 2)
            self.above = self.rank + 2 - 4 * (self.rank // 2)
            half = blocks.shape[1] // 32 * 16
            self.low, self.high = pl.ds(0, half), pl.ds(half, blocks.shape[1] - half)
        else:
            self.swap = Swap("dp", lambda peer: blocks.at[self.rank], blocks.at.__getitem__, sems)

    def copy(self, index, ref, target):
        return send(ref, ref, self.send_sems.at[index], self.recv_sems.at[index], dp=target)

    def start(self):
        if not self.square:
            self.swap.start()
            return
        own = self.blocks.at[self.rank]
        self.copy(0, own, self.beside).start()
        self.copy(1, own, self.above).start()

    def relay(self):
        if not self.square:
            return
        self.copy(0, self.blocks.at[self.beside], self.beside).wait_recv()
        self.copy(2, self.blocks.at[self.beside, self.low], self.above).start()
        self.copy(1, self.blocks.at[self.above], self.above).wait_recv()
        self.copy(3, self.blocks.at[self.above, self.high], self.beside).start()

    def wait(self):
        if not self.square:
            self.swap.wait()
            self.swap.drain()
            return
        far = 3 - self.rank
        own = self.blocks.at[self.rank]
        self.copy(2, self.blocks.at[far, self.low], self.above).wait_recv()
        self.copy(3, self.blocks.at[far, self.high], self.beside).wait_recv()
        self.copy(0, own, self.beside).wait_send()
        self.copy(1, own, self.above).wait_send()
        self.copy(2, self.blocks.at[self.beside, self.low], self.above).wait_send()
        self.copy(3, self.blocks.at[self.above, self.high], self.beside).wait_send()

    semaphores = staticmethod(Swap.semaphores)


class PlaneSum:
    def __init__(self, blocks, landed, sems):
        self.blocks, self.landed = blocks, landed
        self.rank = lax.axis_index("dp")
        self.send_sems, self.recv_sems = sems
        self.swap = Swap("dp", blocks.at.__getitem__, landed.at.__getitem__, sems)
        self.square = blocks.shape[0] == 4
        if self.square:
            self.beside = self.rank + 1 - 2 * (self.rank % 2)
            self.above = self.rank + 2 - 4 * (self.rank // 2)
            half = blocks.shape[1] // 32 * 16
            self.low, self.high = pl.ds(0, half), pl.ds(half, blocks.shape[1] - half)

    def copy(self, index):
        far = 3 - self.rank
        block, slot, rows, target = (
            (far, 0, self.low, self.beside),
            (self.beside, 1, self.low, self.beside),
            (far, 0, self.high, self.above),
            (self.above, 1, self.high, self.above),
            (self.above, 2, self.low, self.above),
            (self.beside, 2, self.high, self.beside),
        )[index]
        return send(
            self.blocks.at[block, rows],
            self.landed.at[slot, rows],
            self.send_sems.at[index],
            self.recv_sems.at[index],
            dp=target,
        )

    def start(self):
        if not self.square:
            self.swap.start()
            return
        for index in range(4):
            self.copy(index).start()

    def relay(self):
        if not self.square:
            return
        for index, block, rows in ((0, self.above, self.low), (2, self.beside, self.high)):
            self.copy(index).wait_recv()
            total = self.blocks[block, rows].astype(WIDE) + self.landed[0, rows].astype(WIDE)
            self.blocks[block, rows] = total.astype(self.blocks.dtype)
            self.copy(4 + index // 2).start()

    def total(self):
        total = self.blocks[self.rank].astype(WIDE)
        if not self.square:
            self.swap.wait()
            for off in range(1, self.swap.size):
                total = total + self.landed[lax.rem(self.rank + off, self.swap.size)].astype(WIDE)
            return total
        for index in (1, 3, 4, 5):
            self.copy(index).wait_recv()
        return total + self.landed[1].astype(WIDE) + self.landed[2].astype(WIDE)

    def drain(self):
        if not self.square:
            self.swap.drain()
            return
        for index in range(6):
            self.copy(index).wait_send()

    @staticmethod
    def semaphores(size):
        return Swap.semaphores(max(size, 6))


class LineGather:
    def __init__(self, blocks, send_sems, recv_sems):
        self.blocks, self.send_sems, self.recv_sems = blocks, send_sems, recv_sems
        self.rank = lax.axis_index("ctx")
        self.chip, self.core = self.rank // 2, self.rank % 2
        self.chips = blocks.shape[0] // 2

    def copy(self, way, origin, target, src=None):
        block = self.blocks.at[origin]
        return send(
            block if src is None else src,
            block,
            self.send_sems.at[way, origin],
            self.recv_sems.at[origin],
            ctx=target,
        )

    def pass_on(self, origin, src=None):
        chip = origin // 2

        @pl.when((chip <= self.chip) & (self.chip < self.chips - 1))
        def _():
            self.copy(0, origin, self.rank + 2, src).start()

        @pl.when((chip >= self.chip) & (self.chip > 0))
        def _():
            self.copy(1, origin, self.rank - 2, src).start()

        self.copy(2, origin, self.rank + 1 - 2 * self.core, src).start()

    def arrive(self, step, part):
        side, other = part % 2, part // 2
        origin_chip = self.chip + jnp.where(side == 0, -step, step)
        origin = 2 * origin_chip + jnp.where(other == 0, self.core, 1 - self.core)
        valid = (origin_chip >= 0) & (origin_chip < self.chips) & ((step > 0) | (side == 0))

        @pl.when(valid & (origin != self.rank))
        def _():
            self.copy(0, origin, self.rank).wait_recv()

            @pl.when(other == 0)
            def _():
                self.pass_on(origin)

        return valid, origin

    def finish(self):
        def one(chip, carry):
            origin = 2 * chip + self.core

            @pl.when((chip <= self.chip) & (self.chip < self.chips - 1))
            def _():
                self.copy(0, origin, self.rank).wait_send()

            @pl.when((chip >= self.chip) & (self.chip > 0))
            def _():
                self.copy(1, origin, self.rank).wait_send()

            self.copy(2, origin, self.rank).wait_send()
            return carry

        lax.fori_loop(0, self.chips, one, 0)

    @staticmethod
    def semaphores(ctx):
        return [pltpu.SemaphoreType.DMA((3, ctx)), pltpu.SemaphoreType.DMA((ctx,))]


class LineSum:
    def __init__(self, blocks, pair, passing, sems):
        self.blocks, self.pair, self.passing = blocks, pair, passing
        self.pair_send, self.pair_recv, self.line_send, self.line_recv = sems
        self.rank = lax.axis_index("ctx")
        self.chip, self.core = self.rank // 2, self.rank % 2
        self.chips = blocks.shape[0] // 2
        self.pieces = self.line_recv.shape[2]
        self.piece = blocks.shape[1] // self.pieces

    def pair_copy(self, chip):
        return send(
            self.blocks.at[2 * chip + 1 - self.core],
            self.pair.at[chip],
            self.pair_send.at[chip],
            self.pair_recv.at[chip],
            ctx=self.rank + 1 - 2 * self.core,
        )

    def line_copy(self, way, chip, piece, target, at):
        rows = pl.ds(piece * self.piece, self.piece)
        slot = jnp.where((way == 1) & (chip == at), self.chips, chip)
        return send(
            self.blocks.at[2 * chip + self.core, rows],
            self.passing.at[slot, rows],
            self.line_send.at[chip, piece],
            self.line_recv.at[way, chip, piece],
            ctx=target,
        )

    def both(self, chip, rows):
        mine = self.blocks[2 * chip + self.core, rows].astype(WIDE)
        return mine + self.pair[chip, rows].astype(WIDE)

    def forward(self, way, chip, valid):
        behind = jnp.where(way == 0, self.chip > 0, self.chip < self.chips - 1)
        target = self.rank + jnp.where(way == 0, 2, -2)

        @pl.when(valid)
        def _():
            self.pair_copy(chip).wait_recv()

            def one(piece, carry):
                rows = pl.ds(pl.multiple_of(piece * self.piece, self.piece), self.piece)
                total = self.both(chip, rows)

                @pl.when(behind)
                def _():
                    self.line_copy(way, chip, piece, target, self.chip).wait_recv()
                    passing = self.passing[chip, rows].astype(WIDE)
                    self.blocks[2 * chip + self.core, rows] = (total + passing).astype(LOW)

                @pl.when(jnp.logical_not(behind))
                def _():
                    self.blocks[2 * chip + self.core, rows] = total.astype(LOW)

                self.line_copy(way, chip, piece, target, target // 2).start()
                return carry

            lax.fori_loop(0, self.pieces, one, 0)

    def near_first(self, step, way):
        last = self.chips - 1
        chip = jnp.where(way == 0, step - self.chip, 2 * last - self.chip - step)
        ahead = jnp.where(way == 0, (chip > self.chip) & (chip <= last), (chip >= 0) & (chip < self.chip))
        self.forward(way, chip, ahead)

    def far_first(self, step, way):
        last = self.chips - 1
        chip = jnp.where(way == 0, last + self.chip - step, step - last + self.chip)
        ahead = jnp.where(way == 0, (chip > self.chip) & (chip <= last), (chip >= 0) & (chip < self.chip))
        self.forward(way, chip, ahead)

    def send_pairs(self):
        def one(chip, carry):
            self.pair_copy(chip).start()
            return carry

        lax.fori_loop(0, self.chips, one, 0)

    def far_steps(self, begin, end):
        def one(index, carry):
            self.far_first(index // 2, index % 2)
            return carry

        lax.fori_loop(2 * begin, 2 * end, one, 0)

    def finish(self, out):
        self.pair_copy(self.chip).wait_recv()

        def one(piece, carry):
            rows = pl.ds(pl.multiple_of(piece * self.piece, self.piece), self.piece)
            out[rows] = self.both(self.chip, rows)

            @pl.when(self.chip > 0)
            def _():
                self.line_copy(0, self.chip, piece, self.rank, self.chip).wait_recv()
                out[rows] = out[rows] + self.passing[self.chip, rows].astype(WIDE)

            @pl.when(self.chip < self.chips - 1)
            def _():
                self.line_copy(1, self.chip, piece, self.rank, self.chip).wait_recv()
                out[rows] = out[rows] + self.passing[self.chips, rows].astype(WIDE)

            return carry

        lax.fori_loop(0, self.pieces, one, 0)

        def sent(chip, carry):
            self.pair_copy(chip).wait_send()

            @pl.when(chip != self.chip)
            def _():
                for piece in range(self.pieces):
                    self.line_copy(0, chip, piece, self.rank, self.chip).wait_send()

            return carry

        lax.fori_loop(0, self.chips, sent, 0)

    @staticmethod
    def scratch(ctx, rows, columns, pieces):
        chips = ctx // 2
        return [
            pltpu.VMEM((ctx, rows, columns), LOW),
            pltpu.VMEM((chips, rows, columns), LOW),
            pltpu.VMEM((chips + 1, rows, columns), LOW),
            pltpu.SemaphoreType.DMA((chips,)),
            pltpu.SemaphoreType.DMA((chips,)),
            pltpu.SemaphoreType.DMA((chips, pieces)),
            pltpu.SemaphoreType.DMA((2, chips, pieces)),
        ]


VMEM = pl.BlockSpec(memory_space=pltpu.VMEM)
HBM = pl.BlockSpec(memory_space=pl.ANY)


def params(number):
    return pltpu.CompilerParams(
        vmem_limit_bytes=63 * MIB, collective_id=number, has_side_effects=True
    )


def packed_rows(count, columns):
    tiles = -(-columns // 128)
    main = count // 16 * 16
    return tiles * main + -(-(tiles * (count - main)) // 16) * 16


def pack(out, index, rows, first, count, lane, columns):
    tiles = -(-columns // 128)
    main = count // 16 * 16
    for tile in range(tiles):
        lanes = slice(lane + tile * 128, lane + tile * 128 + 128)
        part = rows[first : first + main, lanes]
        out[index, tile * main : (tile + 1) * main] = part.astype(LOW)
    left = [
        rows[first + row : first + row + 1, lane + tile * 128 : lane + tile * 128 + 128]
        for row in range(main, count)
        for tile in range(tiles)
    ]
    space = out.shape[1] - tiles * main
    if space:
        left.append(jnp.zeros((space - len(left), 128), WIDE))
        out[index, tiles * main :] = jnp.concatenate(left, 0).astype(LOW)


def unpack(packed, rows, first, count, columns):
    tiles = -(-columns // 128)
    main = count // 16 * 16
    for tile in range(tiles):
        lanes = slice(tile * 128, tile * 128 + 128)
        rows[first : first + main, lanes] = packed[tile * main : (tile + 1) * main].astype(WIDE)
    left = packed[tiles * main :].astype(WIDE)
    for row in range(main, count):
        for tile in range(tiles):
            place = (row - main) * tiles + tile
            lanes = slice(tile * 128, tile * 128 + 128)
            rows[first + row : first + row + 1, lanes] = left[place : place + 1]


def full_lanes(columns):
    return -(-columns // 128) * 128


def head_pieces(ctx, slots):
    width = slots * HEAD_DIM
    pieces = []
    for rank in range(ctx):
        count = min(width, D - rank * width)
        if count > 0:
            for part in range(3):
                pieces.append((rank, part * width, part * D + rank * width, count))
    return pieces


def unit_pieces(ctx, dp):
    units = FF // (ctx * dp)
    return [
        (rank, seq * padded_units(units), (seq * ctx + rank) * units, units)
        for rank in range(ctx)
        for seq in range(dp)
    ]


def divide(rows_ref, wide, blocks, pieces, columns):
    count = rows_ref.shape[0]
    lanes = full_lanes(columns)
    for rank in range(blocks.shape[0]):
        wide[...] = jnp.zeros_like(wide)
        for owner, here, there, size in pieces:
            if owner == rank:
                wide[0:count, here : here + size] = rows_ref[:, there : there + size].astype(WIDE)
        pack(blocks, rank, wide, 0, count, 0, lanes)


class Spread:
    def __init__(self, blocks, landed, wide, out, sems):
        self.blocks, self.landed, self.wide, self.out = blocks, landed, wide, out
        self.swap = Swap("ctx", blocks.at.__getitem__, landed.at.__getitem__, sems[:2])
        self.plane = PlaneGather(out, sems[2:])

    def start(self):
        self.swap.start()
        self.landed[self.swap.rank] = self.blocks[self.swap.rank]

    def cross(self):
        self.swap.wait()
        count = self.out.shape[1] // self.swap.size
        columns = self.out.shape[2]
        for index in range(self.swap.size):
            unpack(self.landed[index], self.wide, index * count, count, columns)
        self.out[self.plane.rank] = self.wide[:, 0:columns].astype(LOW)
        self.plane.start()

    def wait(self):
        self.plane.wait()

    @staticmethod
    def scratch(ctx, dp, rows, columns):
        return [
            pltpu.VMEM((ctx, packed_rows(rows // ctx, columns), 128), LOW),
            pltpu.VMEM((rows, full_lanes(columns)), WIDE),
            *Swap.semaphores(ctx),
            *PlaneGather.semaphores(dp),
        ]


class StreamSum:
    def __init__(self, parts, landed, stage, stage_sems, sems):
        self.parts, self.landed, self.stage, self.stage_sems = parts, landed, stage, stage_sems
        self.plane = PlaneSum(parts, landed, sems)

    def put(self, index, part):
        if index >= 2:
            self.move(index - 2).wait()
        self.stage[index % 2] = part.astype(LOW)
        self.move(index).start()

    def move(self, index):
        slot = index % 2
        return pltpu.make_async_copy(
            self.stage.at[slot], self.parts.at[index], self.stage_sems.at[slot]
        )

    def start(self):
        self.move(2).wait()
        self.move(3).wait()
        self.plane.start()

    def load(self, source, slot, rows):
        return pltpu.make_async_copy(
            source.at[rows], self.stage.at[slot, rows], self.stage_sems.at[slot]
        )

    def relayed(self, index):
        plane = self.plane
        rows, target = ((plane.low, plane.above), (plane.high, plane.beside))[index]
        return send(
            self.stage.at[2, rows],
            self.landed.at[2, rows],
            plane.send_sems.at[4 + index],
            plane.recv_sems.at[4 + index],
            dp=target,
        )

    def relay(self):
        plane = self.plane
        for index, block, rows in ((0, plane.above, plane.low), (1, plane.beside, plane.high)):
            plane.copy(2 * index).wait_recv()
            loads = (
                self.load(self.parts.at[block], 0, rows),
                self.load(self.landed.at[0], 1, rows),
            )
            for load in loads:
                load.start()
            for load in loads:
                load.wait()
            total = self.stage[0, rows].astype(WIDE) + self.stage[1, rows].astype(WIDE)
            self.stage[2, rows] = total.astype(LOW)
            self.relayed(index).start()

    def total(self):
        plane = self.plane
        for index in range(4):
            plane.copy(index).wait_send()
        plane.copy(1).wait_recv()
        plane.copy(3).wait_recv()
        for index in range(2):
            self.relayed(index).wait_send()
            self.relayed(index).wait_recv()
        every = pl.ds(0, self.parts.shape[1])
        loads = (
            self.load(self.parts.at[plane.rank], 0, every),
            self.load(self.landed.at[1], 1, every),
            self.load(self.landed.at[2], 2, every),
        )
        for load in loads:
            load.start()
        for load in loads:
            load.wait()
        total = self.stage[0].astype(WIDE) + self.stage[1].astype(WIDE)
        return total + self.stage[2].astype(WIDE)


class Collect:
    def __init__(self, pieces, plane, wide, blocks, came, out, sems):
        self.pieces, self.plane, self.wide, self.blocks = pieces, plane, wide, blocks
        self.came, self.out = came, out
        self.swap = Swap("ctx", blocks.at.__getitem__, came.at.__getitem__, sems)

    def cross(self):
        rows, columns = self.plane.parts.shape[1:]
        lanes = full_lanes(columns)
        self.wide[0:rows, 0:columns] = self.plane.total()
        if lanes > columns:
            self.wide[0:rows, columns:lanes] = jnp.zeros((rows, lanes - columns), WIDE)
        count = rows // self.swap.size
        for index in range(self.swap.size):
            pack(self.blocks, index, self.wide, index * count, count, 0, columns)
        self.swap.start()
        self.came[self.swap.rank] = self.blocks[self.swap.rank]

    def wait(self):
        self.swap.wait()
        count = self.out.shape[0]
        for rank in range(self.swap.size):
            unpack(self.came[rank], self.wide, 0, count, self.plane.parts.shape[2])
            for owner, here, there, size in self.pieces:
                if owner == rank:
                    self.out[:, there : there + size] = self.wide[0:count, here : here + size]
        self.swap.drain()


class Projection:
    def __init__(self, rows, blocks, wide, out, sems):
        self.rows, self.blocks, self.wide, self.out = rows, blocks, wide, out
        self.rank = lax.axis_index("ctx")
        self.core = self.rank % 2
        self.packed = rows.shape[1]
        self.plane = PlaneGather(blocks.at[self.core], sems[:2])
        self.send_sems, self.recv_sems = sems[2:4]
        self.swap = ChipSwap(lambda peer: rows.at[0], self.place, sems[4:])

    def place(self, chip):
        rows = pl.ds(pl.multiple_of(chip * self.packed, self.packed), self.packed)
        return self.blocks.at[self.core, self.plane.rank, rows]

    def start(self):
        self.swap.start()
        rows = pl.ds(pl.multiple_of(self.swap.rank * self.packed, self.packed), self.packed)
        self.blocks[self.core, self.plane.rank, rows] = self.rows[0]

    def cross(self):
        self.swap.wait()
        self.plane.start()
        self.to_other(self.plane.rank).start()

    def to_other(self, seq):
        block = self.blocks.at[self.core, seq]
        return send(
            block,
            block,
            self.send_sems.at[seq],
            self.recv_sems.at[seq],
            ctx=self.rank + 1 - 2 * self.core,
        )

    def wait(self):
        self.plane.wait()

        def others(off, carry):
            self.to_other(lax.rem(self.plane.rank + off, self.plane.size)).start()
            return carry

        lax.fori_loop(1, self.plane.size, others, 0)
        ctx = 2 * self.swap.size
        count = self.out.shape[1] // ctx

        def order(off, carry):
            seq = lax.rem(self.plane.rank + off, self.plane.size)
            self.to_other(seq).wait_recv()
            for rank in range(ctx):
                first = rank // 2 * self.packed
                rows = self.blocks[rank % 2, seq, first : first + self.packed]
                unpack(rows, self.wide, rank * count, count, D)
            self.out[seq] = self.wide[:, 0:D].astype(LOW)
            return carry

        lax.fori_loop(0, self.plane.size, order, 0)

        def sent(seq, carry):
            self.to_other(seq).wait_send()
            return carry

        lax.fori_loop(0, self.plane.size, sent, 0)
        self.swap.drain()

    @staticmethod
    def scratch(ctx, dp):
        packed = packed_rows(D // (dp * ctx), D)
        return [
            pltpu.VMEM((2, dp, ctx // 2 * packed, 128), LOW),
            pltpu.VMEM((D // dp, full_lanes(D)), WIDE),
            *PlaneGather.semaphores(dp),
            *Swap.semaphores(dp),
            *Swap.semaphores(ctx // 2),
        ]


def vector_pieces(owners, count):
    pieces = []
    for owner in range(owners):
        begin = 0
        while begin < count:
            place = owner * count + begin
            size = min(count - begin, D - place % D)
            pieces.append((owner, begin, place // D, place % D, size))
            begin += size
    return pieces


def unit_bias_pieces(rank, ctx, dp):
    units = FF // (ctx * dp)
    pieces = []
    for seq in range(dp):
        begin = 0
        while begin < units:
            place = (seq * ctx + rank) * units + begin
            size = min(units - begin, D - place % D)
            pieces.append((seq * padded_units(units) + begin, 7 + place // D, place % D, size))
            begin += size
    return pieces


GAIN_ONE, SHIFT_ONE, BIAS_QUERY, BIAS_VALUE, BIAS_PROJ, GAIN_TWO, SHIFT_TWO = range(7)
BIAS_OUT = 11
ROWS = 16


class Build:
    def __init__(self):
        self.ins, self.outs, self.scratch = {}, {}, {}

    def take(self, spec, **values):
        self.ins.update({name: (value, spec) for name, value in values.items()})

    def give(self, kind, spec, **shapes):
        for name, shape in shapes.items():
            self.outs[name] = (jax.ShapeDtypeStruct(shape, kind), spec)

    def hold(self, kind, **shapes):
        self.scratch.update({name: pltpu.VMEM(shape, kind) for name, shape in shapes.items()})

    def sems(self, **shapes):
        self.scratch.update(
            {name: pltpu.SemaphoreType.DMA(shape) for name, shape in shapes.items()}
        )

    def both(self, **sizes):
        for name, size in sizes.items():
            self.sems(**{name + "_send": (size,), name + "_recv": (size,)})

    def line_sum(self, name, ctx, tokens):
        chips = ctx // 2
        shapes = (ctx, tokens, D), (chips, tokens, D), (chips + 1, tokens, D)
        for part, shape in zip(("_blocks", "_pair", "_passing"), shapes, strict=True):
            self.hold(LOW, **{name + part: shape})
        self.both(**{name + "_pair": chips})
        self.sems(
            **{name + "_line_send": (chips, PIECES), name + "_line_recv": (2, chips, PIECES)}
        )

    def call(self, kernel, number, label):
        names = (*self.ins, *self.outs, *self.scratch)
        results = pl.pallas_call(
            functools.partial(kernel, names),
            out_shape=[shape for shape, _ in self.outs.values()],
            in_specs=[spec for _, spec in self.ins.values()],
            out_specs=[spec for _, spec in self.outs.values()],
            scratch_shapes=list(self.scratch.values()),
            compiler_params=params(number),
            name=label,
        )(*[value for value, _ in self.ins.values()])
        return Names(tuple(self.outs), results)


PIECES = 8


class Names:
    def __init__(self, names, refs):
        self.__dict__.update(zip(names, refs, strict=True))


def forward_kernel(block, whole, names, *refs):
    r = Names(names, refs)
    seq, rank = lax.axis_index("dp"), lax.axis_index("ctx")
    ctx, tokens, _ = r.rows.shape
    dp, units = r.units.shape[:2]
    width = r.mixed.shape[1]
    vec_count = 12 * D // (ctx * dp)

    def out(ref, target, index):
        return pltpu.make_async_copy(ref, target, r.out_sems.at[index])

    rows_in = LineGather(r.rows, r.rows_send, r.rows_recv)
    cots = LineGather(r.cots, r.cots_send, r.cots_recv)
    feed = LineGather(r.rows, r.feed_send, r.feed_recv)
    total = LineSum(
        r.sum_blocks,
        r.sum_pair,
        r.sum_passing,
        (r.sum_pair_send, r.sum_pair_recv, r.sum_line_send, r.sum_line_recv),
    )
    chips = feed.chips
    line = Swap(
        "ctx",
        lambda peer: r.small,
        lambda origin: r.smalls.at[seq, origin],
        (r.line_send, r.line_recv),
    )
    plane = Swap(
        "dp",
        lambda peer: r.smalls.at[seq],
        r.smalls.at.__getitem__,
        (r.plane_send, r.plane_recv),
    )
    unit_rows = PlaneGather(r.units, (r.units_send, r.units_recv))
    to_tokens = Swap(
        "ctx",
        lambda peer: r.mixed.at[pl.ds(pl.multiple_of(peer * tokens, tokens), tokens)],
        lambda origin: r.own_mixed.at[:, pl.ds(pl.multiple_of(origin * width, width), width)],
        (r.mixed_send, r.mixed_recv),
    )
    if whole:
        heads = Spread(
            r.qkv_blocks,
            r.qkv_landed,
            r.qkv_wide,
            r.qkv_mat,
            (r.qkv_send, r.qkv_recv, r.qkv_plane_send, r.qkv_plane_recv),
        )
        columns = Spread(
            r.fc_blocks,
            r.fc_landed,
            r.fc_wide,
            r.fc_mat,
            (r.fc_send, r.fc_recv, r.fc_plane_send, r.fc_plane_recv),
        )
        proj = Projection(
            r.proj_packed,
            r.proj_blocks,
            r.proj_wide,
            r.proj_mat,
            (
                r.proj_plane_send,
                r.proj_plane_recv,
                r.proj_pair_send,
                r.proj_pair_recv,
                r.proj_send,
                r.proj_recv,
            ),
        )

    def prepare():
        own = r.in_t[...].astype(WIDE).T.astype(LOW)
        r.own_in[...] = own
        r.rows[rank] = own
        r.smalls[seq, rank] = r.small[...]
        main = r.own_units.shape[0] // 16 * 16
        r.units[seq, 0:main] = r.own_units[0:main]
        if units > main:
            left = r.own_units[main:].astype(WIDE)
            zeros = jnp.zeros((units - r.own_units.shape[0], D), WIDE)
            r.units[seq, main:] = jnp.concatenate([left, zeros], 0).astype(LOW)
        if whole:
            pieces = head_pieces(ctx, width // HEAD_DIM)
            divide(r.qkv_rows, r.qkv_lanes, r.qkv_blocks, pieces, 3 * width)

    greet_all(prepare)

    line.start()
    if whole:
        heads.start()
    unit_rows.start()
    if whole:
        count = r.proj_rows.shape[0]
        r.proj_lanes[0:count, 0:D] = r.proj_rows[...].astype(WIDE)
        r.proj_lanes[0:count, D:] = jnp.zeros((count, full_lanes(D) - D), WIDE)
        pack(r.proj_packed, 0, r.proj_lanes, 0, count, 0, D)
        heads.swap.drain()
        proj.start()
    rows_in.pass_on(rank)
    own_cot = r.cot_t[...].astype(WIDE).T.astype(LOW)
    r.own_cot[...] = own_cot
    r.cots[rank] = own_cot
    line.wait()
    plane.start()
    if whole:
        heads.cross()
        divide(r.fc_rows, r.fc_lanes, r.fc_blocks, unit_pieces(ctx, dp), dp * units)

    def arrivals(gather):
        def arrive(index, carry):
            gather.arrive(1 + index // 4, index % 4)
            return carry

        return arrive

    rows_in.arrive(0, 2)
    lax.fori_loop(0, 4, arrivals(rows_in), 0)
    if whole:
        heads.plane.relay()
        columns.start()
        proj.cross()
    lax.fori_loop(4, 4 * (chips - 1), arrivals(rows_in), 0)
    if whole:
        proj.plane.relay()
    rows_in.finish()
    docs = jnp.broadcast_to(r.docs[...], r.doc_start.shape)
    lane = lax.broadcasted_iota(jnp.int32, docs.shape, 1)
    doc_start = jnp.where(docs != pltpu.roll(docs, 1, 1), lane, 0)
    shift = 1
    while shift < docs.shape[1]:
        earlier = jnp.where(lane >= shift, pltpu.roll(doc_start, shift, 1), 0)
        doc_start = jnp.maximum(doc_start, earlier)
        shift *= 2
    r.doc_start[...] = doc_start
    plane.wait()
    r.vectors[...] = jnp.zeros_like(r.vectors)
    for owner, begin, row, lane, size in vector_pieces(ctx * dp, vec_count):
        r.vectors[row : row + 1, lane : lane + size] = r.smalls[
            owner // ctx, owner % ctx, 0:1, begin : begin + size
        ]
    r.bias_units[...] = jnp.zeros_like(r.bias_units)
    for owner in range(ctx):

        @pl.when(rank == owner)
        def _(owner=owner):
            for here, row, lane, size in unit_bias_pieces(owner, ctx, dp):
                r.bias_units[0:1, here : here + size] = r.vectors[row : row + 1, lane : lane + size]

    if whole:
        heads.wait()
        out(r.qkv_mat, r.qkv_mat_out, 0).start()
    mine = pl.ds(pl.multiple_of(rank * width, width), width)
    bias = jnp.concatenate(
        [
            r.vectors[BIAS_QUERY : BIAS_QUERY + 1, mine],
            jnp.zeros((1, width), WIDE),
            r.vectors[BIAS_VALUE : BIAS_VALUE + 1, mine],
        ],
        1,
    )

    def project(index, carry):
        both = pl.ds(2 * index, 2)
        normed, _ = normalize(r.rows[both].reshape(2 * tokens, D).astype(WIDE))
        attn_in = normed * r.vectors[GAIN_ONE : GAIN_ONE + 1, 0:D]
        attn_in = (attn_in + r.vectors[SHIFT_ONE : SHIFT_ONE + 1, 0:D]).astype(LOW)
        r.rows[both] = attn_in.reshape(2, tokens, D)
        rows = pl.ds(pl.multiple_of(2 * index * tokens, 2 * tokens), 2 * tokens)
        r.qkv[rows] = (dot(attn_in, r.qkv_mat[...].reshape(D, 3 * width)) + bias).astype(LOW)
        return carry

    lax.fori_loop(0, chips, project, 0)
    out(r.rows, r.attn_in_out, 1).start()
    out(r.qkv, r.qkv_out, 2).start()
    cots.pass_on(rank)
    if whole:
        columns.cross()
    attend_body(block, r.qkv, r.doc_start, r.mixed, r.stats, r.value_t)
    out(r.rows, r.attn_in_out, 1).wait()
    to_tokens.start()
    r.own_mixed[:, mine] = r.mixed[pl.ds(pl.multiple_of(rank * tokens, tokens), tokens)]
    if whole:
        proj.wait()
        out(r.proj_mat, r.proj_mat_out, 3).start()
        columns.plane.relay()
    unit_rows.relay()
    to_tokens.wait()
    resid = dot(r.own_mixed[:, 0:D], r.proj_mat[...].reshape(D, D))
    resid = resid + r.own_in[...].astype(WIDE) + r.vectors[BIAS_PROJ : BIAS_PROJ + 1, 0:D]
    r.resid[...] = resid
    normed, _ = normalize(resid)
    ffn_in = normed * r.vectors[GAIN_TWO : GAIN_TWO + 1, 0:D]
    r.rows[rank] = (ffn_in + r.vectors[SHIFT_TWO : SHIFT_TWO + 1, 0:D]).astype(LOW)
    feed.pass_on(rank)
    cots.arrive(0, 2)
    lax.fori_loop(0, 4, arrivals(cots), 0)
    unit_rows.wait()
    if whole:
        columns.wait()

    def keep(chip, slot, which=range(3)):
        both = pl.ds(2 * chip, 2)
        kept = ((r.act, r.act_out), (r.pre, r.pre_out), (r.part, r.part_out))
        return [
            pltpu.make_async_copy(
                kept[index][0].at[slot], kept[index][1].at[both], r.keep_sems.at[index, slot]
            )
            for index in which
        ]

    def pass_rows(chip):
        both = pl.ds(2 * chip, 2)
        return [
            pltpu.make_async_copy(ref.at[both], target.at[both], r.pass_sems.at[index, chip])
            for index, (ref, target) in enumerate(((r.rows, r.ffn_out), (r.cots, r.cots_out)))
        ]

    def work(chip, done):
        both = pl.ds(2 * chip, 2)
        slot = done % 2

        @pl.when(done >= 2)
        def _():
            for copy in keep(chip, slot):
                copy.wait()

        for copy in pass_rows(chip):
            copy.start()
        fc = r.fc_mat[...].reshape(D, dp * units)
        mat = r.units[...].reshape(dp * units, D)
        pre = dot(r.rows[both].reshape(2 * tokens, D), fc) + r.bias_units[0:1]
        bend = jnp.tanh(0.7978845608028654 * (pre + 0.044715 * pre * pre * pre))
        act = (0.5 * pre * (1.0 + bend)).astype(LOW)
        r.act[slot] = act.reshape(2, tokens, -1)
        slope = 0.5 * (1.0 + bend) + 0.5 * pre * (1.0 - bend * bend) * 0.7978845608028654 * (
            1.0 + 3 * 0.044715 * pre * pre
        )
        grad_act = dot(r.cots[both].reshape(2 * tokens, D), mat, 1, 1)
        grad_pre = (slope * grad_act).astype(LOW)
        r.pre[slot] = grad_pre.reshape(2, tokens, -1)
        r.sum_blocks[both] = dot(grad_pre, fc, 1, 1).astype(LOW).reshape(2, tokens, D)
        total.pair_copy(chip).start()
        for copy in keep(chip, slot, (0, 1)):
            copy.start()

    def give_out(chip, done):
        slot = done % 2
        act = r.act[slot].reshape(2 * tokens, dp * units)
        mat = r.units[...].reshape(dp * units, D)
        r.part[slot] = dot(act, mat).astype(LOW).reshape(2, tokens, D)
        keep(chip, slot, (2,))[0].start()

    def step(index, done):
        distance, side = index // 2, index % 2
        near = distance < chips
        origin_chip = rank // 2 + jnp.where(side == 0, -distance, distance)
        valid = near & (origin_chip >= 0) & (origin_chip < chips) & ((distance > 0) | (side == 0))

        @pl.when(near)
        def _():
            @pl.when(side == 0)
            def _():
                @pl.when(distance > 1)
                def _():
                    cots.arrive(distance, 0)
                    cots.arrive(distance, 1)

                feed.arrive(distance, 0)
                feed.arrive(distance, 1)

            @pl.when(distance > 1)
            def _():
                cots.arrive(distance, 2 + side)

            feed.arrive(distance, 2 + side)

            @pl.when(valid)
            def _():
                work(origin_chip, done)

        after = done + valid.astype(jnp.int32)

        @pl.when(side == 1)
        def _():
            def way(index, carry):
                total.near_first(distance, index)
                return carry

            lax.fori_loop(0, 2, way, 0)

            def output(index, carry):
                chip = rank // 2 + jnp.where(index == 0, -distance, distance)
                here = near & (chip >= 0) & (chip < chips) & ((distance > 0) | (index == 0))
                later = (index == 0) & valid & (distance > 0)

                @pl.when(here)
                def _():
                    give_out(chip, after - 1 - later.astype(jnp.int32))

                return carry

            lax.fori_loop(0, 2, output, 0)

        return after

    lax.fori_loop(0, 2 * (2 * chips - 1), step, jnp.int32(0))
    total.finish(r.grad)

    feed.finish()
    cots.finish()
    line.drain()
    plane.drain()
    to_tokens.drain()
    for slot in range(2):
        for copy in keep(0, slot):
            copy.wait()

    def passed(chip, carry):
        for copy in pass_rows(chip):
            copy.wait()
        return carry

    lax.fori_loop(0, chips, passed, 0)
    out(r.qkv, r.qkv_out, 2).wait()
    if whole:
        out(r.qkv_mat, r.qkv_mat_out, 0).wait()
        out(r.proj_mat, r.proj_mat_out, 3).wait()
        columns.swap.drain()


def forward(small, in_t, cot_t, unit_rows, docs, mats, slots, whole, block):
    ctx, dp = lax.axis_size("ctx"), lax.axis_size("dp")
    tokens = in_t.shape[1]
    length = ctx * tokens
    width = slots * HEAD_DIM
    units = padded_units(unit_rows.shape[0])
    columns = dp * units
    chips = ctx // 2
    rows = D // dp
    count = rows // ctx
    high = -(-count // 8) * 8
    b = Build()
    b.take(VMEM, small=small, in_t=in_t, cot_t=cot_t, own_units=unit_rows, docs=docs)
    if whole:
        b.take(VMEM, qkv_rows=mats[0], fc_rows=mats[1], proj_rows=mats[2])
    else:
        b.take(VMEM, qkv_mat=mats[0], fc_mat=mats[1], proj_mat=mats[2])
    b.give(
        WIDE,
        VMEM,
        vectors=(ROWS, max(full_lanes(D), ctx * width)),
        stats=(8, length),
        resid=(tokens, D),
        grad=(tokens, D),
    )
    b.give(
        LOW, VMEM, own_mixed=(tokens, ctx * width), own_in=(tokens, D), own_cot=(tokens, D)
    )
    b.give(jnp.int32, VMEM, doc_start=(8, length))
    b.give(
        LOW,
        HBM,
        attn_in_out=(ctx, tokens, D),
        qkv_out=(length, 3 * width),
        cots_out=(ctx, tokens, D),
        ffn_out=(ctx, tokens, D),
        act_out=(ctx, tokens, columns),
        pre_out=(ctx, tokens, columns),
        part_out=(ctx, tokens, D),
    )
    if whole:
        b.give(LOW, HBM, qkv_mat_out=(dp, rows, 3 * width), proj_mat_out=(dp, rows, D))
    b.hold(
        LOW,
        rows=(ctx, tokens, D),
        cots=(ctx, tokens, D),
        units=(dp, units, D),
        qkv=(length, 3 * width),
        mixed=(length, width),
        value_t=(width, length),
        act=(2, 2, tokens, columns),
        pre=(2, 2, tokens, columns),
        part=(2, 2, tokens, D),
    )
    b.hold(WIDE, smalls=(dp, ctx, *small.shape), bias_units=(8, columns))
    b.line_sum("sum", ctx, tokens)
    b.sems(
        out_sems=(4,),
        keep_sems=(3, 2),
        pass_sems=(2, chips),
        rows_send=(3, ctx),
        rows_recv=(ctx,),
        cots_send=(3, ctx),
        cots_recv=(ctx,),
        feed_send=(3, ctx),
        feed_recv=(ctx,),
    )
    b.both(line=ctx, plane=dp, units=max(dp, 4), mixed=ctx)
    if whole:
        for name, lanes in (("qkv", 3 * width), ("fc", columns)):
            packed = (ctx, packed_rows(count, lanes), 128)
            b.hold(WIDE, **{name + "_lanes": (high, full_lanes(lanes))})
            b.hold(WIDE, **{name + "_wide": (rows, full_lanes(lanes))})
            b.hold(LOW, **{name + "_blocks": packed, name + "_landed": packed})
            b.hold(LOW, **{name + "_mat": (dp, rows, lanes)})
            b.both(**{name: ctx, name + "_plane": max(dp, 4)})
        packed = packed_rows(count, D)
        b.hold(WIDE, proj_lanes=(high, full_lanes(D)), proj_wide=(rows, full_lanes(D)))
        b.hold(
            LOW,
            proj_packed=(1, packed, 128),
            proj_blocks=(2, dp, chips * packed, 128),
            proj_mat=(dp, rows, D),
        )
        b.both(proj_plane=max(dp, 4), proj_pair=dp, proj=chips)
    return b.call(functools.partial(forward_kernel, block, whole), 0, "forward")


def back_kernel(
    block,
    grad_ref,
    resid_ref,
    own_cot,
    vectors_ref,
    proj_ref,
    qkv_ref,
    start_ref,
    stat_ref,
    ffn_hbm,
    pre_hbm,
    act_hbm,
    cot_hbm,
    part_hbm,
    resid_out,
    low_out,
    vector_out,
    units_out,
    rows_out,
    share_out,
    output_ref,
    fc_out,
    ffn,
    pre,
    act,
    cot,
    load_sems,
    own_grad,
    head_grad,
    key_t,
    key_grad,
    value_grad,
    *refs,
):
    total = LineSum(*refs[:3], refs[3:7])
    loads = [
        pltpu.make_async_copy(src, dst, load_sems.at[index])
        for index, (src, dst) in enumerate(
            (
                (part_hbm, total.blocks),
                (ffn_hbm, ffn),
                (pre_hbm, pre),
                (act_hbm, act),
                (cot_hbm, cot),
            )
        )
    ]
    for load in loads:
        load.start()
    tokens = own_cot.shape[0]
    length, width = head_grad.shape
    units = share_out.shape[0]
    swap = Swap(
        "ctx",
        lambda peer: own_grad.at[:, pl.ds(pl.multiple_of(peer * width, width), width)],
        lambda origin: head_grad.at[pl.ds(pl.multiple_of(origin * tokens, tokens), tokens)],
        refs[7:9],
    )
    share = PlaneSum(refs[9], refs[10], refs[11:13])
    dp = share.swap.size
    greet_all()
    loads[0].wait()
    total.send_pairs()
    grad = grad_ref[...]
    normed, scale = normalize(resid_ref[...])
    grad_resid = own_cot[...].astype(WIDE) + norm_back(normed, scale, vectors_ref[GAIN_TWO : GAIN_TWO + 1, 0:D], grad)
    resid_out[...] = grad_resid
    low = grad_resid.astype(LOW)
    low_out[...] = low
    own_grad[:, 0:D] = dot(low, proj_ref[...], 1, 1).astype(LOW)
    own_grad[:, D:] = jnp.zeros((tokens, own_grad.shape[1] - D), LOW)
    swap.start()
    head_grad[pl.ds(pl.multiple_of(swap.rank * tokens, tokens), tokens)] = own_grad[
        :, pl.ds(pl.multiple_of(swap.rank * width, width), width)
    ]
    vector_out[0:1] = jnp.sum(grad_resid, 0, keepdims=True)
    vector_out[1:2] = jnp.sum(grad * normed, 0, keepdims=True)
    vector_out[2:3] = jnp.sum(grad, 0, keepdims=True)
    vector_out[3:4] = jnp.sum(own_cot[...].astype(WIDE), 0, keepdims=True)
    vector_out[4:8] = jnp.zeros((4, D), WIDE)
    loads[1].wait()
    loads[2].wait()
    grad_pre = pre[...].reshape(length, -1)
    units_out[...] = dot(jnp.ones((8, length), LOW), grad_pre)
    for index in range(dp):
        rows = slice(index * (D // dp), (index + 1) * (D // dp))
        fc_out[rows] = dot(ffn[:, :, rows].reshape(length, D // dp), grad_pre, 0, 0)
    total.far_steps(0, 1)
    loads[3].wait()
    loads[4].wait()
    for index in range(dp):
        rows = slice(index * units, (index + 1) * units)
        part = dot(act[:, :, rows].reshape(length, units), cot[...].reshape(length, D), 0, 0)
        share.blocks[index] = part.astype(LOW)
    share.start()
    swap.wait()
    chips = total.chips

    def first():
        total.far_steps(1, 2)

    def second():
        total.far_steps(2, 3)
        share.relay()

    attend_back_body(
        block,
        qkv_ref,
        start_ref,
        stat_ref,
        head_grad,
        rows_out,
        key_t,
        key_grad,
        value_grad,
        {1: first, 2: second},
    )
    total.far_steps(3, 2 * chips - 1)
    total.finish(output_ref)
    bias = vectors_ref[BIAS_OUT : BIAS_OUT + 1, 0:D]
    output_ref[...] = output_ref[...] + resid_ref[...] + bias
    share_out[...] = share.total()
    swap.drain()
    share.drain()


def back(
    grad, resid, own_cot, vectors, proj, qkv, doc_start, stats, ffn, pre, act, cot, part, block
):
    ctx, tokens, _ = cot.shape
    dp = lax.axis_size("dp")
    length = ctx * tokens
    width = qkv.shape[1] // 3
    columns = act.shape[2]
    units = columns // dp
    shapes = [
        jax.ShapeDtypeStruct((tokens, D), WIDE),
        jax.ShapeDtypeStruct((tokens, D), LOW),
        jax.ShapeDtypeStruct((8, D), WIDE),
        jax.ShapeDtypeStruct((8, columns), WIDE),
        jax.ShapeDtypeStruct((length, 3 * width), LOW),
        jax.ShapeDtypeStruct((units, D), WIDE),
        jax.ShapeDtypeStruct((tokens, D), WIDE),
        jax.ShapeDtypeStruct((D, columns), WIDE),
    ]
    scratch = [
        pltpu.VMEM(ffn.shape, LOW),
        pltpu.VMEM(pre.shape, LOW),
        pltpu.VMEM(act.shape, LOW),
        pltpu.VMEM(cot.shape, LOW),
        pltpu.SemaphoreType.DMA((5,)),
        pltpu.VMEM((tokens, ctx * width), LOW),
        pltpu.VMEM((length, width), LOW),
        pltpu.VMEM((width, length), LOW),
        pltpu.VMEM((length, width), WIDE),
        pltpu.VMEM((length, width), WIDE),
        *LineSum.scratch(ctx, tokens, D, 4),
        *Swap.semaphores(ctx),
        pltpu.VMEM((dp, units, D), LOW),
        pltpu.VMEM((dp, units, D), LOW),
        *PlaneSum.semaphores(dp),
    ]
    return pl.pallas_call(
        functools.partial(back_kernel, block),
        out_shape=shapes,
        in_specs=[VMEM] * 8 + [HBM] * 5,
        out_specs=[VMEM] * 8,
        scratch_shapes=scratch,
        compiler_params=params(3),
        name="back",
    )(grad, resid, own_cot, vectors, proj, qkv, doc_start, stats, ffn, pre, act, cot, part)


class ProjectionSum:
    def __init__(self, out, mixed, low, plane, wide, blocks, came, pair_sems, sems):
        self.out, self.mixed, self.low, self.plane = out, mixed, low, plane
        self.wide, self.blocks, self.came = wide, blocks, came
        self.send_sems, self.recv_sems = pair_sems
        self.rank = lax.axis_index("ctx")
        self.core = self.rank % 2
        self.swap = ChipSwap(blocks.at.__getitem__, came.at.__getitem__, sems)

    def pair_copies(self):
        return [
            send(
                ref.at[self.core],
                ref.at[self.core],
                self.send_sems.at[index],
                self.recv_sems.at[index],
                ctx=self.rank + 1 - 2 * self.core,
            )
            for index, ref in enumerate((self.mixed, self.low))
        ]

    def start(self, mixed, low):
        self.mixed[self.core] = mixed
        self.low[self.core] = low
        for copy in self.pair_copies():
            copy.start()

    def multiply(self):
        for copy in self.pair_copies():
            copy.wait_recv()
        dp, rows = self.plane.parts.shape[:2]
        chips = self.swap.size
        tokens = 2 * self.low.shape[1]
        count = self.out.shape[0]
        mixed = self.mixed[...].reshape(tokens, -1)[:, 0:D]
        low = self.low[...].reshape(tokens, D)
        feature = lax.broadcasted_iota(jnp.int32, (D, rows), 0)
        column = lax.broadcasted_iota(jnp.int32, (1, rows), 1)
        for index in range(dp):
            owner = index * 2 * chips + column // count * 2 + self.core
            wanted = jnp.where(column < chips * count, owner * count + column % count, -1)
            chosen = jnp.where(feature == wanted, 1.0, 0.0).astype(LOW)
            picked = dot(mixed, chosen).astype(LOW)
            self.plane.put(index, dot(picked, low, 0, 0))

    def cross(self):
        count = self.out.shape[0]
        rows = self.plane.parts.shape[1]
        lanes = full_lanes(D)
        self.wide[0:rows, 0:D] = self.plane.total()
        self.wide[0:rows, D:lanes] = jnp.zeros((rows, lanes - D), WIDE)
        for chip in range(self.swap.size):
            pack(self.blocks, chip, self.wide, chip * count, count, 0, D)
        self.swap.start()

    def wait(self):
        self.swap.wait()
        total = self.blocks[self.swap.rank].astype(WIDE)
        for off in range(1, self.swap.size):
            total = total + self.came[lax.rem(self.swap.rank + off, self.swap.size)].astype(WIDE)
        count = self.out.shape[0]
        unpack(total, self.wide, 0, count, D)
        self.out[...] = self.wide[0:count, 0:D]
        for copy in self.pair_copies():
            copy.wait_send()
        self.swap.drain()


def partial_sums(total, rows_ref, mat):
    chips, tokens = total.chips, total.blocks.shape[1]

    def one(index, carry):
        off = jnp.where(index % 2 == 0, -(index // 2), index // 2 + 1)
        chip = lax.rem(chips - 1 + off, chips)
        rows = pl.ds(pl.multiple_of(2 * chip * tokens, 2 * tokens), 2 * tokens)
        part = dot(rows_ref[rows], mat[...].reshape(D, -1), 1, 1).astype(LOW)
        total.blocks[pl.ds(2 * chip, 2)] = part.reshape(2, tokens, D)
        total.pair_copy(chip).start()
        return carry

    lax.fori_loop(0, chips, one, 0)


def last_kernel(
    rows_ref,
    mat_ref,
    in_ref,
    own_ref,
    resid_ref,
    vectors_ref,
    grad_out,
    vector_out,
    heads_out,
    mat_out,
    grad,
    *refs,
):
    total = LineSum(*refs[:3], refs[3:7])
    chips = total.chips
    dp = lax.axis_size("dp")
    greet_line(chips)
    partial_sums(total, rows_ref, mat_ref)
    total.far_steps(0, 1)
    for index in range(dp):
        rows = slice(index * (D // dp), (index + 1) * (D // dp))
        mat_out[rows] = dot(in_ref[:, rows], rows_ref[...], 0, 0)
    total.far_steps(1, 2 * chips - 1)
    heads_out[...] = dot(jnp.ones((8, rows_ref.shape[0]), LOW), rows_ref[...])
    total.finish(grad)
    normed, scale = normalize(own_ref[...].astype(WIDE))
    incoming = grad[...]
    gain = vectors_ref[GAIN_ONE : GAIN_ONE + 1, 0:D]
    grad_out[...] = resid_ref[...] + norm_back(normed, scale, gain, incoming)
    vector_out[0:1] = jnp.sum(incoming * normed, 0, keepdims=True)
    vector_out[1:2] = jnp.sum(incoming, 0, keepdims=True)
    vector_out[2:8] = jnp.zeros((6, D), WIDE)


def last(rows, mat, attn_in, own_in, resid, vectors):
    ctx = lax.axis_size("ctx")
    tokens = own_in.shape[0]
    columns = rows.shape[1]
    return pl.pallas_call(
        last_kernel,
        out_shape=[
            jax.ShapeDtypeStruct((tokens, D), WIDE),
            jax.ShapeDtypeStruct((8, D), WIDE),
            jax.ShapeDtypeStruct((8, columns), WIDE),
            jax.ShapeDtypeStruct((D, columns), WIDE),
        ],
        in_specs=[VMEM] * 6,
        out_specs=[VMEM] * 4,
        scratch_shapes=[pltpu.VMEM((tokens, D), WIDE), *LineSum.scratch(ctx, tokens, D, 4)],
        compiler_params=params(4),
        name="last",
    )(rows, mat, attn_in, own_in, resid, vectors)


def vector_kernel(parts_ref, out_ref, plane_landed, line_parts, line_landed, *sems):
    seq = lax.axis_index("dp")
    swap = Swap("dp", parts_ref.at.__getitem__, plane_landed.at.__getitem__, sems[:2])
    line = Swap("ctx", line_parts.at.__getitem__, line_landed.at.__getitem__, sems[2:])
    greet_all()
    swap.start()
    swap.wait()
    total = parts_ref[seq]
    for off in range(1, swap.size):
        total = total + plane_landed[lax.rem(seq + off, swap.size)]
    line_parts[...] = total
    line.start()
    line.wait()
    total = line_parts[line.rank]
    for off in range(1, line.size):
        total = total + line_landed[lax.rem(line.rank + off, line.size)]
    out_ref[...] = total
    swap.drain()
    line.drain()


def sum_vector(parts):
    dp, ctx = parts.shape[:2]
    return pl.pallas_call(
        vector_kernel,
        out_shape=jax.ShapeDtypeStruct(parts.shape[2:], WIDE),
        in_specs=[VMEM],
        out_specs=VMEM,
        scratch_shapes=[
            pltpu.VMEM(parts.shape, WIDE),
            pltpu.VMEM(parts.shape[1:], WIDE),
            pltpu.VMEM(parts.shape[1:], WIDE),
            *PlaneSum.semaphores(dp),
            *Swap.semaphores(ctx),
        ],
        compiler_params=params(5),
        name="sum_vector",
    )(parts)


GRAD_ONE, SUM_ONE, SUM_QUERY, SUM_VALUE, SUM_RESID, GRAD_FFN, SUM_FFN = range(7)
SUM_OUT = 11


def backward_kernel(block, names, *refs):
    r = Names(names, refs)
    seq, rank = lax.axis_index("dp"), lax.axis_index("ctx")
    ctx, tokens, _ = r.big.shape
    length, width = r.head_grad.shape
    dp, owners_rows = r.fc_parts.shape[:2]
    units = r.out_parts.shape[1]
    columns = dp * units
    vec_count = 12 * D // (ctx * dp)

    def load(source, target, index):
        return pltpu.make_async_copy(source, target, r.load_sems.at[index])

    summed = LineSum(
        r.out_blocks,
        r.out_pair,
        r.out_passing,
        (r.out_pair_send, r.out_pair_recv, r.out_line_send, r.out_line_recv),
    )
    total = LineSum(
        r.in_blocks,
        r.in_pair,
        r.in_passing,
        (r.in_pair_send, r.in_pair_recv, r.in_line_send, r.in_line_recv),
    )
    chips = total.chips
    to_heads = Swap(
        "ctx",
        lambda peer: r.own_grad.at[:, pl.ds(pl.multiple_of(peer * width, width), width)],
        lambda origin: r.head_grad.at[pl.ds(pl.multiple_of(origin * tokens, tokens), tokens)],
        (r.heads_send, r.heads_recv),
    )
    some = r.stage_fc.at[:, :, pl.ds(0, 3 * width)]
    fc = Collect(
        unit_pieces(ctx, dp),
        StreamSum(
            r.fc_parts, r.fc_landed, r.stage_fc, r.stage_fc_sems, (r.fc_plane_send, r.fc_plane_recv)
        ),
        r.wide,
        r.fc_blocks,
        r.fc_came,
        r.fc_out,
        (r.fc_send, r.fc_recv),
    )
    qkv = Collect(
        head_pieces(ctx, width // HEAD_DIM),
        StreamSum(
            r.qkv_parts, r.qkv_landed, some, r.stage_fc_sems, (r.qkv_plane_send, r.qkv_plane_recv)
        ),
        r.wide,
        r.qkv_blocks,
        r.qkv_came,
        r.qkv_grad,
        (r.qkv_send, r.qkv_recv),
    )
    share = StreamSum(
        r.out_parts,
        r.out_landed,
        r.stage_out,
        r.stage_out_sems,
        (r.out_plane_send, r.out_plane_recv),
    )
    proj = ProjectionSum(
        r.proj_grad,
        r.mixed_pair,
        r.low_pair,
        StreamSum(
            r.proj_parts,
            r.proj_landed,
            r.stage_out,
            r.stage_out_sems,
            (r.proj_plane_send, r.proj_plane_recv),
        ),
        r.wide,
        r.proj_blocks,
        r.proj_came,
        (r.proj_pair_send, r.proj_pair_recv),
        (r.proj_send, r.proj_recv),
    )
    vec_plane = Swap(
        "dp",
        r.vec_parts.at.__getitem__,
        r.vec_landed.at.__getitem__,
        (r.vec_plane_send, r.vec_plane_recv),
    )
    vec_line = Swap(
        "ctx", r.vec_rows.at.__getitem__, r.vec_came.at.__getitem__, (r.vec_send, r.vec_recv)
    )
    heads_mat = r.mat.at[:, :, pl.ds(0, 3 * width)]
    loads = [
        load(r.proj_mat, r.mat, 0),
        load(r.part, r.out_blocks, 1),
        load(r.ffn, r.big, 2),
        load(r.pre_act, r.feed, 3),
        load(r.qkv_mat, heads_mat, 0),
        load(r.attn_in, r.big, 2),
        load(r.act, r.feed, 3),
        load(r.cots, r.big, 2),
    ]
    for index in range(4):
        loads[index].start()
    greet_all()

    grad = r.grad[...]
    normed, scale = normalize(r.resid[...])
    gain = r.vectors[GAIN_TWO : GAIN_TWO + 1, 0:D]
    own_cot = r.own_cot[...].astype(WIDE)
    grad_resid = own_cot + norm_back(normed, scale, gain, grad)
    r.grad_resid[...] = grad_resid
    low = grad_resid.astype(LOW)
    loads[0].wait()
    r.own_grad[:, 0:D] = dot(low, r.mat[...].reshape(D, D), 1, 1).astype(LOW)
    r.own_grad[:, D:] = jnp.zeros((tokens, r.own_grad.shape[1] - D), LOW)
    to_heads.start()
    loads[4].start()
    mine = pl.ds(pl.multiple_of(rank * width, width), width)
    here = pl.ds(pl.multiple_of(rank * tokens, tokens), tokens)
    r.head_grad[here] = r.own_grad[:, mine]
    proj.start(r.own_mixed[...], low)
    loads[1].wait()
    summed.send_pairs()
    vec = r.vec
    vec[...] = jnp.zeros_like(vec)

    def note(row, value):
        vec[row : row + 1, 0:D] = jnp.sum(value, 0, keepdims=True)

    note(SUM_RESID, grad_resid)
    note(GRAD_FFN, grad * normed)
    note(SUM_FFN, grad)
    note(SUM_OUT, own_cot)

    loads[2].wait()
    loads[3].wait()
    grad_pre = r.feed[...].reshape(length, columns)
    sums = dot(jnp.ones((8, length), LOW), grad_pre)[0:1]
    for owner in range(ctx):

        @pl.when(rank == owner)
        def _(owner=owner):
            for place, row, lane, size in unit_bias_pieces(owner, ctx, dp):
                vec[row : row + 1, lane : lane + size] = sums[:, place : place + size]

    def by_parts(plane, left, right, count):
        for index in range(dp):
            rows = slice(index * count, (index + 1) * count)
            plane.put(index, dot(left[:, :, rows].reshape(length, count), right, 0, 0))
        plane.start()

    by_parts(fc.plane, r.big, grad_pre, owners_rows)
    loads[5].start()
    loads[6].start()
    summed.far_steps(0, 1)
    proj.multiply()

    to_heads.wait()

    def first():
        summed.far_steps(1, 2)

    def second():
        summed.far_steps(2, 3)
        fc.plane.relay()
        proj.plane.start()

    attend_back_body(
        block,
        r.qkv,
        r.doc_start,
        r.stats,
        r.head_grad,
        r.rows,
        r.key_t,
        r.key_grad,
        r.value_grad,
        {1: first, 2: second},
    )
    loads[4].wait()
    partial_sums(total, r.rows, heads_mat)
    total.far_steps(0, 1)
    summed.far_steps(3, 4)
    fc.cross()
    loads[5].wait()
    by_parts(qkv.plane, r.big, r.rows[...], owners_rows)
    loads[7].start()
    total.far_steps(1, 2)
    summed.far_steps(4, 5)
    proj.plane.relay()
    total.far_steps(2, 3)
    summed.far_steps(5, 2 * chips - 1)
    proj.cross()
    qkv.plane.relay()
    loads[6].wait()
    loads[7].wait()
    by_parts(share, r.feed, r.big[...].reshape(length, D), units)
    total.far_steps(3, 2 * chips - 1)
    sums = dot(jnp.ones((8, length), LOW), r.rows[...])
    vec[SUM_QUERY : SUM_QUERY + 1, mine] = sums[0:1, 0:width]
    vec[SUM_VALUE : SUM_VALUE + 1, mine] = sums[0:1, 2 * width :]
    total.finish(r.came)

    incoming = r.came[...]
    normed, scale = normalize(r.own_in[...].astype(WIDE))
    gain = r.vectors[GAIN_ONE : GAIN_ONE + 1, 0:D]
    grad_in = r.grad_resid[...] + norm_back(normed, scale, gain, incoming)
    r.grad_in_t[...] = grad_in.T
    note(GRAD_ONE, incoming * normed)
    note(SUM_ONE, incoming)
    for owner, begin, row, lane, size in vector_pieces(ctx * dp, vec_count):
        r.vec_parts[owner // ctx, owner % ctx, 0:1, begin : begin + size] = vec[
            row : row + 1, lane : lane + size
        ]
    vec_plane.start()
    qkv.cross()
    vec_plane.wait()
    rows = r.vec_parts[seq]
    for off in range(1, dp):
        rows = rows + r.vec_landed[lax.rem(seq + off, dp)]
    r.vec_rows[...] = rows
    vec_line.start()
    summed.finish(r.came)
    bias = r.vectors[BIAS_OUT : BIAS_OUT + 1, 0:D]
    r.output_t[...] = (r.came[...] + r.resid[...] + bias).T
    fc.wait()
    share.relay()
    proj.wait()
    vec_line.wait()
    row = r.vec_rows[rank]
    for off in range(1, ctx):
        row = row + r.vec_came[lax.rem(rank + off, ctx)]
    r.vec_out[...] = row
    qkv.wait()
    r.out_grad[...] = share.total()
    to_heads.drain()
    vec_plane.drain()
    vec_line.drain()


def backward(made, block):
    ctx, dp = lax.axis_size("ctx"), lax.axis_size("dp")
    tokens = made.own_in.shape[0]
    length = ctx * tokens
    width = made.qkv_out.shape[1] // 3
    columns = made.act_out.shape[2]
    units = columns // dp
    chips = ctx // 2
    rows = D // dp
    count = rows // ctx
    lanes = full_lanes(12 * D // (ctx * dp))
    b = Build()
    b.take(
        VMEM,
        grad=made.grad,
        resid=made.resid,
        own_cot=made.own_cot,
        own_in=made.own_in,
        vectors=made.vectors,
        own_mixed=made.own_mixed,
        qkv=made.qkv_out,
        doc_start=made.doc_start,
        stats=made.stats,
    )
    b.take(
        HBM,
        proj_mat=made.proj_mat_out,
        qkv_mat=made.qkv_mat_out,
        part=made.part_out,
        ffn=made.ffn_out,
        pre_act=made.pre_out,
        attn_in=made.attn_in_out,
        act=made.act_out,
        cots=made.cots_out,
    )
    b.give(
        WIDE,
        VMEM,
        output_t=(D, tokens),
        grad_in_t=(D, tokens),
        qkv_grad=(count, 3 * D),
        proj_grad=(count, D),
        fc_out=(count, FF),
        out_grad=(units, D),
        vec_out=(1, lanes),
    )
    for name, shape in (
        ("fc", (rows, columns)),
        ("qkv", (rows, 3 * width)),
        ("out", (units, D)),
        ("proj", (units, D)),
    ):
        b.give(LOW, HBM, **{name + "_parts": (dp, *shape), name + "_landed": (3, *shape)})
        b.both(**{name + "_plane": 6})
    b.hold(
        LOW,
        mat=(dp, rows, D),
        big=(ctx, tokens, D),
        feed=(ctx, tokens, columns),
        stage_fc=(3, rows, columns),
        stage_out=(3, units, D),
        proj_blocks=(chips, packed_rows(count, D), 128),
        proj_came=(chips, packed_rows(count, D), 128),
        mixed_pair=(2, tokens, ctx * width),
        low_pair=(2, tokens, D),
        own_grad=(tokens, ctx * width),
        head_grad=(length, width),
        rows=(length, 3 * width),
        key_t=(width, length),
    )
    for name, wide in (("fc", columns), ("qkv", 3 * width)):
        packed = (ctx, packed_rows(count, wide), 128)
        b.hold(LOW, **{name + "_blocks": packed, name + "_came": packed})
    for name in ("out", "in"):
        b.line_sum(name, ctx, tokens)
    b.hold(
        WIDE,
        wide=(rows, full_lanes(D)),
        key_grad=(length, width),
        value_grad=(length, width),
        grad_resid=(tokens, D),
        came=(tokens, D),
        vec=(ROWS, max(full_lanes(D), ctx * width)),
        vec_parts=(dp, ctx, 1, lanes),
        vec_landed=(dp, ctx, 1, lanes),
        vec_rows=(ctx, 1, lanes),
        vec_came=(ctx, 1, lanes),
    )
    b.both(fc=ctx, qkv=ctx, proj=chips, proj_pair=2, heads=ctx, vec_plane=dp, vec=ctx)
    b.sems(load_sems=(4,), stage_fc_sems=(3,), stage_out_sems=(3,))
    assert units == -(-(chips * count) // 16) * 16
    return b.call(functools.partial(backward_kernel, block), 6, "backward")


def gather_rows(block):
    return lax.all_gather(block, ("dp", "ctx"), axis=0, tiled=True)


def by_rank_heads(rows, ctx, slots):
    count = rows.shape[0]
    split = rows.reshape(count, 3, D)
    split = jnp.pad(split, ((0, 0), (0, 0), (0, (ctx * slots - HEADS) * HEAD_DIM)))
    split = split.reshape(count, 3, ctx, slots * HEAD_DIM)
    return split.transpose(2, 0, 1, 3).reshape(ctx, count, 3 * slots * HEAD_DIM)


def from_rank_heads(blocks, slots):
    ctx, count = blocks.shape[:2]
    split = blocks.reshape(ctx, count, 3, slots * HEAD_DIM).transpose(1, 2, 0, 3)
    return split.reshape(count, 3, ctx * slots * HEAD_DIM)[:, :, :D].reshape(count, 3 * D)


def padded_units(units):
    return -(-units // 16) * 16


def by_rank_units(rows, ctx, dp):
    count = rows.shape[0]
    units = FF // (dp * ctx)
    split = rows.reshape(count, dp, ctx, units).transpose(2, 0, 1, 3)
    split = jnp.pad(split, ((0, 0), (0, 0), (0, 0), (0, padded_units(units) - units)))
    return split.reshape(ctx, count, dp * padded_units(units))


def from_rank_units(blocks, dp):
    ctx, count = blocks.shape[:2]
    units = FF // (dp * ctx)
    split = blocks.reshape(ctx, count, dp, padded_units(units))[..., :units]
    return split.transpose(1, 2, 0, 3).reshape(count, FF)


def shards(
    hidden_in, qkv_weight, proj_weight, fc_weight, out_weight, small_params, segments, cotangent
):
    tokens = hidden_in.shape[1]
    length = segments.shape[1]
    ctx = lax.axis_size("ctx")
    dp = lax.axis_size("dp")
    owners = dp * ctx
    rank = lax.axis_index("ctx")
    slots = -(-HEADS // ctx)
    width = slots * HEAD_DIM
    units = FF // owners
    rows = D // owners
    whole = D % owners == 0 and dp == 4
    block = min(256, length)
    both = ("dp", "ctx")

    vec_count = small_params.shape[0]
    small = jnp.pad(small_params.astype(WIDE), (0, full_lanes(vec_count) - vec_count))[None]
    unit_rows = out_weight.reshape(units, D)
    if whole:
        mats = (
            qkv_weight.reshape(rows, 3 * D),
            fc_weight.reshape(rows, FF),
            proj_weight.reshape(rows, D),
        )
    else:
        mat_qkv = by_rank_heads(gather_rows(qkv_weight).reshape(D, 3 * D), ctx, slots)
        mat_qkv = lax.dynamic_index_in_dim(mat_qkv, rank, 0, keepdims=False)
        mat_fc = by_rank_units(gather_rows(fc_weight).reshape(D, FF), ctx, dp)
        mat_fc = lax.dynamic_index_in_dim(mat_fc, rank, 0, keepdims=False)
        mat_proj = gather_rows(proj_weight).reshape(D, D)
        mats = (mat_qkv, mat_fc, mat_proj)
    made = forward(
        small, hidden_in[0].T, cotangent[0].T, unit_rows, segments, mats, slots, whole, block
    )
    if whole:
        done = backward(made, block)
        return (
            done.output_t.T[None],
            done.grad_in_t.T[None],
            done.qkv_grad.reshape(-1),
            done.proj_grad.reshape(-1),
            done.fc_out.reshape(-1),
            done.out_grad[:units].reshape(-1),
            done.vec_out[0, :vec_count],
        )
    vectors = made.vectors

    grad_resid, resid_low, sums_two, sums_units, grad_rows, grad_out, output, grad_fc = back(
        made.grad,
        made.resid,
        cotangent[0],
        vectors,
        mat_proj,
        made.qkv_out,
        made.doc_start,
        made.stats,
        made.ffn_out,
        made.pre_out,
        made.act_out,
        made.cots_out,
        made.part_out,
        block,
    )
    grad_input, sums_one, sums_heads, grad_qkv = last(
        grad_rows,
        mat_qkv,
        made.attn_in_out.reshape(length, D),
        hidden_in[0],
        grad_resid,
        vectors,
    )
    here = (jnp.arange(ctx) == rank)[:, None, None]
    full_fc = from_rank_units(jnp.where(here, grad_fc[None], 0.0), dp).reshape(-1)
    full_qkv = from_rank_heads(jnp.where(here, grad_qkv[None], 0.0), slots).reshape(-1)
    grad_proj = dot(made.own_mixed[:, :D], resid_low, 0, 0).reshape(-1)
    share_fc, share_qkv, share_proj = [
        lax.psum_scatter(full, both, scatter_dimension=0, tiled=True)
        for full in (full_fc, full_qkv, grad_proj)
    ]

    def spread_heads(part):
        padded = jnp.zeros((ctx * width,), WIDE)
        return lax.dynamic_update_slice_in_dim(padded, part, rank * width, 0)[:D]

    sums_units = sums_units[0].reshape(dp, 1, -1)[:, :, :units]
    sums_units = lax.dynamic_update_slice_in_dim(
        jnp.zeros((dp, ctx, units), WIDE), sums_units, rank, 1
    ).reshape(FF)
    vector = jnp.concatenate(
        [
            sums_one[0],
            sums_one[1],
            spread_heads(sums_heads[0, :width]),
            spread_heads(sums_heads[0, 2 * width :]),
            sums_two[0],
            sums_two[1],
            sums_two[2],
            sums_units,
            sums_two[3],
        ]
    ).reshape(owners, vec_count)
    vec_pad = -(-vec_count // 1024) * 1024
    vector = jnp.pad(vector, ((0, 0), (0, vec_pad - vec_count))).reshape(dp, ctx, -1, 128)
    share_vector = sum_vector(vector)
    return (
        output[None],
        grad_input[None],
        share_qkv.astype(WIDE).reshape(-1),
        share_proj.astype(WIDE).reshape(-1),
        share_fc.astype(WIDE).reshape(-1),
        grad_out[:units].reshape(-1),
        share_vector.reshape(-1)[:vec_count],
    )


def solution(mesh):
    flat = P(("dp", "ctx"))
    rows = P("dp", "ctx", None)
    return jax.shard_map(
        shards,
        mesh=mesh,
        in_specs=(rows, flat, flat, flat, flat, flat, P("dp", None), rows),
        out_specs=(rows, rows, flat, flat, flat, flat, flat),
        check_vma=False,
    )
```

```python
import functools

import jax
import jax.numpy as jnp
from jax import lax
from jax.experimental import pallas as pl
from jax.experimental.pallas import tpu as pltpu
from jax.sharding import PartitionSpec as P

D = 1600
HEADS = 25
HEAD_DIM = 64
FF = 6400
EPSILON = 1e-05
LOW = jnp.bfloat16
WIDE = jnp.float32
MIB = 1024 * 1024


def dot(left, right, left_dim=1, right_dim=0):
    return lax.dot_general(
        left, right, (((left_dim,), (right_dim,)), ((), ())), preferred_element_type=WIDE
    )


def normalize(rows):
    centre = rows - jnp.mean(rows, -1, keepdims=True)
    spread = jnp.mean(centre * centre, -1, keepdims=True)
    scale = lax.rsqrt(spread + EPSILON)
    return centre * scale, scale


def norm_back(normed, scale, gain, incoming):
    scaled = gain * incoming
    return scale * (
        scaled
        - jnp.mean(scaled, -1, keepdims=True)
        - normed * jnp.mean(scaled * normed, -1, keepdims=True)
    )


def head_lanes(head, width):
    lane = lax.broadcasted_iota(jnp.int32, (1, width), 1)
    return (lane // HEAD_DIM) == head


def allowed_scores(scores, doc_start, first_query, keys, block):
    key_pos = lax.broadcasted_iota(jnp.int32, (keys, block), 0)
    query_pos = first_query + lax.broadcasted_iota(jnp.int32, (keys, block), 1)
    seen = (key_pos >= doc_start) & (key_pos <= query_pos)
    return jnp.where(seen, scores, -1e30)


def attend_body(block, qkv_ref, start_ref, mixed_ref, stat_ref, value_t):
    length = qkv_ref.shape[0]
    width = mixed_ref.shape[1]
    slots = width // HEAD_DIM
    value_t[...] = qkv_ref[:, 2 * width : 3 * width].astype(WIDE).T.astype(LOW)
    stat_ref[...] = jnp.zeros_like(stat_ref)
    for index in range(length // block):
        keys = (index + 1) * block
        rows = pl.ds(index * block, block)
        key_rows = qkv_ref[0:keys, width : 2 * width]
        doc_start = start_ref[0:1, rows]
        outs = []
        for head in range(slots):
            query = jnp.where(
                head_lanes(head, width), qkv_ref[rows, 0:width] * LOW(HEAD_DIM**-0.5), LOW(0)
            )
            scores = dot(key_rows, query, 1, 1)
            scores = allowed_scores(scores, doc_start, index * block, keys, block)
            top = jnp.max(scores, 0, keepdims=True)
            expo = jnp.exp(scores - top)
            total = jnp.sum(expo, 0, keepdims=True)
            head_rows = slice(head * HEAD_DIM, (head + 1) * HEAD_DIM)
            out = dot(value_t[head_rows, 0:keys], expo.astype(LOW))
            outs.append(out / total)
            stat_ref[head : head + 1, rows] = top + jnp.log(total)
        mixed_ref[rows, :] = jnp.concatenate(outs, 0).T.astype(LOW)


def attend_back_body(
    block, qkv_ref, start_ref, stat_ref, grad_ref, out_ref, key_t, key_grad, value_grad, after
):
    length = qkv_ref.shape[0]
    width = grad_ref.shape[1]
    slots = width // HEAD_DIM
    scale = HEAD_DIM**-0.5
    key_t[...] = qkv_ref[:, width : 2 * width].astype(WIDE).T.astype(LOW)
    key_grad[...] = jnp.zeros_like(key_grad)
    value_grad[...] = jnp.zeros_like(value_grad)
    for index in range(length // block):
        keys = (index + 1) * block
        rows = pl.ds(index * block, block)
        key_rows = qkv_ref[0:keys, width : 2 * width]
        value_rows = qkv_ref[0:keys, 2 * width : 3 * width]
        doc_start = start_ref[0:1, rows]
        outs = []
        for head in range(slots):
            lanes = head_lanes(head, width)
            head_rows = slice(head * HEAD_DIM, (head + 1) * HEAD_DIM)
            query = jnp.where(lanes, qkv_ref[rows, 0:width] * LOW(scale), LOW(0))
            grad = jnp.where(lanes, grad_ref[rows, :], LOW(0))
            scores = dot(key_rows, query, 1, 1)
            scores = allowed_scores(scores, doc_start, index * block, keys, block)
            probs = jnp.exp(scores - stat_ref[head : head + 1, rows])
            grad_probs = dot(value_rows, grad, 1, 1)
            delta = jnp.sum(probs * grad_probs, 0, keepdims=True)
            grad_scores = (probs * (grad_probs - delta)).astype(LOW)
            value_grad[0:keys, :] += dot(probs.astype(LOW), grad)
            key_grad[0:keys, :] += dot(grad_scores, query)
            outs.append(dot(key_t[head_rows, 0:keys], grad_scores))
        out_ref[rows, 0:width] = (jnp.concatenate(outs, 0).T * scale).astype(LOW)
        if index in after:
            after[index]()
    out_ref[:, width : 2 * width] = key_grad[...].astype(LOW)
    out_ref[:, 2 * width : 3 * width] = value_grad[...].astype(LOW)


MESH = pl.DeviceIdType.MESH


def send(src, dst, send_sem, recv_sem, **target):
    return pltpu.make_async_remote_copy(
        src_ref=src,
        dst_ref=dst,
        send_sem=send_sem,
        recv_sem=recv_sem,
        device_id=target,
        device_id_type=MESH,
    )


def greet_line(chips):
    rank = lax.axis_index("ctx")
    chip, core = rank // 2, rank % 2
    barrier = pltpu.get_barrier_semaphore()
    pl.semaphore_signal(barrier, 1, device_id={"ctx": rank + 1 - 2 * core}, device_id_type=MESH)

    @pl.when(chip > 0)
    def _():
        pl.semaphore_signal(barrier, 1, device_id={"ctx": rank - 2}, device_id_type=MESH)

    @pl.when(chip < chips - 1)
    def _():
        pl.semaphore_signal(barrier, 1, device_id={"ctx": rank + 2}, device_id_type=MESH)

    sides = (chip > 0).astype(jnp.int32) + (chip < chips - 1).astype(jnp.int32)
    pl.semaphore_wait(barrier, 1 + sides)


def greet_all(between=lambda: None):
    barrier = pltpu.get_barrier_semaphore()
    count = 0
    for axis in ("ctx", "dp"):
        size = lax.axis_size(axis)
        here = lax.axis_index(axis)

        def one(off, carry, axis=axis, size=size, here=here):
            peer = lax.rem(here + off, size)
            pl.semaphore_signal(barrier, 1, device_id={axis: peer}, device_id_type=MESH)
            return carry

        lax.fori_loop(1, size, one, 0)
        count += size - 1
    between()
    pl.semaphore_wait(barrier, count)


class Swap:
    def __init__(self, axis, source, target, sems):
        self.axis, self.source, self.target = axis, source, target
        self.send_sems, self.recv_sems = sems
        self.rank = lax.axis_index(axis)
        self.size = lax.axis_size(axis)

    def copy(self, peer, origin, target):
        return send(
            self.source(peer),
            self.target(origin),
            self.send_sems.at[peer],
            self.recv_sems.at[origin],
            **{self.axis: target},
        )

    def every(self, act):
        def one(off, carry):
            act(lax.rem(self.rank + off, self.size))
            return carry

        lax.fori_loop(1, self.size, one, 0)

    def start(self):
        self.every(lambda peer: self.copy(peer, self.rank, peer).start())

    def wait(self):
        self.every(lambda peer: self.copy(peer, peer, self.rank).wait_recv())

    def drain(self):
        self.every(lambda peer: self.copy(peer, self.rank, peer).wait_send())

    @staticmethod
    def semaphores(size):
        return [pltpu.SemaphoreType.DMA((size,)), pltpu.SemaphoreType.DMA((size,))]


class ChipSwap(Swap):
    def __init__(self, source, target, sems):
        super().__init__("ctx", source, target, sems)
        self.core = self.rank % 2
        self.rank, self.size = self.rank // 2, self.size // 2

    def copy(self, peer, origin, target):
        return send(
            self.source(peer),
            self.target(origin),
            self.send_sems.at[peer],
            self.recv_sems.at[origin],
            ctx=2 * target + self.core,
        )


class PlaneGather:
    def __init__(self, blocks, sems):
        self.blocks = blocks
        self.size = blocks.shape[0]
        self.rank = lax.axis_index("dp")
        self.square = self.size == 4
        self.send_sems, self.recv_sems = sems
        if self.square:
            self.beside = self.rank + 1 - 2 * (self.rank % 2)
            self.above = self.rank + 2 - 4 * (self.rank // 2)
            half = blocks.shape[1] // 32 * 16
            self.low, self.high = pl.ds(0, half), pl.ds(half, blocks.shape[1] - half)
        else:
            self.swap = Swap("dp", lambda peer: blocks.at[self.rank], blocks.at.__getitem__, sems)

    def copy(self, index, ref, target):
        return send(ref, ref, self.send_sems.at[index], self.recv_sems.at[index], dp=target)

    def start(self):
        if not self.square:
            self.swap.start()
            return
        own = self.blocks.at[self.rank]
        self.copy(0, own, self.beside).start()
        self.copy(1, own, self.above).start()

    def relay(self):
        if not self.square:
            return
        self.copy(0, self.blocks.at[self.beside], self.beside).wait_recv()
        self.copy(2, self.blocks.at[self.beside, self.low], self.above).start()
        self.copy(1, self.blocks.at[self.above], self.above).wait_recv()
        self.copy(3, self.blocks.at[self.above, self.high], self.beside).start()

    def wait(self):
        if not self.square:
            self.swap.wait()
            self.swap.drain()
            return
        far = 3 - self.rank
        own = self.blocks.at[self.rank]
        self.copy(2, self.blocks.at[far, self.low], self.above).wait_recv()
        self.copy(3, self.blocks.at[far, self.high], self.beside).wait_recv()
        self.copy(0, own, self.beside).wait_send()
        self.copy(1, own, self.above).wait_send()
        self.copy(2, self.blocks.at[self.beside, self.low], self.above).wait_send()
        self.copy(3, self.blocks.at[self.above, self.high], self.beside).wait_send()

    semaphores = staticmethod(Swap.semaphores)


class PlaneSum:
    def __init__(self, blocks, landed, sems):
        self.blocks, self.landed = blocks, landed
        self.rank = lax.axis_index("dp")
        self.send_sems, self.recv_sems = sems
        self.swap = Swap("dp", blocks.at.__getitem__, landed.at.__getitem__, sems)
        self.square = blocks.shape[0] == 4
        if self.square:
            self.beside = self.rank + 1 - 2 * (self.rank % 2)
            self.above = self.rank + 2 - 4 * (self.rank // 2)
            half = blocks.shape[1] // 32 * 16
            self.low, self.high = pl.ds(0, half), pl.ds(half, blocks.shape[1] - half)

    def copy(self, index):
        far = 3 - self.rank
        block, slot, rows, target = (
            (far, 0, self.low, self.beside),
            (self.beside, 1, self.low, self.beside),
            (far, 0, self.high, self.above),
            (self.above, 1, self.high, self.above),
            (self.above, 2, self.low, self.above),
            (self.beside, 2, self.high, self.beside),
        )[index]
        return send(
            self.blocks.at[block, rows],
            self.landed.at[slot, rows],
            self.send_sems.at[index],
            self.recv_sems.at[index],
            dp=target,
        )

    def start(self):
        if not self.square:
            self.swap.start()
            return
        for index in range(4):
            self.copy(index).start()

    def relay(self):
        if not self.square:
            return
        for index, block, rows in ((0, self.above, self.low), (2, self.beside, self.high)):
            self.copy(index).wait_recv()
            total = self.blocks[block, rows].astype(WIDE) + self.landed[0, rows].astype(WIDE)
            self.blocks[block, rows] = total.astype(self.blocks.dtype)
            self.copy(4 + index // 2).start()

    def total(self):
        total = self.blocks[self.rank].astype(WIDE)
        if not self.square:
            self.swap.wait()
            for off in range(1, self.swap.size):
                total = total + self.landed[lax.rem(self.rank + off, self.swap.size)].astype(WIDE)
            return total
        for index in (1, 3, 4, 5):
            self.copy(index).wait_recv()
        return total + self.landed[1].astype(WIDE) + self.landed[2].astype(WIDE)

    def drain(self):
        if not self.square:
            self.swap.drain()
            return
        for index in range(6):
            self.copy(index).wait_send()

    @staticmethod
    def semaphores(size):
        return Swap.semaphores(max(size, 6))


class LineGather:
    def __init__(self, blocks, send_sems, recv_sems):
        self.blocks, self.send_sems, self.recv_sems = blocks, send_sems, recv_sems
        self.rank = lax.axis_index("ctx")
        self.chip, self.core = self.rank // 2, self.rank % 2
        self.chips = blocks.shape[0] // 2

    def copy(self, way, origin, target, src=None):
        block = self.blocks.at[origin]
        return send(
            block if src is None else src,
            block,
            self.send_sems.at[way, origin],
            self.recv_sems.at[origin],
            ctx=target,
        )

    def pass_on(self, origin, src=None):
        chip = origin // 2

        @pl.when((chip <= self.chip) & (self.chip < self.chips - 1))
        def _():
            self.copy(0, origin, self.rank + 2, src).start()

        @pl.when((chip >= self.chip) & (self.chip > 0))
        def _():
            self.copy(1, origin, self.rank - 2, src).start()

        self.copy(2, origin, self.rank + 1 - 2 * self.core, src).start()

    def arrive(self, step, part):
        side, other = part % 2, part // 2
        origin_chip = self.chip + jnp.where(side == 0, -step, step)
        origin = 2 * origin_chip + jnp.where(other == 0, self.core, 1 - self.core)
        valid = (origin_chip >= 0) & (origin_chip < self.chips) & ((step > 0) | (side == 0))

        @pl.when(valid & (origin != self.rank))
        def _():
            self.copy(0, origin, self.rank).wait_recv()

            @pl.when(other == 0)
            def _():
                self.pass_on(origin)

        return valid, origin

    def finish(self):
        def one(chip, carry):
            origin = 2 * chip + self.core

            @pl.when((chip <= self.chip) & (self.chip < self.chips - 1))
            def _():
                self.copy(0, origin, self.rank).wait_send()

            @pl.when((chip >= self.chip) & (self.chip > 0))
            def _():
                self.copy(1, origin, self.rank).wait_send()

            self.copy(2, origin, self.rank).wait_send()
            return carry

        lax.fori_loop(0, self.chips, one, 0)

    @staticmethod
    def semaphores(ctx):
        return [pltpu.SemaphoreType.DMA((3, ctx)), pltpu.SemaphoreType.DMA((ctx,))]


class LineSum:
    def __init__(self, blocks, pair, passing, sems):
        self.blocks, self.pair, self.passing = blocks, pair, passing
        self.pair_send, self.pair_recv, self.line_send, self.line_recv = sems
        self.rank = lax.axis_index("ctx")
        self.chip, self.core = self.rank // 2, self.rank % 2
        self.chips = blocks.shape[0] // 2
        self.pieces = self.line_recv.shape[2]
        self.piece = blocks.shape[1] // self.pieces

    def pair_copy(self, chip):
        return send(
            self.blocks.at[2 * chip + 1 - self.core],
            self.pair.at[chip],
            self.pair_send.at[chip],
            self.pair_recv.at[chip],
            ctx=self.rank + 1 - 2 * self.core,
        )

    def line_copy(self, way, chip, piece, target, at):
        rows = pl.ds(piece * self.piece, self.piece)
        slot = jnp.where((way == 1) & (chip == at), self.chips, chip)
        return send(
            self.blocks.at[2 * chip + self.core, rows],
            self.passing.at[slot, rows],
            self.line_send.at[chip, piece],
            self.line_recv.at[way, chip, piece],
            ctx=target,
        )

    def both(self, chip, rows):
        mine = self.blocks[2 * chip + self.core, rows].astype(WIDE)
        return mine + self.pair[chip, rows].astype(WIDE)

    def forward(self, way, chip, valid):
        behind = jnp.where(way == 0, self.chip > 0, self.chip < self.chips - 1)
        target = self.rank + jnp.where(way == 0, 2, -2)

        @pl.when(valid)
        def _():
            self.pair_copy(chip).wait_recv()

            def one(piece, carry):
                rows = pl.ds(pl.multiple_of(piece * self.piece, self.piece), self.piece)
                total = self.both(chip, rows)

                @pl.when(behind)
                def _():
                    self.line_copy(way, chip, piece, target, self.chip).wait_recv()
                    passing = self.passing[chip, rows].astype(WIDE)
                    self.blocks[2 * chip + self.core, rows] = (total + passing).astype(LOW)

                @pl.when(jnp.logical_not(behind))
                def _():
                    self.blocks[2 * chip + self.core, rows] = total.astype(LOW)

                self.line_copy(way, chip, piece, target, target // 2).start()
                return carry

            lax.fori_loop(0, self.pieces, one, 0)

    def near_first(self, step, way):
        last = self.chips - 1
        chip = jnp.where(way == 0, step - self.chip, 2 * last - self.chip - step)
        ahead = jnp.where(way == 0, (chip > self.chip) & (chip <= last), (chip >= 0) & (chip < self.chip))
        self.forward(way, chip, ahead)

    def far_first(self, step, way):
        last = self.chips - 1
        chip = jnp.where(way == 0, last + self.chip - step, step - last + self.chip)
        ahead = jnp.where(way == 0, (chip > self.chip) & (chip <= last), (chip >= 0) & (chip < self.chip))
        self.forward(way, chip, ahead)

    def send_pairs(self):
        def one(chip, carry):
            self.pair_copy(chip).start()
            return carry

        lax.fori_loop(0, self.chips, one, 0)

    def far_steps(self, begin, end):
        def one(index, carry):
            self.far_first(index // 2, index % 2)
            return carry

        lax.fori_loop(2 * begin, 2 * end, one, 0)

    def finish(self, out):
        self.pair_copy(self.chip).wait_recv()

        def one(piece, carry):
            rows = pl.ds(pl.multiple_of(piece * self.piece, self.piece), self.piece)
            out[rows] = self.both(self.chip, rows)

            @pl.when(self.chip > 0)
            def _():
                self.line_copy(0, self.chip, piece, self.rank, self.chip).wait_recv()
                out[rows] = out[rows] + self.passing[self.chip, rows].astype(WIDE)

            @pl.when(self.chip < self.chips - 1)
            def _():
                self.line_copy(1, self.chip, piece, self.rank, self.chip).wait_recv()
                out[rows] = out[rows] + self.passing[self.chips, rows].astype(WIDE)

            return carry

        lax.fori_loop(0, self.pieces, one, 0)

        def sent(chip, carry):
            self.pair_copy(chip).wait_send()

            @pl.when(chip != self.chip)
            def _():
                for piece in range(self.pieces):
                    self.line_copy(0, chip, piece, self.rank, self.chip).wait_send()

            return carry

        lax.fori_loop(0, self.chips, sent, 0)

    @staticmethod
    def scratch(ctx, rows, columns, pieces):
        chips = ctx // 2
        return [
            pltpu.VMEM((ctx, rows, columns), LOW),
            pltpu.VMEM((chips, rows, columns), LOW),
            pltpu.VMEM((chips + 1, rows, columns), LOW),
            pltpu.SemaphoreType.DMA((chips,)),
            pltpu.SemaphoreType.DMA((chips,)),
            pltpu.SemaphoreType.DMA((chips, pieces)),
            pltpu.SemaphoreType.DMA((2, chips, pieces)),
        ]


VMEM = pl.BlockSpec(memory_space=pltpu.VMEM)
HBM = pl.BlockSpec(memory_space=pl.ANY)


def params(number):
    return pltpu.CompilerParams(
        vmem_limit_bytes=63 * MIB, collective_id=number, has_side_effects=True
    )


def packed_rows(count, columns):
    tiles = -(-columns // 128)
    main = count // 16 * 16
    return tiles * main + -(-(tiles * (count - main)) // 16) * 16


def pack(out, index, rows, first, count, lane, columns):
    tiles = -(-columns // 128)
    main = count // 16 * 16
    for tile in range(tiles):
        lanes = slice(lane + tile * 128, lane + tile * 128 + 128)
        part = rows[first : first + main, lanes]
        out[index, tile * main : (tile + 1) * main] = part.astype(LOW)
    left = [
        rows[first + row : first + row + 1, lane + tile * 128 : lane + tile * 128 + 128]
        for row in range(main, count)
        for tile in range(tiles)
    ]
    space = out.shape[1] - tiles * main
    if space:
        left.append(jnp.zeros((space - len(left), 128), WIDE))
        out[index, tiles * main :] = jnp.concatenate(left, 0).astype(LOW)


def unpack(packed, rows, first, count, columns):
    tiles = -(-columns // 128)
    main = count // 16 * 16
    for tile in range(tiles):
        lanes = slice(tile * 128, tile * 128 + 128)
        rows[first : first + main, lanes] = packed[tile * main : (tile + 1) * main].astype(WIDE)
    left = packed[tiles * main :].astype(WIDE)
    for row in range(main, count):
        for tile in range(tiles):
            place = (row - main) * tiles + tile
            lanes = slice(tile * 128, tile * 128 + 128)
            rows[first + row : first + row + 1, lanes] = left[place : place + 1]


def full_lanes(columns):
    return -(-columns // 128) * 128


def head_pieces(ctx, slots):
    width = slots * HEAD_DIM
    pieces = []
    for rank in range(ctx):
        count = min(width, D - rank * width)
        if count > 0:
            for part in range(3):
                pieces.append((rank, part * width, part * D + rank * width, count))
    return pieces


def unit_pieces(ctx, dp):
    units = FF // (ctx * dp)
    return [
        (rank, seq * padded_units(units), (seq * ctx + rank) * units, units)
        for rank in range(ctx)
        for seq in range(dp)
    ]


def divide(rows_ref, wide, blocks, pieces, columns):
    count = rows_ref.shape[0]
    lanes = full_lanes(columns)
    for rank in range(blocks.shape[0]):
        wide[...] = jnp.zeros_like(wide)
        for owner, here, there, size in pieces:
            if owner == rank:
                wide[0:count, here : here + size] = rows_ref[:, there : there + size].astype(WIDE)
        pack(blocks, rank, wide, 0, count, 0, lanes)


class Spread:
    def __init__(self, blocks, landed, wide, out, sems):
        self.blocks, self.landed, self.wide, self.out = blocks, landed, wide, out
        self.swap = Swap("ctx", blocks.at.__getitem__, landed.at.__getitem__, sems[:2])
        self.plane = PlaneGather(out, sems[2:])

    def start(self):
        self.swap.start()
        self.landed[self.swap.rank] = self.blocks[self.swap.rank]

    def cross(self):
        self.swap.wait()
        count = self.out.shape[1] // self.swap.size
        columns = self.out.shape[2]
        for index in range(self.swap.size):
            unpack(self.landed[index], self.wide, index * count, count, columns)
        self.out[self.plane.rank] = self.wide[:, 0:columns].astype(LOW)
        self.plane.start()

    def wait(self):
        self.plane.wait()

    @staticmethod
    def scratch(ctx, dp, rows, columns):
        return [
            pltpu.VMEM((ctx, packed_rows(rows // ctx, columns), 128), LOW),
            pltpu.VMEM((rows, full_lanes(columns)), WIDE),
            *Swap.semaphores(ctx),
            *PlaneGather.semaphores(dp),
        ]


class StreamSum:
    def __init__(self, parts, landed, stage, stage_sems, sems):
        self.parts, self.landed, self.stage, self.stage_sems = parts, landed, stage, stage_sems
        self.plane = PlaneSum(parts, landed, sems)

    def put(self, index, part):
        if index >= 2:
            self.move(index - 2).wait()
        self.stage[index % 2] = part.astype(LOW)
        self.move(index).start()

    def move(self, index):
        slot = index % 2
        return pltpu.make_async_copy(
            self.stage.at[slot], self.parts.at[index], self.stage_sems.at[slot]
        )

    def start(self):
        self.move(2).wait()
        self.move(3).wait()
        self.plane.start()

    def load(self, source, slot, rows):
        return pltpu.make_async_copy(
            source.at[rows], self.stage.at[slot, rows], self.stage_sems.at[slot]
        )

    def relayed(self, index):
        plane = self.plane
        rows, target = ((plane.low, plane.above), (plane.high, plane.beside))[index]
        return send(
            self.stage.at[2, rows],
            self.landed.at[2, rows],
            plane.send_sems.at[4 + index],
            plane.recv_sems.at[4 + index],
            dp=target,
        )

    def relay(self):
        plane = self.plane
        for index, block, rows in ((0, plane.above, plane.low), (1, plane.beside, plane.high)):
            plane.copy(2 * index).wait_recv()
            loads = (
                self.load(self.parts.at[block], 0, rows),
                self.load(self.landed.at[0], 1, rows),
            )
            for load in loads:
                load.start()
            for load in loads:
                load.wait()
            total = self.stage[0, rows].astype(WIDE) + self.stage[1, rows].astype(WIDE)
            self.stage[2, rows] = total.astype(LOW)
            self.relayed(index).start()

    def total(self):
        plane = self.plane
        for index in range(4):
            plane.copy(index).wait_send()
        plane.copy(1).wait_recv()
        plane.copy(3).wait_recv()
        for index in range(2):
            self.relayed(index).wait_send()
            self.relayed(index).wait_recv()
        every = pl.ds(0, self.parts.shape[1])
        loads = (
            self.load(self.parts.at[plane.rank], 0, every),
            self.load(self.landed.at[1], 1, every),
            self.load(self.landed.at[2], 2, every),
        )
        for load in loads:
            load.start()
        for load in loads:
            load.wait()
        total = self.stage[0].astype(WIDE) + self.stage[1].astype(WIDE)
        return total + self.stage[2].astype(WIDE)


class Collect:
    def __init__(self, pieces, plane, wide, blocks, came, out, sems):
        self.pieces, self.plane, self.wide, self.blocks = pieces, plane, wide, blocks
        self.came, self.out = came, out
        self.swap = Swap("ctx", blocks.at.__getitem__, came.at.__getitem__, sems)

    def cross(self):
        rows, columns = self.plane.parts.shape[1:]
        lanes = full_lanes(columns)
        self.wide[0:rows, 0:columns] = self.plane.total()
        if lanes > columns:
            self.wide[0:rows, columns:lanes] = jnp.zeros((rows, lanes - columns), WIDE)
        count = rows // self.swap.size
        for index in range(self.swap.size):
            pack(self.blocks, index, self.wide, index * count, count, 0, columns)
        self.swap.start()
        self.came[self.swap.rank] = self.blocks[self.swap.rank]

    def wait(self):
        self.swap.wait()
        count = self.out.shape[0]
        for rank in range(self.swap.size):
            unpack(self.came[rank], self.wide, 0, count, self.plane.parts.shape[2])
            for owner, here, there, size in self.pieces:
                if owner == rank:
                    self.out[:, there : there + size] = self.wide[0:count, here : here + size]
        self.swap.drain()


class Projection:
    def __init__(self, rows, blocks, wide, out, sems):
        self.rows, self.blocks, self.wide, self.out = rows, blocks, wide, out
        self.rank = lax.axis_index("ctx")
        self.core = self.rank % 2
        self.packed = rows.shape[1]
        self.plane = PlaneGather(blocks.at[self.core], sems[:2])
        self.send_sems, self.recv_sems = sems[2:4]
        self.swap = ChipSwap(lambda peer: rows.at[0], self.place, sems[4:])

    def place(self, chip):
        rows = pl.ds(pl.multiple_of(chip * self.packed, self.packed), self.packed)
        return self.blocks.at[self.core, self.plane.rank, rows]

    def start(self):
        self.swap.start()
        rows = pl.ds(pl.multiple_of(self.swap.rank * self.packed, self.packed), self.packed)
        self.blocks[self.core, self.plane.rank, rows] = self.rows[0]

    def cross(self):
        self.swap.wait()
        self.plane.start()
        self.to_other(self.plane.rank).start()

    def to_other(self, seq):
        block = self.blocks.at[self.core, seq]
        return send(
            block,
            block,
            self.send_sems.at[seq],
            self.recv_sems.at[seq],
            ctx=self.rank + 1 - 2 * self.core,
        )

    def wait(self):
        self.plane.wait()

        def others(off, carry):
            self.to_other(lax.rem(self.plane.rank + off, self.plane.size)).start()
            return carry

        lax.fori_loop(1, self.plane.size, others, 0)
        ctx = 2 * self.swap.size
        count = self.out.shape[1] // ctx

        def order(off, carry):
            seq = lax.rem(self.plane.rank + off, self.plane.size)
            self.to_other(seq).wait_recv()
            for rank in range(ctx):
                first = rank // 2 * self.packed
                rows = self.blocks[rank % 2, seq, first : first + self.packed]
                unpack(rows, self.wide, rank * count, count, D)
            self.out[seq] = self.wide[:, 0:D].astype(LOW)
            return carry

        lax.fori_loop(0, self.plane.size, order, 0)

        def sent(seq, carry):
            self.to_other(seq).wait_send()
            return carry

        lax.fori_loop(0, self.plane.size, sent, 0)
        self.swap.drain()

    @staticmethod
    def scratch(ctx, dp):
        packed = packed_rows(D // (dp * ctx), D)
        return [
            pltpu.VMEM((2, dp, ctx // 2 * packed, 128), LOW),
            pltpu.VMEM((D // dp, full_lanes(D)), WIDE),
            *PlaneGather.semaphores(dp),
            *Swap.semaphores(dp),
            *Swap.semaphores(ctx // 2),
        ]


def vector_pieces(owners, count):
    pieces = []
    for owner in range(owners):
        begin = 0
        while begin < count:
            place = owner * count + begin
            size = min(count - begin, D - place % D)
            pieces.append((owner, begin, place // D, place % D, size))
            begin += size
    return pieces


def unit_bias_pieces(rank, ctx, dp):
    units = FF // (ctx * dp)
    pieces = []
    for seq in range(dp):
        begin = 0
        while begin < units:
            place = (seq * ctx + rank) * units + begin
            size = min(units - begin, D - place % D)
            pieces.append((seq * padded_units(units) + begin, 7 + place // D, place % D, size))
            begin += size
    return pieces


GAIN_ONE, SHIFT_ONE, BIAS_QUERY, BIAS_VALUE, BIAS_PROJ, GAIN_TWO, SHIFT_TWO = range(7)
BIAS_OUT = 11
ROWS = 16


class Build:
    def __init__(self):
        self.ins, self.outs, self.scratch = {}, {}, {}

    def take(self, spec, **values):
        self.ins.update({name: (value, spec) for name, value in values.items()})

    def give(self, kind, spec, **shapes):
        for name, shape in shapes.items():
            self.outs[name] = (jax.ShapeDtypeStruct(shape, kind), spec)

    def hold(self, kind, **shapes):
        self.scratch.update({name: pltpu.VMEM(shape, kind) for name, shape in shapes.items()})

    def sems(self, **shapes):
        self.scratch.update(
            {name: pltpu.SemaphoreType.DMA(shape) for name, shape in shapes.items()}
        )

    def both(self, **sizes):
        for name, size in sizes.items():
            self.sems(**{name + "_send": (size,), name + "_recv": (size,)})

    def line_sum(self, name, ctx, tokens):
        chips = ctx // 2
        shapes = (ctx, tokens, D), (chips, tokens, D), (chips + 1, tokens, D)
        for part, shape in zip(("_blocks", "_pair", "_passing"), shapes, strict=True):
            self.hold(LOW, **{name + part: shape})
        self.both(**{name + "_pair": chips})
        self.sems(
            **{name + "_line_send": (chips, PIECES), name + "_line_recv": (2, chips, PIECES)}
        )

    def call(self, kernel, number, label):
        names = (*self.ins, *self.outs, *self.scratch)
        results = pl.pallas_call(
            functools.partial(kernel, names),
            out_shape=[shape for shape, _ in self.outs.values()],
            in_specs=[spec for _, spec in self.ins.values()],
            out_specs=[spec for _, spec in self.outs.values()],
            scratch_shapes=list(self.scratch.values()),
            compiler_params=params(number),
            name=label,
        )(*[value for value, _ in self.ins.values()])
        return Names(tuple(self.outs), results)


PIECES = 8


class Names:
    def __init__(self, names, refs):
        self.__dict__.update(zip(names, refs, strict=True))


def forward_kernel(block, whole, names, *refs):
    r = Names(names, refs)
    seq, rank = lax.axis_index("dp"), lax.axis_index("ctx")
    ctx, tokens, _ = r.rows.shape
    dp, units = r.units.shape[:2]
    width = r.mixed.shape[1]
    vec_count = 12 * D // (ctx * dp)

    def out(ref, target, index):
        return pltpu.make_async_copy(ref, target, r.out_sems.at[index])

    rows_in = LineGather(r.rows, r.rows_send, r.rows_recv)
    cots = LineGather(r.cots, r.cots_send, r.cots_recv)
    feed = LineGather(r.rows, r.feed_send, r.feed_recv)
    total = LineSum(
        r.sum_blocks,
        r.sum_pair,
        r.sum_passing,
        (r.sum_pair_send, r.sum_pair_recv, r.sum_line_send, r.sum_line_recv),
    )
    chips = feed.chips
    line = Swap(
        "ctx",
        lambda peer: r.small,
        lambda origin: r.smalls.at[seq, origin],
        (r.line_send, r.line_recv),
    )
    plane = Swap(
        "dp",
        lambda peer: r.smalls.at[seq],
        r.smalls.at.__getitem__,
        (r.plane_send, r.plane_recv),
    )
    unit_rows = PlaneGather(r.units, (r.units_send, r.units_recv))
    to_tokens = Swap(
        "ctx",
        lambda peer: r.mixed.at[pl.ds(pl.multiple_of(peer * tokens, tokens), tokens)],
        lambda origin: r.own_mixed.at[:, pl.ds(pl.multiple_of(origin * width, width), width)],
        (r.mixed_send, r.mixed_recv),
    )
    if whole:
        heads = Spread(
            r.qkv_blocks,
            r.qkv_landed,
            r.qkv_wide,
            r.qkv_mat,
            (r.qkv_send, r.qkv_recv, r.qkv_plane_send, r.qkv_plane_recv),
        )
        columns = Spread(
            r.fc_blocks,
            r.fc_landed,
            r.fc_wide,
            r.fc_mat,
            (r.fc_send, r.fc_recv, r.fc_plane_send, r.fc_plane_recv),
        )
        proj = Projection(
            r.proj_packed,
            r.proj_blocks,
            r.proj_wide,
            r.proj_mat,
            (
                r.proj_plane_send,
                r.proj_plane_recv,
                r.proj_pair_send,
                r.proj_pair_recv,
                r.proj_send,
                r.proj_recv,
            ),
        )

    def prepare():
        own = r.in_t[...].astype(WIDE).T.astype(LOW)
        r.own_in[...] = own
        r.rows[rank] = own
        r.smalls[seq, rank] = r.small[...]
        main = r.own_units.shape[0] // 16 * 16
        r.units[seq, 0:main] = r.own_units[0:main]
        if units > main:
            left = r.own_units[main:].astype(WIDE)
            zeros = jnp.zeros((units - r.own_units.shape[0], D), WIDE)
            r.units[seq, main:] = jnp.concatenate([left, zeros], 0).astype(LOW)
        if whole:
            pieces = head_pieces(ctx, width // HEAD_DIM)
            divide(r.qkv_rows, r.qkv_lanes, r.qkv_blocks, pieces, 3 * width)

    greet_all(prepare)

    line.start()
    if whole:
        heads.start()
    unit_rows.start()
    if whole:
        count = r.proj_rows.shape[0]
        r.proj_lanes[0:count, 0:D] = r.proj_rows[...].astype(WIDE)
        r.proj_lanes[0:count, D:] = jnp.zeros((count, full_lanes(D) - D), WIDE)
        pack(r.proj_packed, 0, r.proj_lanes, 0, count, 0, D)
        heads.swap.drain()
        proj.start()
    rows_in.pass_on(rank)
    own_cot = r.cot_t[...].astype(WIDE).T.astype(LOW)
    r.own_cot[...] = own_cot
    r.cots[rank] = own_cot
    line.wait()
    plane.start()
    if whole:
        heads.cross()
        divide(r.fc_rows, r.fc_lanes, r.fc_blocks, unit_pieces(ctx, dp), dp * units)

    def arrivals(gather):
        def arrive(index, carry):
            gather.arrive(1 + index // 4, index % 4)
            return carry

        return arrive

    rows_in.arrive(0, 2)
    lax.fori_loop(0, 4, arrivals(rows_in), 0)
    if whole:
        heads.plane.relay()
        columns.start()
        proj.cross()
    lax.fori_loop(4, 4 * (chips - 1), arrivals(rows_in), 0)
    if whole:
        proj.plane.relay()
    rows_in.finish()
    docs = jnp.broadcast_to(r.docs[...], r.doc_start.shape)
    lane = lax.broadcasted_iota(jnp.int32, docs.shape, 1)
    doc_start = jnp.where(docs != pltpu.roll(docs, 1, 1), lane, 0)
    shift = 1
    while shift < docs.shape[1]:
        earlier = jnp.where(lane >= shift, pltpu.roll(doc_start, shift, 1), 0)
        doc_start = jnp.maximum(doc_start, earlier)
        shift *= 2
    r.doc_start[...] = doc_start
    plane.wait()
    r.vectors[...] = jnp.zeros_like(r.vectors)
    for owner, begin, row, lane, size in vector_pieces(ctx * dp, vec_count):
        r.vectors[row : row + 1, lane : lane + size] = r.smalls[
            owner // ctx, owner % ctx, 0:1, begin : begin + size
        ]
    r.bias_units[...] = jnp.zeros_like(r.bias_units)
    for owner in range(ctx):

        @pl.when(rank == owner)
        def _(owner=owner):
            for here, row, lane, size in unit_bias_pieces(owner, ctx, dp):
                r.bias_units[0:1, here : here + size] = r.vectors[row : row + 1, lane : lane + size]

    if whole:
        heads.wait()
        out(r.qkv_mat, r.qkv_mat_out, 0).start()
    mine = pl.ds(pl.multiple_of(rank * width, width), width)
    bias = jnp.concatenate(
        [
            r.vectors[BIAS_QUERY : BIAS_QUERY + 1, mine],
            jnp.zeros((1, width), WIDE),
            r.vectors[BIAS_VALUE : BIAS_VALUE + 1, mine],
        ],
        1,
    )

    def project(index, carry):
        both = pl.ds(2 * index, 2)
        normed, _ = normalize(r.rows[both].reshape(2 * tokens, D).astype(WIDE))
        attn_in = normed * r.vectors[GAIN_ONE : GAIN_ONE + 1, 0:D]
        attn_in = (attn_in + r.vectors[SHIFT_ONE : SHIFT_ONE + 1, 0:D]).astype(LOW)
        r.rows[both] = attn_in.reshape(2, tokens, D)
        rows = pl.ds(pl.multiple_of(2 * index * tokens, 2 * tokens), 2 * tokens)
        r.qkv[rows] = (dot(attn_in, r.qkv_mat[...].reshape(D, 3 * width)) + bias).astype(LOW)
        return carry

    lax.fori_loop(0, chips, project, 0)
    out(r.rows, r.attn_in_out, 1).start()
    out(r.qkv, r.qkv_out, 2).start()
    cots.pass_on(rank)
    if whole:
        columns.cross()
    attend_body(block, r.qkv, r.doc_start, r.mixed, r.stats, r.value_t)
    out(r.rows, r.attn_in_out, 1).wait()
    to_tokens.start()
    r.own_mixed[:, mine] = r.mixed[pl.ds(pl.multiple_of(rank * tokens, tokens), tokens)]
    cots.arrive(0, 2)
    lax.fori_loop(0, 4, arrivals(cots), 0)
    if whole:
        proj.wait()
        out(r.proj_mat, r.proj_mat_out, 3).start()
        columns.plane.relay()
    unit_rows.relay()
    to_tokens.wait()
    resid = dot(r.own_mixed[:, 0:D], r.proj_mat[...].reshape(D, D))
    resid = resid + r.own_in[...].astype(WIDE) + r.vectors[BIAS_PROJ : BIAS_PROJ + 1, 0:D]
    r.resid[...] = resid
    normed, _ = normalize(resid)
    ffn_in = normed * r.vectors[GAIN_TWO : GAIN_TWO + 1, 0:D]
    r.rows[rank] = (ffn_in + r.vectors[SHIFT_TWO : SHIFT_TWO + 1, 0:D]).astype(LOW)
    feed.pass_on(rank)
    lax.fori_loop(4, 8, arrivals(cots), 0)
    unit_rows.wait()
    if whole:
        columns.wait()

    def keep(chip, slot, which=range(3)):
        both = pl.ds(2 * chip, 2)
        kept = ((r.act, r.act_out), (r.pre, r.pre_out), (r.part, r.part_out))
        return [
            pltpu.make_async_copy(
                kept[index][0].at[slot], kept[index][1].at[both], r.keep_sems.at[index, slot]
            )
            for index in which
        ]

    def pass_rows(chip):
        both = pl.ds(2 * chip, 2)
        return [
            pltpu.make_async_copy(ref.at[both], target.at[both], r.pass_sems.at[index, chip])
            for index, (ref, target) in enumerate(((r.rows, r.ffn_out), (r.cots, r.cots_out)))
        ]

    def work(chip, done):
        both = pl.ds(2 * chip, 2)
        slot = done % 2

        @pl.when(done >= 2)
        def _():
            for copy in keep(chip, slot):
                copy.wait()

        for copy in pass_rows(chip):
            copy.start()
        fc = r.fc_mat[...].reshape(D, dp * units)
        pre = dot(r.rows[both].reshape(2 * tokens, D), fc) + r.bias_units[0:1]
        bend = jnp.tanh(0.7978845608028654 * (pre + 0.044715 * pre * pre * pre))
        act = (0.5 * pre * (1.0 + bend)).astype(LOW)
        r.act[slot] = act.reshape(2, tokens, -1)
        slope = 0.5 * (1.0 + bend) + 0.5 * pre * (1.0 - bend * bend) * 0.7978845608028654 * (
            1.0 + 3 * 0.044715 * pre * pre
        )
        grad_pre = (slope * r.grad_act[...]).astype(LOW)
        r.pre[slot] = grad_pre.reshape(2, tokens, -1)
        r.sum_blocks[both] = dot(grad_pre, fc, 1, 1).astype(LOW).reshape(2, tokens, D)
        total.pair_copy(chip).start()
        for copy in keep(chip, slot, (0, 1)):
            copy.start()

    def give_out(chip, done):
        slot = done % 2
        act = r.act[slot].reshape(2 * tokens, dp * units)
        mat = r.units[...].reshape(dp * units, D)
        r.part[slot] = dot(act, mat).astype(LOW).reshape(2, tokens, D)
        keep(chip, slot, (2,))[0].start()

    def step(index, done):
        distance, side = index // 2, index % 2
        near = distance < chips
        origin_chip = rank // 2 + jnp.where(side == 0, -distance, distance)
        valid = near & (origin_chip >= 0) & (origin_chip < chips) & ((distance > 0) | (side == 0))

        @pl.when(near)
        def _():
            @pl.when(side == 0)
            def _():
                @pl.when(distance > 2)
                def _():
                    cots.arrive(distance, 0)
                    cots.arrive(distance, 1)

                feed.arrive(distance, 0)
                feed.arrive(distance, 1)

            @pl.when(distance > 2)
            def _():
                cots.arrive(distance, 2 + side)

            @pl.when(valid)
            def _():
                cot = r.cots[pl.ds(2 * origin_chip, 2)].reshape(2 * tokens, D)
                r.grad_act[...] = dot(cot, r.units[...].reshape(dp * units, D), 1, 1)

            feed.arrive(distance, 2 + side)

            @pl.when(valid)
            def _():
                work(origin_chip, done)

        after = done + valid.astype(jnp.int32)

        @pl.when(side == 1)
        def _():
            def way(index, carry):
                total.near_first(distance, index)
                return carry

            lax.fori_loop(0, 2, way, 0)

            def output(index, carry):
                chip = rank // 2 + jnp.where(index == 0, -distance, distance)
                here = near & (chip >= 0) & (chip < chips) & ((distance > 0) | (index == 0))
                later = (index == 0) & valid & (distance > 0)

                @pl.when(here)
                def _():
                    give_out(chip, after - 1 - later.astype(jnp.int32))

                return carry

            lax.fori_loop(0, 2, output, 0)

        return after

    lax.fori_loop(0, 2 * (2 * chips - 1), step, jnp.int32(0))
    total.finish(r.grad)

    feed.finish()
    cots.finish()
    line.drain()
    plane.drain()
    to_tokens.drain()
    for slot in range(2):
        for copy in keep(0, slot):
            copy.wait()

    def passed(chip, carry):
        for copy in pass_rows(chip):
            copy.wait()
        return carry

    lax.fori_loop(0, chips, passed, 0)
    out(r.qkv, r.qkv_out, 2).wait()
    if whole:
        out(r.qkv_mat, r.qkv_mat_out, 0).wait()
        out(r.proj_mat, r.proj_mat_out, 3).wait()
        columns.swap.drain()


def forward(small, in_t, cot_t, unit_rows, docs, mats, slots, whole, block):
    ctx, dp = lax.axis_size("ctx"), lax.axis_size("dp")
    tokens = in_t.shape[1]
    length = ctx * tokens
    width = slots * HEAD_DIM
    units = padded_units(unit_rows.shape[0])
    columns = dp * units
    chips = ctx // 2
    rows = D // dp
    count = rows // ctx
    high = -(-count // 8) * 8
    b = Build()
    b.take(VMEM, small=small, in_t=in_t, cot_t=cot_t, own_units=unit_rows, docs=docs)
    if whole:
        b.take(VMEM, qkv_rows=mats[0], fc_rows=mats[1], proj_rows=mats[2])
    else:
        b.take(VMEM, qkv_mat=mats[0], fc_mat=mats[1], proj_mat=mats[2])
    b.give(
        WIDE,
        VMEM,
        vectors=(ROWS, max(full_lanes(D), ctx * width)),
        stats=(8, length),
        resid=(tokens, D),
        grad=(tokens, D),
    )
    b.give(
        LOW, VMEM, own_mixed=(tokens, ctx * width), own_in=(tokens, D), own_cot=(tokens, D)
    )
    b.give(jnp.int32, VMEM, doc_start=(8, length))
    b.give(
        LOW,
        HBM,
        attn_in_out=(ctx, tokens, D),
        qkv_out=(length, 3 * width),
        cots_out=(ctx, tokens, D),
        ffn_out=(ctx, tokens, D),
        act_out=(ctx, tokens, columns),
        pre_out=(ctx, tokens, columns),
        part_out=(ctx, tokens, D),
    )
    if whole:
        b.give(LOW, HBM, qkv_mat_out=(dp, rows, 3 * width), proj_mat_out=(dp, rows, D))
    b.hold(
        LOW,
        rows=(ctx, tokens, D),
        cots=(ctx, tokens, D),
        units=(dp, units, D),
        qkv=(length, 3 * width),
        mixed=(length, width),
        value_t=(width, length),
        act=(2, 2, tokens, columns),
        pre=(2, 2, tokens, columns),
        part=(2, 2, tokens, D),
    )
    b.hold(
        WIDE,
        smalls=(dp, ctx, *small.shape),
        bias_units=(8, columns),
        grad_act=(2 * tokens, columns),
    )
    b.line_sum("sum", ctx, tokens)
    b.sems(
        out_sems=(4,),
        keep_sems=(3, 2),
        pass_sems=(2, chips),
        rows_send=(3, ctx),
        rows_recv=(ctx,),
        cots_send=(3, ctx),
        cots_recv=(ctx,),
        feed_send=(3, ctx),
        feed_recv=(ctx,),
    )
    b.both(line=ctx, plane=dp, units=max(dp, 4), mixed=ctx)
    if whole:
        for name, lanes in (("qkv", 3 * width), ("fc", columns)):
            packed = (ctx, packed_rows(count, lanes), 128)
            b.hold(WIDE, **{name + "_lanes": (high, full_lanes(lanes))})
            b.hold(WIDE, **{name + "_wide": (rows, full_lanes(lanes))})
            b.hold(LOW, **{name + "_blocks": packed, name + "_landed": packed})
            b.hold(LOW, **{name + "_mat": (dp, rows, lanes)})
            b.both(**{name: ctx, name + "_plane": max(dp, 4)})
        packed = packed_rows(count, D)
        b.hold(WIDE, proj_lanes=(high, full_lanes(D)), proj_wide=(rows, full_lanes(D)))
        b.hold(
            LOW,
            proj_packed=(1, packed, 128),
            proj_blocks=(2, dp, chips * packed, 128),
            proj_mat=(dp, rows, D),
        )
        b.both(proj_plane=max(dp, 4), proj_pair=dp, proj=chips)
    return b.call(functools.partial(forward_kernel, block, whole), 0, "forward")


def back_kernel(
    block,
    grad_ref,
    resid_ref,
    own_cot,
    vectors_ref,
    proj_ref,
    qkv_ref,
    start_ref,
    stat_ref,
    ffn_hbm,
    pre_hbm,
    act_hbm,
    cot_hbm,
    part_hbm,
    resid_out,
    low_out,
    vector_out,
    units_out,
    rows_out,
    share_out,
    output_ref,
    fc_out,
    ffn,
    pre,
    act,
    cot,
    load_sems,
    own_grad,
    head_grad,
    key_t,
    key_grad,
    value_grad,
    *refs,
):
    total = LineSum(*refs[:3], refs[3:7])
    loads = [
        pltpu.make_async_copy(src, dst, load_sems.at[index])
        for index, (src, dst) in enumerate(
            (
                (part_hbm, total.blocks),
                (ffn_hbm, ffn),
                (pre_hbm, pre),
                (act_hbm, act),
                (cot_hbm, cot),
            )
        )
    ]
    for load in loads:
        load.start()
    tokens = own_cot.shape[0]
    length, width = head_grad.shape
    units = share_out.shape[0]
    swap = Swap(
        "ctx",
        lambda peer: own_grad.at[:, pl.ds(pl.multiple_of(peer * width, width), width)],
        lambda origin: head_grad.at[pl.ds(pl.multiple_of(origin * tokens, tokens), tokens)],
        refs[7:9],
    )
    share = PlaneSum(refs[9], refs[10], refs[11:13])
    dp = share.swap.size
    greet_all()
    loads[0].wait()
    total.send_pairs()
    grad = grad_ref[...]
    normed, scale = normalize(resid_ref[...])
    grad_resid = own_cot[...].astype(WIDE) + norm_back(normed, scale, vectors_ref[GAIN_TWO : GAIN_TWO + 1, 0:D], grad)
    resid_out[...] = grad_resid
    low = grad_resid.astype(LOW)
    low_out[...] = low
    own_grad[:, 0:D] = dot(low, proj_ref[...], 1, 1).astype(LOW)
    own_grad[:, D:] = jnp.zeros((tokens, own_grad.shape[1] - D), LOW)
    swap.start()
    head_grad[pl.ds(pl.multiple_of(swap.rank * tokens, tokens), tokens)] = own_grad[
        :, pl.ds(pl.multiple_of(swap.rank * width, width), width)
    ]
    vector_out[0:1] = jnp.sum(grad_resid, 0, keepdims=True)
    vector_out[1:2] = jnp.sum(grad * normed, 0, keepdims=True)
    vector_out[2:3] = jnp.sum(grad, 0, keepdims=True)
    vector_out[3:4] = jnp.sum(own_cot[...].astype(WIDE), 0, keepdims=True)
    vector_out[4:8] = jnp.zeros((4, D), WIDE)
    loads[1].wait()
    loads[2].wait()
    grad_pre = pre[...].reshape(length, -1)
    units_out[...] = dot(jnp.ones((8, length), LOW), grad_pre)
    for index in range(dp):
        rows = slice(index * (D // dp), (index + 1) * (D // dp))
        fc_out[rows] = dot(ffn[:, :, rows].reshape(length, D // dp), grad_pre, 0, 0)
    total.far_steps(0, 1)
    loads[3].wait()
    loads[4].wait()
    for index in range(dp):
        rows = slice(index * units, (index + 1) * units)
        part = dot(act[:, :, rows].reshape(length, units), cot[...].reshape(length, D), 0, 0)
        share.blocks[index] = part.astype(LOW)
    share.start()
    swap.wait()
    chips = total.chips

    def first():
        total.far_steps(1, 2)

    def second():
        total.far_steps(2, 3)
        share.relay()

    attend_back_body(
        block,
        qkv_ref,
        start_ref,
        stat_ref,
        head_grad,
        rows_out,
        key_t,
        key_grad,
        value_grad,
        {1: first, 2: second},
    )
    total.far_steps(3, 2 * chips - 1)
    total.finish(output_ref)
    bias = vectors_ref[BIAS_OUT : BIAS_OUT + 1, 0:D]
    output_ref[...] = output_ref[...] + resid_ref[...] + bias
    share_out[...] = share.total()
    swap.drain()
    share.drain()


def back(
    grad, resid, own_cot, vectors, proj, qkv, doc_start, stats, ffn, pre, act, cot, part, block
):
    ctx, tokens, _ = cot.shape
    dp = lax.axis_size("dp")
    length = ctx * tokens
    width = qkv.shape[1] // 3
    columns = act.shape[2]
    units = columns // dp
    shapes = [
        jax.ShapeDtypeStruct((tokens, D), WIDE),
        jax.ShapeDtypeStruct((tokens, D), LOW),
        jax.ShapeDtypeStruct((8, D), WIDE),
        jax.ShapeDtypeStruct((8, columns), WIDE),
        jax.ShapeDtypeStruct((length, 3 * width), LOW),
        jax.ShapeDtypeStruct((units, D), WIDE),
        jax.ShapeDtypeStruct((tokens, D), WIDE),
        jax.ShapeDtypeStruct((D, columns), WIDE),
    ]
    scratch = [
        pltpu.VMEM(ffn.shape, LOW),
        pltpu.VMEM(pre.shape, LOW),
        pltpu.VMEM(act.shape, LOW),
        pltpu.VMEM(cot.shape, LOW),
        pltpu.SemaphoreType.DMA((5,)),
        pltpu.VMEM((tokens, ctx * width), LOW),
        pltpu.VMEM((length, width), LOW),
        pltpu.VMEM((width, length), LOW),
        pltpu.VMEM((length, width), WIDE),
        pltpu.VMEM((length, width), WIDE),
        *LineSum.scratch(ctx, tokens, D, 4),
        *Swap.semaphores(ctx),
        pltpu.VMEM((dp, units, D), LOW),
        pltpu.VMEM((dp, units, D), LOW),
        *PlaneSum.semaphores(dp),
    ]
    return pl.pallas_call(
        functools.partial(back_kernel, block),
        out_shape=shapes,
        in_specs=[VMEM] * 8 + [HBM] * 5,
        out_specs=[VMEM] * 8,
        scratch_shapes=scratch,
        compiler_params=params(3),
        name="back",
    )(grad, resid, own_cot, vectors, proj, qkv, doc_start, stats, ffn, pre, act, cot, part)


class ProjectionSum:
    def __init__(self, out, mixed, low, plane, wide, blocks, came, pair_sems, sems):
        self.out, self.mixed, self.low, self.plane = out, mixed, low, plane
        self.wide, self.blocks, self.came = wide, blocks, came
        self.send_sems, self.recv_sems = pair_sems
        self.rank = lax.axis_index("ctx")
        self.core = self.rank % 2
        self.swap = ChipSwap(blocks.at.__getitem__, came.at.__getitem__, sems)

    def pair_copies(self):
        return [
            send(
                ref.at[self.core],
                ref.at[self.core],
                self.send_sems.at[index],
                self.recv_sems.at[index],
                ctx=self.rank + 1 - 2 * self.core,
            )
            for index, ref in enumerate((self.mixed, self.low))
        ]

    def start(self, mixed, low):
        self.mixed[self.core] = mixed
        self.low[self.core] = low
        for copy in self.pair_copies():
            copy.start()

    def multiply(self):
        for copy in self.pair_copies():
            copy.wait_recv()
        dp, rows = self.plane.parts.shape[:2]
        chips = self.swap.size
        tokens = 2 * self.low.shape[1]
        count = self.out.shape[0]
        mixed = self.mixed[...].reshape(tokens, -1)[:, 0:D]
        low = self.low[...].reshape(tokens, D)
        feature = lax.broadcasted_iota(jnp.int32, (D, rows), 0)
        column = lax.broadcasted_iota(jnp.int32, (1, rows), 1)
        for index in range(dp):
            owner = index * 2 * chips + column // count * 2 + self.core
            wanted = jnp.where(column < chips * count, owner * count + column % count, -1)
            chosen = jnp.where(feature == wanted, 1.0, 0.0).astype(LOW)
            picked = dot(mixed, chosen).astype(LOW)
            self.plane.put(index, dot(picked, low, 0, 0))

    def cross(self):
        count = self.out.shape[0]
        rows = self.plane.parts.shape[1]
        lanes = full_lanes(D)
        self.wide[0:rows, 0:D] = self.plane.total()
        self.wide[0:rows, D:lanes] = jnp.zeros((rows, lanes - D), WIDE)
        for chip in range(self.swap.size):
            pack(self.blocks, chip, self.wide, chip * count, count, 0, D)
        self.swap.start()

    def wait(self):
        self.swap.wait()
        total = self.blocks[self.swap.rank].astype(WIDE)
        for off in range(1, self.swap.size):
            total = total + self.came[lax.rem(self.swap.rank + off, self.swap.size)].astype(WIDE)
        count = self.out.shape[0]
        unpack(total, self.wide, 0, count, D)
        self.out[...] = self.wide[0:count, 0:D]
        for copy in self.pair_copies():
            copy.wait_send()
        self.swap.drain()


def partial_sums(total, rows_ref, mat):
    chips, tokens = total.chips, total.blocks.shape[1]

    def one(index, carry):
        off = jnp.where(index % 2 == 0, -(index // 2), index // 2 + 1)
        chip = lax.rem(chips - 1 + off, chips)
        rows = pl.ds(pl.multiple_of(2 * chip * tokens, 2 * tokens), 2 * tokens)
        part = dot(rows_ref[rows], mat[...].reshape(D, -1), 1, 1).astype(LOW)
        total.blocks[pl.ds(2 * chip, 2)] = part.reshape(2, tokens, D)
        total.pair_copy(chip).start()
        return carry

    lax.fori_loop(0, chips, one, 0)


def last_kernel(
    rows_ref,
    mat_ref,
    in_ref,
    own_ref,
    resid_ref,
    vectors_ref,
    grad_out,
    vector_out,
    heads_out,
    mat_out,
    grad,
    *refs,
):
    total = LineSum(*refs[:3], refs[3:7])
    chips = total.chips
    dp = lax.axis_size("dp")
    greet_line(chips)
    partial_sums(total, rows_ref, mat_ref)
    total.far_steps(0, 1)
    for index in range(dp):
        rows = slice(index * (D // dp), (index + 1) * (D // dp))
        mat_out[rows] = dot(in_ref[:, rows], rows_ref[...], 0, 0)
    total.far_steps(1, 2 * chips - 1)
    heads_out[...] = dot(jnp.ones((8, rows_ref.shape[0]), LOW), rows_ref[...])
    total.finish(grad)
    normed, scale = normalize(own_ref[...].astype(WIDE))
    incoming = grad[...]
    gain = vectors_ref[GAIN_ONE : GAIN_ONE + 1, 0:D]
    grad_out[...] = resid_ref[...] + norm_back(normed, scale, gain, incoming)
    vector_out[0:1] = jnp.sum(incoming * normed, 0, keepdims=True)
    vector_out[1:2] = jnp.sum(incoming, 0, keepdims=True)
    vector_out[2:8] = jnp.zeros((6, D), WIDE)


def last(rows, mat, attn_in, own_in, resid, vectors):
    ctx = lax.axis_size("ctx")
    tokens = own_in.shape[0]
    columns = rows.shape[1]
    return pl.pallas_call(
        last_kernel,
        out_shape=[
            jax.ShapeDtypeStruct((tokens, D), WIDE),
            jax.ShapeDtypeStruct((8, D), WIDE),
            jax.ShapeDtypeStruct((8, columns), WIDE),
            jax.ShapeDtypeStruct((D, columns), WIDE),
        ],
        in_specs=[VMEM] * 6,
        out_specs=[VMEM] * 4,
        scratch_shapes=[pltpu.VMEM((tokens, D), WIDE), *LineSum.scratch(ctx, tokens, D, 4)],
        compiler_params=params(4),
        name="last",
    )(rows, mat, attn_in, own_in, resid, vectors)


def vector_kernel(parts_ref, out_ref, plane_landed, line_parts, line_landed, *sems):
    seq = lax.axis_index("dp")
    swap = Swap("dp", parts_ref.at.__getitem__, plane_landed.at.__getitem__, sems[:2])
    line = Swap("ctx", line_parts.at.__getitem__, line_landed.at.__getitem__, sems[2:])
    greet_all()
    swap.start()
    swap.wait()
    total = parts_ref[seq]
    for off in range(1, swap.size):
        total = total + plane_landed[lax.rem(seq + off, swap.size)]
    line_parts[...] = total
    line.start()
    line.wait()
    total = line_parts[line.rank]
    for off in range(1, line.size):
        total = total + line_landed[lax.rem(line.rank + off, line.size)]
    out_ref[...] = total
    swap.drain()
    line.drain()


def sum_vector(parts):
    dp, ctx = parts.shape[:2]
    return pl.pallas_call(
        vector_kernel,
        out_shape=jax.ShapeDtypeStruct(parts.shape[2:], WIDE),
        in_specs=[VMEM],
        out_specs=VMEM,
        scratch_shapes=[
            pltpu.VMEM(parts.shape, WIDE),
            pltpu.VMEM(parts.shape[1:], WIDE),
            pltpu.VMEM(parts.shape[1:], WIDE),
            *PlaneSum.semaphores(dp),
            *Swap.semaphores(ctx),
        ],
        compiler_params=params(5),
        name="sum_vector",
    )(parts)


GRAD_ONE, SUM_ONE, SUM_QUERY, SUM_VALUE, SUM_RESID, GRAD_FFN, SUM_FFN = range(7)
SUM_OUT = 11


def backward_kernel(block, names, *refs):
    r = Names(names, refs)
    seq, rank = lax.axis_index("dp"), lax.axis_index("ctx")
    ctx, tokens, _ = r.big.shape
    length, width = r.head_grad.shape
    dp, owners_rows = r.fc_parts.shape[:2]
    units = r.out_parts.shape[1]
    columns = dp * units
    vec_count = 12 * D // (ctx * dp)

    def load(source, target, index):
        return pltpu.make_async_copy(source, target, r.load_sems.at[index])

    summed = LineSum(
        r.out_blocks,
        r.out_pair,
        r.out_passing,
        (r.out_pair_send, r.out_pair_recv, r.out_line_send, r.out_line_recv),
    )
    total = LineSum(
        r.in_blocks,
        r.in_pair,
        r.in_passing,
        (r.in_pair_send, r.in_pair_recv, r.in_line_send, r.in_line_recv),
    )
    chips = total.chips
    to_heads = Swap(
        "ctx",
        lambda peer: r.own_grad.at[:, pl.ds(pl.multiple_of(peer * width, width), width)],
        lambda origin: r.head_grad.at[pl.ds(pl.multiple_of(origin * tokens, tokens), tokens)],
        (r.heads_send, r.heads_recv),
    )
    some = r.stage_fc.at[:, :, pl.ds(0, 3 * width)]
    fc = Collect(
        unit_pieces(ctx, dp),
        StreamSum(
            r.fc_parts, r.fc_landed, r.stage_fc, r.stage_fc_sems, (r.fc_plane_send, r.fc_plane_recv)
        ),
        r.wide,
        r.fc_blocks,
        r.fc_came,
        r.fc_out,
        (r.fc_send, r.fc_recv),
    )
    qkv = Collect(
        head_pieces(ctx, width // HEAD_DIM),
        StreamSum(
            r.qkv_parts, r.qkv_landed, some, r.stage_fc_sems, (r.qkv_plane_send, r.qkv_plane_recv)
        ),
        r.wide,
        r.qkv_blocks,
        r.qkv_came,
        r.qkv_grad,
        (r.qkv_send, r.qkv_recv),
    )
    share = StreamSum(
        r.out_parts,
        r.out_landed,
        r.stage_out,
        r.stage_out_sems,
        (r.out_plane_send, r.out_plane_recv),
    )
    proj = ProjectionSum(
        r.proj_grad,
        r.mixed_pair,
        r.low_pair,
        StreamSum(
            r.proj_parts,
            r.proj_landed,
            r.stage_out,
            r.stage_out_sems,
            (r.proj_plane_send, r.proj_plane_recv),
        ),
        r.wide,
        r.proj_blocks,
        r.proj_came,
        (r.proj_pair_send, r.proj_pair_recv),
        (r.proj_send, r.proj_recv),
    )
    vec_plane = Swap(
        "dp",
        r.vec_parts.at.__getitem__,
        r.vec_landed.at.__getitem__,
        (r.vec_plane_send, r.vec_plane_recv),
    )
    vec_line = Swap(
        "ctx", r.vec_rows.at.__getitem__, r.vec_came.at.__getitem__, (r.vec_send, r.vec_recv)
    )
    heads_mat = r.mat.at[:, :, pl.ds(0, 3 * width)]
    loads = [
        load(r.proj_mat, r.mat, 0),
        load(r.part, r.out_blocks, 1),
        load(r.ffn, r.big, 2),
        load(r.pre_act, r.feed, 3),
        load(r.qkv_mat, heads_mat, 0),
        load(r.attn_in, r.big, 2),
        load(r.act, r.feed, 3),
        load(r.cots, r.big, 2),
    ]
    for index in range(4):
        loads[index].start()
    greet_all()

    grad = r.grad[...]
    normed, scale = normalize(r.resid[...])
    gain = r.vectors[GAIN_TWO : GAIN_TWO + 1, 0:D]
    own_cot = r.own_cot[...].astype(WIDE)
    grad_resid = own_cot + norm_back(normed, scale, gain, grad)
    r.grad_resid[...] = grad_resid
    low = grad_resid.astype(LOW)
    loads[0].wait()
    r.own_grad[:, 0:D] = dot(low, r.mat[...].reshape(D, D), 1, 1).astype(LOW)
    r.own_grad[:, D:] = jnp.zeros((tokens, r.own_grad.shape[1] - D), LOW)
    to_heads.start()
    loads[4].start()
    mine = pl.ds(pl.multiple_of(rank * width, width), width)
    here = pl.ds(pl.multiple_of(rank * tokens, tokens), tokens)
    r.head_grad[here] = r.own_grad[:, mine]
    proj.start(r.own_mixed[...], low)
    loads[1].wait()
    summed.send_pairs()
    vec = r.vec
    vec[...] = jnp.zeros_like(vec)

    def note(row, value):
        vec[row : row + 1, 0:D] = jnp.sum(value, 0, keepdims=True)

    note(SUM_RESID, grad_resid)
    note(GRAD_FFN, grad * normed)
    note(SUM_FFN, grad)
    note(SUM_OUT, own_cot)

    loads[2].wait()
    loads[3].wait()
    grad_pre = r.feed[...].reshape(length, columns)
    sums = dot(jnp.ones((8, length), LOW), grad_pre)[0:1]
    for owner in range(ctx):

        @pl.when(rank == owner)
        def _(owner=owner):
            for place, row, lane, size in unit_bias_pieces(owner, ctx, dp):
                vec[row : row + 1, lane : lane + size] = sums[:, place : place + size]

    def by_parts(plane, left, right, count):
        for index in range(dp):
            rows = slice(index * count, (index + 1) * count)
            plane.put(index, dot(left[:, :, rows].reshape(length, count), right, 0, 0))
        plane.start()

    by_parts(fc.plane, r.big, grad_pre, owners_rows)
    loads[5].start()
    loads[6].start()
    summed.far_steps(0, 1)
    proj.multiply()

    to_heads.wait()

    def first():
        summed.far_steps(1, 2)

    def second():
        summed.far_steps(2, 3)
        fc.plane.relay()
        proj.plane.start()

    attend_back_body(
        block,
        r.qkv,
        r.doc_start,
        r.stats,
        r.head_grad,
        r.rows,
        r.key_t,
        r.key_grad,
        r.value_grad,
        {1: first, 2: second},
    )
    loads[4].wait()
    partial_sums(total, r.rows, heads_mat)
    total.far_steps(0, 1)
    summed.far_steps(3, 4)
    fc.cross()
    loads[5].wait()
    by_parts(qkv.plane, r.big, r.rows[...], owners_rows)
    loads[7].start()
    total.far_steps(1, 2)
    summed.far_steps(4, 5)
    proj.plane.relay()
    total.far_steps(2, 3)
    summed.far_steps(5, 2 * chips - 1)
    proj.cross()
    qkv.plane.relay()
    loads[6].wait()
    loads[7].wait()
    by_parts(share, r.feed, r.big[...].reshape(length, D), units)
    total.far_steps(3, 2 * chips - 1)
    sums = dot(jnp.ones((8, length), LOW), r.rows[...])
    vec[SUM_QUERY : SUM_QUERY + 1, mine] = sums[0:1, 0:width]
    vec[SUM_VALUE : SUM_VALUE + 1, mine] = sums[0:1, 2 * width :]
    total.finish(r.came)

    incoming = r.came[...]
    normed, scale = normalize(r.own_in[...].astype(WIDE))
    gain = r.vectors[GAIN_ONE : GAIN_ONE + 1, 0:D]
    grad_in = r.grad_resid[...] + norm_back(normed, scale, gain, incoming)
    r.grad_in_t[...] = grad_in.T
    note(GRAD_ONE, incoming * normed)
    note(SUM_ONE, incoming)
    for owner, begin, row, lane, size in vector_pieces(ctx * dp, vec_count):
        r.vec_parts[owner // ctx, owner % ctx, 0:1, begin : begin + size] = vec[
            row : row + 1, lane : lane + size
        ]
    vec_plane.start()
    qkv.cross()
    vec_plane.wait()
    rows = r.vec_parts[seq]
    for off in range(1, dp):
        rows = rows + r.vec_landed[lax.rem(seq + off, dp)]
    r.vec_rows[...] = rows
    vec_line.start()
    summed.finish(r.came)
    bias = r.vectors[BIAS_OUT : BIAS_OUT + 1, 0:D]
    r.output_t[...] = (r.came[...] + r.resid[...] + bias).T
    fc.wait()
    share.relay()
    proj.wait()
    vec_line.wait()
    row = r.vec_rows[rank]
    for off in range(1, ctx):
        row = row + r.vec_came[lax.rem(rank + off, ctx)]
    r.vec_out[...] = row
    qkv.wait()
    r.out_grad[...] = share.total()
    to_heads.drain()
    vec_plane.drain()
    vec_line.drain()


def backward(made, block):
    ctx, dp = lax.axis_size("ctx"), lax.axis_size("dp")
    tokens = made.own_in.shape[0]
    length = ctx * tokens
    width = made.qkv_out.shape[1] // 3
    columns = made.act_out.shape[2]
    units = columns // dp
    chips = ctx // 2
    rows = D // dp
    count = rows // ctx
    lanes = full_lanes(12 * D // (ctx * dp))
    b = Build()
    b.take(
        VMEM,
        grad=made.grad,
        resid=made.resid,
        own_cot=made.own_cot,
        own_in=made.own_in,
        vectors=made.vectors,
        own_mixed=made.own_mixed,
        qkv=made.qkv_out,
        doc_start=made.doc_start,
        stats=made.stats,
    )
    b.take(
        HBM,
        proj_mat=made.proj_mat_out,
        qkv_mat=made.qkv_mat_out,
        part=made.part_out,
        ffn=made.ffn_out,
        pre_act=made.pre_out,
        attn_in=made.attn_in_out,
        act=made.act_out,
        cots=made.cots_out,
    )
    b.give(
        WIDE,
        VMEM,
        output_t=(D, tokens),
        grad_in_t=(D, tokens),
        qkv_grad=(count, 3 * D),
        proj_grad=(count, D),
        fc_out=(count, FF),
        out_grad=(units, D),
        vec_out=(1, lanes),
    )
    for name, shape in (
        ("fc", (rows, columns)),
        ("qkv", (rows, 3 * width)),
        ("out", (units, D)),
        ("proj", (units, D)),
    ):
        b.give(LOW, HBM, **{name + "_parts": (dp, *shape), name + "_landed": (3, *shape)})
        b.both(**{name + "_plane": 6})
    b.hold(
        LOW,
        mat=(dp, rows, D),
        big=(ctx, tokens, D),
        feed=(ctx, tokens, columns),
        stage_fc=(3, rows, columns),
        stage_out=(3, units, D),
        proj_blocks=(chips, packed_rows(count, D), 128),
        proj_came=(chips, packed_rows(count, D), 128),
        mixed_pair=(2, tokens, ctx * width),
        low_pair=(2, tokens, D),
        own_grad=(tokens, ctx * width),
        head_grad=(length, width),
        rows=(length, 3 * width),
        key_t=(width, length),
    )
    for name, wide in (("fc", columns), ("qkv", 3 * width)):
        packed = (ctx, packed_rows(count, wide), 128)
        b.hold(LOW, **{name + "_blocks": packed, name + "_came": packed})
    for name in ("out", "in"):
        b.line_sum(name, ctx, tokens)
    b.hold(
        WIDE,
        wide=(rows, full_lanes(D)),
        key_grad=(length, width),
        value_grad=(length, width),
        grad_resid=(tokens, D),
        came=(tokens, D),
        vec=(ROWS, max(full_lanes(D), ctx * width)),
        vec_parts=(dp, ctx, 1, lanes),
        vec_landed=(dp, ctx, 1, lanes),
        vec_rows=(ctx, 1, lanes),
        vec_came=(ctx, 1, lanes),
    )
    b.both(fc=ctx, qkv=ctx, proj=chips, proj_pair=2, heads=ctx, vec_plane=dp, vec=ctx)
    b.sems(load_sems=(4,), stage_fc_sems=(3,), stage_out_sems=(3,))
    assert units == -(-(chips * count) // 16) * 16
    return b.call(functools.partial(backward_kernel, block), 6, "backward")


def gather_rows(block):
    return lax.all_gather(block, ("dp", "ctx"), axis=0, tiled=True)


def by_rank_heads(rows, ctx, slots):
    count = rows.shape[0]
    split = rows.reshape(count, 3, D)
    split = jnp.pad(split, ((0, 0), (0, 0), (0, (ctx * slots - HEADS) * HEAD_DIM)))
    split = split.reshape(count, 3, ctx, slots * HEAD_DIM)
    return split.transpose(2, 0, 1, 3).reshape(ctx, count, 3 * slots * HEAD_DIM)


def from_rank_heads(blocks, slots):
    ctx, count = blocks.shape[:2]
    split = blocks.reshape(ctx, count, 3, slots * HEAD_DIM).transpose(1, 2, 0, 3)
    return split.reshape(count, 3, ctx * slots * HEAD_DIM)[:, :, :D].reshape(count, 3 * D)


def padded_units(units):
    return -(-units // 16) * 16


def by_rank_units(rows, ctx, dp):
    count = rows.shape[0]
    units = FF // (dp * ctx)
    split = rows.reshape(count, dp, ctx, units).transpose(2, 0, 1, 3)
    split = jnp.pad(split, ((0, 0), (0, 0), (0, 0), (0, padded_units(units) - units)))
    return split.reshape(ctx, count, dp * padded_units(units))


def from_rank_units(blocks, dp):
    ctx, count = blocks.shape[:2]
    units = FF // (dp * ctx)
    split = blocks.reshape(ctx, count, dp, padded_units(units))[..., :units]
    return split.transpose(1, 2, 0, 3).reshape(count, FF)


def shards(
    hidden_in, qkv_weight, proj_weight, fc_weight, out_weight, small_params, segments, cotangent
):
    tokens = hidden_in.shape[1]
    length = segments.shape[1]
    ctx = lax.axis_size("ctx")
    dp = lax.axis_size("dp")
    owners = dp * ctx
    rank = lax.axis_index("ctx")
    slots = -(-HEADS // ctx)
    width = slots * HEAD_DIM
    units = FF // owners
    rows = D // owners
    whole = D % owners == 0 and dp == 4
    block = min(256, length)
    both = ("dp", "ctx")

    vec_count = small_params.shape[0]
    small = jnp.pad(small_params.astype(WIDE), (0, full_lanes(vec_count) - vec_count))[None]
    unit_rows = out_weight.reshape(units, D)
    if whole:
        mats = (
            qkv_weight.reshape(rows, 3 * D),
            fc_weight.reshape(rows, FF),
            proj_weight.reshape(rows, D),
        )
    else:
        mat_qkv = by_rank_heads(gather_rows(qkv_weight).reshape(D, 3 * D), ctx, slots)
        mat_qkv = lax.dynamic_index_in_dim(mat_qkv, rank, 0, keepdims=False)
        mat_fc = by_rank_units(gather_rows(fc_weight).reshape(D, FF), ctx, dp)
        mat_fc = lax.dynamic_index_in_dim(mat_fc, rank, 0, keepdims=False)
        mat_proj = gather_rows(proj_weight).reshape(D, D)
        mats = (mat_qkv, mat_fc, mat_proj)
    made = forward(
        small, hidden_in[0].T, cotangent[0].T, unit_rows, segments, mats, slots, whole, block
    )
    if whole:
        done = backward(made, block)
        return (
            done.output_t.T[None],
            done.grad_in_t.T[None],
            done.qkv_grad.reshape(-1),
            done.proj_grad.reshape(-1),
            done.fc_out.reshape(-1),
            done.out_grad[:units].reshape(-1),
            done.vec_out[0, :vec_count],
        )
    vectors = made.vectors

    grad_resid, resid_low, sums_two, sums_units, grad_rows, grad_out, output, grad_fc = back(
        made.grad,
        made.resid,
        cotangent[0],
        vectors,
        mat_proj,
        made.qkv_out,
        made.doc_start,
        made.stats,
        made.ffn_out,
        made.pre_out,
        made.act_out,
        made.cots_out,
        made.part_out,
        block,
    )
    grad_input, sums_one, sums_heads, grad_qkv = last(
        grad_rows,
        mat_qkv,
        made.attn_in_out.reshape(length, D),
        hidden_in[0],
        grad_resid,
        vectors,
    )
    here = (jnp.arange(ctx) == rank)[:, None, None]
    full_fc = from_rank_units(jnp.where(here, grad_fc[None], 0.0), dp).reshape(-1)
    full_qkv = from_rank_heads(jnp.where(here, grad_qkv[None], 0.0), slots).reshape(-1)
    grad_proj = dot(made.own_mixed[:, :D], resid_low, 0, 0).reshape(-1)
    share_fc, share_qkv, share_proj = [
        lax.psum_scatter(full, both, scatter_dimension=0, tiled=True)
        for full in (full_fc, full_qkv, grad_proj)
    ]

    def spread_heads(part):
        padded = jnp.zeros((ctx * width,), WIDE)
        return lax.dynamic_update_slice_in_dim(padded, part, rank * width, 0)[:D]

    sums_units = sums_units[0].reshape(dp, 1, -1)[:, :, :units]
    sums_units = lax.dynamic_update_slice_in_dim(
        jnp.zeros((dp, ctx, units), WIDE), sums_units, rank, 1
    ).reshape(FF)
    vector = jnp.concatenate(
        [
            sums_one[0],
            sums_one[1],
            spread_heads(sums_heads[0, :width]),
            spread_heads(sums_heads[0, 2 * width :]),
            sums_two[0],
            sums_two[1],
            sums_two[2],
            sums_units,
            sums_two[3],
        ]
    ).reshape(owners, vec_count)
    vec_pad = -(-vec_count // 1024) * 1024
    vector = jnp.pad(vector, ((0, 0), (0, vec_pad - vec_count))).reshape(dp, ctx, -1, 128)
    share_vector = sum_vector(vector)
    return (
        output[None],
        grad_input[None],
        share_qkv.astype(WIDE).reshape(-1),
        share_proj.astype(WIDE).reshape(-1),
        share_fc.astype(WIDE).reshape(-1),
        grad_out[:units].reshape(-1),
        share_vector.reshape(-1)[:vec_count],
    )


def solution(mesh):
    flat = P(("dp", "ctx"))
    rows = P("dp", "ctx", None)
    return jax.shard_map(
        shards,
        mesh=mesh,
        in_specs=(rows, flat, flat, flat, flat, flat, P("dp", None), rows),
        out_specs=(rows, rows, flat, flat, flat, flat, flat),
        check_vma=False,
    )
```

```python
import functools

import jax
import jax.numpy as jnp
from jax import lax
from jax.experimental import pallas as pl
from jax.experimental.pallas import tpu as pltpu
from jax.sharding import PartitionSpec as P

D = 1600
HEADS = 25
HEAD_DIM = 64
FF = 6400
EPSILON = 1e-05
LOW = jnp.bfloat16
WIDE = jnp.float32
MIB = 1024 * 1024


def dot(left, right, left_dim=1, right_dim=0):
    return lax.dot_general(
        left, right, (((left_dim,), (right_dim,)), ((), ())), preferred_element_type=WIDE
    )


def normalize(rows):
    centre = rows - jnp.mean(rows, -1, keepdims=True)
    spread = jnp.mean(centre * centre, -1, keepdims=True)
    scale = lax.rsqrt(spread + EPSILON)
    return centre * scale, scale


def norm_back(normed, scale, gain, incoming):
    scaled = gain * incoming
    return scale * (
        scaled
        - jnp.mean(scaled, -1, keepdims=True)
        - normed * jnp.mean(scaled * normed, -1, keepdims=True)
    )


def head_lanes(head, width):
    lane = lax.broadcasted_iota(jnp.int32, (1, width), 1)
    return (lane // HEAD_DIM) == head


def allowed_scores(scores, doc_start, first_query, keys, block):
    key_pos = lax.broadcasted_iota(jnp.int32, (keys, block), 0)
    query_pos = first_query + lax.broadcasted_iota(jnp.int32, (keys, block), 1)
    seen = (key_pos >= doc_start) & (key_pos <= query_pos)
    return jnp.where(seen, scores, -1e30)


def attend_body(block, qkv_ref, start_ref, mixed_ref, stat_ref, value_t):
    length = qkv_ref.shape[0]
    width = mixed_ref.shape[1]
    slots = width // HEAD_DIM
    value_t[...] = qkv_ref[:, 2 * width : 3 * width].astype(WIDE).T.astype(LOW)
    stat_ref[...] = jnp.zeros_like(stat_ref)
    for index in range(length // block):
        keys = (index + 1) * block
        rows = pl.ds(index * block, block)
        key_rows = qkv_ref[0:keys, width : 2 * width]
        doc_start = start_ref[0:1, rows]
        outs = []
        for head in range(slots):
            query = jnp.where(
                head_lanes(head, width), qkv_ref[rows, 0:width] * LOW(HEAD_DIM**-0.5), LOW(0)
            )
            scores = dot(key_rows, query, 1, 1)
            scores = allowed_scores(scores, doc_start, index * block, keys, block)
            top = jnp.max(scores, 0, keepdims=True)
            expo = jnp.exp(scores - top)
            total = jnp.sum(expo, 0, keepdims=True)
            head_rows = slice(head * HEAD_DIM, (head + 1) * HEAD_DIM)
            out = dot(value_t[head_rows, 0:keys], expo.astype(LOW))
            outs.append(out / total)
            stat_ref[head : head + 1, rows] = top + jnp.log(total)
        mixed_ref[rows, :] = jnp.concatenate(outs, 0).T.astype(LOW)


def attend_back_body(
    block, qkv_ref, start_ref, stat_ref, grad_ref, out_ref, key_t, key_grad, value_grad, after
):
    length = qkv_ref.shape[0]
    width = grad_ref.shape[1]
    slots = width // HEAD_DIM
    scale = HEAD_DIM**-0.5
    key_t[...] = qkv_ref[:, width : 2 * width].astype(WIDE).T.astype(LOW)
    key_grad[...] = jnp.zeros_like(key_grad)
    value_grad[...] = jnp.zeros_like(value_grad)
    for index in range(length // block):
        keys = (index + 1) * block
        rows = pl.ds(index * block, block)
        key_rows = qkv_ref[0:keys, width : 2 * width]
        value_rows = qkv_ref[0:keys, 2 * width : 3 * width]
        doc_start = start_ref[0:1, rows]
        outs = []
        for head in range(slots):
            lanes = head_lanes(head, width)
            head_rows = slice(head * HEAD_DIM, (head + 1) * HEAD_DIM)
            query = jnp.where(lanes, qkv_ref[rows, 0:width] * LOW(scale), LOW(0))
            grad = jnp.where(lanes, grad_ref[rows, :], LOW(0))
            scores = dot(key_rows, query, 1, 1)
            scores = allowed_scores(scores, doc_start, index * block, keys, block)
            probs = jnp.exp(scores - stat_ref[head : head + 1, rows])
            grad_probs = dot(value_rows, grad, 1, 1)
            delta = jnp.sum(probs * grad_probs, 0, keepdims=True)
            grad_scores = (probs * (grad_probs - delta)).astype(LOW)
            value_grad[0:keys, :] += dot(probs.astype(LOW), grad)
            key_grad[0:keys, :] += dot(grad_scores, query)
            outs.append(dot(key_t[head_rows, 0:keys], grad_scores))
        out_ref[rows, 0:width] = (jnp.concatenate(outs, 0).T * scale).astype(LOW)
        if index in after:
            after[index]()
    out_ref[:, width : 2 * width] = key_grad[...].astype(LOW)
    out_ref[:, 2 * width : 3 * width] = value_grad[...].astype(LOW)


MESH = pl.DeviceIdType.MESH


def send(src, dst, send_sem, recv_sem, **target):
    return pltpu.make_async_remote_copy(
        src_ref=src,
        dst_ref=dst,
        send_sem=send_sem,
        recv_sem=recv_sem,
        device_id=target,
        device_id_type=MESH,
    )


def greet_line(chips):
    rank = lax.axis_index("ctx")
    chip, core = rank // 2, rank % 2
    barrier = pltpu.get_barrier_semaphore()
    pl.semaphore_signal(barrier, 1, device_id={"ctx": rank + 1 - 2 * core}, device_id_type=MESH)

    @pl.when(chip > 0)
    def _():
        pl.semaphore_signal(barrier, 1, device_id={"ctx": rank - 2}, device_id_type=MESH)

    @pl.when(chip < chips - 1)
    def _():
        pl.semaphore_signal(barrier, 1, device_id={"ctx": rank + 2}, device_id_type=MESH)

    sides = (chip > 0).astype(jnp.int32) + (chip < chips - 1).astype(jnp.int32)
    pl.semaphore_wait(barrier, 1 + sides)


def greet_all(between=lambda: None):
    barrier = pltpu.get_barrier_semaphore()
    count = 0
    for axis in ("ctx", "dp"):
        size = lax.axis_size(axis)
        here = lax.axis_index(axis)

        def one(off, carry, axis=axis, size=size, here=here):
            peer = lax.rem(here + off, size)
            pl.semaphore_signal(barrier, 1, device_id={axis: peer}, device_id_type=MESH)
            return carry

        lax.fori_loop(1, size, one, 0)
        count += size - 1
    between()
    pl.semaphore_wait(barrier, count)


class Swap:
    def __init__(self, axis, source, target, sems):
        self.axis, self.source, self.target = axis, source, target
        self.send_sems, self.recv_sems = sems
        self.rank = lax.axis_index(axis)
        self.size = lax.axis_size(axis)

    def copy(self, peer, origin, target):
        return send(
            self.source(peer),
            self.target(origin),
            self.send_sems.at[peer],
            self.recv_sems.at[origin],
            **{self.axis: target},
        )

    def every(self, act):
        def one(off, carry):
            act(lax.rem(self.rank + off, self.size))
            return carry

        lax.fori_loop(1, self.size, one, 0)

    def start(self):
        self.every(lambda peer: self.copy(peer, self.rank, peer).start())

    def wait(self):
        self.every(lambda peer: self.copy(peer, peer, self.rank).wait_recv())

    def drain(self):
        self.every(lambda peer: self.copy(peer, self.rank, peer).wait_send())

    @staticmethod
    def semaphores(size):
        return [pltpu.SemaphoreType.DMA((size,)), pltpu.SemaphoreType.DMA((size,))]


class ChipSwap(Swap):
    def __init__(self, source, target, sems):
        super().__init__("ctx", source, target, sems)
        self.core = self.rank % 2
        self.rank, self.size = self.rank // 2, self.size // 2

    def copy(self, peer, origin, target):
        return send(
            self.source(peer),
            self.target(origin),
            self.send_sems.at[peer],
            self.recv_sems.at[origin],
            ctx=2 * target + self.core,
        )


class PlaneGather:
    def __init__(self, blocks, sems):
        self.blocks = blocks
        self.size = blocks.shape[0]
        self.rank = lax.axis_index("dp")
        self.square = self.size == 4
        self.send_sems, self.recv_sems = sems
        if self.square:
            self.beside = self.rank + 1 - 2 * (self.rank % 2)
            self.above = self.rank + 2 - 4 * (self.rank // 2)
            half = blocks.shape[1] // 32 * 16
            self.low, self.high = pl.ds(0, half), pl.ds(half, blocks.shape[1] - half)
        else:
            self.swap = Swap("dp", lambda peer: blocks.at[self.rank], blocks.at.__getitem__, sems)

    def copy(self, index, ref, target):
        return send(ref, ref, self.send_sems.at[index], self.recv_sems.at[index], dp=target)

    def start(self):
        if not self.square:
            self.swap.start()
            return
        own = self.blocks.at[self.rank]
        self.copy(0, own, self.beside).start()
        self.copy(1, own, self.above).start()

    def relay(self):
        if not self.square:
            return
        self.copy(0, self.blocks.at[self.beside], self.beside).wait_recv()
        self.copy(2, self.blocks.at[self.beside, self.low], self.above).start()
        self.copy(1, self.blocks.at[self.above], self.above).wait_recv()
        self.copy(3, self.blocks.at[self.above, self.high], self.beside).start()

    def wait(self):
        if not self.square:
            self.swap.wait()
            self.swap.drain()
            return
        far = 3 - self.rank
        own = self.blocks.at[self.rank]
        self.copy(2, self.blocks.at[far, self.low], self.above).wait_recv()
        self.copy(3, self.blocks.at[far, self.high], self.beside).wait_recv()
        self.copy(0, own, self.beside).wait_send()
        self.copy(1, own, self.above).wait_send()
        self.copy(2, self.blocks.at[self.beside, self.low], self.above).wait_send()
        self.copy(3, self.blocks.at[self.above, self.high], self.beside).wait_send()

    semaphores = staticmethod(Swap.semaphores)


class PlaneSum:
    def __init__(self, blocks, landed, sems):
        self.blocks, self.landed = blocks, landed
        self.rank = lax.axis_index("dp")
        self.send_sems, self.recv_sems = sems
        self.swap = Swap("dp", blocks.at.__getitem__, landed.at.__getitem__, sems)
        self.square = blocks.shape[0] == 4
        if self.square:
            self.beside = self.rank + 1 - 2 * (self.rank % 2)
            self.above = self.rank + 2 - 4 * (self.rank // 2)
            half = blocks.shape[1] // 32 * 16
            self.low, self.high = pl.ds(0, half), pl.ds(half, blocks.shape[1] - half)

    def copy(self, index):
        far = 3 - self.rank
        block, slot, rows, target = (
            (far, 0, self.low, self.beside),
            (self.beside, 1, self.low, self.beside),
            (far, 0, self.high, self.above),
            (self.above, 1, self.high, self.above),
            (self.above, 2, self.low, self.above),
            (self.beside, 2, self.high, self.beside),
        )[index]
        return send(
            self.blocks.at[block, rows],
            self.landed.at[slot, rows],
            self.send_sems.at[index],
            self.recv_sems.at[index],
            dp=target,
        )

    def start(self):
        if not self.square:
            self.swap.start()
            return
        for index in range(4):
            self.copy(index).start()

    def relay(self):
        if not self.square:
            return
        for index, block, rows in ((0, self.above, self.low), (2, self.beside, self.high)):
            self.copy(index).wait_recv()
            total = self.blocks[block, rows].astype(WIDE) + self.landed[0, rows].astype(WIDE)
            self.blocks[block, rows] = total.astype(self.blocks.dtype)
            self.copy(4 + index // 2).start()

    def total(self):
        total = self.blocks[self.rank].astype(WIDE)
        if not self.square:
            self.swap.wait()
            for off in range(1, self.swap.size):
                total = total + self.landed[lax.rem(self.rank + off, self.swap.size)].astype(WIDE)
            return total
        for index in (1, 3, 4, 5):
            self.copy(index).wait_recv()
        return total + self.landed[1].astype(WIDE) + self.landed[2].astype(WIDE)

    def drain(self):
        if not self.square:
            self.swap.drain()
            return
        for index in range(6):
            self.copy(index).wait_send()

    @staticmethod
    def semaphores(size):
        return Swap.semaphores(max(size, 6))


class LineGather:
    def __init__(self, blocks, send_sems, recv_sems):
        self.blocks, self.send_sems, self.recv_sems = blocks, send_sems, recv_sems
        self.rank = lax.axis_index("ctx")
        self.chip, self.core = self.rank // 2, self.rank % 2
        self.chips = blocks.shape[0] // 2

    def copy(self, way, origin, target, src=None):
        block = self.blocks.at[origin]
        return send(
            block if src is None else src,
            block,
            self.send_sems.at[way, origin],
            self.recv_sems.at[origin],
            ctx=target,
        )

    def pass_on(self, origin, src=None):
        chip = origin // 2

        @pl.when((chip <= self.chip) & (self.chip < self.chips - 1))
        def _():
            self.copy(0, origin, self.rank + 2, src).start()

        @pl.when((chip >= self.chip) & (self.chip > 0))
        def _():
            self.copy(1, origin, self.rank - 2, src).start()

        self.copy(2, origin, self.rank + 1 - 2 * self.core, src).start()

    def arrive(self, step, part):
        side, other = part % 2, part // 2
        origin_chip = self.chip + jnp.where(side == 0, -step, step)
        origin = 2 * origin_chip + jnp.where(other == 0, self.core, 1 - self.core)
        valid = (origin_chip >= 0) & (origin_chip < self.chips) & ((step > 0) | (side == 0))

        @pl.when(valid & (origin != self.rank))
        def _():
            self.copy(0, origin, self.rank).wait_recv()

            @pl.when(other == 0)
            def _():
                self.pass_on(origin)

        return valid, origin

    def finish(self):
        def one(chip, carry):
            origin = 2 * chip + self.core

            @pl.when((chip <= self.chip) & (self.chip < self.chips - 1))
            def _():
                self.copy(0, origin, self.rank).wait_send()

            @pl.when((chip >= self.chip) & (self.chip > 0))
            def _():
                self.copy(1, origin, self.rank).wait_send()

            self.copy(2, origin, self.rank).wait_send()
            return carry

        lax.fori_loop(0, self.chips, one, 0)

    @staticmethod
    def semaphores(ctx):
        return [pltpu.SemaphoreType.DMA((3, ctx)), pltpu.SemaphoreType.DMA((ctx,))]


class LineSum:
    def __init__(self, blocks, pair, passing, sems):
        self.blocks, self.pair, self.passing = blocks, pair, passing
        self.pair_send, self.pair_recv, self.line_send, self.line_recv = sems
        self.rank = lax.axis_index("ctx")
        self.chip, self.core = self.rank // 2, self.rank % 2
        self.chips = blocks.shape[0] // 2
        self.pieces = self.line_recv.shape[2]
        self.piece = blocks.shape[1] // self.pieces

    def pair_copy(self, chip):
        return send(
            self.blocks.at[2 * chip + 1 - self.core],
            self.pair.at[chip],
            self.pair_send.at[chip],
            self.pair_recv.at[chip],
            ctx=self.rank + 1 - 2 * self.core,
        )

    def line_copy(self, way, chip, piece, target, at):
        rows = pl.ds(piece * self.piece, self.piece)
        slot = jnp.where((way == 1) & (chip == at), self.chips, chip)
        return send(
            self.blocks.at[2 * chip + self.core, rows],
            self.passing.at[slot, rows],
            self.line_send.at[chip, piece],
            self.line_recv.at[way, chip, piece],
            ctx=target,
        )

    def both(self, chip, rows):
        mine = self.blocks[2 * chip + self.core, rows].astype(WIDE)
        return mine + self.pair[chip, rows].astype(WIDE)

    def forward(self, way, chip, valid):
        behind = jnp.where(way == 0, self.chip > 0, self.chip < self.chips - 1)
        target = self.rank + jnp.where(way == 0, 2, -2)

        @pl.when(valid)
        def _():
            self.pair_copy(chip).wait_recv()

            def one(piece, carry):
                rows = pl.ds(pl.multiple_of(piece * self.piece, self.piece), self.piece)
                total = self.both(chip, rows)

                @pl.when(behind)
                def _():
                    self.line_copy(way, chip, piece, target, self.chip).wait_recv()
                    passing = self.passing[chip, rows].astype(WIDE)
                    self.blocks[2 * chip + self.core, rows] = (total + passing).astype(LOW)

                @pl.when(jnp.logical_not(behind))
                def _():
                    self.blocks[2 * chip + self.core, rows] = total.astype(LOW)

                self.line_copy(way, chip, piece, target, target // 2).start()
                return carry

            lax.fori_loop(0, self.pieces, one, 0)

    def near_first(self, step, way):
        last = self.chips - 1
        chip = jnp.where(way == 0, step - self.chip, 2 * last - self.chip - step)
        ahead = jnp.where(way == 0, (chip > self.chip) & (chip <= last), (chip >= 0) & (chip < self.chip))
        self.forward(way, chip, ahead)

    def far_first(self, step, way):
        last = self.chips - 1
        chip = jnp.where(way == 0, last + self.chip - step, step - last + self.chip)
        ahead = jnp.where(way == 0, (chip > self.chip) & (chip <= last), (chip >= 0) & (chip < self.chip))
        self.forward(way, chip, ahead)

    def send_pairs(self):
        def one(chip, carry):
            self.pair_copy(chip).start()
            return carry

        lax.fori_loop(0, self.chips, one, 0)

    def far_steps(self, begin, end):
        def one(index, carry):
            self.far_first(index // 2, index % 2)
            return carry

        lax.fori_loop(2 * begin, 2 * end, one, 0)

    def finish(self, out):
        self.pair_copy(self.chip).wait_recv()

        def one(piece, carry):
            rows = pl.ds(pl.multiple_of(piece * self.piece, self.piece), self.piece)
            out[rows] = self.both(self.chip, rows)

            @pl.when(self.chip > 0)
            def _():
                self.line_copy(0, self.chip, piece, self.rank, self.chip).wait_recv()
                out[rows] = out[rows] + self.passing[self.chip, rows].astype(WIDE)

            @pl.when(self.chip < self.chips - 1)
            def _():
                self.line_copy(1, self.chip, piece, self.rank, self.chip).wait_recv()
                out[rows] = out[rows] + self.passing[self.chips, rows].astype(WIDE)

            return carry

        lax.fori_loop(0, self.pieces, one, 0)

        def sent(chip, carry):
            self.pair_copy(chip).wait_send()

            @pl.when(chip != self.chip)
            def _():
                for piece in range(self.pieces):
                    self.line_copy(0, chip, piece, self.rank, self.chip).wait_send()

            return carry

        lax.fori_loop(0, self.chips, sent, 0)

    @staticmethod
    def scratch(ctx, rows, columns, pieces):
        chips = ctx // 2
        return [
            pltpu.VMEM((ctx, rows, columns), LOW),
            pltpu.VMEM((chips, rows, columns), LOW),
            pltpu.VMEM((chips + 1, rows, columns), LOW),
            pltpu.SemaphoreType.DMA((chips,)),
            pltpu.SemaphoreType.DMA((chips,)),
            pltpu.SemaphoreType.DMA((chips, pieces)),
            pltpu.SemaphoreType.DMA((2, chips, pieces)),
        ]


VMEM = pl.BlockSpec(memory_space=pltpu.VMEM)
HBM = pl.BlockSpec(memory_space=pl.ANY)


def params(number):
    return pltpu.CompilerParams(
        vmem_limit_bytes=63 * MIB, collective_id=number, has_side_effects=True
    )


def packed_rows(count, columns):
    tiles = -(-columns // 128)
    main = count // 16 * 16
    return tiles * main + -(-(tiles * (count - main)) // 16) * 16


def pack(out, index, rows, first, count, lane, columns):
    tiles = -(-columns // 128)
    main = count // 16 * 16
    for tile in range(tiles):
        lanes = slice(lane + tile * 128, lane + tile * 128 + 128)
        part = rows[first : first + main, lanes]
        out[index, tile * main : (tile + 1) * main] = part.astype(LOW)
    left = [
        rows[first + row : first + row + 1, lane + tile * 128 : lane + tile * 128 + 128]
        for row in range(main, count)
        for tile in range(tiles)
    ]
    space = out.shape[1] - tiles * main
    if space:
        left.append(jnp.zeros((space - len(left), 128), WIDE))
        out[index, tiles * main :] = jnp.concatenate(left, 0).astype(LOW)


def unpack(packed, rows, first, count, columns):
    tiles = -(-columns // 128)
    main = count // 16 * 16
    for tile in range(tiles):
        lanes = slice(tile * 128, tile * 128 + 128)
        rows[first : first + main, lanes] = packed[tile * main : (tile + 1) * main].astype(WIDE)
    left = packed[tiles * main :].astype(WIDE)
    for row in range(main, count):
        for tile in range(tiles):
            place = (row - main) * tiles + tile
            lanes = slice(tile * 128, tile * 128 + 128)
            rows[first + row : first + row + 1, lanes] = left[place : place + 1]


def full_lanes(columns):
    return -(-columns // 128) * 128


def head_pieces(ctx, slots):
    width = slots * HEAD_DIM
    pieces = []
    for rank in range(ctx):
        count = min(width, D - rank * width)
        if count > 0:
            for part in range(3):
                pieces.append((rank, part * width, part * D + rank * width, count))
    return pieces


def unit_pieces(ctx, dp):
    units = FF // (ctx * dp)
    return [
        (rank, seq * padded_units(units), (seq * ctx + rank) * units, units)
        for rank in range(ctx)
        for seq in range(dp)
    ]


def divide(rows_ref, wide, blocks, pieces, columns):
    count = rows_ref.shape[0]
    lanes = full_lanes(columns)
    for rank in range(blocks.shape[0]):
        wide[...] = jnp.zeros_like(wide)
        for owner, here, there, size in pieces:
            if owner == rank:
                wide[0:count, here : here + size] = rows_ref[:, there : there + size].astype(WIDE)
        pack(blocks, rank, wide, 0, count, 0, lanes)


class Spread:
    def __init__(self, blocks, landed, wide, out, sems):
        self.blocks, self.landed, self.wide, self.out = blocks, landed, wide, out
        self.swap = Swap("ctx", blocks.at.__getitem__, landed.at.__getitem__, sems[:2])
        self.plane = PlaneGather(out, sems[2:])

    def start(self):
        self.swap.start()
        self.landed[self.swap.rank] = self.blocks[self.swap.rank]

    def cross(self):
        self.swap.wait()
        count = self.out.shape[1] // self.swap.size
        columns = self.out.shape[2]
        for index in range(self.swap.size):
            unpack(self.landed[index], self.wide, index * count, count, columns)
        self.out[self.plane.rank] = self.wide[:, 0:columns].astype(LOW)
        self.plane.start()

    def wait(self):
        self.plane.wait()

    @staticmethod
    def scratch(ctx, dp, rows, columns):
        return [
            pltpu.VMEM((ctx, packed_rows(rows // ctx, columns), 128), LOW),
            pltpu.VMEM((rows, full_lanes(columns)), WIDE),
            *Swap.semaphores(ctx),
            *PlaneGather.semaphores(dp),
        ]


class StreamSum:
    def __init__(self, parts, landed, stage, stage_sems, sems):
        self.parts, self.landed, self.stage, self.stage_sems = parts, landed, stage, stage_sems
        self.plane = PlaneSum(parts, landed, sems)

    def put(self, index, part):
        if index >= 2:
            self.move(index - 2).wait()
        self.stage[index % 2] = part.astype(LOW)
        self.move(index).start()

    def move(self, index):
        slot = index % 2
        return pltpu.make_async_copy(
            self.stage.at[slot], self.parts.at[index], self.stage_sems.at[slot]
        )

    def start(self):
        self.move(2).wait()
        self.move(3).wait()
        self.plane.start()

    def load(self, source, slot, rows):
        return pltpu.make_async_copy(
            source.at[rows], self.stage.at[slot, rows], self.stage_sems.at[slot]
        )

    def relayed(self, index):
        plane = self.plane
        rows, target = ((plane.low, plane.above), (plane.high, plane.beside))[index]
        return send(
            self.stage.at[2, rows],
            self.landed.at[2, rows],
            plane.send_sems.at[4 + index],
            plane.recv_sems.at[4 + index],
            dp=target,
        )

    def relay(self):
        plane = self.plane
        for index, block, rows in ((0, plane.above, plane.low), (1, plane.beside, plane.high)):
            plane.copy(2 * index).wait_recv()
            loads = (
                self.load(self.parts.at[block], 0, rows),
                self.load(self.landed.at[0], 1, rows),
            )
            for load in loads:
                load.start()
            for load in loads:
                load.wait()
            total = self.stage[0, rows].astype(WIDE) + self.stage[1, rows].astype(WIDE)
            self.stage[2, rows] = total.astype(LOW)
            self.relayed(index).start()

    def total(self):
        plane = self.plane
        for index in range(4):
            plane.copy(index).wait_send()
        plane.copy(1).wait_recv()
        plane.copy(3).wait_recv()
        for index in range(2):
            self.relayed(index).wait_send()
            self.relayed(index).wait_recv()
        every = pl.ds(0, self.parts.shape[1])
        loads = (
            self.load(self.parts.at[plane.rank], 0, every),
            self.load(self.landed.at[1], 1, every),
            self.load(self.landed.at[2], 2, every),
        )
        for load in loads:
            load.start()
        for load in loads:
            load.wait()
        total = self.stage[0].astype(WIDE) + self.stage[1].astype(WIDE)
        return total + self.stage[2].astype(WIDE)


class Collect:
    def __init__(self, pieces, plane, wide, blocks, came, out, sems):
        self.pieces, self.plane, self.wide, self.blocks = pieces, plane, wide, blocks
        self.came, self.out = came, out
        self.swap = Swap("ctx", blocks.at.__getitem__, came.at.__getitem__, sems)

    def cross(self):
        rows, columns = self.plane.parts.shape[1:]
        lanes = full_lanes(columns)
        self.wide[0:rows, 0:columns] = self.plane.total()
        if lanes > columns:
            self.wide[0:rows, columns:lanes] = jnp.zeros((rows, lanes - columns), WIDE)
        count = rows // self.swap.size
        for index in range(self.swap.size):
            pack(self.blocks, index, self.wide, index * count, count, 0, columns)
        self.swap.start()
        self.came[self.swap.rank] = self.blocks[self.swap.rank]

    def wait(self):
        self.swap.wait()
        count = self.out.shape[0]
        for rank in range(self.swap.size):
            unpack(self.came[rank], self.wide, 0, count, self.plane.parts.shape[2])
            for owner, here, there, size in self.pieces:
                if owner == rank:
                    self.out[:, there : there + size] = self.wide[0:count, here : here + size]
        self.swap.drain()


class Projection:
    def __init__(self, rows, blocks, wide, out, sems):
        self.rows, self.blocks, self.wide, self.out = rows, blocks, wide, out
        self.rank = lax.axis_index("ctx")
        self.core = self.rank % 2
        self.packed = rows.shape[1]
        self.plane = PlaneGather(blocks.at[self.core], sems[:2])
        self.send_sems, self.recv_sems = sems[2:4]
        self.swap = ChipSwap(lambda peer: rows.at[0], self.place, sems[4:])

    def place(self, chip):
        rows = pl.ds(pl.multiple_of(chip * self.packed, self.packed), self.packed)
        return self.blocks.at[self.core, self.plane.rank, rows]

    def start(self):
        self.swap.start()
        rows = pl.ds(pl.multiple_of(self.swap.rank * self.packed, self.packed), self.packed)
        self.blocks[self.core, self.plane.rank, rows] = self.rows[0]

    def cross(self):
        self.swap.wait()
        self.plane.start()
        self.to_other(self.plane.rank).start()

    def to_other(self, seq):
        block = self.blocks.at[self.core, seq]
        return send(
            block,
            block,
            self.send_sems.at[seq],
            self.recv_sems.at[seq],
            ctx=self.rank + 1 - 2 * self.core,
        )

    def wait(self):
        self.plane.wait()

        def others(off, carry):
            self.to_other(lax.rem(self.plane.rank + off, self.plane.size)).start()
            return carry

        lax.fori_loop(1, self.plane.size, others, 0)
        ctx = 2 * self.swap.size
        count = self.out.shape[1] // ctx

        def order(off, carry):
            seq = lax.rem(self.plane.rank + off, self.plane.size)
            self.to_other(seq).wait_recv()
            for rank in range(ctx):
                first = rank // 2 * self.packed
                rows = self.blocks[rank % 2, seq, first : first + self.packed]
                unpack(rows, self.wide, rank * count, count, D)
            self.out[seq] = self.wide[:, 0:D].astype(LOW)
            return carry

        lax.fori_loop(0, self.plane.size, order, 0)

        def sent(seq, carry):
            self.to_other(seq).wait_send()
            return carry

        lax.fori_loop(0, self.plane.size, sent, 0)
        self.swap.drain()

    @staticmethod
    def scratch(ctx, dp):
        packed = packed_rows(D // (dp * ctx), D)
        return [
            pltpu.VMEM((2, dp, ctx // 2 * packed, 128), LOW),
            pltpu.VMEM((D // dp, full_lanes(D)), WIDE),
            *PlaneGather.semaphores(dp),
            *Swap.semaphores(dp),
            *Swap.semaphores(ctx // 2),
        ]


def vector_pieces(owners, count):
    pieces = []
    for owner in range(owners):
        begin = 0
        while begin < count:
            place = owner * count + begin
            size = min(count - begin, D - place % D)
            pieces.append((owner, begin, place // D, place % D, size))
            begin += size
    return pieces


def unit_bias_pieces(rank, ctx, dp):
    units = FF // (ctx * dp)
    pieces = []
    for seq in range(dp):
        begin = 0
        while begin < units:
            place = (seq * ctx + rank) * units + begin
            size = min(units - begin, D - place % D)
            pieces.append((seq * padded_units(units) + begin, 7 + place // D, place % D, size))
            begin += size
    return pieces


GAIN_ONE, SHIFT_ONE, BIAS_QUERY, BIAS_VALUE, BIAS_PROJ, GAIN_TWO, SHIFT_TWO = range(7)
BIAS_OUT = 11
ROWS = 16


class Build:
    def __init__(self):
        self.ins, self.outs, self.scratch = {}, {}, {}

    def take(self, spec, **values):
        self.ins.update({name: (value, spec) for name, value in values.items()})

    def give(self, kind, spec, **shapes):
        for name, shape in shapes.items():
            self.outs[name] = (jax.ShapeDtypeStruct(shape, kind), spec)

    def hold(self, kind, **shapes):
        self.scratch.update({name: pltpu.VMEM(shape, kind) for name, shape in shapes.items()})

    def sems(self, **shapes):
        self.scratch.update(
            {name: pltpu.SemaphoreType.DMA(shape) for name, shape in shapes.items()}
        )

    def both(self, **sizes):
        for name, size in sizes.items():
            self.sems(**{name + "_send": (size,), name + "_recv": (size,)})

    def line_sum(self, name, ctx, tokens):
        chips = ctx // 2
        shapes = (ctx, tokens, D), (chips, tokens, D), (chips + 1, tokens, D)
        for part, shape in zip(("_blocks", "_pair", "_passing"), shapes, strict=True):
            self.hold(LOW, **{name + part: shape})
        self.both(**{name + "_pair": chips})
        self.sems(
            **{name + "_line_send": (chips, PIECES), name + "_line_recv": (2, chips, PIECES)}
        )

    def call(self, kernel, number, label):
        names = (*self.ins, *self.outs, *self.scratch)
        results = pl.pallas_call(
            functools.partial(kernel, names),
            out_shape=[shape for shape, _ in self.outs.values()],
            in_specs=[spec for _, spec in self.ins.values()],
            out_specs=[spec for _, spec in self.outs.values()],
            scratch_shapes=list(self.scratch.values()),
            compiler_params=params(number),
            name=label,
        )(*[value for value, _ in self.ins.values()])
        return Names(tuple(self.outs), results)


PIECES = 8


class Names:
    def __init__(self, names, refs):
        self.__dict__.update(zip(names, refs, strict=True))


def forward_kernel(block, whole, names, *refs):
    r = Names(names, refs)
    seq, rank = lax.axis_index("dp"), lax.axis_index("ctx")
    ctx, tokens, _ = r.rows.shape
    dp, units = r.units.shape[:2]
    width = r.mixed.shape[1]
    vec_count = 12 * D // (ctx * dp)

    def out(ref, target, index):
        return pltpu.make_async_copy(ref, target, r.out_sems.at[index])

    rows_in = LineGather(r.rows, r.rows_send, r.rows_recv)
    cots = LineGather(r.cots, r.cots_send, r.cots_recv)
    feed = LineGather(r.rows, r.feed_send, r.feed_recv)
    total = LineSum(
        r.sum_blocks,
        r.sum_pair,
        r.sum_passing,
        (r.sum_pair_send, r.sum_pair_recv, r.sum_line_send, r.sum_line_recv),
    )
    chips = feed.chips
    line = Swap(
        "ctx",
        lambda peer: r.small,
        lambda origin: r.smalls.at[seq, origin],
        (r.line_send, r.line_recv),
    )
    plane = Swap(
        "dp",
        lambda peer: r.smalls.at[seq],
        r.smalls.at.__getitem__,
        (r.plane_send, r.plane_recv),
    )
    unit_rows = PlaneGather(r.units, (r.units_send, r.units_recv))
    to_tokens = Swap(
        "ctx",
        lambda peer: r.mixed.at[pl.ds(pl.multiple_of(peer * tokens, tokens), tokens)],
        lambda origin: r.own_mixed.at[:, pl.ds(pl.multiple_of(origin * width, width), width)],
        (r.mixed_send, r.mixed_recv),
    )
    if whole:
        heads = Spread(
            r.qkv_blocks,
            r.qkv_landed,
            r.qkv_wide,
            r.qkv_mat,
            (r.qkv_send, r.qkv_recv, r.qkv_plane_send, r.qkv_plane_recv),
        )
        columns = Spread(
            r.fc_blocks,
            r.fc_landed,
            r.fc_wide,
            r.fc_mat,
            (r.fc_send, r.fc_recv, r.fc_plane_send, r.fc_plane_recv),
        )
        proj = Projection(
            r.proj_packed,
            r.proj_blocks,
            r.proj_wide,
            r.proj_mat,
            (
                r.proj_plane_send,
                r.proj_plane_recv,
                r.proj_pair_send,
                r.proj_pair_recv,
                r.proj_send,
                r.proj_recv,
            ),
        )

    def prepare():
        own = r.in_t[...].astype(WIDE).T.astype(LOW)
        r.own_in[...] = own
        r.rows[rank] = own
        r.smalls[seq, rank] = r.small[...]
        main = r.own_units.shape[0] // 16 * 16
        r.units[seq, 0:main] = r.own_units[0:main]
        if units > main:
            left = r.own_units[main:].astype(WIDE)
            zeros = jnp.zeros((units - r.own_units.shape[0], D), WIDE)
            r.units[seq, main:] = jnp.concatenate([left, zeros], 0).astype(LOW)
        if whole:
            pieces = head_pieces(ctx, width // HEAD_DIM)
            divide(r.qkv_rows, r.qkv_lanes, r.qkv_blocks, pieces, 3 * width)

    greet_all(prepare)

    line.start()
    if whole:
        heads.start()
    unit_rows.start()
    if whole:
        count = r.proj_rows.shape[0]
        r.proj_lanes[0:count, 0:D] = r.proj_rows[...].astype(WIDE)
        r.proj_lanes[0:count, D:] = jnp.zeros((count, full_lanes(D) - D), WIDE)
        pack(r.proj_packed, 0, r.proj_lanes, 0, count, 0, D)
        heads.swap.drain()
        proj.start()
    rows_in.pass_on(rank)
    own_cot = r.cot_t[...].astype(WIDE).T.astype(LOW)
    r.own_cot[...] = own_cot
    r.cots[rank] = own_cot
    line.wait()
    plane.start()
    if whole:
        heads.cross()
        divide(r.fc_rows, r.fc_lanes, r.fc_blocks, unit_pieces(ctx, dp), dp * units)

    def arrivals(gather):
        def arrive(index, carry):
            gather.arrive(1 + index // 4, index % 4)
            return carry

        return arrive

    rows_in.arrive(0, 2)
    lax.fori_loop(0, 4, arrivals(rows_in), 0)
    if whole:
        heads.plane.relay()
        columns.start()
        proj.cross()
    lax.fori_loop(4, 4 * (chips - 1), arrivals(rows_in), 0)
    if whole:
        proj.plane.relay()
    unit_rows.relay()
    rows_in.finish()
    docs = jnp.broadcast_to(r.docs[...], r.doc_start.shape)
    lane = lax.broadcasted_iota(jnp.int32, docs.shape, 1)
    doc_start = jnp.where(docs != pltpu.roll(docs, 1, 1), lane, 0)
    shift = 1
    while shift < docs.shape[1]:
        earlier = jnp.where(lane >= shift, pltpu.roll(doc_start, shift, 1), 0)
        doc_start = jnp.maximum(doc_start, earlier)
        shift *= 2
    r.doc_start[...] = doc_start
    plane.wait()
    r.vectors[...] = jnp.zeros_like(r.vectors)
    for owner, begin, row, lane, size in vector_pieces(ctx * dp, vec_count):
        r.vectors[row : row + 1, lane : lane + size] = r.smalls[
            owner // ctx, owner % ctx, 0:1, begin : begin + size
        ]
    r.bias_units[...] = jnp.zeros_like(r.bias_units)
    for owner in range(ctx):

        @pl.when(rank == owner)
        def _(owner=owner):
            for here, row, lane, size in unit_bias_pieces(owner, ctx, dp):
                r.bias_units[0:1, here : here + size] = r.vectors[row : row + 1, lane : lane + size]

    if whole:
        heads.wait()
        out(r.qkv_mat, r.qkv_mat_out, 0).start()
    mine = pl.ds(pl.multiple_of(rank * width, width), width)
    bias = jnp.concatenate(
        [
            r.vectors[BIAS_QUERY : BIAS_QUERY + 1, mine],
            jnp.zeros((1, width), WIDE),
            r.vectors[BIAS_VALUE : BIAS_VALUE + 1, mine],
        ],
        1,
    )

    def project(index, carry):
        both = pl.ds(2 * index, 2)
        normed, _ = normalize(r.rows[both].reshape(2 * tokens, D).astype(WIDE))
        attn_in = normed * r.vectors[GAIN_ONE : GAIN_ONE + 1, 0:D]
        attn_in = (attn_in + r.vectors[SHIFT_ONE : SHIFT_ONE + 1, 0:D]).astype(LOW)
        r.rows[both] = attn_in.reshape(2, tokens, D)
        rows = pl.ds(pl.multiple_of(2 * index * tokens, 2 * tokens), 2 * tokens)
        r.qkv[rows] = (dot(attn_in, r.qkv_mat[...].reshape(D, 3 * width)) + bias).astype(LOW)
        return carry

    lax.fori_loop(0, chips, project, 0)
    out(r.rows, r.attn_in_out, 1).start()
    out(r.qkv, r.qkv_out, 2).start()
    cots.pass_on(rank)
    if whole:
        columns.cross()
    attend_body(block, r.qkv, r.doc_start, r.mixed, r.stats, r.value_t)
    out(r.rows, r.attn_in_out, 1).wait()
    to_tokens.start()
    r.own_mixed[:, mine] = r.mixed[pl.ds(pl.multiple_of(rank * tokens, tokens), tokens)]
    cots.arrive(0, 2)
    lax.fori_loop(0, 4, arrivals(cots), 0)
    if whole:
        proj.wait()
        out(r.proj_mat, r.proj_mat_out, 3).start()
        columns.plane.relay()
    to_tokens.wait()
    resid = dot(r.own_mixed[:, 0:D], r.proj_mat[...].reshape(D, D))
    resid = resid + r.own_in[...].astype(WIDE) + r.vectors[BIAS_PROJ : BIAS_PROJ + 1, 0:D]
    r.resid[...] = resid
    normed, _ = normalize(resid)
    ffn_in = normed * r.vectors[GAIN_TWO : GAIN_TWO + 1, 0:D]
    r.rows[rank] = (ffn_in + r.vectors[SHIFT_TWO : SHIFT_TWO + 1, 0:D]).astype(LOW)
    feed.pass_on(rank)
    lax.fori_loop(4, 8, arrivals(cots), 0)
    unit_rows.wait()
    if whole:
        columns.wait()

    def keep(chip, slot, which=range(3)):
        both = pl.ds(2 * chip, 2)
        kept = ((r.act, r.act_out), (r.pre, r.pre_out), (r.part, r.part_out))
        return [
            pltpu.make_async_copy(
                kept[index][0].at[slot], kept[index][1].at[both], r.keep_sems.at[index, slot]
            )
            for index in which
        ]

    def pass_rows(chip):
        both = pl.ds(2 * chip, 2)
        return [
            pltpu.make_async_copy(ref.at[both], target.at[both], r.pass_sems.at[index, chip])
            for index, (ref, target) in enumerate(((r.rows, r.ffn_out), (r.cots, r.cots_out)))
        ]

    def work(chip, done):
        both = pl.ds(2 * chip, 2)
        slot = done % 2

        @pl.when(done >= 2)
        def _():
            for copy in keep(chip, slot):
                copy.wait()

        for copy in pass_rows(chip):
            copy.start()
        fc = r.fc_mat[...].reshape(D, dp * units)
        pre = dot(r.rows[both].reshape(2 * tokens, D), fc) + r.bias_units[0:1]
        bend = jnp.tanh(0.7978845608028654 * (pre + 0.044715 * pre * pre * pre))
        act = (0.5 * pre * (1.0 + bend)).astype(LOW)
        r.act[slot] = act.reshape(2, tokens, -1)
        slope = 0.5 * (1.0 + bend) + 0.5 * pre * (1.0 - bend * bend) * 0.7978845608028654 * (
            1.0 + 3 * 0.044715 * pre * pre
        )
        grad_pre = (slope * r.grad_act[...]).astype(LOW)
        r.pre[slot] = grad_pre.reshape(2, tokens, -1)
        r.sum_blocks[both] = dot(grad_pre, fc, 1, 1).astype(LOW).reshape(2, tokens, D)
        total.pair_copy(chip).start()
        for copy in keep(chip, slot, (0, 1)):
            copy.start()

    def give_out(chip, done):
        slot = done % 2
        act = r.act[slot].reshape(2 * tokens, dp * units)
        mat = r.units[...].reshape(dp * units, D)
        r.part[slot] = dot(act, mat).astype(LOW).reshape(2, tokens, D)
        keep(chip, slot, (2,))[0].start()

    def step(index, done):
        distance, side = index // 2, index % 2
        near = distance < chips
        origin_chip = rank // 2 + jnp.where(side == 0, -distance, distance)
        valid = near & (origin_chip >= 0) & (origin_chip < chips) & ((distance > 0) | (side == 0))

        @pl.when(near)
        def _():
            @pl.when(side == 0)
            def _():
                @pl.when(distance > 2)
                def _():
                    cots.arrive(distance, 0)
                    cots.arrive(distance, 1)

                feed.arrive(distance, 0)
                feed.arrive(distance, 1)

            @pl.when(distance > 2)
            def _():
                cots.arrive(distance, 2 + side)

            @pl.when(valid)
            def _():
                cot = r.cots[pl.ds(2 * origin_chip, 2)].reshape(2 * tokens, D)
                r.grad_act[...] = dot(cot, r.units[...].reshape(dp * units, D), 1, 1)

            feed.arrive(distance, 2 + side)

            @pl.when(valid)
            def _():
                work(origin_chip, done)

        after = done + valid.astype(jnp.int32)

        @pl.when(side == 1)
        def _():
            def way(index, carry):
                total.near_first(distance, index)
                return carry

            lax.fori_loop(0, 2, way, 0)

            def output(index, carry):
                chip = rank // 2 + jnp.where(index == 0, -distance, distance)
                here = near & (chip >= 0) & (chip < chips) & ((distance > 0) | (index == 0))
                later = (index == 0) & valid & (distance > 0)

                @pl.when(here)
                def _():
                    give_out(chip, after - 1 - later.astype(jnp.int32))

                return carry

            lax.fori_loop(0, 2, output, 0)

        return after

    lax.fori_loop(0, 2 * (2 * chips - 1), step, jnp.int32(0))
    total.finish(r.grad)

    feed.finish()
    cots.finish()
    line.drain()
    plane.drain()
    to_tokens.drain()
    for slot in range(2):
        for copy in keep(0, slot):
            copy.wait()

    def passed(chip, carry):
        for copy in pass_rows(chip):
            copy.wait()
        return carry

    lax.fori_loop(0, chips, passed, 0)
    out(r.qkv, r.qkv_out, 2).wait()
    if whole:
        out(r.qkv_mat, r.qkv_mat_out, 0).wait()
        out(r.proj_mat, r.proj_mat_out, 3).wait()
        columns.swap.drain()


def forward(small, in_t, cot_t, unit_rows, docs, mats, slots, whole, block):
    ctx, dp = lax.axis_size("ctx"), lax.axis_size("dp")
    tokens = in_t.shape[1]
    length = ctx * tokens
    width = slots * HEAD_DIM
    units = padded_units(unit_rows.shape[0])
    columns = dp * units
    chips = ctx // 2
    rows = D // dp
    count = rows // ctx
    high = -(-count // 8) * 8
    b = Build()
    b.take(VMEM, small=small, in_t=in_t, cot_t=cot_t, own_units=unit_rows, docs=docs)
    if whole:
        b.take(VMEM, qkv_rows=mats[0], fc_rows=mats[1], proj_rows=mats[2])
    else:
        b.take(VMEM, qkv_mat=mats[0], fc_mat=mats[1], proj_mat=mats[2])
    b.give(
        WIDE,
        VMEM,
        vectors=(ROWS, max(full_lanes(D), ctx * width)),
        stats=(8, length),
        resid=(tokens, D),
        grad=(tokens, D),
    )
    b.give(
        LOW, VMEM, own_mixed=(tokens, ctx * width), own_in=(tokens, D), own_cot=(tokens, D)
    )
    b.give(jnp.int32, VMEM, doc_start=(8, length))
    b.give(
        LOW,
        HBM,
        attn_in_out=(ctx, tokens, D),
        qkv_out=(length, 3 * width),
        cots_out=(ctx, tokens, D),
        ffn_out=(ctx, tokens, D),
        act_out=(ctx, tokens, columns),
        pre_out=(ctx, tokens, columns),
        part_out=(ctx, tokens, D),
    )
    if whole:
        b.give(LOW, HBM, qkv_mat_out=(dp, rows, 3 * width), proj_mat_out=(dp, rows, D))
    b.hold(
        LOW,
        rows=(ctx, tokens, D),
        cots=(ctx, tokens, D),
        units=(dp, units, D),
        qkv=(length, 3 * width),
        mixed=(length, width),
        value_t=(width, length),
        act=(2, 2, tokens, columns),
        pre=(2, 2, tokens, columns),
        part=(2, 2, tokens, D),
    )
    b.hold(
        WIDE,
        smalls=(dp, ctx, *small.shape),
        bias_units=(8, columns),
        grad_act=(2 * tokens, columns),
    )
    b.line_sum("sum", ctx, tokens)
    b.sems(
        out_sems=(4,),
        keep_sems=(3, 2),
        pass_sems=(2, chips),
        rows_send=(3, ctx),
        rows_recv=(ctx,),
        cots_send=(3, ctx),
        cots_recv=(ctx,),
        feed_send=(3, ctx),
        feed_recv=(ctx,),
    )
    b.both(line=ctx, plane=dp, units=max(dp, 4), mixed=ctx)
    if whole:
        for name, lanes in (("qkv", 3 * width), ("fc", columns)):
            packed = (ctx, packed_rows(count, lanes), 128)
            b.hold(WIDE, **{name + "_lanes": (high, full_lanes(lanes))})
            b.hold(WIDE, **{name + "_wide": (rows, full_lanes(lanes))})
            b.hold(LOW, **{name + "_blocks": packed, name + "_landed": packed})
            b.hold(LOW, **{name + "_mat": (dp, rows, lanes)})
            b.both(**{name: ctx, name + "_plane": max(dp, 4)})
        packed = packed_rows(count, D)
        b.hold(WIDE, proj_lanes=(high, full_lanes(D)), proj_wide=(rows, full_lanes(D)))
        b.hold(
            LOW,
            proj_packed=(1, packed, 128),
            proj_blocks=(2, dp, chips * packed, 128),
            proj_mat=(dp, rows, D),
        )
        b.both(proj_plane=max(dp, 4), proj_pair=dp, proj=chips)
    return b.call(functools.partial(forward_kernel, block, whole), 0, "forward")


def back_kernel(
    block,
    grad_ref,
    resid_ref,
    own_cot,
    vectors_ref,
    proj_ref,
    qkv_ref,
    start_ref,
    stat_ref,
    ffn_hbm,
    pre_hbm,
    act_hbm,
    cot_hbm,
    part_hbm,
    resid_out,
    low_out,
    vector_out,
    units_out,
    rows_out,
    share_out,
    output_ref,
    fc_out,
    ffn,
    pre,
    act,
    cot,
    load_sems,
    own_grad,
    head_grad,
    key_t,
    key_grad,
    value_grad,
    *refs,
):
    total = LineSum(*refs[:3], refs[3:7])
    loads = [
        pltpu.make_async_copy(src, dst, load_sems.at[index])
        for index, (src, dst) in enumerate(
            (
                (part_hbm, total.blocks),
                (ffn_hbm, ffn),
                (pre_hbm, pre),
                (act_hbm, act),
                (cot_hbm, cot),
            )
        )
    ]
    for load in loads:
        load.start()
    tokens = own_cot.shape[0]
    length, width = head_grad.shape
    units = share_out.shape[0]
    swap = Swap(
        "ctx",
        lambda peer: own_grad.at[:, pl.ds(pl.multiple_of(peer * width, width), width)],
        lambda origin: head_grad.at[pl.ds(pl.multiple_of(origin * tokens, tokens), tokens)],
        refs[7:9],
    )
    share = PlaneSum(refs[9], refs[10], refs[11:13])
    dp = share.swap.size
    greet_all()
    loads[0].wait()
    total.send_pairs()
    grad = grad_ref[...]
    normed, scale = normalize(resid_ref[...])
    grad_resid = own_cot[...].astype(WIDE) + norm_back(normed, scale, vectors_ref[GAIN_TWO : GAIN_TWO + 1, 0:D], grad)
    resid_out[...] = grad_resid
    low = grad_resid.astype(LOW)
    low_out[...] = low
    own_grad[:, 0:D] = dot(low, proj_ref[...], 1, 1).astype(LOW)
    own_grad[:, D:] = jnp.zeros((tokens, own_grad.shape[1] - D), LOW)
    swap.start()
    head_grad[pl.ds(pl.multiple_of(swap.rank * tokens, tokens), tokens)] = own_grad[
        :, pl.ds(pl.multiple_of(swap.rank * width, width), width)
    ]
    vector_out[0:1] = jnp.sum(grad_resid, 0, keepdims=True)
    vector_out[1:2] = jnp.sum(grad * normed, 0, keepdims=True)
    vector_out[2:3] = jnp.sum(grad, 0, keepdims=True)
    vector_out[3:4] = jnp.sum(own_cot[...].astype(WIDE), 0, keepdims=True)
    vector_out[4:8] = jnp.zeros((4, D), WIDE)
    loads[1].wait()
    loads[2].wait()
    grad_pre = pre[...].reshape(length, -1)
    units_out[...] = dot(jnp.ones((8, length), LOW), grad_pre)
    for index in range(dp):
        rows = slice(index * (D // dp), (index + 1) * (D // dp))
        fc_out[rows] = dot(ffn[:, :, rows].reshape(length, D // dp), grad_pre, 0, 0)
    total.far_steps(0, 1)
    loads[3].wait()
    loads[4].wait()
    for index in range(dp):
        rows = slice(index * units, (index + 1) * units)
        part = dot(act[:, :, rows].reshape(length, units), cot[...].reshape(length, D), 0, 0)
        share.blocks[index] = part.astype(LOW)
    share.start()
    swap.wait()
    chips = total.chips

    def first():
        total.far_steps(1, 2)

    def second():
        total.far_steps(2, 3)
        share.relay()

    attend_back_body(
        block,
        qkv_ref,
        start_ref,
        stat_ref,
        head_grad,
        rows_out,
        key_t,
        key_grad,
        value_grad,
        {1: first, 2: second},
    )
    total.far_steps(3, 2 * chips - 1)
    total.finish(output_ref)
    bias = vectors_ref[BIAS_OUT : BIAS_OUT + 1, 0:D]
    output_ref[...] = output_ref[...] + resid_ref[...] + bias
    share_out[...] = share.total()
    swap.drain()
    share.drain()


def back(
    grad, resid, own_cot, vectors, proj, qkv, doc_start, stats, ffn, pre, act, cot, part, block
):
    ctx, tokens, _ = cot.shape
    dp = lax.axis_size("dp")
    length = ctx * tokens
    width = qkv.shape[1] // 3
    columns = act.shape[2]
    units = columns // dp
    shapes = [
        jax.ShapeDtypeStruct((tokens, D), WIDE),
        jax.ShapeDtypeStruct((tokens, D), LOW),
        jax.ShapeDtypeStruct((8, D), WIDE),
        jax.ShapeDtypeStruct((8, columns), WIDE),
        jax.ShapeDtypeStruct((length, 3 * width), LOW),
        jax.ShapeDtypeStruct((units, D), WIDE),
        jax.ShapeDtypeStruct((tokens, D), WIDE),
        jax.ShapeDtypeStruct((D, columns), WIDE),
    ]
    scratch = [
        pltpu.VMEM(ffn.shape, LOW),
        pltpu.VMEM(pre.shape, LOW),
        pltpu.VMEM(act.shape, LOW),
        pltpu.VMEM(cot.shape, LOW),
        pltpu.SemaphoreType.DMA((5,)),
        pltpu.VMEM((tokens, ctx * width), LOW),
        pltpu.VMEM((length, width), LOW),
        pltpu.VMEM((width, length), LOW),
        pltpu.VMEM((length, width), WIDE),
        pltpu.VMEM((length, width), WIDE),
        *LineSum.scratch(ctx, tokens, D, 4),
        *Swap.semaphores(ctx),
        pltpu.VMEM((dp, units, D), LOW),
        pltpu.VMEM((dp, units, D), LOW),
        *PlaneSum.semaphores(dp),
    ]
    return pl.pallas_call(
        functools.partial(back_kernel, block),
        out_shape=shapes,
        in_specs=[VMEM] * 8 + [HBM] * 5,
        out_specs=[VMEM] * 8,
        scratch_shapes=scratch,
        compiler_params=params(3),
        name="back",
    )(grad, resid, own_cot, vectors, proj, qkv, doc_start, stats, ffn, pre, act, cot, part)


class ProjectionSum:
    def __init__(self, out, mixed, low, plane, wide, blocks, came, pair_sems, sems):
        self.out, self.mixed, self.low, self.plane = out, mixed, low, plane
        self.wide, self.blocks, self.came = wide, blocks, came
        self.send_sems, self.recv_sems = pair_sems
        self.rank = lax.axis_index("ctx")
        self.core = self.rank % 2
        self.swap = ChipSwap(blocks.at.__getitem__, came.at.__getitem__, sems)

    def pair_copies(self):
        return [
            send(
                ref.at[self.core],
                ref.at[self.core],
                self.send_sems.at[index],
                self.recv_sems.at[index],
                ctx=self.rank + 1 - 2 * self.core,
            )
            for index, ref in enumerate((self.mixed, self.low))
        ]

    def start(self, mixed, low):
        self.mixed[self.core] = mixed
        self.low[self.core] = low
        for copy in self.pair_copies():
            copy.start()

    def multiply(self):
        for copy in self.pair_copies():
            copy.wait_recv()
        dp, rows = self.plane.parts.shape[:2]
        chips = self.swap.size
        tokens = 2 * self.low.shape[1]
        count = self.out.shape[0]
        mixed = self.mixed[...].reshape(tokens, -1)[:, 0:D]
        low = self.low[...].reshape(tokens, D)
        feature = lax.broadcasted_iota(jnp.int32, (D, rows), 0)
        column = lax.broadcasted_iota(jnp.int32, (1, rows), 1)
        for index in range(dp):
            owner = index * 2 * chips + column // count * 2 + self.core
            wanted = jnp.where(column < chips * count, owner * count + column % count, -1)
            chosen = jnp.where(feature == wanted, 1.0, 0.0).astype(LOW)
            picked = dot(mixed, chosen).astype(LOW)
            self.plane.put(index, dot(picked, low, 0, 0))

    def cross(self):
        count = self.out.shape[0]
        rows = self.plane.parts.shape[1]
        lanes = full_lanes(D)
        self.wide[0:rows, 0:D] = self.plane.total()
        self.wide[0:rows, D:lanes] = jnp.zeros((rows, lanes - D), WIDE)
        for chip in range(self.swap.size):
            pack(self.blocks, chip, self.wide, chip * count, count, 0, D)
        self.swap.start()

    def wait(self):
        self.swap.wait()
        total = self.blocks[self.swap.rank].astype(WIDE)
        for off in range(1, self.swap.size):
            total = total + self.came[lax.rem(self.swap.rank + off, self.swap.size)].astype(WIDE)
        count = self.out.shape[0]
        unpack(total, self.wide, 0, count, D)
        self.out[...] = self.wide[0:count, 0:D]
        for copy in self.pair_copies():
            copy.wait_send()
        self.swap.drain()


def partial_sums(total, rows_ref, mat):
    chips, tokens = total.chips, total.blocks.shape[1]

    def one(index, carry):
        off = jnp.where(index % 2 == 0, -(index // 2), index // 2 + 1)
        chip = lax.rem(chips - 1 + off, chips)
        rows = pl.ds(pl.multiple_of(2 * chip * tokens, 2 * tokens), 2 * tokens)
        part = dot(rows_ref[rows], mat[...].reshape(D, -1), 1, 1).astype(LOW)
        total.blocks[pl.ds(2 * chip, 2)] = part.reshape(2, tokens, D)
        total.pair_copy(chip).start()
        return carry

    lax.fori_loop(0, chips, one, 0)


def last_kernel(
    rows_ref,
    mat_ref,
    in_ref,
    own_ref,
    resid_ref,
    vectors_ref,
    grad_out,
    vector_out,
    heads_out,
    mat_out,
    grad,
    *refs,
):
    total = LineSum(*refs[:3], refs[3:7])
    chips = total.chips
    dp = lax.axis_size("dp")
    greet_line(chips)
    partial_sums(total, rows_ref, mat_ref)
    total.far_steps(0, 1)
    for index in range(dp):
        rows = slice(index * (D // dp), (index + 1) * (D // dp))
        mat_out[rows] = dot(in_ref[:, rows], rows_ref[...], 0, 0)
    total.far_steps(1, 2 * chips - 1)
    heads_out[...] = dot(jnp.ones((8, rows_ref.shape[0]), LOW), rows_ref[...])
    total.finish(grad)
    normed, scale = normalize(own_ref[...].astype(WIDE))
    incoming = grad[...]
    gain = vectors_ref[GAIN_ONE : GAIN_ONE + 1, 0:D]
    grad_out[...] = resid_ref[...] + norm_back(normed, scale, gain, incoming)
    vector_out[0:1] = jnp.sum(incoming * normed, 0, keepdims=True)
    vector_out[1:2] = jnp.sum(incoming, 0, keepdims=True)
    vector_out[2:8] = jnp.zeros((6, D), WIDE)


def last(rows, mat, attn_in, own_in, resid, vectors):
    ctx = lax.axis_size("ctx")
    tokens = own_in.shape[0]
    columns = rows.shape[1]
    return pl.pallas_call(
        last_kernel,
        out_shape=[
            jax.ShapeDtypeStruct((tokens, D), WIDE),
            jax.ShapeDtypeStruct((8, D), WIDE),
            jax.ShapeDtypeStruct((8, columns), WIDE),
            jax.ShapeDtypeStruct((D, columns), WIDE),
        ],
        in_specs=[VMEM] * 6,
        out_specs=[VMEM] * 4,
        scratch_shapes=[pltpu.VMEM((tokens, D), WIDE), *LineSum.scratch(ctx, tokens, D, 4)],
        compiler_params=params(4),
        name="last",
    )(rows, mat, attn_in, own_in, resid, vectors)


def vector_kernel(parts_ref, out_ref, plane_landed, line_parts, line_landed, *sems):
    seq = lax.axis_index("dp")
    swap = Swap("dp", parts_ref.at.__getitem__, plane_landed.at.__getitem__, sems[:2])
    line = Swap("ctx", line_parts.at.__getitem__, line_landed.at.__getitem__, sems[2:])
    greet_all()
    swap.start()
    swap.wait()
    total = parts_ref[seq]
    for off in range(1, swap.size):
        total = total + plane_landed[lax.rem(seq + off, swap.size)]
    line_parts[...] = total
    line.start()
    line.wait()
    total = line_parts[line.rank]
    for off in range(1, line.size):
        total = total + line_landed[lax.rem(line.rank + off, line.size)]
    out_ref[...] = total
    swap.drain()
    line.drain()


def sum_vector(parts):
    dp, ctx = parts.shape[:2]
    return pl.pallas_call(
        vector_kernel,
        out_shape=jax.ShapeDtypeStruct(parts.shape[2:], WIDE),
        in_specs=[VMEM],
        out_specs=VMEM,
        scratch_shapes=[
            pltpu.VMEM(parts.shape, WIDE),
            pltpu.VMEM(parts.shape[1:], WIDE),
            pltpu.VMEM(parts.shape[1:], WIDE),
            *PlaneSum.semaphores(dp),
            *Swap.semaphores(ctx),
        ],
        compiler_params=params(5),
        name="sum_vector",
    )(parts)


GRAD_ONE, SUM_ONE, SUM_QUERY, SUM_VALUE, SUM_RESID, GRAD_FFN, SUM_FFN = range(7)
SUM_OUT = 11


def backward_kernel(block, names, *refs):
    r = Names(names, refs)
    seq, rank = lax.axis_index("dp"), lax.axis_index("ctx")
    ctx, tokens, _ = r.big.shape
    length, width = r.head_grad.shape
    dp, owners_rows = r.fc_parts.shape[:2]
    units = r.out_parts.shape[1]
    columns = dp * units
    vec_count = 12 * D // (ctx * dp)

    def load(source, target, index):
        return pltpu.make_async_copy(source, target, r.load_sems.at[index])

    summed = LineSum(
        r.out_blocks,
        r.out_pair,
        r.out_passing,
        (r.out_pair_send, r.out_pair_recv, r.out_line_send, r.out_line_recv),
    )
    total = LineSum(
        r.in_blocks,
        r.in_pair,
        r.in_passing,
        (r.in_pair_send, r.in_pair_recv, r.in_line_send, r.in_line_recv),
    )
    chips = total.chips
    to_heads = Swap(
        "ctx",
        lambda peer: r.own_grad.at[:, pl.ds(pl.multiple_of(peer * width, width), width)],
        lambda origin: r.head_grad.at[pl.ds(pl.multiple_of(origin * tokens, tokens), tokens)],
        (r.heads_send, r.heads_recv),
    )
    some = r.stage_fc.at[:, :, pl.ds(0, 3 * width)]
    fc = Collect(
        unit_pieces(ctx, dp),
        StreamSum(
            r.fc_parts, r.fc_landed, r.stage_fc, r.stage_fc_sems, (r.fc_plane_send, r.fc_plane_recv)
        ),
        r.wide,
        r.fc_blocks,
        r.fc_came,
        r.fc_out,
        (r.fc_send, r.fc_recv),
    )
    qkv = Collect(
        head_pieces(ctx, width // HEAD_DIM),
        StreamSum(
            r.qkv_parts, r.qkv_landed, some, r.stage_fc_sems, (r.qkv_plane_send, r.qkv_plane_recv)
        ),
        r.wide,
        r.qkv_blocks,
        r.qkv_came,
        r.qkv_grad,
        (r.qkv_send, r.qkv_recv),
    )
    share = StreamSum(
        r.out_parts,
        r.out_landed,
        r.stage_out,
        r.stage_out_sems,
        (r.out_plane_send, r.out_plane_recv),
    )
    proj = ProjectionSum(
        r.proj_grad,
        r.mixed_pair,
        r.low_pair,
        StreamSum(
            r.proj_parts,
            r.proj_landed,
            r.stage_out,
            r.stage_out_sems,
            (r.proj_plane_send, r.proj_plane_recv),
        ),
        r.wide,
        r.proj_blocks,
        r.proj_came,
        (r.proj_pair_send, r.proj_pair_recv),
        (r.proj_send, r.proj_recv),
    )
    vec_plane = Swap(
        "dp",
        r.vec_parts.at.__getitem__,
        r.vec_landed.at.__getitem__,
        (r.vec_plane_send, r.vec_plane_recv),
    )
    vec_line = Swap(
        "ctx", r.vec_rows.at.__getitem__, r.vec_came.at.__getitem__, (r.vec_send, r.vec_recv)
    )
    heads_mat = r.mat.at[:, :, pl.ds(0, 3 * width)]
    loads = [
        load(r.proj_mat, r.mat, 0),
        load(r.part, r.out_blocks, 1),
        load(r.ffn, r.big, 2),
        load(r.pre_act, r.feed, 3),
        load(r.qkv_mat, heads_mat, 0),
        load(r.attn_in, r.big, 2),
        load(r.act, r.feed, 3),
        load(r.cots, r.big, 2),
    ]
    for index in (2, 3, 0, 1):
        loads[index].start()
    greet_all()

    vec = r.vec
    vec[...] = jnp.zeros_like(vec)

    loads[2].wait()
    loads[3].wait()
    grad_pre = r.feed[...].reshape(length, columns)
    sums = dot(jnp.ones((8, length), LOW), grad_pre)[0:1]
    for owner in range(ctx):

        @pl.when(rank == owner)
        def _(owner=owner):
            for place, row, lane, size in unit_bias_pieces(owner, ctx, dp):
                vec[row : row + 1, lane : lane + size] = sums[:, place : place + size]

    def by_parts(plane, left, right, count):
        for index in range(dp):
            rows = slice(index * count, (index + 1) * count)
            plane.put(index, dot(left[:, :, rows].reshape(length, count), right, 0, 0))
        plane.start()

    by_parts(fc.plane, r.big, grad_pre, owners_rows)
    loads[5].start()
    loads[6].start()

    grad = r.grad[...]
    normed, scale = normalize(r.resid[...])
    gain = r.vectors[GAIN_TWO : GAIN_TWO + 1, 0:D]
    own_cot = r.own_cot[...].astype(WIDE)
    grad_resid = own_cot + norm_back(normed, scale, gain, grad)
    r.grad_resid[...] = grad_resid
    low = grad_resid.astype(LOW)
    loads[0].wait()
    r.own_grad[:, 0:D] = dot(low, r.mat[...].reshape(D, D), 1, 1).astype(LOW)
    r.own_grad[:, D:] = jnp.zeros((tokens, r.own_grad.shape[1] - D), LOW)
    to_heads.start()
    loads[4].start()
    mine = pl.ds(pl.multiple_of(rank * width, width), width)
    here = pl.ds(pl.multiple_of(rank * tokens, tokens), tokens)
    r.head_grad[here] = r.own_grad[:, mine]
    proj.start(r.own_mixed[...], low)
    loads[1].wait()
    summed.send_pairs()
    def note(row, value):
        vec[row : row + 1, 0:D] = jnp.sum(value, 0, keepdims=True)

    note(SUM_RESID, grad_resid)
    note(GRAD_FFN, grad * normed)
    note(SUM_FFN, grad)
    note(SUM_OUT, own_cot)

    summed.far_steps(0, 1)
    proj.multiply()

    to_heads.wait()

    def first():
        summed.far_steps(1, 2)

    def second():
        summed.far_steps(2, 3)
        fc.plane.relay()
        proj.plane.start()

    attend_back_body(
        block,
        r.qkv,
        r.doc_start,
        r.stats,
        r.head_grad,
        r.rows,
        r.key_t,
        r.key_grad,
        r.value_grad,
        {1: first, 2: second},
    )
    loads[4].wait()
    partial_sums(total, r.rows, heads_mat)
    total.far_steps(0, 1)
    summed.far_steps(3, 4)
    fc.cross()
    loads[5].wait()
    by_parts(qkv.plane, r.big, r.rows[...], owners_rows)
    loads[7].start()
    total.far_steps(1, 2)
    summed.far_steps(4, 5)
    proj.plane.relay()
    total.far_steps(2, 3)
    summed.far_steps(5, 2 * chips - 1)
    proj.cross()
    qkv.plane.relay()
    loads[6].wait()
    loads[7].wait()
    by_parts(share, r.feed, r.big[...].reshape(length, D), units)
    total.far_steps(3, 2 * chips - 1)
    sums = dot(jnp.ones((8, length), LOW), r.rows[...])
    vec[SUM_QUERY : SUM_QUERY + 1, mine] = sums[0:1, 0:width]
    vec[SUM_VALUE : SUM_VALUE + 1, mine] = sums[0:1, 2 * width :]
    total.finish(r.came)

    incoming = r.came[...]
    normed, scale = normalize(r.own_in[...].astype(WIDE))
    gain = r.vectors[GAIN_ONE : GAIN_ONE + 1, 0:D]
    grad_in = r.grad_resid[...] + norm_back(normed, scale, gain, incoming)
    r.grad_in_t[...] = grad_in.T
    note(GRAD_ONE, incoming * normed)
    note(SUM_ONE, incoming)
    for owner, begin, row, lane, size in vector_pieces(ctx * dp, vec_count):
        r.vec_parts[owner // ctx, owner % ctx, 0:1, begin : begin + size] = vec[
            row : row + 1, lane : lane + size
        ]
    vec_plane.start()
    qkv.cross()
    vec_plane.wait()
    rows = r.vec_parts[seq]
    for off in range(1, dp):
        rows = rows + r.vec_landed[lax.rem(seq + off, dp)]
    r.vec_rows[...] = rows
    vec_line.start()
    summed.finish(r.came)
    bias = r.vectors[BIAS_OUT : BIAS_OUT + 1, 0:D]
    r.output_t[...] = (r.came[...] + r.resid[...] + bias).T
    fc.wait()
    share.relay()
    proj.wait()
    vec_line.wait()
    row = r.vec_rows[rank]
    for off in range(1, ctx):
        row = row + r.vec_came[lax.rem(rank + off, ctx)]
    r.vec_out[...] = row
    qkv.wait()
    r.out_grad[...] = share.total()[0 : r.out_grad.shape[0]]
    to_heads.drain()
    vec_plane.drain()
    vec_line.drain()


def backward(made, block):
    ctx, dp = lax.axis_size("ctx"), lax.axis_size("dp")
    tokens = made.own_in.shape[0]
    length = ctx * tokens
    width = made.qkv_out.shape[1] // 3
    columns = made.act_out.shape[2]
    units = columns // dp
    chips = ctx // 2
    rows = D // dp
    count = rows // ctx
    lanes = full_lanes(12 * D // (ctx * dp))
    b = Build()
    b.take(
        VMEM,
        grad=made.grad,
        resid=made.resid,
        own_cot=made.own_cot,
        own_in=made.own_in,
        vectors=made.vectors,
        own_mixed=made.own_mixed,
        qkv=made.qkv_out,
        doc_start=made.doc_start,
        stats=made.stats,
    )
    b.take(
        HBM,
        proj_mat=made.proj_mat_out,
        qkv_mat=made.qkv_mat_out,
        part=made.part_out,
        ffn=made.ffn_out,
        pre_act=made.pre_out,
        attn_in=made.attn_in_out,
        act=made.act_out,
        cots=made.cots_out,
    )
    b.give(
        WIDE,
        VMEM,
        output_t=(D, tokens),
        grad_in_t=(D, tokens),
        qkv_grad=(count, 3 * D),
        proj_grad=(count, D),
        fc_out=(count, FF),
        out_grad=(FF // (ctx * dp), D),
        vec_out=(1, lanes),
    )
    for name, shape in (
        ("fc", (rows, columns)),
        ("qkv", (rows, 3 * width)),
        ("out", (units, D)),
        ("proj", (units, D)),
    ):
        b.give(LOW, HBM, **{name + "_parts": (dp, *shape), name + "_landed": (3, *shape)})
        b.both(**{name + "_plane": 6})
    b.hold(
        LOW,
        mat=(dp, rows, D),
        big=(ctx, tokens, D),
        feed=(ctx, tokens, columns),
        stage_fc=(3, rows, columns),
        stage_out=(3, units, D),
        proj_blocks=(chips, packed_rows(count, D), 128),
        proj_came=(chips, packed_rows(count, D), 128),
        mixed_pair=(2, tokens, ctx * width),
        low_pair=(2, tokens, D),
        own_grad=(tokens, ctx * width),
        head_grad=(length, width),
        rows=(length, 3 * width),
        key_t=(width, length),
    )
    for name, wide in (("fc", columns), ("qkv", 3 * width)):
        packed = (ctx, packed_rows(count, wide), 128)
        b.hold(LOW, **{name + "_blocks": packed, name + "_came": packed})
    for name in ("out", "in"):
        b.line_sum(name, ctx, tokens)
    b.hold(
        WIDE,
        wide=(rows, full_lanes(D)),
        key_grad=(length, width),
        value_grad=(length, width),
        grad_resid=(tokens, D),
        came=(tokens, D),
        vec=(ROWS, max(full_lanes(D), ctx * width)),
        vec_parts=(dp, ctx, 1, lanes),
        vec_landed=(dp, ctx, 1, lanes),
        vec_rows=(ctx, 1, lanes),
        vec_came=(ctx, 1, lanes),
    )
    b.both(fc=ctx, qkv=ctx, proj=chips, proj_pair=2, heads=ctx, vec_plane=dp, vec=ctx)
    b.sems(load_sems=(4,), stage_fc_sems=(3,), stage_out_sems=(3,))
    assert units == -(-(chips * count) // 16) * 16
    return b.call(functools.partial(backward_kernel, block), 6, "backward")


def gather_rows(block):
    return lax.all_gather(block, ("dp", "ctx"), axis=0, tiled=True)


def by_rank_heads(rows, ctx, slots):
    count = rows.shape[0]
    split = rows.reshape(count, 3, D)
    split = jnp.pad(split, ((0, 0), (0, 0), (0, (ctx * slots - HEADS) * HEAD_DIM)))
    split = split.reshape(count, 3, ctx, slots * HEAD_DIM)
    return split.transpose(2, 0, 1, 3).reshape(ctx, count, 3 * slots * HEAD_DIM)


def from_rank_heads(blocks, slots):
    ctx, count = blocks.shape[:2]
    split = blocks.reshape(ctx, count, 3, slots * HEAD_DIM).transpose(1, 2, 0, 3)
    return split.reshape(count, 3, ctx * slots * HEAD_DIM)[:, :, :D].reshape(count, 3 * D)


def padded_units(units):
    return -(-units // 16) * 16


def by_rank_units(rows, ctx, dp):
    count = rows.shape[0]
    units = FF // (dp * ctx)
    split = rows.reshape(count, dp, ctx, units).transpose(2, 0, 1, 3)
    split = jnp.pad(split, ((0, 0), (0, 0), (0, 0), (0, padded_units(units) - units)))
    return split.reshape(ctx, count, dp * padded_units(units))


def from_rank_units(blocks, dp):
    ctx, count = blocks.shape[:2]
    units = FF // (dp * ctx)
    split = blocks.reshape(ctx, count, dp, padded_units(units))[..., :units]
    return split.transpose(1, 2, 0, 3).reshape(count, FF)


def shards(
    hidden_in, qkv_weight, proj_weight, fc_weight, out_weight, small_params, segments, cotangent
):
    tokens = hidden_in.shape[1]
    length = segments.shape[1]
    ctx = lax.axis_size("ctx")
    dp = lax.axis_size("dp")
    owners = dp * ctx
    rank = lax.axis_index("ctx")
    slots = -(-HEADS // ctx)
    width = slots * HEAD_DIM
    units = FF // owners
    rows = D // owners
    whole = D % owners == 0 and dp == 4
    block = min(256, length)
    both = ("dp", "ctx")

    vec_count = small_params.shape[0]
    small = jnp.pad(small_params.astype(WIDE), (0, full_lanes(vec_count) - vec_count))[None]
    unit_rows = out_weight.reshape(units, D)
    if whole:
        mats = (
            qkv_weight.reshape(rows, 3 * D),
            fc_weight.reshape(rows, FF),
            proj_weight.reshape(rows, D),
        )
    else:
        mat_qkv = by_rank_heads(gather_rows(qkv_weight).reshape(D, 3 * D), ctx, slots)
        mat_qkv = lax.dynamic_index_in_dim(mat_qkv, rank, 0, keepdims=False)
        mat_fc = by_rank_units(gather_rows(fc_weight).reshape(D, FF), ctx, dp)
        mat_fc = lax.dynamic_index_in_dim(mat_fc, rank, 0, keepdims=False)
        mat_proj = gather_rows(proj_weight).reshape(D, D)
        mats = (mat_qkv, mat_fc, mat_proj)
    made = forward(
        small, hidden_in[0].T, cotangent[0].T, unit_rows, segments, mats, slots, whole, block
    )
    if whole:
        done = backward(made, block)
        return (
            done.output_t.T[None],
            done.grad_in_t.T[None],
            done.qkv_grad.reshape(-1),
            done.proj_grad.reshape(-1),
            done.fc_out.reshape(-1),
            done.out_grad.reshape(-1),
            done.vec_out[0, :vec_count],
        )
    vectors = made.vectors

    grad_resid, resid_low, sums_two, sums_units, grad_rows, grad_out, output, grad_fc = back(
        made.grad,
        made.resid,
        cotangent[0],
        vectors,
        mat_proj,
        made.qkv_out,
        made.doc_start,
        made.stats,
        made.ffn_out,
        made.pre_out,
        made.act_out,
        made.cots_out,
        made.part_out,
        block,
    )
    grad_input, sums_one, sums_heads, grad_qkv = last(
        grad_rows,
        mat_qkv,
        made.attn_in_out.reshape(length, D),
        hidden_in[0],
        grad_resid,
        vectors,
    )
    here = (jnp.arange(ctx) == rank)[:, None, None]
    full_fc = from_rank_units(jnp.where(here, grad_fc[None], 0.0), dp).reshape(-1)
    full_qkv = from_rank_heads(jnp.where(here, grad_qkv[None], 0.0), slots).reshape(-1)
    grad_proj = dot(made.own_mixed[:, :D], resid_low, 0, 0).reshape(-1)
    share_fc, share_qkv, share_proj = [
        lax.psum_scatter(full, both, scatter_dimension=0, tiled=True)
        for full in (full_fc, full_qkv, grad_proj)
    ]

    def spread_heads(part):
        padded = jnp.zeros((ctx * width,), WIDE)
        return lax.dynamic_update_slice_in_dim(padded, part, rank * width, 0)[:D]

    sums_units = sums_units[0].reshape(dp, 1, -1)[:, :, :units]
    sums_units = lax.dynamic_update_slice_in_dim(
        jnp.zeros((dp, ctx, units), WIDE), sums_units, rank, 1
    ).reshape(FF)
    vector = jnp.concatenate(
        [
            sums_one[0],
            sums_one[1],
            spread_heads(sums_heads[0, :width]),
            spread_heads(sums_heads[0, 2 * width :]),
            sums_two[0],
            sums_two[1],
            sums_two[2],
            sums_units,
            sums_two[3],
        ]
    ).reshape(owners, vec_count)
    vec_pad = -(-vec_count // 1024) * 1024
    vector = jnp.pad(vector, ((0, 0), (0, vec_pad - vec_count))).reshape(dp, ctx, -1, 128)
    share_vector = sum_vector(vector)
    return (
        output[None],
        grad_input[None],
        share_qkv.astype(WIDE).reshape(-1),
        share_proj.astype(WIDE).reshape(-1),
        share_fc.astype(WIDE).reshape(-1),
        grad_out[:units].reshape(-1),
        share_vector.reshape(-1)[:vec_count],
    )


def solution(mesh):
    flat = P(("dp", "ctx"))
    rows = P("dp", "ctx", None)
    return jax.shard_map(
        shards,
        mesh=mesh,
        in_specs=(rows, flat, flat, flat, flat, flat, P("dp", None), rows),
        out_specs=(rows, rows, flat, flat, flat, flat, flat),
        check_vma=False,
    )
```

```python
import functools

import jax
import jax.numpy as jnp
from jax import lax
from jax.experimental import pallas as pl
from jax.experimental.pallas import tpu as pltpu
from jax.sharding import PartitionSpec as P

D = 1600
HEADS = 25
HEAD_DIM = 64
FF = 6400
EPSILON = 1e-05
LOW = jnp.bfloat16
WIDE = jnp.float32
MIB = 1024 * 1024


def dot(left, right, left_dim=1, right_dim=0):
    return lax.dot_general(
        left, right, (((left_dim,), (right_dim,)), ((), ())), preferred_element_type=WIDE
    )


def normalize(rows):
    centre = rows - jnp.mean(rows, -1, keepdims=True)
    spread = jnp.mean(centre * centre, -1, keepdims=True)
    scale = lax.rsqrt(spread + EPSILON)
    return centre * scale, scale


def norm_back(normed, scale, gain, incoming):
    scaled = gain * incoming
    return scale * (
        scaled
        - jnp.mean(scaled, -1, keepdims=True)
        - normed * jnp.mean(scaled * normed, -1, keepdims=True)
    )


def head_lanes(head, width):
    lane = lax.broadcasted_iota(jnp.int32, (1, width), 1)
    return (lane // HEAD_DIM) == head


def allowed_scores(scores, doc_start, first_query, keys, block):
    key_pos = lax.broadcasted_iota(jnp.int32, (keys, block), 0)
    query_pos = first_query + lax.broadcasted_iota(jnp.int32, (keys, block), 1)
    seen = (key_pos >= doc_start) & (key_pos <= query_pos)
    return jnp.where(seen, scores, -1e30)


def attend_body(block, qkv_ref, start_ref, mixed_ref, stat_ref, value_t):
    length = qkv_ref.shape[0]
    width = mixed_ref.shape[1]
    slots = width // HEAD_DIM
    value_t[...] = qkv_ref[:, 2 * width : 3 * width].astype(WIDE).T.astype(LOW)
    stat_ref[...] = jnp.zeros_like(stat_ref)
    for index in range(length // block):
        keys = (index + 1) * block
        rows = pl.ds(index * block, block)
        key_rows = qkv_ref[0:keys, width : 2 * width]
        doc_start = start_ref[0:1, rows]
        outs = []
        for head in range(slots):
            query = jnp.where(
                head_lanes(head, width), qkv_ref[rows, 0:width] * LOW(HEAD_DIM**-0.5), LOW(0)
            )
            scores = dot(key_rows, query, 1, 1)
            scores = allowed_scores(scores, doc_start, index * block, keys, block)
            top = jnp.max(scores, 0, keepdims=True)
            expo = jnp.exp(scores - top)
            total = jnp.sum(expo, 0, keepdims=True)
            head_rows = slice(head * HEAD_DIM, (head + 1) * HEAD_DIM)
            out = dot(value_t[head_rows, 0:keys], expo.astype(LOW))
            outs.append(out / total)
            stat_ref[head : head + 1, rows] = top + jnp.log(total)
        mixed_ref[rows, :] = jnp.concatenate(outs, 0).T.astype(LOW)


def attend_back_body(
    block, qkv_ref, start_ref, stat_ref, grad_ref, out_ref, key_t, key_grad, value_grad, after
):
    length = qkv_ref.shape[0]
    width = grad_ref.shape[1]
    slots = width // HEAD_DIM
    scale = HEAD_DIM**-0.5
    key_t[...] = qkv_ref[:, width : 2 * width].astype(WIDE).T.astype(LOW)
    key_grad[...] = jnp.zeros_like(key_grad)
    value_grad[...] = jnp.zeros_like(value_grad)
    for index in range(length // block):
        keys = (index + 1) * block
        rows = pl.ds(index * block, block)
        key_rows = qkv_ref[0:keys, width : 2 * width]
        value_rows = qkv_ref[0:keys, 2 * width : 3 * width]
        doc_start = start_ref[0:1, rows]
        outs = []
        for head in range(slots):
            lanes = head_lanes(head, width)
            head_rows = slice(head * HEAD_DIM, (head + 1) * HEAD_DIM)
            query = jnp.where(lanes, qkv_ref[rows, 0:width] * LOW(scale), LOW(0))
            grad = jnp.where(lanes, grad_ref[rows, :], LOW(0))
            scores = dot(key_rows, query, 1, 1)
            scores = allowed_scores(scores, doc_start, index * block, keys, block)
            probs = jnp.exp(scores - stat_ref[head : head + 1, rows])
            grad_probs = dot(value_rows, grad, 1, 1)
            delta = jnp.sum(probs * grad_probs, 0, keepdims=True)
            grad_scores = (probs * (grad_probs - delta)).astype(LOW)
            value_grad[0:keys, :] += dot(probs.astype(LOW), grad)
            key_grad[0:keys, :] += dot(grad_scores, query)
            outs.append(dot(key_t[head_rows, 0:keys], grad_scores))
        out_ref[rows, 0:width] = (jnp.concatenate(outs, 0).T * scale).astype(LOW)
        if index in after:
            after[index]()
    out_ref[:, width : 2 * width] = key_grad[...].astype(LOW)
    out_ref[:, 2 * width : 3 * width] = value_grad[...].astype(LOW)


MESH = pl.DeviceIdType.MESH


def send(src, dst, send_sem, recv_sem, **target):
    return pltpu.make_async_remote_copy(
        src_ref=src,
        dst_ref=dst,
        send_sem=send_sem,
        recv_sem=recv_sem,
        device_id=target,
        device_id_type=MESH,
    )


def greet_line(chips):
    rank = lax.axis_index("ctx")
    chip, core = rank // 2, rank % 2
    barrier = pltpu.get_barrier_semaphore()
    pl.semaphore_signal(barrier, 1, device_id={"ctx": rank + 1 - 2 * core}, device_id_type=MESH)

    @pl.when(chip > 0)
    def _():
        pl.semaphore_signal(barrier, 1, device_id={"ctx": rank - 2}, device_id_type=MESH)

    @pl.when(chip < chips - 1)
    def _():
        pl.semaphore_signal(barrier, 1, device_id={"ctx": rank + 2}, device_id_type=MESH)

    sides = (chip > 0).astype(jnp.int32) + (chip < chips - 1).astype(jnp.int32)
    pl.semaphore_wait(barrier, 1 + sides)


def greet_all(between=lambda: None):
    barrier = pltpu.get_barrier_semaphore()
    count = 0
    for axis in ("ctx", "dp"):
        size = lax.axis_size(axis)
        here = lax.axis_index(axis)

        def one(off, carry, axis=axis, size=size, here=here):
            peer = lax.rem(here + off, size)
            pl.semaphore_signal(barrier, 1, device_id={axis: peer}, device_id_type=MESH)
            return carry

        lax.fori_loop(1, size, one, 0)
        count += size - 1
    between()
    pl.semaphore_wait(barrier, count)


class Swap:
    def __init__(self, axis, source, target, sems):
        self.axis, self.source, self.target = axis, source, target
        self.send_sems, self.recv_sems = sems
        self.rank = lax.axis_index(axis)
        self.size = lax.axis_size(axis)

    def copy(self, peer, origin, target):
        return send(
            self.source(peer),
            self.target(origin),
            self.send_sems.at[peer],
            self.recv_sems.at[origin],
            **{self.axis: target},
        )

    def every(self, act):
        def one(off, carry):
            act(lax.rem(self.rank + off, self.size))
            return carry

        lax.fori_loop(1, self.size, one, 0)

    def start(self):
        self.every(lambda peer: self.copy(peer, self.rank, peer).start())

    def wait(self):
        self.every(lambda peer: self.copy(peer, peer, self.rank).wait_recv())

    def drain(self):
        self.every(lambda peer: self.copy(peer, self.rank, peer).wait_send())

    @staticmethod
    def semaphores(size):
        return [pltpu.SemaphoreType.DMA((size,)), pltpu.SemaphoreType.DMA((size,))]


class ChipSwap(Swap):
    def __init__(self, source, target, sems):
        super().__init__("ctx", source, target, sems)
        self.core = self.rank % 2
        self.rank, self.size = self.rank // 2, self.size // 2

    def copy(self, peer, origin, target):
        return send(
            self.source(peer),
            self.target(origin),
            self.send_sems.at[peer],
            self.recv_sems.at[origin],
            ctx=2 * target + self.core,
        )


class PlaneGather:
    def __init__(self, blocks, sems):
        self.blocks = blocks
        self.size = blocks.shape[0]
        self.rank = lax.axis_index("dp")
        self.square = self.size == 4
        self.send_sems, self.recv_sems = sems
        if self.square:
            self.beside = self.rank + 1 - 2 * (self.rank % 2)
            self.above = self.rank + 2 - 4 * (self.rank // 2)
            half = blocks.shape[1] // 32 * 16
            self.low, self.high = pl.ds(0, half), pl.ds(half, blocks.shape[1] - half)
        else:
            self.swap = Swap("dp", lambda peer: blocks.at[self.rank], blocks.at.__getitem__, sems)

    def copy(self, index, ref, target):
        return send(ref, ref, self.send_sems.at[index], self.recv_sems.at[index], dp=target)

    def start(self):
        if not self.square:
            self.swap.start()
            return
        own = self.blocks.at[self.rank]
        self.copy(0, own, self.beside).start()
        self.copy(1, own, self.above).start()

    def relay(self):
        if not self.square:
            return
        self.copy(0, self.blocks.at[self.beside], self.beside).wait_recv()
        self.copy(2, self.blocks.at[self.beside, self.low], self.above).start()
        self.copy(1, self.blocks.at[self.above], self.above).wait_recv()
        self.copy(3, self.blocks.at[self.above, self.high], self.beside).start()

    def wait(self):
        if not self.square:
            self.swap.wait()
            self.swap.drain()
            return
        far = 3 - self.rank
        own = self.blocks.at[self.rank]
        self.copy(2, self.blocks.at[far, self.low], self.above).wait_recv()
        self.copy(3, self.blocks.at[far, self.high], self.beside).wait_recv()
        self.copy(0, own, self.beside).wait_send()
        self.copy(1, own, self.above).wait_send()
        self.copy(2, self.blocks.at[self.beside, self.low], self.above).wait_send()
        self.copy(3, self.blocks.at[self.above, self.high], self.beside).wait_send()

    semaphores = staticmethod(Swap.semaphores)


class PlaneSum:
    def __init__(self, blocks, landed, sems):
        self.blocks, self.landed = blocks, landed
        self.rank = lax.axis_index("dp")
        self.send_sems, self.recv_sems = sems
        self.swap = Swap("dp", blocks.at.__getitem__, landed.at.__getitem__, sems)
        self.square = blocks.shape[0] == 4
        if self.square:
            self.beside = self.rank + 1 - 2 * (self.rank % 2)
            self.above = self.rank + 2 - 4 * (self.rank // 2)
            half = blocks.shape[1] // 32 * 16
            self.low, self.high = pl.ds(0, half), pl.ds(half, blocks.shape[1] - half)

    def copy(self, index):
        far = 3 - self.rank
        block, slot, rows, target = (
            (far, 0, self.low, self.beside),
            (self.beside, 1, self.low, self.beside),
            (far, 0, self.high, self.above),
            (self.above, 1, self.high, self.above),
            (self.above, 2, self.low, self.above),
            (self.beside, 2, self.high, self.beside),
        )[index]
        return send(
            self.blocks.at[block, rows],
            self.landed.at[slot, rows],
            self.send_sems.at[index],
            self.recv_sems.at[index],
            dp=target,
        )

    def start(self):
        if not self.square:
            self.swap.start()
            return
        for index in range(4):
            self.copy(index).start()

    def relay(self):
        if not self.square:
            return
        for index, block, rows in ((0, self.above, self.low), (2, self.beside, self.high)):
            self.copy(index).wait_recv()
            total = self.blocks[block, rows].astype(WIDE) + self.landed[0, rows].astype(WIDE)
            self.blocks[block, rows] = total.astype(self.blocks.dtype)
            self.copy(4 + index // 2).start()

    def total(self):
        total = self.blocks[self.rank].astype(WIDE)
        if not self.square:
            self.swap.wait()
            for off in range(1, self.swap.size):
                total = total + self.landed[lax.rem(self.rank + off, self.swap.size)].astype(WIDE)
            return total
        for index in (1, 3, 4, 5):
            self.copy(index).wait_recv()
        return total + self.landed[1].astype(WIDE) + self.landed[2].astype(WIDE)

    def drain(self):
        if not self.square:
            self.swap.drain()
            return
        for index in range(6):
            self.copy(index).wait_send()

    @staticmethod
    def semaphores(size):
        return Swap.semaphores(max(size, 6))


class LineGather:
    def __init__(self, blocks, send_sems, recv_sems):
        self.blocks, self.send_sems, self.recv_sems = blocks, send_sems, recv_sems
        self.rank = lax.axis_index("ctx")
        self.chip, self.core = self.rank // 2, self.rank % 2
        self.chips = blocks.shape[0] // 2

    def copy(self, way, origin, target, src=None):
        block = self.blocks.at[origin]
        return send(
            block if src is None else src,
            block,
            self.send_sems.at[way, origin],
            self.recv_sems.at[origin],
            ctx=target,
        )

    def pass_on(self, origin, src=None):
        chip = origin // 2

        @pl.when((chip <= self.chip) & (self.chip < self.chips - 1))
        def _():
            self.copy(0, origin, self.rank + 2, src).start()

        @pl.when((chip >= self.chip) & (self.chip > 0))
        def _():
            self.copy(1, origin, self.rank - 2, src).start()

        self.copy(2, origin, self.rank + 1 - 2 * self.core, src).start()

    def arrive(self, step, part):
        side, other = part % 2, part // 2
        origin_chip = self.chip + jnp.where(side == 0, -step, step)
        origin = 2 * origin_chip + jnp.where(other == 0, self.core, 1 - self.core)
        valid = (origin_chip >= 0) & (origin_chip < self.chips) & ((step > 0) | (side == 0))

        @pl.when(valid & (origin != self.rank))
        def _():
            self.copy(0, origin, self.rank).wait_recv()

            @pl.when(other == 0)
            def _():
                self.pass_on(origin)

        return valid, origin

    def finish(self):
        def one(chip, carry):
            origin = 2 * chip + self.core

            @pl.when((chip <= self.chip) & (self.chip < self.chips - 1))
            def _():
                self.copy(0, origin, self.rank).wait_send()

            @pl.when((chip >= self.chip) & (self.chip > 0))
            def _():
                self.copy(1, origin, self.rank).wait_send()

            self.copy(2, origin, self.rank).wait_send()
            return carry

        lax.fori_loop(0, self.chips, one, 0)

    @staticmethod
    def semaphores(ctx):
        return [pltpu.SemaphoreType.DMA((3, ctx)), pltpu.SemaphoreType.DMA((ctx,))]


class LineSum:
    def __init__(self, blocks, pair, passing, sems):
        self.blocks, self.pair, self.passing = blocks, pair, passing
        self.pair_send, self.pair_recv, self.line_send, self.line_recv = sems
        self.rank = lax.axis_index("ctx")
        self.chip, self.core = self.rank // 2, self.rank % 2
        self.chips = blocks.shape[0] // 2
        self.pieces = self.line_recv.shape[2]
        self.piece = blocks.shape[1] // self.pieces

    def pair_copy(self, chip):
        return send(
            self.blocks.at[2 * chip + 1 - self.core],
            self.pair.at[chip],
            self.pair_send.at[chip],
            self.pair_recv.at[chip],
            ctx=self.rank + 1 - 2 * self.core,
        )

    def line_copy(self, way, chip, piece, target, at):
        rows = pl.ds(piece * self.piece, self.piece)
        slot = jnp.where((way == 1) & (chip == at), self.chips, chip)
        return send(
            self.blocks.at[2 * chip + self.core, rows],
            self.passing.at[slot, rows],
            self.line_send.at[chip, piece],
            self.line_recv.at[way, chip, piece],
            ctx=target,
        )

    def both(self, chip, rows):
        mine = self.blocks[2 * chip + self.core, rows].astype(WIDE)
        return mine + self.pair[chip, rows].astype(WIDE)

    def forward(self, way, chip, valid):
        behind = jnp.where(way == 0, self.chip > 0, self.chip < self.chips - 1)
        target = self.rank + jnp.where(way == 0, 2, -2)

        @pl.when(valid)
        def _():
            self.pair_copy(chip).wait_recv()

            def one(piece, carry):
                rows = pl.ds(pl.multiple_of(piece * self.piece, self.piece), self.piece)
                total = self.both(chip, rows)

                @pl.when(behind)
                def _():
                    self.line_copy(way, chip, piece, target, self.chip).wait_recv()
                    passing = self.passing[chip, rows].astype(WIDE)
                    self.blocks[2 * chip + self.core, rows] = (total + passing).astype(LOW)

                @pl.when(jnp.logical_not(behind))
                def _():
                    self.blocks[2 * chip + self.core, rows] = total.astype(LOW)

                self.line_copy(way, chip, piece, target, target // 2).start()
                return carry

            lax.fori_loop(0, self.pieces, one, 0)

    def near_first(self, step, way):
        last = self.chips - 1
        chip = jnp.where(way == 0, step - self.chip, 2 * last - self.chip - step)
        ahead = jnp.where(way == 0, (chip > self.chip) & (chip <= last), (chip >= 0) & (chip < self.chip))
        self.forward(way, chip, ahead)

    def far_first(self, step, way):
        last = self.chips - 1
        chip = jnp.where(way == 0, last + self.chip - step, step - last + self.chip)
        ahead = jnp.where(way == 0, (chip > self.chip) & (chip <= last), (chip >= 0) & (chip < self.chip))
        self.forward(way, chip, ahead)

    def send_pairs(self):
        def one(chip, carry):
            self.pair_copy(chip).start()
            return carry

        lax.fori_loop(0, self.chips, one, 0)

    def far_steps(self, begin, end):
        def one(index, carry):
            self.far_first(index // 2, index % 2)
            return carry

        lax.fori_loop(2 * begin, 2 * end, one, 0)

    def finish(self, out):
        self.pair_copy(self.chip).wait_recv()

        def one(piece, carry):
            rows = pl.ds(pl.multiple_of(piece * self.piece, self.piece), self.piece)
            out[rows] = self.both(self.chip, rows)

            @pl.when(self.chip > 0)
            def _():
                self.line_copy(0, self.chip, piece, self.rank, self.chip).wait_recv()
                out[rows] = out[rows] + self.passing[self.chip, rows].astype(WIDE)

            @pl.when(self.chip < self.chips - 1)
            def _():
                self.line_copy(1, self.chip, piece, self.rank, self.chip).wait_recv()
                out[rows] = out[rows] + self.passing[self.chips, rows].astype(WIDE)

            return carry

        lax.fori_loop(0, self.pieces, one, 0)

        def sent(chip, carry):
            self.pair_copy(chip).wait_send()

            @pl.when(chip != self.chip)
            def _():
                for piece in range(self.pieces):
                    self.line_copy(0, chip, piece, self.rank, self.chip).wait_send()

            return carry

        lax.fori_loop(0, self.chips, sent, 0)

    @staticmethod
    def scratch(ctx, rows, columns, pieces):
        chips = ctx // 2
        return [
            pltpu.VMEM((ctx, rows, columns), LOW),
            pltpu.VMEM((chips, rows, columns), LOW),
            pltpu.VMEM((chips + 1, rows, columns), LOW),
            pltpu.SemaphoreType.DMA((chips,)),
            pltpu.SemaphoreType.DMA((chips,)),
            pltpu.SemaphoreType.DMA((chips, pieces)),
            pltpu.SemaphoreType.DMA((2, chips, pieces)),
        ]


VMEM = pl.BlockSpec(memory_space=pltpu.VMEM)
HBM = pl.BlockSpec(memory_space=pl.ANY)


def params(number):
    return pltpu.CompilerParams(
        vmem_limit_bytes=63 * MIB, collective_id=number, has_side_effects=True
    )


def packed_rows(count, columns):
    tiles = -(-columns // 128)
    main = count // 16 * 16
    return tiles * main + -(-(tiles * (count - main)) // 16) * 16


def pack(out, index, rows, first, count, lane, columns):
    tiles = -(-columns // 128)
    main = count // 16 * 16
    for tile in range(tiles):
        lanes = slice(lane + tile * 128, lane + tile * 128 + 128)
        part = rows[first : first + main, lanes]
        out[index, tile * main : (tile + 1) * main] = part.astype(LOW)
    left = [
        rows[first + row : first + row + 1, lane + tile * 128 : lane + tile * 128 + 128]
        for row in range(main, count)
        for tile in range(tiles)
    ]
    space = out.shape[1] - tiles * main
    if space:
        left.append(jnp.zeros((space - len(left), 128), WIDE))
        out[index, tiles * main :] = jnp.concatenate(left, 0).astype(LOW)


def unpack(packed, rows, first, count, columns):
    tiles = -(-columns // 128)
    main = count // 16 * 16
    for tile in range(tiles):
        lanes = slice(tile * 128, tile * 128 + 128)
        rows[first : first + main, lanes] = packed[tile * main : (tile + 1) * main].astype(WIDE)
    left = packed[tiles * main :].astype(WIDE)
    for row in range(main, count):
        for tile in range(tiles):
            place = (row - main) * tiles + tile
            lanes = slice(tile * 128, tile * 128 + 128)
            rows[first + row : first + row + 1, lanes] = left[place : place + 1]


def full_lanes(columns):
    return -(-columns // 128) * 128


def head_pieces(ctx, slots):
    width = slots * HEAD_DIM
    pieces = []
    for rank in range(ctx):
        count = min(width, D - rank * width)
        if count > 0:
            for part in range(3):
                pieces.append((rank, part * width, part * D + rank * width, count))
    return pieces


def unit_pieces(ctx, dp):
    units = FF // (ctx * dp)
    return [
        (rank, seq * padded_units(units), (seq * ctx + rank) * units, units)
        for rank in range(ctx)
        for seq in range(dp)
    ]


def divide(rows_ref, wide, blocks, pieces, columns):
    count = rows_ref.shape[0]
    lanes = full_lanes(columns)
    for rank in range(blocks.shape[0]):
        wide[...] = jnp.zeros_like(wide)
        for owner, here, there, size in pieces:
            if owner == rank:
                wide[0:count, here : here + size] = rows_ref[:, there : there + size].astype(WIDE)
        pack(blocks, rank, wide, 0, count, 0, lanes)


class Spread:
    def __init__(self, blocks, landed, wide, out, sems):
        self.blocks, self.landed, self.wide, self.out = blocks, landed, wide, out
        self.swap = Swap("ctx", blocks.at.__getitem__, landed.at.__getitem__, sems[:2])
        self.plane = PlaneGather(out, sems[2:])

    def start(self):
        self.swap.start()
        self.landed[self.swap.rank] = self.blocks[self.swap.rank]

    def cross(self):
        self.swap.wait()
        count = self.out.shape[1] // self.swap.size
        columns = self.out.shape[2]
        for index in range(self.swap.size):
            unpack(self.landed[index], self.wide, index * count, count, columns)
        self.out[self.plane.rank] = self.wide[:, 0:columns].astype(LOW)
        self.plane.start()

    def wait(self):
        self.plane.wait()

    @staticmethod
    def scratch(ctx, dp, rows, columns):
        return [
            pltpu.VMEM((ctx, packed_rows(rows // ctx, columns), 128), LOW),
            pltpu.VMEM((rows, full_lanes(columns)), WIDE),
            *Swap.semaphores(ctx),
            *PlaneGather.semaphores(dp),
        ]


class StreamSum:
    def __init__(self, parts, landed, stage, stage_sems, sems):
        self.parts, self.landed, self.stage, self.stage_sems = parts, landed, stage, stage_sems
        self.plane = PlaneSum(parts, landed, sems)

    def put(self, index, part):
        if index >= 2:
            self.move(index - 2).wait()
        self.stage[index % 2] = part.astype(LOW)
        self.move(index).start()

    def move(self, index):
        slot = index % 2
        return pltpu.make_async_copy(
            self.stage.at[slot], self.parts.at[index], self.stage_sems.at[slot]
        )

    def start(self):
        self.move(2).wait()
        self.move(3).wait()
        self.plane.start()

    def load(self, source, slot, rows):
        return pltpu.make_async_copy(
            source.at[rows], self.stage.at[slot, rows], self.stage_sems.at[slot]
        )

    def relayed(self, index):
        plane = self.plane
        rows, target = ((plane.low, plane.above), (plane.high, plane.beside))[index]
        return send(
            self.stage.at[2, rows],
            self.landed.at[2, rows],
            plane.send_sems.at[4 + index],
            plane.recv_sems.at[4 + index],
            dp=target,
        )

    def relay(self):
        plane = self.plane
        for index, block, rows in ((0, plane.above, plane.low), (1, plane.beside, plane.high)):
            plane.copy(2 * index).wait_recv()
            loads = (
                self.load(self.parts.at[block], 0, rows),
                self.load(self.landed.at[0], 1, rows),
            )
            for load in loads:
                load.start()
            for load in loads:
                load.wait()
            total = self.stage[0, rows].astype(WIDE) + self.stage[1, rows].astype(WIDE)
            self.stage[2, rows] = total.astype(LOW)
            self.relayed(index).start()

    def total(self):
        plane = self.plane
        for index in range(4):
            plane.copy(index).wait_send()
        plane.copy(1).wait_recv()
        plane.copy(3).wait_recv()
        for index in range(2):
            self.relayed(index).wait_send()
            self.relayed(index).wait_recv()
        every = pl.ds(0, self.parts.shape[1])
        loads = (
            self.load(self.parts.at[plane.rank], 0, every),
            self.load(self.landed.at[1], 1, every),
            self.load(self.landed.at[2], 2, every),
        )
        for load in loads:
            load.start()
        for load in loads:
            load.wait()
        total = self.stage[0].astype(WIDE) + self.stage[1].astype(WIDE)
        return total + self.stage[2].astype(WIDE)


class Collect:
    def __init__(self, pieces, plane, wide, blocks, came, out, sems):
        self.pieces, self.plane, self.wide, self.blocks = pieces, plane, wide, blocks
        self.came, self.out = came, out
        self.swap = Swap("ctx", blocks.at.__getitem__, came.at.__getitem__, sems)

    def cross(self):
        rows, columns = self.plane.parts.shape[1:]
        lanes = full_lanes(columns)
        self.wide[0:rows, 0:columns] = self.plane.total()
        if lanes > columns:
            self.wide[0:rows, columns:lanes] = jnp.zeros((rows, lanes - columns), WIDE)
        count = rows // self.swap.size
        for index in range(self.swap.size):
            pack(self.blocks, index, self.wide, index * count, count, 0, columns)
        self.swap.start()
        self.came[self.swap.rank] = self.blocks[self.swap.rank]

    def wait(self):
        self.swap.wait()
        count = self.out.shape[0]
        for rank in range(self.swap.size):
            unpack(self.came[rank], self.wide, 0, count, self.plane.parts.shape[2])
            for owner, here, there, size in self.pieces:
                if owner == rank:
                    self.out[:, there : there + size] = self.wide[0:count, here : here + size]
        self.swap.drain()


class Projection:
    def __init__(self, rows, blocks, wide, out, sems):
        self.rows, self.blocks, self.wide, self.out = rows, blocks, wide, out
        self.rank = lax.axis_index("ctx")
        self.core = self.rank % 2
        self.packed = rows.shape[1]
        self.plane = PlaneGather(blocks.at[self.core], sems[:2])
        self.send_sems, self.recv_sems = sems[2:4]
        self.swap = ChipSwap(lambda peer: rows.at[0], self.place, sems[4:])

    def place(self, chip):
        rows = pl.ds(pl.multiple_of(chip * self.packed, self.packed), self.packed)
        return self.blocks.at[self.core, self.plane.rank, rows]

    def start(self):
        self.swap.start()
        rows = pl.ds(pl.multiple_of(self.swap.rank * self.packed, self.packed), self.packed)
        self.blocks[self.core, self.plane.rank, rows] = self.rows[0]

    def cross(self):
        self.swap.wait()
        self.plane.start()
        self.to_other(self.plane.rank).start()

    def to_other(self, seq):
        block = self.blocks.at[self.core, seq]
        return send(
            block,
            block,
            self.send_sems.at[seq],
            self.recv_sems.at[seq],
            ctx=self.rank + 1 - 2 * self.core,
        )

    def wait(self):
        self.plane.wait()

        def others(off, carry):
            self.to_other(lax.rem(self.plane.rank + off, self.plane.size)).start()
            return carry

        lax.fori_loop(1, self.plane.size, others, 0)
        ctx = 2 * self.swap.size
        count = self.out.shape[1] // ctx

        def order(off, carry):
            seq = lax.rem(self.plane.rank + off, self.plane.size)
            self.to_other(seq).wait_recv()
            for rank in range(ctx):
                first = rank // 2 * self.packed
                rows = self.blocks[rank % 2, seq, first : first + self.packed]
                unpack(rows, self.wide, rank * count, count, D)
            self.out[seq] = self.wide[:, 0:D].astype(LOW)
            return carry

        lax.fori_loop(0, self.plane.size, order, 0)

        def sent(seq, carry):
            self.to_other(seq).wait_send()
            return carry

        lax.fori_loop(0, self.plane.size, sent, 0)
        self.swap.drain()

    @staticmethod
    def scratch(ctx, dp):
        packed = packed_rows(D // (dp * ctx), D)
        return [
            pltpu.VMEM((2, dp, ctx // 2 * packed, 128), LOW),
            pltpu.VMEM((D // dp, full_lanes(D)), WIDE),
            *PlaneGather.semaphores(dp),
            *Swap.semaphores(dp),
            *Swap.semaphores(ctx // 2),
        ]


def vector_pieces(owners, count):
    pieces = []
    for owner in range(owners):
        begin = 0
        while begin < count:
            place = owner * count + begin
            size = min(count - begin, D - place % D)
            pieces.append((owner, begin, place // D, place % D, size))
            begin += size
    return pieces


def unit_bias_pieces(rank, ctx, dp):
    units = FF // (ctx * dp)
    pieces = []
    for seq in range(dp):
        begin = 0
        while begin < units:
            place = (seq * ctx + rank) * units + begin
            size = min(units - begin, D - place % D)
            pieces.append((seq * padded_units(units) + begin, 7 + place // D, place % D, size))
            begin += size
    return pieces


GAIN_ONE, SHIFT_ONE, BIAS_QUERY, BIAS_VALUE, BIAS_PROJ, GAIN_TWO, SHIFT_TWO = range(7)
BIAS_OUT = 11
ROWS = 16


class Build:
    def __init__(self):
        self.ins, self.outs, self.scratch = {}, {}, {}

    def take(self, spec, **values):
        self.ins.update({name: (value, spec) for name, value in values.items()})

    def give(self, kind, spec, **shapes):
        for name, shape in shapes.items():
            self.outs[name] = (jax.ShapeDtypeStruct(shape, kind), spec)

    def hold(self, kind, **shapes):
        self.scratch.update({name: pltpu.VMEM(shape, kind) for name, shape in shapes.items()})

    def sems(self, **shapes):
        self.scratch.update(
            {name: pltpu.SemaphoreType.DMA(shape) for name, shape in shapes.items()}
        )

    def both(self, **sizes):
        for name, size in sizes.items():
            self.sems(**{name + "_send": (size,), name + "_recv": (size,)})

    def line_sum(self, name, ctx, tokens):
        chips = ctx // 2
        shapes = (ctx, tokens, D), (chips, tokens, D), (chips + 1, tokens, D)
        for part, shape in zip(("_blocks", "_pair", "_passing"), shapes, strict=True):
            self.hold(LOW, **{name + part: shape})
        self.both(**{name + "_pair": chips})
        self.sems(
            **{name + "_line_send": (chips, PIECES), name + "_line_recv": (2, chips, PIECES)}
        )

    def call(self, kernel, number, label):
        names = (*self.ins, *self.outs, *self.scratch)
        results = pl.pallas_call(
            functools.partial(kernel, names),
            out_shape=[shape for shape, _ in self.outs.values()],
            in_specs=[spec for _, spec in self.ins.values()],
            out_specs=[spec for _, spec in self.outs.values()],
            scratch_shapes=list(self.scratch.values()),
            compiler_params=params(number),
            name=label,
        )(*[value for value, _ in self.ins.values()])
        return Names(tuple(self.outs), results)


PIECES = 8


class Names:
    def __init__(self, names, refs):
        self.__dict__.update(zip(names, refs, strict=True))


def forward_kernel(block, whole, names, *refs):
    r = Names(names, refs)
    seq, rank = lax.axis_index("dp"), lax.axis_index("ctx")
    ctx, tokens, _ = r.rows.shape
    dp, units = r.units.shape[:2]
    width = r.mixed.shape[1]
    vec_count = 12 * D // (ctx * dp)

    def out(ref, target, index):
        return pltpu.make_async_copy(ref, target, r.out_sems.at[index])

    rows_in = LineGather(r.rows, r.rows_send, r.rows_recv)
    cots = LineGather(r.cots, r.cots_send, r.cots_recv)
    feed = LineGather(r.rows, r.feed_send, r.feed_recv)
    total = LineSum(
        r.sum_blocks,
        r.sum_pair,
        r.sum_passing,
        (r.sum_pair_send, r.sum_pair_recv, r.sum_line_send, r.sum_line_recv),
    )
    chips = feed.chips
    line = Swap(
        "ctx",
        lambda peer: r.small,
        lambda origin: r.smalls.at[seq, origin],
        (r.line_send, r.line_recv),
    )
    plane = Swap(
        "dp",
        lambda peer: r.smalls.at[seq],
        r.smalls.at.__getitem__,
        (r.plane_send, r.plane_recv),
    )
    unit_rows = PlaneGather(r.units, (r.units_send, r.units_recv))
    to_tokens = Swap(
        "ctx",
        lambda peer: r.mixed.at[pl.ds(pl.multiple_of(peer * tokens, tokens), tokens)],
        lambda origin: r.own_mixed.at[:, pl.ds(pl.multiple_of(origin * width, width), width)],
        (r.mixed_send, r.mixed_recv),
    )
    if whole:
        heads = Spread(
            r.qkv_blocks,
            r.qkv_landed,
            r.qkv_wide,
            r.qkv_mat,
            (r.qkv_send, r.qkv_recv, r.qkv_plane_send, r.qkv_plane_recv),
        )
        columns = Spread(
            r.fc_blocks,
            r.fc_landed,
            r.fc_wide,
            r.fc_mat,
            (r.fc_send, r.fc_recv, r.fc_plane_send, r.fc_plane_recv),
        )
        proj = Projection(
            r.proj_packed,
            r.proj_blocks,
            r.proj_wide,
            r.proj_mat,
            (
                r.proj_plane_send,
                r.proj_plane_recv,
                r.proj_pair_send,
                r.proj_pair_recv,
                r.proj_send,
                r.proj_recv,
            ),
        )

    def prepare():
        own = r.in_t[...].astype(WIDE).T.astype(LOW)
        r.own_in[...] = own
        r.rows[rank] = own
        r.smalls[seq, rank] = r.small[...]
        main = r.own_units.shape[0] // 16 * 16
        r.units[seq, 0:main] = r.own_units[0:main]
        if units > main:
            left = r.own_units[main:].astype(WIDE)
            zeros = jnp.zeros((units - r.own_units.shape[0], D), WIDE)
            r.units[seq, main:] = jnp.concatenate([left, zeros], 0).astype(LOW)
        if whole:
            pieces = head_pieces(ctx, width // HEAD_DIM)
            divide(r.qkv_rows, r.qkv_lanes, r.qkv_blocks, pieces, 3 * width)

    greet_all(prepare)

    line.start()
    if whole:
        heads.start()
    unit_rows.start()
    if whole:
        count = r.proj_rows.shape[0]
        r.proj_lanes[0:count, 0:D] = r.proj_rows[...].astype(WIDE)
        r.proj_lanes[0:count, D:] = jnp.zeros((count, full_lanes(D) - D), WIDE)
        pack(r.proj_packed, 0, r.proj_lanes, 0, count, 0, D)
        heads.swap.drain()
        proj.start()
    rows_in.pass_on(rank)
    own_cot = r.cot_t[...].astype(WIDE).T.astype(LOW)
    r.own_cot[...] = own_cot
    r.cots[rank] = own_cot
    line.wait()
    plane.start()
    if whole:
        heads.cross()
        divide(r.fc_rows, r.fc_lanes, r.fc_blocks, unit_pieces(ctx, dp), dp * units)

    def arrivals(gather):
        def arrive(index, carry):
            gather.arrive(1 + index // 4, index % 4)
            return carry

        return arrive

    rows_in.arrive(0, 2)
    lax.fori_loop(0, 4, arrivals(rows_in), 0)
    if whole:
        heads.plane.relay()
        columns.start()
        proj.cross()
    lax.fori_loop(4, 4 * (chips - 1), arrivals(rows_in), 0)
    if whole:
        proj.plane.relay()
    rows_in.finish()
    docs = jnp.broadcast_to(r.docs[...], r.doc_start.shape)
    lane = lax.broadcasted_iota(jnp.int32, docs.shape, 1)
    doc_start = jnp.where(docs != pltpu.roll(docs, 1, 1), lane, 0)
    shift = 1
    while shift < docs.shape[1]:
        earlier = jnp.where(lane >= shift, pltpu.roll(doc_start, shift, 1), 0)
        doc_start = jnp.maximum(doc_start, earlier)
        shift *= 2
    r.doc_start[...] = doc_start
    plane.wait()
    r.vectors[...] = jnp.zeros_like(r.vectors)
    for owner, begin, row, lane, size in vector_pieces(ctx * dp, vec_count):
        r.vectors[row : row + 1, lane : lane + size] = r.smalls[
            owner // ctx, owner % ctx, 0:1, begin : begin + size
        ]
    r.bias_units[...] = jnp.zeros_like(r.bias_units)
    for owner in range(ctx):

        @pl.when(rank == owner)
        def _(owner=owner):
            for here, row, lane, size in unit_bias_pieces(owner, ctx, dp):
                r.bias_units[0:1, here : here + size] = r.vectors[row : row + 1, lane : lane + size]

    if whole:
        heads.wait()
        out(r.qkv_mat, r.qkv_mat_out, 0).start()
    mine = pl.ds(pl.multiple_of(rank * width, width), width)
    bias = jnp.concatenate(
        [
            r.vectors[BIAS_QUERY : BIAS_QUERY + 1, mine],
            jnp.zeros((1, width), WIDE),
            r.vectors[BIAS_VALUE : BIAS_VALUE + 1, mine],
        ],
        1,
    )

    def project(index, carry):
        both = pl.ds(2 * index, 2)
        normed, _ = normalize(r.rows[both].reshape(2 * tokens, D).astype(WIDE))
        attn_in = normed * r.vectors[GAIN_ONE : GAIN_ONE + 1, 0:D]
        attn_in = (attn_in + r.vectors[SHIFT_ONE : SHIFT_ONE + 1, 0:D]).astype(LOW)
        r.rows[both] = attn_in.reshape(2, tokens, D)
        rows = pl.ds(pl.multiple_of(2 * index * tokens, 2 * tokens), 2 * tokens)
        r.qkv[rows] = (dot(attn_in, r.qkv_mat[...].reshape(D, 3 * width)) + bias).astype(LOW)
        return carry

    lax.fori_loop(0, chips, project, 0)
    out(r.rows, r.attn_in_out, 1).start()
    out(r.qkv, r.qkv_out, 2).start()
    cots.pass_on(rank)
    if whole:
        columns.cross()
    attend_body(block, r.qkv, r.doc_start, r.mixed, r.stats, r.value_t)
    out(r.rows, r.attn_in_out, 1).wait()
    to_tokens.start()
    r.own_mixed[:, mine] = r.mixed[pl.ds(pl.multiple_of(rank * tokens, tokens), tokens)]
    cots.arrive(0, 2)
    lax.fori_loop(0, 4, arrivals(cots), 0)
    if whole:
        proj.wait()
        out(r.proj_mat, r.proj_mat_out, 3).start()
        columns.plane.relay()
    unit_rows.relay()
    to_tokens.wait()
    resid = dot(r.own_mixed[:, 0:D], r.proj_mat[...].reshape(D, D))
    resid = resid + r.own_in[...].astype(WIDE) + r.vectors[BIAS_PROJ : BIAS_PROJ + 1, 0:D]
    r.resid[...] = resid
    normed, _ = normalize(resid)
    ffn_in = normed * r.vectors[GAIN_TWO : GAIN_TWO + 1, 0:D]
    r.rows[rank] = (ffn_in + r.vectors[SHIFT_TWO : SHIFT_TWO + 1, 0:D]).astype(LOW)
    feed.pass_on(rank)
    lax.fori_loop(4, 8, arrivals(cots), 0)
    unit_rows.wait()
    if whole:
        columns.wait()

    def keep(chip, slot, which=range(3)):
        both = pl.ds(2 * chip, 2)
        kept = ((r.act, r.act_out), (r.pre, r.pre_out), (r.part, r.part_out))
        return [
            pltpu.make_async_copy(
                kept[index][0].at[slot], kept[index][1].at[both], r.keep_sems.at[index, slot]
            )
            for index in which
        ]

    def pass_rows(chip):
        both = pl.ds(2 * chip, 2)
        return [
            pltpu.make_async_copy(ref.at[both], target.at[both], r.pass_sems.at[index, chip])
            for index, (ref, target) in enumerate(((r.rows, r.ffn_out), (r.cots, r.cots_out)))
        ]

    def work(chip, done):
        both = pl.ds(2 * chip, 2)
        slot = done % 2

        @pl.when(done >= 2)
        def _():
            for copy in keep(chip, slot):
                copy.wait()

        for copy in pass_rows(chip):
            copy.start()
        fc = r.fc_mat[...].reshape(D, dp * units)
        pre = dot(r.rows[both].reshape(2 * tokens, D), fc) + r.bias_units[0:1]
        bend = jnp.tanh(0.7978845608028654 * (pre + 0.044715 * pre * pre * pre))
        act = (0.5 * pre * (1.0 + bend)).astype(LOW)
        r.act[slot] = act.reshape(2, tokens, -1)
        slope = 0.5 * (1.0 + bend) + 0.5 * pre * (1.0 - bend * bend) * 0.7978845608028654 * (
            1.0 + 3 * 0.044715 * pre * pre
        )
        grad_pre = (slope * r.grad_act[...]).astype(LOW)
        r.pre[slot] = grad_pre.reshape(2, tokens, -1)
        r.sum_blocks[both] = dot(grad_pre, fc, 1, 1).astype(LOW).reshape(2, tokens, D)
        total.pair_copy(chip).start()
        for copy in keep(chip, slot, (0, 1)):
            copy.start()

    def give_out(chip, done):
        slot = done % 2
        act = r.act[slot].reshape(2 * tokens, dp * units)
        mat = r.units[...].reshape(dp * units, D)
        r.part[slot] = dot(act, mat).astype(LOW).reshape(2, tokens, D)
        keep(chip, slot, (2,))[0].start()

    def step(index, done):
        distance, side = index // 2, index % 2
        near = distance < chips
        origin_chip = rank // 2 + jnp.where(side == 0, -distance, distance)
        valid = near & (origin_chip >= 0) & (origin_chip < chips) & ((distance > 0) | (side == 0))

        @pl.when(near)
        def _():
            @pl.when(side == 0)
            def _():
                @pl.when(distance > 2)
                def _():
                    cots.arrive(distance, 0)
                    cots.arrive(distance, 1)

                feed.arrive(distance, 0)
                feed.arrive(distance, 1)

            @pl.when(distance > 2)
            def _():
                cots.arrive(distance, 2 + side)

            @pl.when(valid)
            def _():
                cot = r.cots[pl.ds(2 * origin_chip, 2)].reshape(2 * tokens, D)
                r.grad_act[...] = dot(cot, r.units[...].reshape(dp * units, D), 1, 1)

            feed.arrive(distance, 2 + side)

            @pl.when(valid)
            def _():
                work(origin_chip, done)

        after = done + valid.astype(jnp.int32)

        @pl.when(side == 1)
        def _():
            def way(index, carry):
                total.near_first(distance, index)
                return carry

            lax.fori_loop(0, 2, way, 0)

            def output(index, carry):
                chip = rank // 2 + jnp.where(index == 0, -distance, distance)
                here = near & (chip >= 0) & (chip < chips) & ((distance > 0) | (index == 0))
                later = (index == 0) & valid & (distance > 0)

                @pl.when(here)
                def _():
                    give_out(chip, after - 1 - later.astype(jnp.int32))

                return carry

            lax.fori_loop(0, 2, output, 0)

        return after

    lax.fori_loop(0, 2 * (2 * chips - 1), step, jnp.int32(0))
    total.finish(r.grad)

    feed.finish()
    cots.finish()
    line.drain()
    plane.drain()
    to_tokens.drain()
    for slot in range(2):
        for copy in keep(0, slot):
            copy.wait()

    def passed(chip, carry):
        for copy in pass_rows(chip):
            copy.wait()
        return carry

    lax.fori_loop(0, chips, passed, 0)
    out(r.qkv, r.qkv_out, 2).wait()
    if whole:
        out(r.qkv_mat, r.qkv_mat_out, 0).wait()
        out(r.proj_mat, r.proj_mat_out, 3).wait()
        columns.swap.drain()


def forward(small, in_t, cot_t, unit_rows, docs, mats, slots, whole, block):
    ctx, dp = lax.axis_size("ctx"), lax.axis_size("dp")
    tokens = in_t.shape[1]
    length = ctx * tokens
    width = slots * HEAD_DIM
    units = padded_units(unit_rows.shape[0])
    columns = dp * units
    chips = ctx // 2
    rows = D // dp
    count = rows // ctx
    high = -(-count // 8) * 8
    b = Build()
    b.take(VMEM, small=small, in_t=in_t, cot_t=cot_t, own_units=unit_rows, docs=docs)
    if whole:
        b.take(VMEM, qkv_rows=mats[0], fc_rows=mats[1], proj_rows=mats[2])
    else:
        b.take(VMEM, qkv_mat=mats[0], fc_mat=mats[1], proj_mat=mats[2])
    b.give(
        WIDE,
        VMEM,
        vectors=(ROWS, max(full_lanes(D), ctx * width)),
        stats=(8, length),
        resid=(tokens, D),
        grad=(tokens, D),
    )
    b.give(
        LOW, VMEM, own_mixed=(tokens, ctx * width), own_in=(tokens, D), own_cot=(tokens, D)
    )
    b.give(jnp.int32, VMEM, doc_start=(8, length))
    b.give(
        LOW,
        HBM,
        attn_in_out=(ctx, tokens, D),
        qkv_out=(length, 3 * width),
        cots_out=(ctx, tokens, D),
        ffn_out=(ctx, tokens, D),
        act_out=(ctx, tokens, columns),
        pre_out=(ctx, tokens, columns),
        part_out=(ctx, tokens, D),
    )
    if whole:
        b.give(LOW, HBM, qkv_mat_out=(dp, rows, 3 * width), proj_mat_out=(dp, rows, D))
    b.hold(
        LOW,
        rows=(ctx, tokens, D),
        cots=(ctx, tokens, D),
        units=(dp, units, D),
        qkv=(length, 3 * width),
        mixed=(length, width),
        value_t=(width, length),
        act=(2, 2, tokens, columns),
        pre=(2, 2, tokens, columns),
        part=(2, 2, tokens, D),
    )
    b.hold(
        WIDE,
        smalls=(dp, ctx, *small.shape),
        bias_units=(8, columns),
        grad_act=(2 * tokens, columns),
    )
    b.line_sum("sum", ctx, tokens)
    b.sems(
        out_sems=(4,),
        keep_sems=(3, 2),
        pass_sems=(2, chips),
        rows_send=(3, ctx),
        rows_recv=(ctx,),
        cots_send=(3, ctx),
        cots_recv=(ctx,),
        feed_send=(3, ctx),
        feed_recv=(ctx,),
    )
    b.both(line=ctx, plane=dp, units=max(dp, 4), mixed=ctx)
    if whole:
        for name, lanes in (("qkv", 3 * width), ("fc", columns)):
            packed = (ctx, packed_rows(count, lanes), 128)
            b.hold(WIDE, **{name + "_lanes": (high, full_lanes(lanes))})
            b.hold(WIDE, **{name + "_wide": (rows, full_lanes(lanes))})
            b.hold(LOW, **{name + "_blocks": packed, name + "_landed": packed})
            b.hold(LOW, **{name + "_mat": (dp, rows, lanes)})
            b.both(**{name: ctx, name + "_plane": max(dp, 4)})
        packed = packed_rows(count, D)
        b.hold(WIDE, proj_lanes=(high, full_lanes(D)), proj_wide=(rows, full_lanes(D)))
        b.hold(
            LOW,
            proj_packed=(1, packed, 128),
            proj_blocks=(2, dp, chips * packed, 128),
            proj_mat=(dp, rows, D),
        )
        b.both(proj_plane=max(dp, 4), proj_pair=dp, proj=chips)
    return b.call(functools.partial(forward_kernel, block, whole), 0, "forward")


def back_kernel(
    block,
    grad_ref,
    resid_ref,
    own_cot,
    vectors_ref,
    proj_ref,
    qkv_ref,
    start_ref,
    stat_ref,
    ffn_hbm,
    pre_hbm,
    act_hbm,
    cot_hbm,
    part_hbm,
    resid_out,
    low_out,
    vector_out,
    units_out,
    rows_out,
    share_out,
    output_ref,
    fc_out,
    ffn,
    pre,
    act,
    cot,
    load_sems,
    own_grad,
    head_grad,
    key_t,
    key_grad,
    value_grad,
    *refs,
):
    total = LineSum(*refs[:3], refs[3:7])
    loads = [
        pltpu.make_async_copy(src, dst, load_sems.at[index])
        for index, (src, dst) in enumerate(
            (
                (part_hbm, total.blocks),
                (ffn_hbm, ffn),
                (pre_hbm, pre),
                (act_hbm, act),
                (cot_hbm, cot),
            )
        )
    ]
    for load in loads:
        load.start()
    tokens = own_cot.shape[0]
    length, width = head_grad.shape
    units = share_out.shape[0]
    swap = Swap(
        "ctx",
        lambda peer: own_grad.at[:, pl.ds(pl.multiple_of(peer * width, width), width)],
        lambda origin: head_grad.at[pl.ds(pl.multiple_of(origin * tokens, tokens), tokens)],
        refs[7:9],
    )
    share = PlaneSum(refs[9], refs[10], refs[11:13])
    dp = share.swap.size
    greet_all()
    loads[0].wait()
    total.send_pairs()
    grad = grad_ref[...]
    normed, scale = normalize(resid_ref[...])
    grad_resid = own_cot[...].astype(WIDE) + norm_back(normed, scale, vectors_ref[GAIN_TWO : GAIN_TWO + 1, 0:D], grad)
    resid_out[...] = grad_resid
    low = grad_resid.astype(LOW)
    low_out[...] = low
    own_grad[:, 0:D] = dot(low, proj_ref[...], 1, 1).astype(LOW)
    own_grad[:, D:] = jnp.zeros((tokens, own_grad.shape[1] - D), LOW)
    swap.start()
    head_grad[pl.ds(pl.multiple_of(swap.rank * tokens, tokens), tokens)] = own_grad[
        :, pl.ds(pl.multiple_of(swap.rank * width, width), width)
    ]
    vector_out[0:1] = jnp.sum(grad_resid, 0, keepdims=True)
    vector_out[1:2] = jnp.sum(grad * normed, 0, keepdims=True)
    vector_out[2:3] = jnp.sum(grad, 0, keepdims=True)
    vector_out[3:4] = jnp.sum(own_cot[...].astype(WIDE), 0, keepdims=True)
    vector_out[4:8] = jnp.zeros((4, D), WIDE)
    loads[1].wait()
    loads[2].wait()
    grad_pre = pre[...].reshape(length, -1)
    units_out[...] = dot(jnp.ones((8, length), LOW), grad_pre)
    for index in range(dp):
        rows = slice(index * (D // dp), (index + 1) * (D // dp))
        fc_out[rows] = dot(ffn[:, :, rows].reshape(length, D // dp), grad_pre, 0, 0)
    total.far_steps(0, 1)
    loads[3].wait()
    loads[4].wait()
    for index in range(dp):
        rows = slice(index * units, (index + 1) * units)
        part = dot(act[:, :, rows].reshape(length, units), cot[...].reshape(length, D), 0, 0)
        share.blocks[index] = part.astype(LOW)
    share.start()
    swap.wait()
    chips = total.chips

    def first():
        total.far_steps(1, 2)

    def second():
        total.far_steps(2, 3)
        share.relay()

    attend_back_body(
        block,
        qkv_ref,
        start_ref,
        stat_ref,
        head_grad,
        rows_out,
        key_t,
        key_grad,
        value_grad,
        {1: first, 2: second},
    )
    total.far_steps(3, 2 * chips - 1)
    total.finish(output_ref)
    bias = vectors_ref[BIAS_OUT : BIAS_OUT + 1, 0:D]
    output_ref[...] = output_ref[...] + resid_ref[...] + bias
    share_out[...] = share.total()
    swap.drain()
    share.drain()


def back(
    grad, resid, own_cot, vectors, proj, qkv, doc_start, stats, ffn, pre, act, cot, part, block
):
    ctx, tokens, _ = cot.shape
    dp = lax.axis_size("dp")
    length = ctx * tokens
    width = qkv.shape[1] // 3
    columns = act.shape[2]
    units = columns // dp
    shapes = [
        jax.ShapeDtypeStruct((tokens, D), WIDE),
        jax.ShapeDtypeStruct((tokens, D), LOW),
        jax.ShapeDtypeStruct((8, D), WIDE),
        jax.ShapeDtypeStruct((8, columns), WIDE),
        jax.ShapeDtypeStruct((length, 3 * width), LOW),
        jax.ShapeDtypeStruct((units, D), WIDE),
        jax.ShapeDtypeStruct((tokens, D), WIDE),
        jax.ShapeDtypeStruct((D, columns), WIDE),
    ]
    scratch = [
        pltpu.VMEM(ffn.shape, LOW),
        pltpu.VMEM(pre.shape, LOW),
        pltpu.VMEM(act.shape, LOW),
        pltpu.VMEM(cot.shape, LOW),
        pltpu.SemaphoreType.DMA((5,)),
        pltpu.VMEM((tokens, ctx * width), LOW),
        pltpu.VMEM((length, width), LOW),
        pltpu.VMEM((width, length), LOW),
        pltpu.VMEM((length, width), WIDE),
        pltpu.VMEM((length, width), WIDE),
        *LineSum.scratch(ctx, tokens, D, 4),
        *Swap.semaphores(ctx),
        pltpu.VMEM((dp, units, D), LOW),
        pltpu.VMEM((dp, units, D), LOW),
        *PlaneSum.semaphores(dp),
    ]
    return pl.pallas_call(
        functools.partial(back_kernel, block),
        out_shape=shapes,
        in_specs=[VMEM] * 8 + [HBM] * 5,
        out_specs=[VMEM] * 8,
        scratch_shapes=scratch,
        compiler_params=params(3),
        name="back",
    )(grad, resid, own_cot, vectors, proj, qkv, doc_start, stats, ffn, pre, act, cot, part)


class ProjectionSum:
    def __init__(self, out, mixed, low, plane, wide, blocks, came, pair_sems, sems):
        self.out, self.mixed, self.low, self.plane = out, mixed, low, plane
        self.wide, self.blocks, self.came = wide, blocks, came
        self.send_sems, self.recv_sems = pair_sems
        self.rank = lax.axis_index("ctx")
        self.core = self.rank % 2
        self.swap = ChipSwap(blocks.at.__getitem__, came.at.__getitem__, sems)

    def pair_copies(self):
        return [
            send(
                ref.at[self.core],
                ref.at[self.core],
                self.send_sems.at[index],
                self.recv_sems.at[index],
                ctx=self.rank + 1 - 2 * self.core,
            )
            for index, ref in enumerate((self.mixed, self.low))
        ]

    def start(self, mixed, low):
        self.mixed[self.core] = mixed
        self.low[self.core] = low
        for copy in self.pair_copies():
            copy.start()

    def multiply(self):
        for copy in self.pair_copies():
            copy.wait_recv()
        dp, rows = self.plane.parts.shape[:2]
        chips = self.swap.size
        tokens = 2 * self.low.shape[1]
        count = self.out.shape[0]
        mixed = self.mixed[...].reshape(tokens, -1)[:, 0:D]
        low = self.low[...].reshape(tokens, D)
        feature = lax.broadcasted_iota(jnp.int32, (D, rows), 0)
        column = lax.broadcasted_iota(jnp.int32, (1, rows), 1)
        for index in range(dp):
            owner = index * 2 * chips + column // count * 2 + self.core
            wanted = jnp.where(column < chips * count, owner * count + column % count, -1)
            chosen = jnp.where(feature == wanted, 1.0, 0.0).astype(LOW)
            picked = dot(mixed, chosen).astype(LOW)
            self.plane.put(index, dot(picked, low, 0, 0))

    def cross(self):
        count = self.out.shape[0]
        rows = self.plane.parts.shape[1]
        lanes = full_lanes(D)
        self.wide[0:rows, 0:D] = self.plane.total()
        self.wide[0:rows, D:lanes] = jnp.zeros((rows, lanes - D), WIDE)
        for chip in range(self.swap.size):
            pack(self.blocks, chip, self.wide, chip * count, count, 0, D)
        self.swap.start()

    def wait(self):
        self.swap.wait()
        total = self.blocks[self.swap.rank].astype(WIDE)
        for off in range(1, self.swap.size):
            total = total + self.came[lax.rem(self.swap.rank + off, self.swap.size)].astype(WIDE)
        count = self.out.shape[0]
        unpack(total, self.wide, 0, count, D)
        self.out[...] = self.wide[0:count, 0:D]
        for copy in self.pair_copies():
            copy.wait_send()
        self.swap.drain()


def partial_sums(total, rows_ref, mat):
    chips, tokens = total.chips, total.blocks.shape[1]

    def one(index, carry):
        off = jnp.where(index % 2 == 0, -(index // 2), index // 2 + 1)
        chip = lax.rem(chips - 1 + off, chips)
        rows = pl.ds(pl.multiple_of(2 * chip * tokens, 2 * tokens), 2 * tokens)
        part = dot(rows_ref[rows], mat[...].reshape(D, -1), 1, 1).astype(LOW)
        total.blocks[pl.ds(2 * chip, 2)] = part.reshape(2, tokens, D)
        total.pair_copy(chip).start()
        return carry

    lax.fori_loop(0, chips, one, 0)


def last_kernel(
    rows_ref,
    mat_ref,
    in_ref,
    own_ref,
    resid_ref,
    vectors_ref,
    grad_out,
    vector_out,
    heads_out,
    mat_out,
    grad,
    *refs,
):
    total = LineSum(*refs[:3], refs[3:7])
    chips = total.chips
    dp = lax.axis_size("dp")
    greet_line(chips)
    partial_sums(total, rows_ref, mat_ref)
    total.far_steps(0, 1)
    for index in range(dp):
        rows = slice(index * (D // dp), (index + 1) * (D // dp))
        mat_out[rows] = dot(in_ref[:, rows], rows_ref[...], 0, 0)
    total.far_steps(1, 2 * chips - 1)
    heads_out[...] = dot(jnp.ones((8, rows_ref.shape[0]), LOW), rows_ref[...])
    total.finish(grad)
    normed, scale = normalize(own_ref[...].astype(WIDE))
    incoming = grad[...]
    gain = vectors_ref[GAIN_ONE : GAIN_ONE + 1, 0:D]
    grad_out[...] = resid_ref[...] + norm_back(normed, scale, gain, incoming)
    vector_out[0:1] = jnp.sum(incoming * normed, 0, keepdims=True)
    vector_out[1:2] = jnp.sum(incoming, 0, keepdims=True)
    vector_out[2:8] = jnp.zeros((6, D), WIDE)


def last(rows, mat, attn_in, own_in, resid, vectors):
    ctx = lax.axis_size("ctx")
    tokens = own_in.shape[0]
    columns = rows.shape[1]
    return pl.pallas_call(
        last_kernel,
        out_shape=[
            jax.ShapeDtypeStruct((tokens, D), WIDE),
            jax.ShapeDtypeStruct((8, D), WIDE),
            jax.ShapeDtypeStruct((8, columns), WIDE),
            jax.ShapeDtypeStruct((D, columns), WIDE),
        ],
        in_specs=[VMEM] * 6,
        out_specs=[VMEM] * 4,
        scratch_shapes=[pltpu.VMEM((tokens, D), WIDE), *LineSum.scratch(ctx, tokens, D, 4)],
        compiler_params=params(4),
        name="last",
    )(rows, mat, attn_in, own_in, resid, vectors)


def vector_kernel(parts_ref, out_ref, plane_landed, line_parts, line_landed, *sems):
    seq = lax.axis_index("dp")
    swap = Swap("dp", parts_ref.at.__getitem__, plane_landed.at.__getitem__, sems[:2])
    line = Swap("ctx", line_parts.at.__getitem__, line_landed.at.__getitem__, sems[2:])
    greet_all()
    swap.start()
    swap.wait()
    total = parts_ref[seq]
    for off in range(1, swap.size):
        total = total + plane_landed[lax.rem(seq + off, swap.size)]
    line_parts[...] = total
    line.start()
    line.wait()
    total = line_parts[line.rank]
    for off in range(1, line.size):
        total = total + line_landed[lax.rem(line.rank + off, line.size)]
    out_ref[...] = total
    swap.drain()
    line.drain()


def sum_vector(parts):
    dp, ctx = parts.shape[:2]
    return pl.pallas_call(
        vector_kernel,
        out_shape=jax.ShapeDtypeStruct(parts.shape[2:], WIDE),
        in_specs=[VMEM],
        out_specs=VMEM,
        scratch_shapes=[
            pltpu.VMEM(parts.shape, WIDE),
            pltpu.VMEM(parts.shape[1:], WIDE),
            pltpu.VMEM(parts.shape[1:], WIDE),
            *PlaneSum.semaphores(dp),
            *Swap.semaphores(ctx),
        ],
        compiler_params=params(5),
        name="sum_vector",
    )(parts)


GRAD_ONE, SUM_ONE, SUM_QUERY, SUM_VALUE, SUM_RESID, GRAD_FFN, SUM_FFN = range(7)
SUM_OUT = 11


def backward_kernel(block, names, *refs):
    r = Names(names, refs)
    seq, rank = lax.axis_index("dp"), lax.axis_index("ctx")
    ctx, tokens, _ = r.big.shape
    length, width = r.head_grad.shape
    dp, owners_rows = r.fc_parts.shape[:2]
    units = r.out_parts.shape[1]
    columns = dp * units
    vec_count = 12 * D // (ctx * dp)

    def load(source, target, index):
        return pltpu.make_async_copy(source, target, r.load_sems.at[index])

    summed = LineSum(
        r.out_blocks,
        r.out_pair,
        r.out_passing,
        (r.out_pair_send, r.out_pair_recv, r.out_line_send, r.out_line_recv),
    )
    total = LineSum(
        r.in_blocks,
        r.in_pair,
        r.in_passing,
        (r.in_pair_send, r.in_pair_recv, r.in_line_send, r.in_line_recv),
    )
    chips = total.chips
    to_heads = Swap(
        "ctx",
        lambda peer: r.own_grad.at[:, pl.ds(pl.multiple_of(peer * width, width), width)],
        lambda origin: r.head_grad.at[pl.ds(pl.multiple_of(origin * tokens, tokens), tokens)],
        (r.heads_send, r.heads_recv),
    )
    some = r.stage_fc.at[:, :, pl.ds(0, 3 * width)]
    fc = Collect(
        unit_pieces(ctx, dp),
        StreamSum(
            r.fc_parts, r.fc_landed, r.stage_fc, r.stage_fc_sems, (r.fc_plane_send, r.fc_plane_recv)
        ),
        r.wide,
        r.fc_blocks,
        r.fc_came,
        r.fc_out,
        (r.fc_send, r.fc_recv),
    )
    qkv = Collect(
        head_pieces(ctx, width // HEAD_DIM),
        StreamSum(
            r.qkv_parts, r.qkv_landed, some, r.stage_fc_sems, (r.qkv_plane_send, r.qkv_plane_recv)
        ),
        r.wide,
        r.qkv_blocks,
        r.qkv_came,
        r.qkv_grad,
        (r.qkv_send, r.qkv_recv),
    )
    share = StreamSum(
        r.out_parts,
        r.out_landed,
        r.stage_out,
        r.stage_out_sems,
        (r.out_plane_send, r.out_plane_recv),
    )
    proj = ProjectionSum(
        r.proj_grad,
        r.mixed_pair,
        r.low_pair,
        StreamSum(
            r.proj_parts,
            r.proj_landed,
            r.stage_out,
            r.stage_out_sems,
            (r.proj_plane_send, r.proj_plane_recv),
        ),
        r.wide,
        r.proj_blocks,
        r.proj_came,
        (r.proj_pair_send, r.proj_pair_recv),
        (r.proj_send, r.proj_recv),
    )
    vec_plane = Swap(
        "dp",
        r.vec_parts.at.__getitem__,
        r.vec_landed.at.__getitem__,
        (r.vec_plane_send, r.vec_plane_recv),
    )
    vec_line = Swap(
        "ctx", r.vec_rows.at.__getitem__, r.vec_came.at.__getitem__, (r.vec_send, r.vec_recv)
    )
    heads_mat = r.mat.at[:, :, pl.ds(0, 3 * width)]
    loads = [
        load(r.proj_mat, r.mat, 0),
        load(r.part, r.out_blocks, 1),
        load(r.ffn, r.big, 2),
        load(r.pre_act, r.feed, 3),
        load(r.qkv_mat, heads_mat, 0),
        load(r.attn_in, r.big, 2),
        load(r.act, r.feed, 3),
        load(r.cots, r.big, 2),
    ]
    for index in range(4):
        loads[index].start()
    greet_all()

    grad = r.grad[...]
    normed, scale = normalize(r.resid[...])
    gain = r.vectors[GAIN_TWO : GAIN_TWO + 1, 0:D]
    own_cot = r.own_cot[...].astype(WIDE)
    grad_resid = own_cot + norm_back(normed, scale, gain, grad)
    r.grad_resid[...] = grad_resid
    low = grad_resid.astype(LOW)
    loads[0].wait()
    r.own_grad[:, 0:D] = dot(low, r.mat[...].reshape(D, D), 1, 1).astype(LOW)
    r.own_grad[:, D:] = jnp.zeros((tokens, r.own_grad.shape[1] - D), LOW)
    to_heads.start()
    loads[4].start()
    mine = pl.ds(pl.multiple_of(rank * width, width), width)
    here = pl.ds(pl.multiple_of(rank * tokens, tokens), tokens)
    r.head_grad[here] = r.own_grad[:, mine]
    proj.start(r.own_mixed[...], low)
    loads[1].wait()
    summed.send_pairs()
    vec = r.vec
    vec[...] = jnp.zeros_like(vec)

    def note(row, value):
        vec[row : row + 1, 0:D] = jnp.sum(value, 0, keepdims=True)

    note(SUM_RESID, grad_resid)
    note(GRAD_FFN, grad * normed)
    note(SUM_FFN, grad)
    note(SUM_OUT, own_cot)

    loads[2].wait()
    loads[3].wait()
    grad_pre = r.feed[...].reshape(length, columns)
    sums = dot(jnp.ones((8, length), LOW), grad_pre)[0:1]
    for owner in range(ctx):

        @pl.when(rank == owner)
        def _(owner=owner):
            for place, row, lane, size in unit_bias_pieces(owner, ctx, dp):
                vec[row : row + 1, lane : lane + size] = sums[:, place : place + size]

    def by_parts(plane, left, right, count):
        for index in range(dp):
            rows = slice(index * count, (index + 1) * count)
            plane.put(index, dot(left[:, :, rows].reshape(length, count), right, 0, 0))
        plane.start()

    by_parts(fc.plane, r.big, grad_pre, owners_rows)
    loads[5].start()
    loads[6].start()
    summed.far_steps(0, 1)
    proj.multiply()

    to_heads.wait()

    attend_back_body(
        block,
        r.qkv,
        r.doc_start,
        r.stats,
        r.head_grad,
        r.rows,
        r.key_t,
        r.key_grad,
        r.value_grad,
        {2: lambda: summed.far_steps(1, 2)},
    )
    fc.plane.relay()
    proj.plane.start()
    loads[4].wait()
    partial_sums(total, r.rows, heads_mat)
    total.far_steps(0, 1)
    summed.far_steps(2, 3)
    fc.cross()
    loads[5].wait()
    by_parts(qkv.plane, r.big, r.rows[...], owners_rows)
    loads[7].start()
    total.far_steps(1, 2)
    proj.plane.relay()
    total.far_steps(2, 3)
    summed.far_steps(3, 2 * chips - 1)
    proj.cross()
    qkv.plane.relay()
    loads[6].wait()
    loads[7].wait()
    by_parts(share, r.feed, r.big[...].reshape(length, D), units)
    total.far_steps(3, 2 * chips - 1)
    sums = dot(jnp.ones((8, length), LOW), r.rows[...])
    vec[SUM_QUERY : SUM_QUERY + 1, mine] = sums[0:1, 0:width]
    vec[SUM_VALUE : SUM_VALUE + 1, mine] = sums[0:1, 2 * width :]
    total.finish(r.came)

    incoming = r.came[...]
    normed, scale = normalize(r.own_in[...].astype(WIDE))
    gain = r.vectors[GAIN_ONE : GAIN_ONE + 1, 0:D]
    grad_in = r.grad_resid[...] + norm_back(normed, scale, gain, incoming)
    r.grad_in_t[...] = grad_in.T
    note(GRAD_ONE, incoming * normed)
    note(SUM_ONE, incoming)
    for owner, begin, row, lane, size in vector_pieces(ctx * dp, vec_count):
        r.vec_parts[owner // ctx, owner % ctx, 0:1, begin : begin + size] = vec[
            row : row + 1, lane : lane + size
        ]
    vec_plane.start()
    qkv.cross()
    vec_plane.wait()
    rows = r.vec_parts[seq]
    for off in range(1, dp):
        rows = rows + r.vec_landed[lax.rem(seq + off, dp)]
    r.vec_rows[...] = rows
    vec_line.start()
    summed.finish(r.came)
    bias = r.vectors[BIAS_OUT : BIAS_OUT + 1, 0:D]
    r.output_t[...] = (r.came[...] + r.resid[...] + bias).T
    fc.wait()
    share.relay()
    proj.wait()
    vec_line.wait()
    row = r.vec_rows[rank]
    for off in range(1, ctx):
        row = row + r.vec_came[lax.rem(rank + off, ctx)]
    r.vec_out[...] = row
    qkv.wait()
    r.out_grad[...] = share.total()
    to_heads.drain()
    vec_plane.drain()
    vec_line.drain()


def backward(made, block):
    ctx, dp = lax.axis_size("ctx"), lax.axis_size("dp")
    tokens = made.own_in.shape[0]
    length = ctx * tokens
    width = made.qkv_out.shape[1] // 3
    columns = made.act_out.shape[2]
    units = columns // dp
    chips = ctx // 2
    rows = D // dp
    count = rows // ctx
    lanes = full_lanes(12 * D // (ctx * dp))
    b = Build()
    b.take(
        VMEM,
        grad=made.grad,
        resid=made.resid,
        own_cot=made.own_cot,
        own_in=made.own_in,
        vectors=made.vectors,
        own_mixed=made.own_mixed,
        qkv=made.qkv_out,
        doc_start=made.doc_start,
        stats=made.stats,
    )
    b.take(
        HBM,
        proj_mat=made.proj_mat_out,
        qkv_mat=made.qkv_mat_out,
        part=made.part_out,
        ffn=made.ffn_out,
        pre_act=made.pre_out,
        attn_in=made.attn_in_out,
        act=made.act_out,
        cots=made.cots_out,
    )
    b.give(
        WIDE,
        VMEM,
        output_t=(D, tokens),
        grad_in_t=(D, tokens),
        qkv_grad=(count, 3 * D),
        proj_grad=(count, D),
        fc_out=(count, FF),
        out_grad=(units, D),
        vec_out=(1, lanes),
    )
    for name, shape in (
        ("fc", (rows, columns)),
        ("qkv", (rows, 3 * width)),
        ("out", (units, D)),
        ("proj", (units, D)),
    ):
        b.give(LOW, HBM, **{name + "_parts": (dp, *shape), name + "_landed": (3, *shape)})
        b.both(**{name + "_plane": 6})
    b.hold(
        LOW,
        mat=(dp, rows, D),
        big=(ctx, tokens, D),
        feed=(ctx, tokens, columns),
        stage_fc=(3, rows, columns),
        stage_out=(3, units, D),
        proj_blocks=(chips, packed_rows(count, D), 128),
        proj_came=(chips, packed_rows(count, D), 128),
        mixed_pair=(2, tokens, ctx * width),
        low_pair=(2, tokens, D),
        own_grad=(tokens, ctx * width),
        head_grad=(length, width),
        rows=(length, 3 * width),
        key_t=(width, length),
    )
    for name, wide in (("fc", columns), ("qkv", 3 * width)):
        packed = (ctx, packed_rows(count, wide), 128)
        b.hold(LOW, **{name + "_blocks": packed, name + "_came": packed})
    for name in ("out", "in"):
        b.line_sum(name, ctx, tokens)
    b.hold(
        WIDE,
        wide=(rows, full_lanes(D)),
        key_grad=(length, width),
        value_grad=(length, width),
        grad_resid=(tokens, D),
        came=(tokens, D),
        vec=(ROWS, max(full_lanes(D), ctx * width)),
        vec_parts=(dp, ctx, 1, lanes),
        vec_landed=(dp, ctx, 1, lanes),
        vec_rows=(ctx, 1, lanes),
        vec_came=(ctx, 1, lanes),
    )
    b.both(fc=ctx, qkv=ctx, proj=chips, proj_pair=2, heads=ctx, vec_plane=dp, vec=ctx)
    b.sems(load_sems=(4,), stage_fc_sems=(3,), stage_out_sems=(3,))
    assert units == -(-(chips * count) // 16) * 16
    return b.call(functools.partial(backward_kernel, block), 6, "backward")


def gather_rows(block):
    return lax.all_gather(block, ("dp", "ctx"), axis=0, tiled=True)


def by_rank_heads(rows, ctx, slots):
    count = rows.shape[0]
    split = rows.reshape(count, 3, D)
    split = jnp.pad(split, ((0, 0), (0, 0), (0, (ctx * slots - HEADS) * HEAD_DIM)))
    split = split.reshape(count, 3, ctx, slots * HEAD_DIM)
    return split.transpose(2, 0, 1, 3).reshape(ctx, count, 3 * slots * HEAD_DIM)


def from_rank_heads(blocks, slots):
    ctx, count = blocks.shape[:2]
    split = blocks.reshape(ctx, count, 3, slots * HEAD_DIM).transpose(1, 2, 0, 3)
    return split.reshape(count, 3, ctx * slots * HEAD_DIM)[:, :, :D].reshape(count, 3 * D)


def padded_units(units):
    return -(-units // 16) * 16


def by_rank_units(rows, ctx, dp):
    count = rows.shape[0]
    units = FF // (dp * ctx)
    split = rows.reshape(count, dp, ctx, units).transpose(2, 0, 1, 3)
    split = jnp.pad(split, ((0, 0), (0, 0), (0, 0), (0, padded_units(units) - units)))
    return split.reshape(ctx, count, dp * padded_units(units))


def from_rank_units(blocks, dp):
    ctx, count = blocks.shape[:2]
    units = FF // (dp * ctx)
    split = blocks.reshape(ctx, count, dp, padded_units(units))[..., :units]
    return split.transpose(1, 2, 0, 3).reshape(count, FF)


def shards(
    hidden_in, qkv_weight, proj_weight, fc_weight, out_weight, small_params, segments, cotangent
):
    tokens = hidden_in.shape[1]
    length = segments.shape[1]
    ctx = lax.axis_size("ctx")
    dp = lax.axis_size("dp")
    owners = dp * ctx
    rank = lax.axis_index("ctx")
    slots = -(-HEADS // ctx)
    width = slots * HEAD_DIM
    units = FF // owners
    rows = D // owners
    whole = D % owners == 0 and dp == 4
    block = min(256, length)
    both = ("dp", "ctx")

    vec_count = small_params.shape[0]
    small = jnp.pad(small_params.astype(WIDE), (0, full_lanes(vec_count) - vec_count))[None]
    unit_rows = out_weight.reshape(units, D)
    if whole:
        mats = (
            qkv_weight.reshape(rows, 3 * D),
            fc_weight.reshape(rows, FF),
            proj_weight.reshape(rows, D),
        )
    else:
        mat_qkv = by_rank_heads(gather_rows(qkv_weight).reshape(D, 3 * D), ctx, slots)
        mat_qkv = lax.dynamic_index_in_dim(mat_qkv, rank, 0, keepdims=False)
        mat_fc = by_rank_units(gather_rows(fc_weight).reshape(D, FF), ctx, dp)
        mat_fc = lax.dynamic_index_in_dim(mat_fc, rank, 0, keepdims=False)
        mat_proj = gather_rows(proj_weight).reshape(D, D)
        mats = (mat_qkv, mat_fc, mat_proj)
    made = forward(
        small, hidden_in[0].T, cotangent[0].T, unit_rows, segments, mats, slots, whole, block
    )
    if whole:
        done = backward(made, block)
        return (
            done.output_t.T[None],
            done.grad_in_t.T[None],
            done.qkv_grad.reshape(-1),
            done.proj_grad.reshape(-1),
            done.fc_out.reshape(-1),
            done.out_grad[:units].reshape(-1),
            done.vec_out[0, :vec_count],
        )
    vectors = made.vectors

    grad_resid, resid_low, sums_two, sums_units, grad_rows, grad_out, output, grad_fc = back(
        made.grad,
        made.resid,
        cotangent[0],
        vectors,
        mat_proj,
        made.qkv_out,
        made.doc_start,
        made.stats,
        made.ffn_out,
        made.pre_out,
        made.act_out,
        made.cots_out,
        made.part_out,
        block,
    )
    grad_input, sums_one, sums_heads, grad_qkv = last(
        grad_rows,
        mat_qkv,
        made.attn_in_out.reshape(length, D),
        hidden_in[0],
        grad_resid,
        vectors,
    )
    here = (jnp.arange(ctx) == rank)[:, None, None]
    full_fc = from_rank_units(jnp.where(here, grad_fc[None], 0.0), dp).reshape(-1)
    full_qkv = from_rank_heads(jnp.where(here, grad_qkv[None], 0.0), slots).reshape(-1)
    grad_proj = dot(made.own_mixed[:, :D], resid_low, 0, 0).reshape(-1)
    share_fc, share_qkv, share_proj = [
        lax.psum_scatter(full, both, scatter_dimension=0, tiled=True)
        for full in (full_fc, full_qkv, grad_proj)
    ]

    def spread_heads(part):
        padded = jnp.zeros((ctx * width,), WIDE)
        return lax.dynamic_update_slice_in_dim(padded, part, rank * width, 0)[:D]

    sums_units = sums_units[0].reshape(dp, 1, -1)[:, :, :units]
    sums_units = lax.dynamic_update_slice_in_dim(
        jnp.zeros((dp, ctx, units), WIDE), sums_units, rank, 1
    ).reshape(FF)
    vector = jnp.concatenate(
        [
            sums_one[0],
            sums_one[1],
            spread_heads(sums_heads[0, :width]),
            spread_heads(sums_heads[0, 2 * width :]),
            sums_two[0],
            sums_two[1],
            sums_two[2],
            sums_units,
            sums_two[3],
        ]
    ).reshape(owners, vec_count)
    vec_pad = -(-vec_count // 1024) * 1024
    vector = jnp.pad(vector, ((0, 0), (0, vec_pad - vec_count))).reshape(dp, ctx, -1, 128)
    share_vector = sum_vector(vector)
    return (
        output[None],
        grad_input[None],
        share_qkv.astype(WIDE).reshape(-1),
        share_proj.astype(WIDE).reshape(-1),
        share_fc.astype(WIDE).reshape(-1),
        grad_out[:units].reshape(-1),
        share_vector.reshape(-1)[:vec_count],
    )


def solution(mesh):
    flat = P(("dp", "ctx"))
    rows = P("dp", "ctx", None)
    return jax.shard_map(
        shards,
        mesh=mesh,
        in_specs=(rows, flat, flat, flat, flat, flat, P("dp", None), rows),
        out_specs=(rows, rows, flat, flat, flat, flat, flat),
        check_vma=False,
    )
```
